32 devices in a mesh: grp: 2 (over y), lon: 8 (over z, x), lat: 2 (over core).
Axes of the slice: x: 2, y: 2, z: 4, core: 2. Of those that a mesh axis runs over, the one named last changes fastest.
Arguments:
- tokens: bfloat16 [4, 24, 192, 192], P('grp', 'lat', 'lon'), parts along dimension 0, may hold values from -6 to 6
- cotangent: bfloat16 [4, 24, 192, 192], P('grp', 'lat', 'lon'), parts along dimension 0, may hold values from -6 to 6
- qkv_weight: bfloat16 [2, 192, 576], replicated, may hold values from -0.4375 to 0.4375
- proj_weight: bfloat16 [2, 192, 192], replicated, may hold values from -0.4375 to 0.4375
- up_weight: bfloat16 [2, 192, 768], replicated, may hold values from -0.4375 to 0.4375
- down_weight: bfloat16 [2, 768, 192], replicated, may hold values from -0.21875 to 0.21875
- norm_gain: float32 [2, 2, 192], replicated, may hold values from 0.5 to 1.5
- bias_table: float32 [2, 2, 6, 6336], P(None, 'lat'), may hold values from -4 to 316
Outputs:
- tokens_grad: bfloat16 [4, 24, 192, 192], P('grp', 'lat', 'lon'), parts along dimension 0
- update: bfloat16 [1771008], P('grp'), parts along dimension 0
- bias_grad: float32 [4, 2, 6, 6336], P('grp', 'lat'), parts along dimension 0
The draws below stay inside these ranges and needn't reach their ends.
There are 2 independent parts, one for each index of `grp`. The reference program is written for one: setup_inputs(seed, part) draws one part's arguments, and reference() takes and returns one part's arrays. A program takes and returns all parts, laid end to end along the dimension named above; an argument that names none is the same for every part. Nothing has to cross between parts.
All inputs are finite; a program needn't handle non-finite values.
Results may differ from the reference program's by a relative error of at most 0.02.
Values may be sent and summed in bfloat16 or wider, within the bound.
No kernel may reach another device: no remote copies, remote signals or barrier semaphores. Data moves between devices by JAX's collectives and lax.ppermute only.
A program may use at most 128 MiB of HBM per device.

```python
import jax
import jax.numpy as jnp
from jax import lax

C = 192
HEADS = 6
HID = 768
BLOCKS = 2
LEVELS = 2
WLAT = 12
WLON = 6
PAD = 5
NPOS = 6336
LAT_TOK = 24
LON_TOK = 192
TYPES = 2


def draw_bias_table(key, part):
    key = jax.random.fold_in(key, 7)
    shape = (BLOCKS, TYPES, HEADS, NPOS)
    return jax.random.truncated_normal(key, -4.0, 4.0, shape, jnp.float32)


def shard_levels(key, extent, cuts, smallest, largest):
    def one(axis_at, parts):
        heights = jax.random.uniform(jax.random.fold_in(jax.random.fold_in(key, 6), axis_at), (parts,), jnp.float32, smallest / len(cuts), largest / len(cuts))
        return jnp.repeat(jnp.exp(heights), extent[axis_at] // parts).reshape((-1,) + (1,) * (len(extent) - axis_at - 1))

    level = one(*cuts[0])
    for cut in cuts[1:]:
        level = level * one(*cut)
    return level


def bell_draw(key, shape, deviation, bound, cuts=(), dtype=jnp.bfloat16):
    entries = jax.random.normal(key, shape, jnp.float32) * deviation
    if len(cuts) > 0:
        entries = shard_levels(key, shape, cuts, -0.22, 0.18) * entries
    return jnp.clip(entries, min=-bound, max=bound).astype(dtype)


def setup_inputs(seed: int = 0, part: int = 0) -> dict:
    keys = jax.random.split(jax.random.key(seed), 9)
    part_keys = jax.random.split(jax.random.fold_in(keys[8], part), 9)
    tokens = bell_draw(part_keys[0], (LEVELS, LAT_TOK, LON_TOK, C), 1.0, 6.0, ((1, 2), (2, 8)))
    cotangent = bell_draw(part_keys[1], (LEVELS, LAT_TOK, LON_TOK, C), 1.0, 6.0, ((1, 2), (2, 8)))
    qkv_weight = bell_draw(keys[2], (BLOCKS, C, 3 * C), C ** -0.5, 0.4375)
    proj_weight = bell_draw(keys[3], (BLOCKS, C, C), C ** -0.5, 0.4375)
    up_weight = bell_draw(keys[4], (BLOCKS, C, HID), C ** -0.5, 0.4375)
    down_weight = bell_draw(keys[5], (BLOCKS, HID, C), HID ** -0.5, 0.21875)
    norm_gain = jnp.clip(1.0 + 0.1 * jax.random.normal(keys[6], (BLOCKS, 2, C), jnp.float32), 0.5, 1.5)
    bias_table = draw_bias_table(jax.random.fold_in(keys[8], 71), part)
    return {"tokens": tokens, "cotangent": cotangent, "qkv_weight": qkv_weight, "proj_weight": proj_weight, "up_weight": up_weight, "down_weight": down_weight, "norm_gain": norm_gain, "bias_table": bias_table}


EPS = 1e-05
NEGATIVE = -1000000000.0
ROOT_HALF = 0.7071067811865476
INV_ROOT_TAU = 0.3989422804014327

def norm_forward(field, gain_row):
    average = lax.optimization_barrier(jnp.mean(field, axis=-1, keepdims=True))
    centred = field - average
    variance = lax.optimization_barrier(jnp.mean(centred * centred, axis=-1, keepdims=True))
    inv_std = lax.rsqrt(variance + EPS)
    standard = centred * inv_std
    return (standard * gain_row, standard, inv_std)

def norm_backward(upstream, gain_row, standard, inv_std):
    scaled = upstream * gain_row
    gain_grad = lax.optimization_barrier(jnp.sum(upstream * standard, axis=(0, 1, 2)))
    first_mean = lax.optimization_barrier(jnp.mean(scaled, axis=-1, keepdims=True))
    second_mean = lax.optimization_barrier(jnp.mean(scaled * standard, axis=-1, keepdims=True))
    return (inv_std * (scaled - first_mean - standard * second_mean), gain_grad)

def gelu_value(hidden):
    return 0.5 * hidden * (1.0 + lax.erf(hidden * ROOT_HALF))

def gelu_slope(hidden):
    return 0.5 * (1.0 + lax.erf(hidden * ROOT_HALF)) + hidden * jnp.exp(-0.5 * hidden * hidden) * INV_ROOT_TAU

def token_outer(left, right):
    left_rows = left.reshape(-1, left.shape[-1])
    right_rows = right.reshape(-1, right.shape[-1])
    return lax.dot_general(left_rows, right_rows, (((0,), (0,)), ((), ())), preferred_element_type=jnp.float32)

def to_windows(field):
    levels, lat_rows, lon_cols, width = field.shape
    field = field.reshape(levels, lat_rows // WLAT, WLAT, lon_cols // WLON, WLON, width)
    field = field.transpose(1, 3, 0, 2, 4, 5)
    return field.reshape(lat_rows // WLAT, lon_cols // WLON, levels * WLAT * WLON, width)

def from_windows(windows, levels):
    row_count, col_count, tokens_w, width = windows.shape
    field = windows.reshape(row_count, col_count, levels, WLAT, WLON, width)
    field = field.transpose(2, 0, 3, 1, 4, 5)
    return field.reshape(levels, row_count * WLAT, col_count * WLON, width)

def shift_table():
    query_lon = jnp.arange(WLON)[:, None]
    key_lon = jnp.arange(WLON)[None, :]
    target = (query_lon - key_lon + WLON - 1).reshape(-1)
    return (jnp.arange(2 * WLON - 1)[:, None] == target[None, :]).astype(jnp.float32)

def expand_bias(rows_table, levels):
    row_count, head_count = (rows_table.shape[0], rows_table.shape[1])
    grid = rows_table.reshape(row_count, head_count, levels, levels, WLAT, WLAT, 2 * WLON - 1)
    spread = jnp.dot(grid, shift_table(), precision=lax.Precision.HIGHEST)
    spread = spread.reshape(row_count, head_count, levels, levels, WLAT, WLAT, WLON, WLON)
    spread = spread.transpose(0, 1, 2, 4, 6, 3, 5, 7)
    tokens_w = levels * WLAT * WLON
    return spread.reshape(row_count, head_count, tokens_w, tokens_w)

def fold_bias(full_grad, levels):
    row_count, head_count = (full_grad.shape[0], full_grad.shape[1])
    grid = full_grad.reshape(row_count, head_count, levels, WLAT, WLON, levels, WLAT, WLON)
    grid = grid.transpose(0, 1, 2, 5, 3, 6, 4, 7)
    grid = grid.reshape(row_count, head_count, levels, levels, WLAT, WLAT, WLON * WLON)
    folded = jnp.dot(grid, shift_table().T, precision=lax.Precision.HIGHEST)
    return folded.reshape(row_count, head_count, -1)

def allowed_rows(first_row, row_count, lat_total, levels, shifted):
    tokens_w = levels * WLAT * WLON
    lat_inside = jnp.arange(tokens_w) // WLON % WLAT
    rolled_row = (first_row + jnp.arange(row_count))[:, None] * WLAT + lat_inside[None, :]
    if shifted:
        anchor = (rolled_row + WLAT // 2) % lat_total
        region = rolled_row >= lat_total - WLAT // 2
    else:
        anchor = rolled_row
        region = rolled_row < 0
    usable = anchor < lat_total - PAD
    return usable[:, None, :] & (region[:, :, None] == region[:, None, :])

def row_scores(qkv_row, bias_row, allowed_row, heads):
    window_count, tokens_w, three_width = qkv_row.shape
    head_dim = three_width // (3 * heads)
    split = qkv_row.astype(jnp.float32).reshape(window_count, tokens_w, 3, heads, head_dim)
    queries = split[:, :, 0]
    keys_part = split[:, :, 1]
    values_part = split[:, :, 2]
    logits = jnp.einsum('wihd,wjhd->whij', queries, keys_part) * head_dim ** (-0.5) + bias_row[None]
    logits = jnp.where(allowed_row[None, None], logits, NEGATIVE)
    peak = lax.optimization_barrier(jnp.max(logits, axis=-1, keepdims=True))
    weights = jnp.exp(logits - peak)
    probs = weights / lax.optimization_barrier(jnp.sum(weights, axis=-1, keepdims=True))
    return (probs, queries, keys_part, values_part)

def row_forward(qkv_row, bias_row, allowed_row, heads):
    probs, queries, keys_part, values_part = row_scores(qkv_row, bias_row, allowed_row, heads)
    rounded = lax.optimization_barrier(probs.astype(jnp.bfloat16)).astype(jnp.float32)
    mixed = jnp.einsum('whij,wjhd->wihd', rounded, values_part)
    return mixed.reshape(mixed.shape[0], mixed.shape[1], -1).astype(jnp.bfloat16)

def row_backward(qkv_row, bias_row, allowed_row, dmix_row, heads):
    probs, queries, keys_part, values_part = row_scores(qkv_row, bias_row, allowed_row, heads)
    window_count, tokens_w, head_count, head_dim = queries.shape
    rounded = lax.optimization_barrier(probs.astype(jnp.bfloat16)).astype(jnp.float32)
    upstream = dmix_row.astype(jnp.float32).reshape(window_count, tokens_w, head_count, head_dim)
    prob_grad = jnp.einsum('wihd,wjhd->whij', upstream, values_part)
    logit_grad = probs * (prob_grad - lax.optimization_barrier(jnp.sum(probs * prob_grad, axis=-1, keepdims=True)))
    logit_low = lax.optimization_barrier(logit_grad.astype(jnp.bfloat16)).astype(jnp.float32)
    scale = head_dim ** (-0.5)
    query_grad = jnp.einsum('whij,wjhd->wihd', logit_low, keys_part) * scale
    key_grad = jnp.einsum('whij,wihd->wjhd', logit_low, queries) * scale
    value_grad = jnp.einsum('whij,wihd->wjhd', rounded, upstream)
    qkv_grad = jnp.stack([query_grad, key_grad, value_grad], axis=2)
    qkv_grad = qkv_grad.reshape(window_count, tokens_w, -1).astype(jnp.bfloat16)
    return (qkv_grad, lax.optimization_barrier(jnp.sum(logit_grad, axis=0)))

def roll_ahead(field):
    return jnp.roll(field, (-(WLAT // 2), -(WLON // 2)), axis=(1, 2))

def roll_behind(field):
    return jnp.roll(field, (WLAT // 2, WLON // 2), axis=(1, 2))

def forward_block(field, shifted, weights, heads):
    qkv_w, proj_w, up_w, down_w, gains, bias_rows = weights
    levels, lat_total = (field.shape[0], field.shape[1])
    field32 = field.astype(jnp.float32)
    normed, stand_one, inv_one = norm_forward(field32, gains[0])
    normed = normed.astype(jnp.bfloat16)
    if shifted:
        normed = roll_ahead(normed)
    qkv = jnp.dot(normed, qkv_w, preferred_element_type=jnp.float32).astype(jnp.bfloat16)
    qkv_rows = to_windows(qkv)
    bias_full = expand_bias(bias_rows, levels)
    allowed = allowed_rows(0, bias_rows.shape[0], lat_total, levels, shifted)
    mixed_rows = lax.map(lambda packed: row_forward(packed[0], packed[1], packed[2], heads), (qkv_rows, bias_full, allowed))
    mixed = from_windows(mixed_rows, levels)
    attended = jnp.dot(mixed, proj_w, preferred_element_type=jnp.float32).astype(jnp.bfloat16)
    if shifted:
        attended = roll_behind(attended)
    resid = (field32 + attended.astype(jnp.float32)).astype(jnp.bfloat16)
    resid32 = lax.optimization_barrier(resid).astype(jnp.float32)
    normed_two, stand_two, inv_two = norm_forward(resid32, gains[1])
    normed_two = normed_two.astype(jnp.bfloat16)
    hidden = jnp.dot(normed_two, up_w, preferred_element_type=jnp.float32)
    active = gelu_value(hidden).astype(jnp.bfloat16)
    result = (resid32 + jnp.dot(active, down_w, preferred_element_type=jnp.float32)).astype(jnp.bfloat16)
    saved = (normed, stand_one, inv_one, qkv_rows, bias_full, allowed, mixed, stand_two, inv_two, normed_two, hidden, active)
    return (saved, result)

def backward_block(upstream, saved, shifted, weights, heads):
    qkv_w, proj_w, up_w, down_w, gains, bias_rows = weights
    normed, stand_one, inv_one, qkv_rows, bias_full, allowed, mixed, stand_two, inv_two, normed_two, hidden, active = saved
    levels = normed.shape[0]
    upstream_low = upstream.astype(jnp.bfloat16)
    down_grad = token_outer(active, upstream_low)
    hidden_grad = jnp.dot(upstream_low, down_w.T, preferred_element_type=jnp.float32) * gelu_slope(hidden)
    hidden_grad = hidden_grad.astype(jnp.bfloat16)
    up_grad = token_outer(normed_two, hidden_grad)
    resid_part, gain_two = norm_backward(jnp.dot(hidden_grad, up_w.T, preferred_element_type=jnp.float32), gains[1], stand_two, inv_two)
    resid_grad = upstream + resid_part
    resid_low = resid_grad.astype(jnp.bfloat16)
    if shifted:
        resid_low = roll_ahead(resid_low)
    proj_grad = token_outer(mixed, resid_low)
    mixed_grad = jnp.dot(resid_low, proj_w.T, preferred_element_type=jnp.float32).astype(jnp.bfloat16)
    qkv_grad_rows, logit_rows = lax.map(lambda packed: row_backward(packed[0], packed[1], packed[2], packed[3], heads), (qkv_rows, bias_full, allowed, to_windows(mixed_grad)))
    qkv_grad_field = from_windows(qkv_grad_rows, levels)
    qkv_grad = token_outer(normed, qkv_grad_field)
    normed_grad = jnp.dot(qkv_grad_field, qkv_w.T, preferred_element_type=jnp.float32).astype(jnp.bfloat16)
    if shifted:
        normed_grad = roll_behind(normed_grad)
    field_part, gain_one = norm_backward(normed_grad.astype(jnp.float32), gains[0], stand_one, inv_one)
    bias_grad = fold_bias(logit_rows, levels)
    return (resid_grad + field_part, qkv_grad, proj_grad, up_grad, down_grad, jnp.stack([gain_one, gain_two]), bias_grad)

def reference(tokens, cotangent, qkv_weight, proj_weight, up_weight, down_weight, norm_gain, bias_table):
    heads = bias_table.shape[2]
    lat_total = tokens.shape[1]
    keep_rows = (jnp.arange(lat_total) < lat_total - PAD)[None, :, None, None]
    upstream = jnp.where(keep_rows, cotangent.astype(jnp.float32), jnp.float32(0.0))
    saved_list = []
    field = tokens
    for layer_index in range(BLOCKS):
        weights = (qkv_weight[layer_index], proj_weight[layer_index], up_weight[layer_index], down_weight[layer_index], norm_gain[layer_index], bias_table[layer_index])
        saved, field = forward_block(field, layer_index % 2 == 1, weights, heads)
        saved_list.append(saved)
    outcomes = [None] * BLOCKS
    tokens_grad = tokens
    for layer_index in reversed(range(BLOCKS)):
        weights = (qkv_weight[layer_index], proj_weight[layer_index], up_weight[layer_index], down_weight[layer_index], norm_gain[layer_index], bias_table[layer_index])
        outcome = backward_block(upstream, saved_list[layer_index], layer_index % 2 == 1, weights, heads)
        outcomes[layer_index] = outcome
        tokens_grad = outcome[0].astype(jnp.bfloat16)
        upstream = lax.optimization_barrier(tokens_grad).astype(jnp.float32)
    flat = jnp.concatenate([jnp.stack([entry[1] for entry in outcomes]).reshape(-1), jnp.stack([entry[2] for entry in outcomes]).reshape(-1), jnp.stack([entry[3] for entry in outcomes]).reshape(-1), jnp.stack([entry[4] for entry in outcomes]).reshape(-1), jnp.stack([entry[5] for entry in outcomes]).reshape(-1)])
    update = (flat * lax.rsqrt(jnp.mean(flat * flat) + 1e-06)).astype(jnp.bfloat16)
    bias_grad = jnp.stack([entry[6] for entry in outcomes])
    return (tokens_grad, update, bias_grad)
```

```python
import functools

import jax
import jax.numpy as jnp
import numpy as np
from jax import lax
from jax.experimental import pallas as pl
from jax.experimental.pallas import tpu as pltpu
from jax.sharding import PartitionSpec as P

WLAT = 12
WLON = 6
PAD = 5
LEVELS = 2
HEADS = 6
CHUNK = LEVELS * WLAT
WIN = CHUNK * WLON
SHIFTS = 2 * WLON - 1
PAIR = WLAT * SHIFTS
WIDE = 384

EPS = 1e-05
NEGATIVE = -1000000000.0
ROOT_HALF = 0.7071067811865476
INV_ROOT_TAU = 0.3989422804014327

F32 = jnp.float32
BF16 = jnp.bfloat16
UNIT = 24
BIAS_UNITS = CHUNK * 8 // UNIT * (WIDE // 128)
VMEM_LIMIT = 48 * 1024 * 1024


def dot(a, b):
    return lax.dot_general(a, b, (((1,), (0,)), ((), ())), preferred_element_type=F32)


def dot_nt(a, b):
    return lax.dot_general(a, b, (((1,), (1,)), ((), ())), preferred_element_type=F32)


def dot_tn(a, b):
    return lax.dot_general(a, b, (((0,), (0,)), ((), ())), preferred_element_type=F32)


def row_mean(v):
    return jnp.sum(v, axis=-1, keepdims=True) * (1.0 / v.shape[-1])


def standardize(x):
    centred = x - row_mean(x)
    inv = lax.rsqrt(row_mean(centred * centred) + EPS)
    return centred * inv, inv


def norm_back(d, gain, stand, inv):
    scaled = d * gain
    first = row_mean(scaled)
    second = row_mean(scaled * stand)
    gain_grad = jnp.sum(d * stand, axis=0, keepdims=True)
    return inv * (scaled - first - stand * second), gain_grad


def gelu_parts(hidden):
    half = 0.5 * (1.0 + lax.erf(hidden * ROOT_HALF))
    slope = half + hidden * jnp.exp(-0.5 * hidden * hidden) * INV_ROOT_TAU
    return hidden * half, slope


def split3(v):
    hi = v.astype(BF16)
    rest = v - hi.astype(F32)
    mid = rest.astype(BF16)
    low = (rest - mid.astype(F32)).astype(BF16)
    return hi, mid, low


def spread_matrices():
    out = np.zeros((LEVELS, PAIR, WIDE), np.float32)
    for zj in range(LEVELS):
        for aj in range(WLAT):
            for d in range(SHIFTS):
                out[zj, aj * SHIFTS + d, (SHIFTS - 1 - d) * CHUNK + zj * WLAT + aj] = 1.0
    return out


def put(scr, rows, value):
    width = value.shape[1]
    for tile in range(-(-width // 128)):
        lanes = min(128, width - tile * 128)
        scr[tile, rows, 0:lanes] = value[:, tile * 128 : tile * 128 + lanes]


def get(scr, rows, width):
    parts = [scr[tile, rows, :] for tile in range(-(-width // 128))]
    return jnp.concatenate(parts, axis=1)[:, 0:width]


def head_masks(width, dtype):
    lane = lax.broadcasted_iota(jnp.int32, (1, width), 1)
    size = width // HEADS
    return [((lane >= h * size) & (lane < (h + 1) * size)).astype(dtype) for h in range(HEADS)]


def lat_inside(n):
    return lax.rem(n, WLAT)


def lat_row(row_iota, lat, shifted, lat_total):
    row = lat * WLAT + lat_inside(row_iota)
    if shifted:
        row = row + WLAT // 2
        row = jnp.where(row >= lat_total, row - lat_total, row)
    return row


def expand_bias(table, spread, rows_scr, wide_scr, bias_scr, lat, shifted, lat_total):
    for zi in range(LEVELS):
        for zj in range(LEVELS):
            for ai in range(WLAT):
                at = ((zi * LEVELS + zj) * WLAT + ai) * PAIR
                row = zj * CHUNK * 8 + (zi * WLAT + ai) * 8
                rows_scr[row : row + HEADS, 0:PAIR] = table[:, at : at + PAIR]
    count = CHUNK * 8
    total = jnp.zeros((count, WIDE), F32)
    for zj in range(LEVELS):
        parts = split3(rows_scr[zj * count : (zj + 1) * count, 0:PAIR])
        for part in parts:
            total = total + dot(part, spread[zj])
    put(wide_scr, slice(None), total)
    i = lax.broadcasted_iota(jnp.int32, (CHUNK, WIN), 0)
    j = lax.broadcasted_iota(jnp.int32, (CHUNK, WIN), 1)
    allowed = lat_row(j, lat, shifted, lat_total) < lat_total - PAD
    if shifted:
        last = lat_total - WLAT // 2
        region_i = (lat * WLAT + lat_inside(i)) >= last
        region_j = (lat * WLAT + lat_inside(j)) >= last
        allowed = allowed & (region_i == region_j)
    for h in range(HEADS):
        wide = get(wide_scr, pl.ds(h, CHUNK, stride=8), WIDE)
        for oi in range(WLON):
            back = (WLON - 1 - oi) * CHUNK
            moved = wide if back == 0 else pltpu.roll(wide, WIDE - back, axis=1)
            at = h * WIN + oi * CHUNK
            bias_scr[at : at + CHUNK, :] = jnp.where(allowed, moved[:, 0:WIN], NEGATIVE)


def fold_bias(sums, wide_scr, out):
    wide_scr[...] = jnp.zeros(wide_scr.shape, F32)
    for h in range(HEADS):
        total = jnp.zeros((CHUNK, WIDE), F32)
        for oi in range(WLON):
            back = (WLON - 1 - oi) * CHUNK
            at = h * WIN + oi * CHUNK
            part = sums[at : at + CHUNK, :]
            total = total + (part if back == 0 else pltpu.roll(part, back, axis=1))
        put(wide_scr, pl.ds(h, CHUNK, stride=8), total)
    count, per = out.shape[:2]
    for k in range(count * per):
        tile, at = k % (WIDE // 128), k // (WIDE // 128) * UNIT
        if k < BIAS_UNITS:
            out[k // per, k % per] = wide_scr[tile, at : at + UNIT, :].astype(BF16)
        else:
            out[k // per, k % per] = jnp.zeros((UNIT, 128), BF16)


def attend(qkv, bias, mixed, probs, width):
    masks = head_masks(width, BF16)
    masks32 = head_masks(width, F32)
    scale = (width // HEADS) ** -0.5

    def window(w, carry):
        rows = pl.ds(pl.multiple_of(w * WIN, 16), WIN)
        q = qkv[rows, 0:width]
        k = qkv[rows, width : 2 * width]
        v = qkv[rows, 2 * width : 3 * width]
        total = jnp.zeros((WIN, width), F32)
        for h in range(HEADS):
            logits = dot_nt(q * masks[h], k) * scale + bias[h * WIN : (h + 1) * WIN, :]
            weights = jnp.exp(logits - jnp.max(logits, axis=-1, keepdims=True))
            p = weights * (1.0 / jnp.sum(weights, axis=-1, keepdims=True))
            probs[w, h] = p
            total = total + dot(p.astype(BF16), v) * masks32[h]
        mixed[rows, :] = total.astype(BF16)
        return carry

    lax.fori_loop(0, probs.shape[0], window, 0)


def attend_back(qkv, probs, dmix, field, sums, width):
    masks = head_masks(width, BF16)
    masks32 = head_masks(width, F32)
    scale = (width // HEADS) ** -0.5
    sums[...] = jnp.zeros(sums.shape, F32)

    def window(w, carry):
        rows = pl.ds(pl.multiple_of(w * WIN, 16), WIN)
        q = qkv[rows, 0:width]
        k = qkv[rows, width : 2 * width]
        v = qkv[rows, 2 * width : 3 * width]
        up = dmix[rows, :]
        dq = jnp.zeros((WIN, width), F32)
        dk = jnp.zeros((WIN, width), F32)
        dv = jnp.zeros((WIN, width), F32)
        for h in range(HEADS):
            p = probs[w, h]
            up_h = up * masks[h]
            dp = dot_nt(up_h, v)
            ds = p * (dp - jnp.sum(p * dp, axis=-1, keepdims=True))
            sums[h * WIN : (h + 1) * WIN, 0:WIN] += ds
            low = ds.astype(BF16)
            dq = dq + dot(low, k) * masks32[h]
            dk = dk + dot_tn(low, q * masks[h])
            dv = dv + dot_tn(p.astype(BF16), up_h)
        field[rows, 0:width] = (dq * scale).astype(BF16)
        field[rows, width : 2 * width] = (dk * scale).astype(BF16)
        field[rows, 2 * width : 3 * width] = dv.astype(BF16)
        return carry

    lax.fori_loop(0, probs.shape[0], window, 0)


def lon_major(src, scr):
    levels, lats, lons, width = src.shape
    for z in range(levels):
        for a in range(lats):
            at = (z * lats + a) * lons
            put(scr, slice(at, at + lons), src[z, a].astype(F32))


def lon_column(scr, lon, lons, width):
    return get(scr, pl.ds(lon, CHUNK, stride=lons), width)


def flat_store(dst, at, mat, cols):
    rows = mat.shape[1]
    if cols % 128 == 0:
        per = cols // 128
        for c in range(per):
            dst[pl.ds(at + c, rows, stride=per), :] = mat[c]
        return rows * per
    per = 2 * cols // 128
    half = cols // 128
    even = get(mat, pl.ds(0, rows // 2, stride=2), cols)
    odd = get(mat, pl.ds(1, rows // 2, stride=2), cols)
    for c in range(half):
        dst[pl.ds(at + c, rows // 2, stride=per), :] = even[:, c * 128 : (c + 1) * 128]
    dst[pl.ds(at + half, rows // 2, stride=per), :] = jnp.concatenate(
        [even[:, half * 128 : half * 128 + 64], odd[:, 0:64]], axis=1
    )
    for c in range(half):
        dst[pl.ds(at + half + 1 + c, rows // 2, stride=per), :] = odd[
            :, 64 + c * 128 : 64 + (c + 1) * 128
        ]
    return rows * cols // 128


def send_units(scr, out):
    lats, lons, units = out.shape[:3]
    at = 0
    for i in range(lats):
        for j in range(lons):
            for u in range(units):
                if at < scr.shape[0]:
                    out[i, j, u] = scr[at : at + UNIT, :].astype(BF16)
                else:
                    out[i, j, u] = jnp.zeros((UNIT, 128), BF16)
                at += UNIT


def forward_core(x, b, lat, lat_total, refs, qkv_scr, bias_scr, mixed, probs):
    qkv_w, proj_w, gains = refs
    width = x.shape[-1]
    stand, inv = standardize(x)
    normed = (stand * gains[b, 0:1, :]).astype(BF16)
    qkv_scr[...] = dot(normed, qkv_w[b]).astype(BF16)
    attend(qkv_scr, bias_scr, mixed, probs, width)
    att = dot(mixed[...], proj_w[b]).astype(BF16)
    resid = (x + att.astype(F32)).astype(BF16).astype(F32)
    return resid, normed


def first_kernel(
    lat_total, tokens, table, spread, qkv_w, proj_w, up_w, down_w, gains,
    x_out, tail_out, head_out, qkv_out, mixed_out, probs_out, resid_out, slope_out, active_out,
    scr, rows_scr, wide_scr, bias_scr,
):
    lat = lax.axis_index("lat")
    width = tokens.shape[-1]
    lons = tokens.shape[2]
    expand_bias(
        table.at[0, 0], spread, rows_scr, wide_scr, bias_scr, lat, False, lat_total
    )
    lon_major(tokens, scr)
    x = jnp.concatenate([lon_column(scr, lon, lons, width) for lon in range(lons)], axis=0)
    x_out[...] = x.astype(BF16)
    resid, _ = forward_core(
        x, 0, lat, lat_total, (qkv_w, proj_w, gains), qkv_out, bias_scr, mixed_out, probs_out
    )
    resid_out[...] = resid.astype(BF16)
    stand, _ = standardize(resid)
    normed = (stand * gains[0, 1:2, :]).astype(BF16)
    active, slope = gelu_parts(dot(normed, up_w[0]))
    active = active.astype(BF16)
    active_out[...] = active
    slope_out[...] = slope.astype(BF16)
    result = resid + dot(active, down_w[0])
    cut = CHUNK * (WLON // 2)
    head_out[...] = result[0:cut, :].astype(BF16)
    tail_out[...] = result[cut:, :].astype(BF16)


def merge_ahead(scr_own, scr_oth, rows):
    half = WLAT // 2
    n = lax.broadcasted_iota(jnp.int32, (rows, 1), 0)
    return jnp.where(
        lat_inside(n) < half,
        pltpu.roll(scr_own[...], rows - half, axis=0),
        pltpu.roll(scr_oth[...], half, axis=0),
    )


def merge_behind(scr_own, scr_oth, rows):
    half = WLAT // 2
    n = lax.broadcasted_iota(jnp.int32, (rows, 1), 0)
    return jnp.where(
        lat_inside(n) >= half,
        pltpu.roll(scr_own[...], half, axis=0),
        pltpu.roll(scr_oth[...], rows - half, axis=0),
    )


def second_kernel(
    lat_total,
    tail, lon_head, lat_tail, diag_head, cot, cot_lon, cot_lat, cot_diag,
    table, spread, qkv_w, proj_w, up_w, down_w, gains,
    head_out, tail_out, n1_out, field_out, mixed_out, low_out, n2_out, hg_out, active_out, g_out,
    sums_out, gain_out,
    scr, scr_own, scr_oth, rows_scr, wide_scr, bias_scr, qkv_scr, probs_scr, dmix_scr,
):
    lat = lax.axis_index("lat")
    rows, width = scr_own.shape
    lons = cot.shape[2]
    cut = CHUNK * (WLON // 2)
    step = WLON // 2
    expand_bias(table.at[0, 0], spread, rows_scr, wide_scr, bias_scr, lat, True, lat_total)

    def columns(src, dst, first, last, at):
        lon_major(src, scr)
        for lon in range(first, last):
            dst[at : at + CHUNK, :] = lon_column(scr, lon, lons, width)
            at += CHUNK

    columns(cot, scr_own, step, lons, 0)
    columns(cot_lon, scr_own, 0, step, rows - cut)
    columns(cot_lat, scr_oth, step, lons, 0)
    columns(cot_diag, scr_oth, 0, step, rows - cut)
    g = merge_ahead(scr_own, scr_oth, rows)
    n = lax.broadcasted_iota(jnp.int32, (rows, 1), 0)
    keep = lat_row(n, lat, True, lat_total) < lat_total - PAD
    g = jnp.where(keep, g, 0.0)
    g_out[...] = g.astype(BF16)

    scr_own[0 : rows - cut, :] = tail[...].astype(F32)
    scr_own[rows - cut :, :] = lon_head[...].astype(F32)
    scr_oth[0 : rows - cut, :] = lat_tail[...].astype(F32)
    scr_oth[rows - cut :, :] = diag_head[...].astype(F32)
    x = merge_ahead(scr_own, scr_oth, rows)

    resid, normed = forward_core(
        x, 1, lat, lat_total, (qkv_w, proj_w, gains), qkv_scr, bias_scr, mixed_out, probs_scr
    )
    n1_out[...] = normed
    stand2, inv2 = standardize(resid)
    normed2 = (stand2 * gains[1, 1:2, :]).astype(BF16)
    n2_out[...] = normed2
    active, slope = gelu_parts(dot(normed2, up_w[1]))
    active_out[...] = active.astype(BF16)

    hg = (dot_nt(g_out[...], down_w[1]) * slope).astype(BF16)
    hg_out[...] = hg
    part, gain_two = norm_back(dot_nt(hg, up_w[1]), gains[1, 1:2, :], stand2, inv2)
    rg = g + part
    low = rg.astype(BF16)
    low_out[...] = low
    dmix_scr[...] = dot_nt(low, proj_w[1]).astype(BF16)
    attend_back(qkv_scr, probs_scr, dmix_scr, field_out, sums_out, width)
    ng = dot_nt(field_out[...], qkv_w[1]).astype(BF16).astype(F32)
    stand1, inv1 = standardize(x)
    part, gain_one = norm_back(ng, gains[1, 0:1, :], stand1, inv1)
    dx = rg + part
    head_out[...] = dx[0 : rows - cut, :].astype(BF16)
    tail_out[...] = dx[rows - cut :, :].astype(BF16)
    gain_out[0:1, :] = gain_one
    gain_out[1:2, :] = gain_two


def outer_kernel(
    n1, field, mixed, low, n2, hg, active, g, sums,
    flat_out, bias_out,
    m576, m192, m768, mdown, flat_scr, wide_scr,
):
    put(m576, slice(None), dot_tn(n1[...], field[...]))
    at = flat_store(flat_scr, 0, m576, field.shape[1])
    put(m192, slice(None), dot_tn(mixed[...], low[...]))
    at += flat_store(flat_scr, at, m192, mixed.shape[1])
    put(m768, slice(None), dot_tn(n2[...], hg[...]))
    at += flat_store(flat_scr, at, m768, active.shape[1])
    put(mdown, slice(None), dot_tn(active[...], g[...]))
    at += flat_store(flat_scr, at, mdown, mixed.shape[1])
    send_units(flat_scr, flat_out)
    fold_bias(sums, wide_scr, bias_out)


def third_kernel(
    head, lon_tail, lat_head, diag_tail, resid_in, slope, active, mixed,
    proj_w, up_w, down_w, gains,
    flat_out, rg_out, dmix_out, gain_out,
    scr_own, scr_oth, m192, m768, mdown, flat_scr,
):
    rows, width = scr_own.shape
    cut = CHUNK * (WLON // 2)
    scr_own[0:cut, :] = lon_tail[...].astype(F32)
    scr_own[cut:, :] = head[...].astype(F32)
    scr_oth[0:cut, :] = diag_tail[...].astype(F32)
    scr_oth[cut:, :] = lat_head[...].astype(F32)
    g = merge_behind(scr_own, scr_oth, rows)
    g_low = g.astype(BF16)
    hg = (dot_nt(g_low, down_w[0]) * slope[...].astype(F32)).astype(BF16)
    stand2, inv2 = standardize(resid_in[...].astype(F32))
    normed2 = (stand2 * gains[0, 1:2, :]).astype(BF16)
    part, gain_two = norm_back(dot_nt(hg, up_w[0]), gains[0, 1:2, :], stand2, inv2)
    rg = g + part
    rg_out[...] = rg
    low = rg.astype(BF16)
    dmix_out[...] = dot_nt(low, proj_w[0]).astype(BF16)
    gain_out[...] = gain_two
    put(m192, slice(None), dot_tn(mixed[...], low))
    at = flat_store(flat_scr, 0, m192, mixed.shape[1])
    put(m768, slice(None), dot_tn(normed2, hg))
    at += flat_store(flat_scr, at, m768, active.shape[1])
    put(mdown, slice(None), dot_tn(active[...], g_low))
    at += flat_store(flat_scr, at, mdown, mixed.shape[1])
    send_units(flat_scr, flat_out)


def gain_rows(one, two):
    return jnp.concatenate(
        [
            one[:, 0:128],
            jnp.concatenate([one[:, 128:192], two[:, 0:64]], axis=1),
            two[:, 64:192],
        ],
        axis=0,
    )


def fourth_kernel(
    x_in, qkv, probs, dmix, rg, gain_two, gains_late, qkv_w, gains,
    flat_out, bias_out, tokens_out,
    field, sums, m576, flat_scr, wide_scr, dx_scr,
):
    width = x_in.shape[-1]
    levels, lats, lons = tokens_out.shape[:3]
    attend_back(qkv, probs, dmix, field, sums, width)
    stand1, inv1 = standardize(x_in[...].astype(F32))
    normed = (stand1 * gains[0, 0:1, :]).astype(BF16)
    ng = dot_nt(field[...], qkv_w[0]).astype(BF16).astype(F32)
    part, gain_one = norm_back(ng, gains[0, 0:1, :], stand1, inv1)
    put(m576, slice(None), dot_tn(normed, field[...]))
    at = flat_store(flat_scr, 0, m576, field.shape[1])
    flat_scr[at:, :] = jnp.zeros((flat_scr.shape[0] - at, 128), F32)
    flat_scr[at : at + 3, :] = gain_rows(gain_one, gain_two[...])
    flat_scr[at + 3 : at + 6, :] = gain_rows(gains_late[0:1, :], gains_late[1:2, :])
    send_units(flat_scr, flat_out)
    fold_bias(sums, wide_scr, bias_out)
    put(dx_scr, slice(None), rg[...] + part)
    for z in range(levels):
        for a in range(lats):
            tokens_out[z, a] = get(
                dx_scr, pl.ds(z * lats + a, lons, stride=CHUNK), width
            ).astype(BF16)


def last_kernel(
    own_a, oth_a, own_b, oth_b, own_c, oth_c, spread, update_out, bias_out,
    scr, rows_scr, wide_scr,
):
    lat = lax.axis_index("lat")
    lons = own_a.shape[0]
    extra = -(-BIAS_UNITS // lons)

    def place(own, oth, dests):
        total = jnp.zeros((UNIT, 128), F32)
        per = oth.shape[1]
        k = 0
        for where, room in dests:
            for at in range(where, where + room * UNIT, UNIT):
                half, j, u = k // (per * lons), k // per % lons, k % per
                value = jnp.where(lat == half, own[j, u], oth[j, u]).astype(F32)
                scr[at : at + UNIT, :] = value
                total = total + value * value
                k += 1
        return total

    total = place(own_a, oth_a, [(864, 36), (2016, 12), (3456, 48), (5760, 48)])
    total = total + place(own_b, oth_b, [(1728, 12), (2304, 48), (4608, 48)])
    total = total + place(own_c, oth_c, [(0, 36), (6912, 1)])
    count = update_out.shape[0]
    mean = jnp.sum(total) * (1.0 / (count * 128))
    scale = lax.rsqrt(mean + 1e-06)
    update_out[...] = (scr[0:count, :] * scale).astype(BF16)

    for b, piece in enumerate((own_c, own_a)):
        base = piece.shape[1] - extra
        for k in range(BIAS_UNITS):
            tile, at = k % (WIDE // 128), k // (WIDE // 128) * UNIT
            value = piece[k // extra, base + k % extra]
            wide_scr[tile, at : at + UNIT, :] = value.astype(F32)
        low = get(wide_scr, slice(None), WIDE).astype(BF16)
        for zj in range(LEVELS):
            rows_scr[...] = dot_nt(low, spread[zj])
            for zi in range(LEVELS):
                for ai in range(WLAT):
                    at = ((zi * LEVELS + zj) * WLAT + ai) * PAIR
                    row = (zi * WLAT + ai) * 8
                    bias_out[b, 0, :, at : at + PAIR] = rows_scr[row : row + HEADS, 0:PAIR]


def call(kernel, outs, scratch, args, flops=0, moved=0):
    specs = []
    for arg in args:
        specs.append(pl.BlockSpec(memory_space=pltpu.VMEM))
    return pl.pallas_call(
        kernel,
        out_shape=[jax.ShapeDtypeStruct(shape, dtype) for shape, dtype in outs],
        in_specs=specs,
        out_specs=[pl.BlockSpec(memory_space=pltpu.VMEM)] * len(outs),
        scratch_shapes=[pltpu.VMEM(shape, dtype) for shape, dtype in scratch],
        compiler_params=pltpu.CompilerParams(vmem_limit_bytes=VMEM_LIMIT),
        cost_estimate=pl.CostEstimate(flops=flops, bytes_accessed=moved, transcendentals=0),
    )(*args)


def send(value, axes, pairs):
    return lax.ppermute(value, axes, pairs)


def lat_swap(value):
    return lax.ppermute(value, "lat", [(0, 1), (1, 0)])


def lon_send(value, step):
    count = lax.axis_size("lon")
    return lax.ppermute(value, "lon", [(s, (s + step) % count) for s in range(count)])


def diag_send(value, step):
    count = lax.axis_size("lon")
    pairs = []
    for s in range(count):
        for t in range(2):
            pairs.append((2 * s + t, 2 * ((s + step) % count) + 1 - t))
    return lax.ppermute(value, ("lon", "lat"), pairs)


def scatter_sum(flat, bias):
    lat = lax.axis_index("lat")
    mine = lax.dynamic_index_in_dim(flat, lat, 0, keepdims=False)
    theirs = lax.dynamic_index_in_dim(flat, 1 - lat, 0, keepdims=False)
    got = lat_swap(theirs)
    part = (mine.astype(F32) + got.astype(F32)).astype(BF16)
    if bias is not None:
        part = jnp.concatenate([part, bias], axis=1)
    pieces = lax.all_to_all(part, "lon", 0, 0)
    return jnp.sum(pieces.astype(F32), axis=0).astype(BF16)


def gather(piece, units):
    count = lax.axis_size("lon")
    whole = lax.all_to_all(jnp.broadcast_to(piece[None], (count,) + piece.shape), "lon", 0, 0)
    return whole, lat_swap(whole[:, :units])


def shards(
    tokens, cotangent, qkv_weight, proj_weight, up_weight, down_weight, norm_gain, bias_table
):
    levels, lats, lons, width = tokens.shape
    rows = levels * lats * lons
    wins = rows // WIN
    hid = up_weight.shape[-1]
    heads = bias_table.shape[2]
    lon_size = lax.axis_size("lon")
    lat_total = lats * lax.axis_size("lat")
    cut = CHUNK * (WLON // 2)
    spread = jnp.asarray(spread_matrices(), BF16)
    token = (rows, width)
    bias_scr = ((heads * WIN, WIN), F32)
    sums_shape = ((heads * WIN, WIDE), F32)
    rows_scr = ((LEVELS * CHUNK * 8, PAIR), F32)
    wide_scr = ((WIDE // 128, CHUNK * 8, 128), F32)
    tiles = -(-width // 128)
    token_scr = ((tiles, rows, 128), F32)
    m576 = ((-(-3 * width // 128), width, 128), F32)
    m192 = ((tiles, width, 128), F32)
    m768 = ((hid // 128, width, 128), F32)
    mdown = ((tiles, hid, 128), F32)
    field_shape = ((rows, 3 * width), BF16)

    cot_lon = lon_send(cotangent, -1)
    cot_lat = lat_swap(cotangent)
    cot_diag = diag_send(cotangent, -1)

    x0, tail, head, qkv0, mixed0, probs0, resid0, slope0, active0 = call(
        functools.partial(first_kernel, lat_total),
        [
            (token, BF16),
            ((rows - cut, width), BF16),
            ((cut, width), BF16),
            field_shape,
            (token, BF16),
            ((wins, heads, WIN, WIN), F32),
            (token, BF16),
            ((rows, hid), BF16),
            ((rows, hid), BF16),
        ],
        [token_scr, rows_scr, wide_scr, bias_scr],
        (tokens, bias_table[0:1], spread, qkv_weight, proj_weight, up_weight, down_weight, norm_gain),
        flops=10**9 * 6,
        moved=10**7,
    )
    lon_head = lon_send(head, -1)
    diag_head = diag_send(head, -1)
    lat_tail = lat_swap(tail)

    (
        dhead, dtail, n1, field1, mixed1, low1, n2, hg1, active1, g1, sums1, gains1,
    ) = call(
        functools.partial(second_kernel, lat_total),
        [
            ((rows - cut, width), BF16),
            ((cut, width), BF16),
            (token, BF16),
            field_shape,
            (token, BF16),
            (token, BF16),
            (token, BF16),
            ((rows, hid), BF16),
            ((rows, hid), BF16),
            (token, BF16),
            sums_shape,
            ((2, width), F32),
        ],
        [
            token_scr,
            (token, F32),
            (token, F32),
            rows_scr,
            wide_scr,
            bias_scr,
            field_shape,
            ((wins, heads, WIN, WIN), F32),
            (token, BF16),
        ],
        (
            tail, lon_head, lat_tail, diag_head, cotangent, cot_lon, cot_lat, cot_diag,
            bias_table[1:2], spread, qkv_weight, proj_weight, up_weight, down_weight, norm_gain,
        ),
        flops=10**9 * 10,
        moved=10**7,
    )
    lon_tail = lon_send(dtail, 1)
    diag_tail = diag_send(dtail, 1)
    lat_dhead = lat_swap(dhead)

    total_a = (qkv_weight[0].size + proj_weight[0].size + 2 * up_weight[0].size) // 128
    units_a, units_b, units_c = [-(-count // (2 * lon_size)) for count in (total_a // UNIT, 108, 37)]
    extra = -(-BIAS_UNITS // lon_size)
    flat_a, bias_a = call(
        outer_kernel,
        [((2, lon_size, units_a, UNIT, 128), BF16), ((lon_size, extra, UNIT, 128), BF16)],
        [
            m576,
            m192,
            m768,
            mdown,
            ((total_a, 128), F32),
            wide_scr,
        ],
        (n1, field1, mixed1, low1, n2, hg1, active1, g1, sums1),
        flops=10**9 * 6,
        moved=10**7,
    )

    flat_b, rg0, dmix0, gain_two = call(
        third_kernel,
        [
            ((2, lon_size, units_b, UNIT, 128), BF16),
            (token, F32),
            (token, BF16),
            ((1, width), F32),
        ],
        [
            (token, F32),
            (token, F32),
            m192,
            m768,
            mdown,
            ((108 * UNIT, 128), F32),
        ],
        (
            dhead, lon_tail, lat_dhead, diag_tail, resid0, slope0, active0, mixed0,
            proj_weight, up_weight, down_weight, norm_gain,
        ),
        flops=10**9 * 6,
        moved=10**7,
    )

    flat_c, bias_c, tokens_grad = call(
        fourth_kernel,
        [
            ((2, lon_size, units_c, UNIT, 128), BF16),
            ((lon_size, extra, UNIT, 128), BF16),
            (tokens.shape, BF16),
        ],
        [
            field_shape,
            sums_shape,
            m576,
            ((37 * UNIT, 128), F32),
            wide_scr,
            token_scr,
        ],
        (x0, qkv0, probs0, dmix0, rg0, gain_two, gains1, qkv_weight, norm_gain),
        flops=10**9 * 6,
        moved=10**7,
    )

    own_a, oth_a = gather(scatter_sum(flat_a, bias_a), units_a)
    own_b, oth_b = gather(scatter_sum(flat_b, None), units_b)
    own_c, oth_c = gather(scatter_sum(flat_c, bias_c), units_c)

    flat_rows = (
        2 * (qkv_weight[0].size + proj_weight[0].size + 2 * up_weight[0].size) + norm_gain.size
    ) // 128
    update, bias_grad = call(
        last_kernel,
        [((flat_rows, 128), BF16), (bias_table.shape, F32)],
        [((flat_rows + 18, 128), F32), ((CHUNK * 8, PAIR), F32), wide_scr],
        (own_a, oth_a, own_b, oth_b, own_c, oth_c, spread),
        flops=10**9,
        moved=10**7,
    )
    return (tokens_grad, update.reshape(-1), bias_grad)


def solution(mesh):
    return jax.shard_map(
        shards,
        mesh=mesh,
        in_specs=(
            P("grp", "lat", "lon", None),
            P("grp", "lat", "lon", None),
            P(),
            P(),
            P(),
            P(),
            P(),
            P(None, "lat", None, None),
        ),
        out_specs=(P("grp", "lat", "lon", None), P("grp"), P("grp", "lat", None, None)),
        check_vma=False,
    )
```

```python
import functools

import jax
import jax.numpy as jnp
import numpy as np
from jax import lax
from jax.experimental import pallas as pl
from jax.experimental.pallas import tpu as pltpu
from jax.sharding import PartitionSpec as P

WLAT = 12
WLON = 6
PAD = 5
LEVELS = 2
HEADS = 6
CHUNK = LEVELS * WLAT
WIN = CHUNK * WLON
SHIFTS = 2 * WLON - 1
PAIR = WLAT * SHIFTS
WIDE = 384

EPS = 1e-05
NEGATIVE = -1000000000.0
ROOT_HALF = 0.7071067811865476
INV_ROOT_TAU = 0.3989422804014327

F32 = jnp.float32
BF16 = jnp.bfloat16
UNIT = 8
BIAS_UNITS = (2 * HEADS + 1) * CHUNK // UNIT
MIB = 1024 * 1024


def dot(a, b):
    return lax.dot_general(a, b, (((1,), (0,)), ((), ())), preferred_element_type=F32)


def dot_nt(a, b):
    return lax.dot_general(a, b, (((1,), (1,)), ((), ())), preferred_element_type=F32)


def dot_tn(a, b):
    return lax.dot_general(a, b, (((0,), (0,)), ((), ())), preferred_element_type=F32)


def row_mean(v):
    return jnp.sum(v, axis=-1, keepdims=True) * (1.0 / v.shape[-1])


def standardize(x):
    centred = x - row_mean(x)
    inv = lax.rsqrt(row_mean(centred * centred) + EPS)
    return centred * inv, inv


def norm_back(d, gain, stand, inv):
    scaled = d * gain
    first = row_mean(scaled)
    second = row_mean(scaled * stand)
    gain_grad = jnp.sum(d * stand, axis=0, keepdims=True)
    return inv * (scaled - first - stand * second), gain_grad


def gelu_parts(hidden):
    half = 0.5 * (1.0 + lax.erf(hidden * ROOT_HALF))
    slope = half + hidden * jnp.exp(-0.5 * hidden * hidden) * INV_ROOT_TAU
    return hidden * half, slope


def split3(v):
    hi = v.astype(BF16)
    rest = v - hi.astype(F32)
    mid = rest.astype(BF16)
    low = (rest - mid.astype(F32)).astype(BF16)
    return hi, mid, low


def spread_matrices():
    out = np.zeros((LEVELS, PAIR, WIDE), np.float32)
    for zj in range(LEVELS):
        for aj in range(WLAT):
            for d in range(SHIFTS):
                out[zj, aj * SHIFTS + d, (SHIFTS - 1 - d) * CHUNK + zj * WLAT + aj] = 1.0
    return out


def put(scr, rows, value):
    width = value.shape[1]
    for tile in range(-(-width // 128)):
        lanes = min(128, width - tile * 128)
        scr[tile, rows, 0:lanes] = value[:, tile * 128 : tile * 128 + lanes]


def get(scr, rows, width):
    parts = [scr[tile, rows, :] for tile in range(-(-width // 128))]
    return jnp.concatenate(parts, axis=1)[:, 0:width]


def head_masks(width, dtype):
    lane = lax.broadcasted_iota(jnp.int32, (1, width), 1)
    size = width // HEADS
    return [((lane >= h * size) & (lane < (h + 1) * size)).astype(dtype) for h in range(HEADS)]


def lat_inside(n):
    return lax.rem(n, WLAT)


def lat_row(row_iota, lat, shifted, lat_total):
    row = lat * WLAT + lat_inside(row_iota)
    if shifted:
        row = row + WLAT // 2
        row = jnp.where(row >= lat_total, row - lat_total, row)
    return row


def expand_bias(table, spread, tab_scr, rows_scr, wide_scr, bias_scr, lat, shifted, lat_total):
    for h in range(HEADS):
        tab_scr[h : h + 1, :] = table[h]
    for zi in range(LEVELS):
        for zj in range(LEVELS):
            for ai in range(WLAT):
                at = ((zi * LEVELS + zj) * WLAT + ai) * PAIR
                row = zj * CHUNK * 8 + (zi * WLAT + ai) * 8
                rows_scr[row : row + HEADS, 0:PAIR] = tab_scr[0:HEADS, at : at + PAIR]
    count = CHUNK * 8
    total = jnp.zeros((count, WIDE), F32)
    for zj in range(LEVELS):
        parts = split3(rows_scr[zj * count : (zj + 1) * count, 0:PAIR])
        for part in parts:
            total = total + dot(part, spread[zj])
    put(wide_scr, slice(None), total)
    i = lax.broadcasted_iota(jnp.int32, (CHUNK, WIN), 0)
    j = lax.broadcasted_iota(jnp.int32, (CHUNK, WIN), 1)
    allowed = lat_row(j, lat, shifted, lat_total) < lat_total - PAD
    if shifted:
        last = lat_total - WLAT // 2
        region_i = (lat * WLAT + lat_inside(i)) >= last
        region_j = (lat * WLAT + lat_inside(j)) >= last
        allowed = allowed & (region_i == region_j)
    for h in range(HEADS):
        wide = get(wide_scr, pl.ds(h, CHUNK, stride=8), WIDE)
        for oi in range(WLON):
            back = (WLON - 1 - oi) * CHUNK
            moved = wide if back == 0 else pltpu.roll(wide, WIDE - back, axis=1)
            at = h * WIN + oi * CHUNK
            bias_scr[at : at + CHUNK, :] = jnp.where(allowed, moved[:, 0:WIN], NEGATIVE)


def fold_bias(sums, put_unit):
    rest = jnp.zeros((CHUNK, 128), F32)

    def emit(at, value):
        for r in range(CHUNK // UNIT):
            put_unit(at * (CHUNK // UNIT) + r, value[r * UNIT : (r + 1) * UNIT, :].astype(BF16))

    for h in range(HEADS):
        total = jnp.zeros((CHUNK, WIDE), F32)
        for oi in range(WLON):
            back = (WLON - 1 - oi) * CHUNK
            at = h * WIN + oi * CHUNK
            part = sums[at : at + CHUNK, :]
            total = total + (part if back == 0 else pltpu.roll(part, back, axis=1))
        emit(h, total[:, 0:128])
        emit(HEADS + h, total[:, 128:256])
        last = total[:, 256:384]
        rest = rest + (last if h == 0 else pltpu.roll(last, 8 * h, axis=1))
    emit(2 * HEADS, rest)

def attend(qkv, bias, mixed, probs, width):
    masks = head_masks(width, BF16)
    masks32 = head_masks(width, F32)
    scale = (width // HEADS) ** -0.5

    def window(w, carry):
        rows = pl.ds(pl.multiple_of(w * WIN, 16), WIN)
        q = qkv[rows, 0:width]
        k = qkv[rows, width : 2 * width]
        v = qkv[rows, 2 * width : 3 * width]
        total = jnp.zeros((WIN, width), F32)
        for h in range(HEADS):
            logits = dot_nt(q * masks[h], k) * scale + bias[h * WIN : (h + 1) * WIN, :]
            weights = jnp.exp(logits - jnp.max(logits, axis=-1, keepdims=True))
            p = weights * (1.0 / jnp.sum(weights, axis=-1, keepdims=True))
            probs[w, h] = p
            total = total + dot(p.astype(BF16), v) * masks32[h]
        mixed[rows, :] = total.astype(BF16)
        return carry

    lax.fori_loop(0, probs.shape[0], window, 0)


def attend_back(qkv, probs, dmix, field, sums, width, first, last):
    masks = head_masks(width, BF16)
    masks32 = head_masks(width, F32)
    scale = (width // HEADS) ** -0.5

    def window(w, carry):
        rows = pl.ds(pl.multiple_of(w * WIN, 16), WIN)
        q = qkv[rows, 0:width]
        k = qkv[rows, width : 2 * width]
        v = qkv[rows, 2 * width : 3 * width]
        up = dmix[rows, :]
        dq = jnp.zeros((WIN, width), F32)
        dk = jnp.zeros((WIN, width), F32)
        dv = jnp.zeros((WIN, width), F32)
        for h in range(HEADS):
            p = probs[w, h]
            up_h = up * masks[h]
            dp = dot_nt(up_h, v)
            ds = p * (dp - jnp.sum(p * dp, axis=-1, keepdims=True))
            sums[h * WIN : (h + 1) * WIN, 0:WIN] += ds
            low = ds.astype(BF16)
            dq = dq + dot(low, k) * masks32[h]
            dk = dk + dot_tn(low, q * masks[h])
            dv = dv + dot_tn(p.astype(BF16), up_h)
        field[rows, 0:width] = (dq * scale).astype(BF16)
        field[rows, width : 2 * width] = (dk * scale).astype(BF16)
        field[rows, 2 * width : 3 * width] = dv.astype(BF16)
        return carry

    lax.fori_loop(first, last, window, 0)


def lon_major(src, scr):
    levels, lats, lons, width = src.shape
    for z in range(levels):
        for a in range(lats):
            at = (z * lats + a) * lons
            put(scr, slice(at, at + lons), src[z, a].astype(F32))


def lon_column(scr, lon, lons, width):
    return get(scr, pl.ds(lon, CHUNK, stride=lons), width)


def flat_store(dst, at, mat, cols):
    rows = mat.shape[1]
    if cols % 128 == 0:
        per = cols // 128
        for c in range(per):
            dst[pl.ds(at + c, rows, stride=per), :] = mat[c]
        return rows * per
    per = 2 * cols // 128
    half = cols // 128
    even = get(mat, pl.ds(0, rows // 2, stride=2), cols)
    odd = get(mat, pl.ds(1, rows // 2, stride=2), cols)
    for c in range(half):
        dst[pl.ds(at + c, rows // 2, stride=per), :] = even[:, c * 128 : (c + 1) * 128]
    dst[pl.ds(at + half, rows // 2, stride=per), :] = jnp.concatenate(
        [even[:, half * 128 : half * 128 + 64], odd[:, 0:64]], axis=1
    )
    for c in range(half):
        dst[pl.ds(at + half + 1 + c, rows // 2, stride=per), :] = odd[
            :, 64 + c * 128 : 64 + (c + 1) * 128
        ]
    return rows * cols // 128


def send_units(scr, base, out):
    lons, units = out.shape[:2]
    for j in range(lons):
        for u in range(units):
            at = base + (j * units + u) * UNIT
            if not isinstance(at, int):
                at = pl.multiple_of(at, UNIT)
            out[j, u] = scr[pl.ds(at, UNIT), :].astype(BF16)


def halves(scr, lat, keep, give):
    half = keep.shape[0] * keep.shape[1] * UNIT
    send_units(scr, lat * half, keep)
    send_units(scr, (1 - lat) * half, give)


def bias_units(sums, out):
    lons, per = out.shape[:2]

    def put_unit(k, value):
        out[k // per, k % per] = value

    fold_bias(sums, put_unit)
    for k in range(BIAS_UNITS, lons * per):
        put_unit(k, jnp.zeros((UNIT, 128), BF16))

def forward_core(x, b, lat, lat_total, refs, qkv_scr, bias_scr, mixed, probs):
    qkv_w, proj_w, gains = refs
    width = x.shape[-1]
    stand, inv = standardize(x)
    normed = (stand * gains[b, 0:1, :]).astype(BF16)
    qkv_scr[...] = dot(normed, qkv_w[b]).astype(BF16)
    attend(qkv_scr, bias_scr, mixed, probs, width)
    att = dot(mixed[...], proj_w[b]).astype(BF16)
    resid = (x + att.astype(F32)).astype(BF16).astype(F32)
    return resid, normed


def first_kernel(
    lat_total, tokens, cot, table, spread, qkv_w, proj_w, up_w, down_w, gains,
    x_out, tail_out, head_out, qkv_out, mixed_out, probs_out, resid_out, slope_out, active_out,
    scr, cot_scr, tab_scr, rows_scr, wide_scr, bias_scr,
):
    lat = lax.axis_index("lat")
    width = tokens.shape[-1]
    lons = tokens.shape[2]
    cut = CHUNK * (WLON // 2)
    lon_major(cot, cot_scr)
    g = jnp.concatenate([lon_column(cot_scr, lon, lons, width) for lon in range(lons)], axis=0)
    head_out[1] = g[0:cut, :].astype(BF16)
    tail_out[1] = g[cut:, :].astype(BF16)
    expand_bias(
        table.at[0], spread, tab_scr, rows_scr, wide_scr, bias_scr, lat, False, lat_total
    )
    lon_major(tokens, scr)
    x = jnp.concatenate([lon_column(scr, lon, lons, width) for lon in range(lons)], axis=0)
    x_out[...] = x.astype(BF16)
    resid, _ = forward_core(
        x, 0, lat, lat_total, (qkv_w, proj_w, gains), qkv_out, bias_scr, mixed_out, probs_out
    )
    resid_out[...] = resid.astype(BF16)
    stand, _ = standardize(resid)
    normed = (stand * gains[0, 1:2, :]).astype(BF16)
    active, slope = gelu_parts(dot(normed, up_w[0]))
    active = active.astype(BF16)
    active_out[...] = active
    slope_out[...] = slope.astype(BF16)
    result = resid + dot_nt(active, down_w[0])
    head_out[0] = result[0:cut, :].astype(BF16)
    tail_out[0] = result[cut:, :].astype(BF16)


def bias_kernel(lat_total, table, spread, bias_out, tab_scr, rows_scr, wide_scr):
    lat = lax.axis_index("lat")
    expand_bias(
        table.at[1], spread, tab_scr, rows_scr, wide_scr, bias_out, lat, True, lat_total
    )


def merge_ahead(scr_own, scr_oth, rows):
    half = WLAT // 2
    n = lax.broadcasted_iota(jnp.int32, (rows, 1), 0)
    return jnp.where(
        lat_inside(n) < half,
        pltpu.roll(scr_own[...], rows - half, axis=0),
        pltpu.roll(scr_oth[...], half, axis=0),
    )


def merge_behind(scr_own, scr_oth, rows):
    half = WLAT // 2
    n = lax.broadcasted_iota(jnp.int32, (rows, 1), 0)
    return jnp.where(
        lat_inside(n) >= half,
        pltpu.roll(scr_own[...], half, axis=0),
        pltpu.roll(scr_oth[...], rows - half, axis=0),
    )


def second_kernel(
    lat_total,
    tail, lon_head, lat_tail, diag_head, bias, qkv_w, proj_w, up_w, down_w, gains,
    head_out, tail_out, n1_out, field_out, mixed_out, low_out, n2_out, hg_out, active_out, g_out,
    sums_out, gain_out,
    scr_own, scr_oth, qkv_scr, probs_scr, dmix_scr,
):
    lat = lax.axis_index("lat")
    rows, width = scr_own.shape
    cut = CHUNK * (WLON // 2)

    def rolled(which):
        scr_own[0 : rows - cut, :] = tail[which].astype(F32)
        scr_own[rows - cut :, :] = lon_head[which].astype(F32)
        scr_oth[0 : rows - cut, :] = lat_tail[which].astype(F32)
        scr_oth[rows - cut :, :] = diag_head[which].astype(F32)
        return merge_ahead(scr_own, scr_oth, rows)

    g = rolled(1)
    n = lax.broadcasted_iota(jnp.int32, (rows, 1), 0)
    keep = lat_row(n, lat, True, lat_total) < lat_total - PAD
    g = jnp.where(keep, g, 0.0)
    g_out[...] = g.astype(BF16)

    x = rolled(0)

    resid, normed = forward_core(
        x, 1, lat, lat_total, (qkv_w, proj_w, gains), qkv_scr, bias, mixed_out, probs_scr
    )
    n1_out[...] = normed
    stand2, inv2 = standardize(resid)
    normed2 = (stand2 * gains[1, 1:2, :]).astype(BF16)
    n2_out[...] = normed2
    active, slope = gelu_parts(dot(normed2, up_w[1]))
    active_out[...] = active.astype(BF16)

    hg = (dot(g_out[...], down_w[1]) * slope).astype(BF16)
    hg_out[...] = hg
    part, gain_two = norm_back(dot_nt(hg, up_w[1]), gains[1, 1:2, :], stand2, inv2)
    rg = g + part
    low = rg.astype(BF16)
    low_out[...] = low
    dmix_scr[...] = dot_nt(low, proj_w[1]).astype(BF16)
    sums_out[...] = jnp.zeros(sums_out.shape, F32)
    attend_back(
        qkv_scr, probs_scr, dmix_scr, field_out, sums_out, width, 0, probs_scr.shape[0]
    )
    ng = dot_nt(field_out[...], qkv_w[1]).astype(BF16).astype(F32)
    stand1, inv1 = standardize(x)
    part, gain_one = norm_back(ng, gains[1, 0:1, :], stand1, inv1)
    dx = rg + part
    head_out[...] = dx[0 : rows - cut, :].astype(BF16)
    tail_out[...] = dx[rows - cut :, :].astype(BF16)
    gain_out[0:1, :] = gain_one
    gain_out[1:2, :] = gain_two


def outer_kernel(
    n1, field, mixed, low, n2, hg, active, g, sums,
    keep, give, bias_out,
    m576, m192, m768, mdown, flat_scr,
):
    put(m576, slice(None), dot_tn(n1[...], field[...]))
    at = flat_store(flat_scr, 0, m576, field.shape[1])
    put(m192, slice(None), dot_tn(mixed[...], low[...]))
    at += flat_store(flat_scr, at, m192, mixed.shape[1])
    put(m768, slice(None), dot_tn(n2[...], hg[...]))
    at += flat_store(flat_scr, at, m768, active.shape[1])
    put(mdown, slice(None), dot_tn(active[...], g[...]))
    at += flat_store(flat_scr, at, mdown, mixed.shape[1])
    halves(flat_scr, lax.axis_index("lat"), keep, give)
    bias_units(sums, bias_out)


def split_x(x, keep, got, bias, keep_out, give_out):
    units = keep.shape[1]
    for z in range(keep_out.shape[0]):
        for out, side in ((keep_out, x), (give_out, 1 - x)):
            at = 2 * z + side
            out[z, 0:units] = (keep[at].astype(F32) + got[at].astype(F32)).astype(BF16)
            if bias is not None:
                out[z, units:] = bias[at]


def split_z(z, keep, got, own_out, *give_outs):
    count = keep.shape[0]
    for k, out in enumerate((own_out,) + give_outs):
        at = lax.rem(z + k, count)
        out[...] = (keep[at].astype(F32) + got[at].astype(F32)).astype(BF16)


def sum_all(*refs):
    total = refs[0][...].astype(F32)
    for ref in refs[1:-1]:
        total = total + ref[...].astype(F32)
    refs[-1][...] = total.astype(BF16)


def join_z(z, *refs):
    count = len(refs) - 1
    for k in range(count):
        refs[-1][lax.rem(z + count - k, count)] = refs[k][...]


def join_x(x, mine, other, whole_out, flat_out):
    units = flat_out.shape[1]
    for z in range(mine.shape[0]):
        whole_out[2 * z + x] = mine[z]
        whole_out[2 * z + 1 - x] = other[z]
        flat_out[2 * z + x] = mine[z, 0:units]
        flat_out[2 * z + 1 - x] = other[z, 0:units]


def third_kernel(
    head, lon_tail, lat_head, diag_tail, resid_in, slope, active, mixed,
    proj_w, up_w, down_w, gains, keep_a, got_a, bias_a,
    keep_out, give_out, rg_out, dmix_out, gain_out, keep_xa, give_xa,
    scr_own, scr_oth, m192, m768, mdown, flat_scr,
):
    split_x(lax.rem(lax.axis_index("lon"), 2), keep_a, got_a, bias_a, keep_xa, give_xa)
    rows, width = scr_own.shape
    cut = CHUNK * (WLON // 2)
    scr_own[0:cut, :] = lon_tail[...].astype(F32)
    scr_own[cut:, :] = head[...].astype(F32)
    scr_oth[0:cut, :] = diag_tail[...].astype(F32)
    scr_oth[cut:, :] = lat_head[...].astype(F32)
    g = merge_behind(scr_own, scr_oth, rows)
    g_low = g.astype(BF16)
    hg = (dot(g_low, down_w[0]) * slope[...].astype(F32)).astype(BF16)
    stand2, inv2 = standardize(resid_in[...].astype(F32))
    normed2 = (stand2 * gains[0, 1:2, :]).astype(BF16)
    part, gain_two = norm_back(dot_nt(hg, up_w[0]), gains[0, 1:2, :], stand2, inv2)
    rg = g + part
    rg_out[...] = rg
    low = rg.astype(BF16)
    dmix_out[...] = dot_nt(low, proj_w[0]).astype(BF16)
    gain_out[...] = gain_two
    put(m192, slice(None), dot_tn(mixed[...], low))
    at = flat_store(flat_scr, 0, m192, mixed.shape[1])
    put(m768, slice(None), dot_tn(normed2, hg))
    at += flat_store(flat_scr, at, m768, active.shape[1])
    put(mdown, slice(None), dot_tn(active[...], g_low))
    at += flat_store(flat_scr, at, mdown, mixed.shape[1])
    flat_scr[at:, :] = jnp.zeros((flat_scr.shape[0] - at, 128), F32)
    halves(flat_scr, lax.axis_index("lat"), keep_out, give_out)


def gain_rows(one, two):
    return jnp.concatenate(
        [
            one[:, 0:128],
            jnp.concatenate([one[:, 128:192], two[:, 0:64]], axis=1),
            two[:, 64:192],
        ],
        axis=0,
    )


def fourth_kernel(qkv, probs, dmix, field_out, sums_out):
    width = dmix.shape[-1]
    sums_out[...] = jnp.zeros(sums_out.shape, F32)
    attend_back(qkv, probs, dmix, field_out, sums_out, width, 0, probs.shape[0] // 2)


def fifth_kernel(
    x_in, qkv, probs, dmix, rg, gain_two, gains_late, field_in, sums_in, order, qkv_w, gains,
    tokens_out, own_out, *rest,
):
    field, sums, m576, flat_scr, dx_scr, bias_scr = rest[-6:]
    rest = rest[:-6]
    width = x_in.shape[-1]
    levels, lats, lons = tokens_out.shape[:3]
    done = probs.shape[0] // 2 * WIN
    field[0:done, :] = field_in[...]
    sums[...] = sums_in[...]
    attend_back(qkv, probs, dmix, field, sums, width, probs.shape[0] // 2, probs.shape[0])
    stand1, inv1 = standardize(x_in[...].astype(F32))
    normed = (stand1 * gains[0, 0:1, :]).astype(BF16)
    ng = dot_nt(field[...], qkv_w[0]).astype(BF16).astype(F32)
    part, gain_one = norm_back(ng, gains[0, 0:1, :], stand1, inv1)
    put(m576, slice(None), dot_tn(normed, field[...]))
    at = flat_store(flat_scr, 0, m576, field.shape[1])
    flat_scr[at:, :] = jnp.zeros((flat_scr.shape[0] - at, 128), F32)
    flat_scr[at : at + 3, :] = gain_rows(gain_one, gain_two[...])
    flat_scr[at + 3 : at + 6, :] = gain_rows(gains_late[0:1, :], gains_late[1:2, :])
    bias_units(sums, bias_scr)
    lat, lon = lax.axis_index("lat"), lax.axis_index("lon")
    count = (len(rest) + 1) // 2
    extra = bias_scr.shape[1]
    units = own_out.shape[0] - extra
    for k in range(count):
        to = lax.rem(lon + k, count)
        same = own_out if k == 0 else rest[k - 1]
        for out, side in ((same, lat), (rest[count - 1 + k], 1 - lat)):
            base = (side * count + to) * (units * UNIT)
            for u in range(units):
                out[u] = flat_scr[pl.ds(pl.multiple_of(base + u * UNIT, UNIT), UNIT), :].astype(BF16)
        same[units:] = bias_scr[to]
    put(dx_scr, slice(None), rg[...] + part)
    for z in range(levels):
        for a in range(lats):
            tokens_out[z, a] = get(
                dx_scr, pl.ds(z * lats + a, lons, stride=CHUNK), width
            ).astype(BF16)


def sum_direct(*refs):
    out = refs[-1]
    fulls = [ref for ref in refs[:-1] if ref.shape == out.shape]
    flats = [ref for ref in refs[:-1] if ref.shape != out.shape]
    units = flats[0].shape[0]
    total = fulls[0][...].astype(F32)
    for ref in fulls[1:]:
        total = total + ref[...].astype(F32)
    part = total[0:units]
    for ref in flats:
        part = part + ref[...].astype(F32)
    out[0:units] = part.astype(BF16)
    out[units:] = total[units:].astype(BF16)


def step_one(keep_xa, got_xa, keep_b, got_b, *outs):
    lon = lax.axis_index("lon")
    split_x(lax.rem(lon, 2), keep_b, got_b, None, outs[0], outs[1])
    split_z(lax.div(lon, 2), keep_xa, got_xa, *outs[2:])


def step_two(zs, *refs):
    lon = lax.axis_index("lon")
    a_in, keep_xb, got_xb = refs[:zs], refs[zs], refs[zs + 1]
    outs = refs[zs + 2 :]
    sum_all(*a_in, outs[0])
    split_z(lax.div(lon, 2), keep_xb, got_xb, *outs[1:])


def step_three(zs, fulls, *refs):
    lon = lax.axis_index("lon")
    c_in, a_in, b_in = refs[:fulls], refs[fulls : fulls + zs], refs[fulls + zs : fulls + 2 * zs]
    c_out, a_out, b_out = refs[fulls + 2 * zs :]
    sum_direct(*c_in, c_out)
    join_z(lax.div(lon, 2), *a_in, a_out)
    sum_all(*b_in, b_out)


def step_four(zs, mine_a, other_a, *refs):
    lon = lax.axis_index("lon")
    b_in = refs[:zs]
    whole_a, flat_a, join_b = refs[zs:]
    join_x(lax.rem(lon, 2), mine_a, other_a, whole_a, flat_a)
    join_z(lax.div(lon, 2), *b_in, join_b)


def step_five(mine_b, other_b, whole_b, flat_b):
    join_x(lax.rem(lax.axis_index("lon"), 2), mine_b, other_b, whole_b, flat_b)


def last_kernel(spread, own_a, oth_a, own_b, oth_b, *refs):
    update_out, bias_out, scr, rows_scr, wide_scr, c_own, c_oth = refs[-7:]
    pieces = refs[:-7]
    lat, lon = lax.axis_index("lat"), lax.axis_index("lon")
    lons = own_a.shape[0]
    for k in range(lons):
        at = lax.rem(lon + lons - k, lons)
        c_own[at] = pieces[k][...]
        c_oth[at] = pieces[lons + k][...]
    extra = -(-BIAS_UNITS // lons)

    def place(own, oth, dests):
        total = jnp.zeros((UNIT, 128), F32)
        per = oth.shape[1]
        k = 0
        for where, room in dests:
            for at in range(where, where + room, UNIT):
                half, j, u = k // (per * lons), k // per % lons, k % per
                value = jnp.where(lat == half, own[j, u].astype(F32), oth[j, u].astype(F32))
                scr[at : at + UNIT, :] = value
                total = total + value * value
                k += 1
        return total

    total = place(own_a, oth_a, [(864, 864), (2016, 288), (3456, 1152), (5760, 1152)])
    total = total + place(own_b, oth_b, [(1728, 288), (2304, 1152), (4608, 1152)])
    total = total + place(c_own, c_oth, [(0, 864), (6912, 8)])
    count = update_out.shape[0]
    mean = jnp.sum(total) * (1.0 / (count * 128))
    scale = lax.rsqrt(mean + 1e-06)
    update_out[...] = (scr[0:count, :] * scale).astype(BF16)

    for b, piece in enumerate((c_own, own_a)):
        base = piece.shape[1] - extra

        def read(at):
            parts = []
            for r in range(CHUNK // UNIT):
                k = at * (CHUNK // UNIT) + r
                parts.append(piece[k // extra, base + k % extra].astype(F32))
            return jnp.concatenate(parts, axis=0)

        rest = read(2 * HEADS)
        for h in range(HEADS):
            rows = pl.ds(h, CHUNK, stride=8)
            wide_scr[0, rows, :] = read(h)
            wide_scr[1, rows, :] = read(HEADS + h)
            wide_scr[2, rows, :] = rest if h == 0 else pltpu.roll(rest, 128 - 8 * h, axis=1)
        low = get(wide_scr, slice(None), WIDE).astype(BF16)
        for zj in range(LEVELS):
            rows_scr[...] = dot_nt(low, spread[zj])
            for zi in range(LEVELS):
                for ai in range(WLAT):
                    at = ((zi * LEVELS + zj) * WLAT + ai) * PAIR
                    row = (zi * WLAT + ai) * 8
                    bias_out[b, 0, :, at : at + PAIR] = rows_scr[row : row + HEADS, 0:PAIR]


def call(kernel, outs, scratch, args, micros, mib):
    return pl.pallas_call(
        kernel,
        out_shape=[jax.ShapeDtypeStruct(shape, dtype) for shape, dtype in outs],
        in_specs=[pl.BlockSpec(memory_space=pltpu.VMEM)] * len(args),
        out_specs=[pl.BlockSpec(memory_space=pltpu.VMEM)] * len(outs),
        scratch_shapes=[pltpu.VMEM(shape, dtype) for shape, dtype in scratch],
        compiler_params=pltpu.CompilerParams(vmem_limit_bytes=mib * MIB),
        cost_estimate=pl.CostEstimate(
            flops=int(micros * 1.1e9), bytes_accessed=10**5, transcendentals=0
        ),
    )(*args)


def lat_swap(value):
    return lax.ppermute(value, "lat", [(0, 1), (1, 0)])


def lon_send(value, step):
    count = lax.axis_size("lon")
    return lax.ppermute(value, "lon", [(s, (s + step) % count) for s in range(count)])


def x_swap(value):
    count = lax.axis_size("lon")
    return lax.ppermute(value, "lon", [(s, s ^ 1) for s in range(count)])


def diag_send(value, step):
    count = lax.axis_size("lon")
    pairs = []
    for s in range(count):
        for t in range(2):
            pairs.append((2 * s + t, 2 * ((s + step) % count) + 1 - t))
    return lax.ppermute(value, ("lon", "lat"), pairs)


def shards(
    tokens, cotangent, qkv_weight, proj_weight, up_weight, down_weight, norm_gain, bias_table
):
    levels, lats, lons, width = tokens.shape
    rows = levels * lats * lons
    wins = rows // WIN
    hid = up_weight.shape[-1]
    heads = bias_table.shape[2]
    lon_size = lax.axis_size("lon")
    zs = lon_size // 2
    lat_total = lats * lax.axis_size("lat")
    cut = CHUNK * (WLON // 2)
    spread = jnp.asarray(spread_matrices(), BF16)
    down_turned = jnp.swapaxes(down_weight, 1, 2)
    table = jnp.swapaxes(bias_table, 1, 2)
    token = (rows, width)
    field_shape = ((rows, 3 * width), BF16)
    probs_shape = ((wins, heads, WIN, WIN), F32)
    bias_shape = ((heads * WIN, WIN), F32)
    sums_shape = ((heads * WIN, WIDE), F32)
    tab_scr = ((8, table.shape[-1]), F32)
    rows_scr = ((LEVELS * CHUNK * 8, PAIR), F32)
    wide_scr = ((WIDE // 128, CHUNK * 8, 128), F32)
    tiles = -(-width // 128)
    token_scr = ((tiles, rows, 128), F32)
    m576 = ((-(-3 * width // 128), width, 128), F32)
    m192 = ((tiles, width, 128), F32)
    m768 = ((hid // 128, width, 128), F32)
    mdown = ((tiles, hid, 128), F32)

    block_rows = (qkv_weight[0].size + proj_weight[0].size + 2 * up_weight[0].size) // 128
    qkv_rows = qkv_weight[0].size // 128
    counts = (block_rows, block_rows - qkv_rows, qkv_rows + 8)
    units_a, units_b, units_c = [-(-count // (2 * lon_size * UNIT)) for count in counts]
    extra = -(-BIAS_UNITS // lon_size)

    def units(*lead):
        return (lead + (UNIT, 128), BF16)

    def flat_scr(per):
        return ((2 * lon_size * per * UNIT, 128), F32)

    x0, tail, head, qkv0, mixed0, probs0, resid0, slope0, active0 = call(
        functools.partial(first_kernel, lat_total),
        [
            (token, BF16),
            ((2, rows - cut, width), BF16),
            ((2, cut, width), BF16),
            field_shape,
            (token, BF16),
            probs_shape,
            (token, BF16),
            ((rows, hid), BF16),
            ((rows, hid), BF16),
        ],
        [token_scr, token_scr, tab_scr, rows_scr, wide_scr, bias_shape],
        (
            tokens, cotangent, table, spread, qkv_weight, proj_weight, up_weight, down_turned,
            norm_gain,
        ),
        9,
        28,
    )
    lon_head = lon_send(head, -1)
    diag_head = diag_send(head, -1)
    lat_tail = lat_swap(tail)
    (bias1,) = call(
        functools.partial(bias_kernel, lat_total),
        [bias_shape],
        [tab_scr, rows_scr, wide_scr],
        (table, spread),
        2,
        10,
    )

    (
        dhead, dtail, n1, field1, mixed1, low1, n2, hg1, active1, g1, sums1, gains1,
    ) = call(
        functools.partial(second_kernel, lat_total),
        [
            ((rows - cut, width), BF16),
            ((cut, width), BF16),
            (token, BF16),
            field_shape,
            (token, BF16),
            (token, BF16),
            (token, BF16),
            ((rows, hid), BF16),
            ((rows, hid), BF16),
            (token, BF16),
            sums_shape,
            ((2, width), F32),
        ],
        [(token, F32), (token, F32), field_shape, probs_shape, (token, BF16)],
        (
            tail, lon_head, lat_tail, diag_head, bias1, qkv_weight, proj_weight, up_weight,
            down_turned, norm_gain,
        ),
        19,
        28,
    )
    lon_tail = lon_send(dtail, 1)
    diag_tail = diag_send(dtail, 1)
    lat_dhead = lat_swap(dhead)

    keep_a, give_a, bias_a = call(
        outer_kernel,
        [units(lon_size, units_a), units(lon_size, units_a), units(lon_size, extra)],
        [m576, m192, m768, mdown, flat_scr(units_a)],
        (n1, field1, mixed1, low1, n2, hg1, active1, g1, sums1),
        3,
        20,
    )
    got_a = lat_swap(give_a)

    keep_b, give_b, rg0, dmix0, gain_two, keep_xa, give_xa = call(
        third_kernel,
        [
            units(lon_size, units_b),
            units(lon_size, units_b),
            (token, F32),
            (token, BF16),
            ((1, width), F32),
            units(zs, units_a + extra),
            units(zs, units_a + extra),
        ],
        [(token, F32), (token, F32), m192, m768, mdown, flat_scr(units_b)],
        (
            dhead, lon_tail, lat_dhead, diag_tail, resid0, slope0, active0, mixed0,
            proj_weight, up_weight, down_turned, norm_gain, keep_a, got_a, bias_a,
        ),
        3,
        20,
    )
    got_b = lat_swap(give_b)
    got_xa = x_swap(give_xa)

    field0, sums0 = call(
        fourth_kernel,
        [((wins // 2 * WIN, 3 * width), BF16), sums_shape],
        [],
        (qkv0, probs0, dmix0),
        6,
        20,
    )
    stepped = call(
        step_one,
        [units(zs, units_b)] * 2 + [units(units_a + extra)] * zs,
        [],
        (keep_xa, got_xa, keep_b, got_b),
        1,
        10,
    )
    keep_xb, give_xb = stepped[:2]
    own_a, gives_a = stepped[2], stepped[3:]
    got_xb = x_swap(give_xb)
    gots_a = [lon_send(give, 2 * (k + 1)) for k, give in enumerate(gives_a)]

    fulls, flats = [units(units_c + extra)] * lon_size, [units(units_c)] * lon_size
    finished = call(
        fifth_kernel,
        [(tokens.shape, BF16)] + fulls + flats,
        [
            field_shape,
            sums_shape,
            m576,
            flat_scr(units_c),
            token_scr,
            units(lon_size, extra),
        ],
        (
            x0, qkv0, probs0, dmix0, rg0, gain_two, gains1, field0, sums0, own_a, qkv_weight,
            norm_gain,
        ),
        7,
        24,
    )
    tokens_grad = finished[0]
    same, cross = finished[1 : 1 + lon_size], finished[1 + lon_size :]

    def spread_direct(same, cross):
        fulls = [same[0]] + [lon_send(same[k], k) for k in range(1, lon_size)]
        flats = [lat_swap(cross[0])] + [diag_send(cross[k], k) for k in range(1, lon_size)]
        return fulls + flats

    gots_c = spread_direct(same, cross)

    stepped = call(
        functools.partial(step_two, zs),
        [units(units_a + extra)] + [units(units_b)] * zs,
        [],
        (own_a, *gots_a, keep_xb, got_xb),
        1,
        10,
    )
    sum_a, own_b, gives_b = stepped[0], stepped[1], stepped[2:]
    gots_b = [lon_send(give, 2 * (k + 1)) for k, give in enumerate(gives_b)]
    all_a = [sum_a] + [lon_send(sum_a, 2 * k) for k in range(1, zs)]

    sum_c, join_a, sum_b = call(
        functools.partial(step_three, zs, 2 * lon_size),
        [units(units_c + extra), units(zs, units_a + extra), units(units_b)],
        [],
        (*gots_c, *all_a, own_b, *gots_b),
        1,
        10,
    )
    flat_c = sum_c[:units_c]
    pieces_c = spread_direct([sum_c] * lon_size, [flat_c] * lon_size)
    all_b = [sum_b] + [lon_send(sum_b, 2 * k) for k in range(1, zs)]
    other_a = x_swap(join_a)

    whole_a, flat_a, join_b = call(
        functools.partial(step_four, zs),
        [units(lon_size, units_a + extra), units(lon_size, units_a), units(zs, units_b)],
        [],
        (join_a, other_a, *all_b),
        1,
        10,
    )
    oth_a = lat_swap(flat_a)
    other_b = x_swap(join_b)
    whole_b, flat_b = call(
        step_five,
        [units(lon_size, units_b), units(lon_size, units_b)],
        [],
        (join_b, other_b),
        1,
        10,
    )
    oth_b = lat_swap(flat_b)

    flat_rows = (2 * block_rows * 128 + norm_gain.size) // 128
    update, bias_grad = call(
        last_kernel,
        [((flat_rows, 128), BF16), (bias_table.shape, F32)],
        [
            ((flat_rows + 2, 128), F32),
            ((CHUNK * 8, PAIR), F32),
            wide_scr,
            units(lon_size, units_c + extra),
            units(lon_size, units_c),
        ],
        (spread, whole_a, oth_a, whole_b, oth_b, *pieces_c),
        3,
        20,
    )
    return (tokens_grad, update.reshape(-1), bias_grad)


def solution(mesh):
    return jax.shard_map(
        shards,
        mesh=mesh,
        in_specs=(
            P("grp", "lat", "lon", None),
            P("grp", "lat", "lon", None),
            P(),
            P(),
            P(),
            P(),
            P(),
            P(None, "lat", None, None),
        ),
        out_specs=(P("grp", "lat", "lon", None), P("grp"), P("grp", "lat", None, None)),
        check_vma=False,
    )
```

```python
import functools

import jax
import jax.numpy as jnp
import numpy as np
from jax import lax
from jax.experimental import pallas as pl
from jax.experimental.pallas import tpu as pltpu
from jax.sharding import PartitionSpec as P

WLAT = 12
WLON = 6
PAD = 5
LEVELS = 2
HEADS = 6
CHUNK = LEVELS * WLAT
WIN = CHUNK * WLON
SHIFTS = 2 * WLON - 1
PAIR = WLAT * SHIFTS
WIDE = 384

EPS = 1e-05
NEGATIVE = -1000000000.0
ROOT_HALF = 0.7071067811865476
INV_ROOT_TAU = 0.3989422804014327

F32 = jnp.float32
BF16 = jnp.bfloat16
UNIT = 8
BIAS_UNITS = (2 * HEADS + 1) * CHUNK // UNIT
MIB = 1024 * 1024


def dot(a, b):
    return lax.dot_general(a, b, (((1,), (0,)), ((), ())), preferred_element_type=F32)


def dot_nt(a, b):
    return lax.dot_general(a, b, (((1,), (1,)), ((), ())), preferred_element_type=F32)


def dot_tn(a, b):
    return lax.dot_general(a, b, (((0,), (0,)), ((), ())), preferred_element_type=F32)


def row_mean(v):
    return jnp.sum(v, axis=-1, keepdims=True) * (1.0 / v.shape[-1])


def standardize(x):
    centred = x - row_mean(x)
    inv = lax.rsqrt(row_mean(centred * centred) + EPS)
    return centred * inv, inv


def norm_back(d, gain, stand, inv):
    scaled = d * gain
    first = row_mean(scaled)
    second = row_mean(scaled * stand)
    gain_grad = jnp.sum(d * stand, axis=0, keepdims=True)
    return inv * (scaled - first - stand * second), gain_grad


def gelu_parts(hidden):
    half = 0.5 * (1.0 + lax.erf(hidden * ROOT_HALF))
    slope = half + hidden * jnp.exp(-0.5 * hidden * hidden) * INV_ROOT_TAU
    return hidden * half, slope


def split3(v):
    hi = v.astype(BF16)
    rest = v - hi.astype(F32)
    mid = rest.astype(BF16)
    low = (rest - mid.astype(F32)).astype(BF16)
    return hi, mid, low


def spread_matrices():
    out = np.zeros((LEVELS, PAIR, WIDE), np.float32)
    for zj in range(LEVELS):
        for aj in range(WLAT):
            for d in range(SHIFTS):
                out[zj, aj * SHIFTS + d, (SHIFTS - 1 - d) * CHUNK + zj * WLAT + aj] = 1.0
    return out


def put(scr, rows, value):
    width = value.shape[1]
    for tile in range(-(-width // 128)):
        lanes = min(128, width - tile * 128)
        scr[tile, rows, 0:lanes] = value[:, tile * 128 : tile * 128 + lanes]


def get(scr, rows, width):
    parts = [scr[tile, rows, :] for tile in range(-(-width // 128))]
    return jnp.concatenate(parts, axis=1)[:, 0:width]


def head_masks(width, dtype):
    lane = lax.broadcasted_iota(jnp.int32, (1, width), 1)
    size = width // HEADS
    return [((lane >= h * size) & (lane < (h + 1) * size)).astype(dtype) for h in range(HEADS)]


def lat_inside(n):
    return lax.rem(n, WLAT)


def lat_row(row_iota, lat, shifted, lat_total):
    row = lat * WLAT + lat_inside(row_iota)
    if shifted:
        row = row + WLAT // 2
        row = jnp.where(row >= lat_total, row - lat_total, row)
    return row


def expand_bias(table, spread, tab_scr, rows_scr, wide_scr, bias_scr, lat, shifted, lat_total):
    for h in range(HEADS):
        tab_scr[h : h + 1, :] = table[h]
    for zi in range(LEVELS):
        for zj in range(LEVELS):
            for ai in range(WLAT):
                at = ((zi * LEVELS + zj) * WLAT + ai) * PAIR
                row = zj * CHUNK * 8 + (zi * WLAT + ai) * 8
                rows_scr[row : row + HEADS, 0:PAIR] = tab_scr[0:HEADS, at : at + PAIR]
    count = CHUNK * 8
    total = jnp.zeros((count, WIDE), F32)
    for zj in range(LEVELS):
        parts = split3(rows_scr[zj * count : (zj + 1) * count, 0:PAIR])
        for part in parts:
            total = total + dot(part, spread[zj])
    put(wide_scr, slice(None), total)
    i = lax.broadcasted_iota(jnp.int32, (CHUNK, WIN), 0)
    j = lax.broadcasted_iota(jnp.int32, (CHUNK, WIN), 1)
    allowed = lat_row(j, lat, shifted, lat_total) < lat_total - PAD
    if shifted:
        last = lat_total - WLAT // 2
        region_i = (lat * WLAT + lat_inside(i)) >= last
        region_j = (lat * WLAT + lat_inside(j)) >= last
        allowed = allowed & (region_i == region_j)
    for h in range(HEADS):
        wide = get(wide_scr, pl.ds(h, CHUNK, stride=8), WIDE)
        for oi in range(WLON):
            back = (WLON - 1 - oi) * CHUNK
            moved = wide if back == 0 else pltpu.roll(wide, WIDE - back, axis=1)
            at = h * WIN + oi * CHUNK
            bias_scr[at : at + CHUNK, :] = jnp.where(allowed, moved[:, 0:WIN], NEGATIVE)


def fold_bias(sums, put_unit):
    rest = jnp.zeros((CHUNK, 128), F32)

    def emit(at, value):
        for r in range(CHUNK // UNIT):
            put_unit(at * (CHUNK // UNIT) + r, value[r * UNIT : (r + 1) * UNIT, :].astype(BF16))

    for h in range(HEADS):
        total = jnp.zeros((CHUNK, WIDE), F32)
        for oi in range(WLON):
            back = (WLON - 1 - oi) * CHUNK
            at = h * WIN + oi * CHUNK
            part = sums[at : at + CHUNK, :]
            total = total + (part if back == 0 else pltpu.roll(part, back, axis=1))
        emit(h, total[:, 0:128])
        emit(HEADS + h, total[:, 128:256])
        last = total[:, 256:384]
        rest = rest + (last if h == 0 else pltpu.roll(last, 8 * h, axis=1))
    emit(2 * HEADS, rest)

def attend(qkv, bias, mixed, probs, width):
    masks = head_masks(width, BF16)
    masks32 = head_masks(width, F32)
    scale = (width // HEADS) ** -0.5

    def window(w, carry):
        rows = pl.ds(pl.multiple_of(w * WIN, 16), WIN)
        q = qkv[rows, 0:width]
        k = qkv[rows, width : 2 * width]
        v = qkv[rows, 2 * width : 3 * width]
        total = jnp.zeros((WIN, width), F32)
        for h in range(HEADS):
            logits = dot_nt(q * masks[h], k) * scale + bias[h * WIN : (h + 1) * WIN, :]
            weights = jnp.exp(logits - jnp.max(logits, axis=-1, keepdims=True))
            p = weights * (1.0 / jnp.sum(weights, axis=-1, keepdims=True))
            probs[w, h] = p
            total = total + dot(p.astype(BF16), v) * masks32[h]
        mixed[rows, :] = total.astype(BF16)
        return carry

    lax.fori_loop(0, probs.shape[0], window, 0)


def attend_back(qkv, probs, dmix, field, sums, width, first, last):
    masks = head_masks(width, BF16)
    masks32 = head_masks(width, F32)
    scale = (width // HEADS) ** -0.5

    def window(w, carry):
        rows = pl.ds(pl.multiple_of(w * WIN, 16), WIN)
        q = qkv[rows, 0:width]
        k = qkv[rows, width : 2 * width]
        v = qkv[rows, 2 * width : 3 * width]
        up = dmix[rows, :]
        dq = jnp.zeros((WIN, width), F32)
        dk = jnp.zeros((WIN, width), F32)
        dv = jnp.zeros((WIN, width), F32)
        for h in range(HEADS):
            p = probs[w, h]
            up_h = up * masks[h]
            dp = dot_nt(up_h, v)
            ds = p * (dp - jnp.sum(p * dp, axis=-1, keepdims=True))
            sums[h * WIN : (h + 1) * WIN, 0:WIN] += ds
            low = ds.astype(BF16)
            dq = dq + dot(low, k) * masks32[h]
            dk = dk + dot_tn(low, q * masks[h])
            dv = dv + dot_tn(p.astype(BF16), up_h)
        field[rows, 0:width] = (dq * scale).astype(BF16)
        field[rows, width : 2 * width] = (dk * scale).astype(BF16)
        field[rows, 2 * width : 3 * width] = dv.astype(BF16)
        return carry

    lax.fori_loop(first, last, window, 0)


def lon_major(src, scr):
    levels, lats, lons, width = src.shape
    for z in range(levels):
        for a in range(lats):
            at = (z * lats + a) * lons
            put(scr, slice(at, at + lons), src[z, a].astype(F32))


def lon_column(scr, lon, lons, width):
    return get(scr, pl.ds(lon, CHUNK, stride=lons), width)


def flat_store(dst, at, mat, cols):
    rows = mat.shape[1]
    if cols % 128 == 0:
        per = cols // 128
        for c in range(per):
            dst[pl.ds(at + c, rows, stride=per), :] = mat[c]
        return rows * per
    per = 2 * cols // 128
    half = cols // 128
    even = get(mat, pl.ds(0, rows // 2, stride=2), cols)
    odd = get(mat, pl.ds(1, rows // 2, stride=2), cols)
    for c in range(half):
        dst[pl.ds(at + c, rows // 2, stride=per), :] = even[:, c * 128 : (c + 1) * 128]
    dst[pl.ds(at + half, rows // 2, stride=per), :] = jnp.concatenate(
        [even[:, half * 128 : half * 128 + 64], odd[:, 0:64]], axis=1
    )
    for c in range(half):
        dst[pl.ds(at + half + 1 + c, rows // 2, stride=per), :] = odd[
            :, 64 + c * 128 : 64 + (c + 1) * 128
        ]
    return rows * cols // 128


def send_units(scr, base, out):
    lons, units = out.shape[:2]
    for j in range(lons):
        for u in range(units):
            at = base + (j * units + u) * UNIT
            if not isinstance(at, int):
                at = pl.multiple_of(at, UNIT)
            out[j, u] = scr[pl.ds(at, UNIT), :].astype(BF16)


def halves(scr, lat, keep, give):
    half = keep.shape[0] * keep.shape[1] * UNIT
    send_units(scr, lat * half, keep)
    send_units(scr, (1 - lat) * half, give)


def bias_units(sums, out):
    lons, per = out.shape[:2]

    def put_unit(k, value):
        out[k // per, k % per] = value

    fold_bias(sums, put_unit)
    for k in range(BIAS_UNITS, lons * per):
        put_unit(k, jnp.zeros((UNIT, 128), BF16))

def forward_core(x, b, lat, lat_total, refs, qkv_scr, bias_scr, mixed, probs):
    qkv_w, proj_w, gains = refs
    width = x.shape[-1]
    stand, inv = standardize(x)
    normed = (stand * gains[b, 0:1, :]).astype(BF16)
    qkv_scr[...] = dot(normed, qkv_w[b]).astype(BF16)
    attend(qkv_scr, bias_scr, mixed, probs, width)
    att = dot(mixed[...], proj_w[b]).astype(BF16)
    resid = (x + att.astype(F32)).astype(BF16).astype(F32)
    return resid, normed


def first_kernel(
    lat_total, tokens_in, cot_in, table_in, spread_in, qkv_in, proj_in, up_in, down_in, gains_in,
    x_out, tail_out, head_out, qkv_out, mixed_out, probs_out, resid_out, slope_out, active_out,
    scr, cot_scr, tab_scr, rows_scr, wide_scr, bias_scr,
    cot, table, spread, tokens, qkv_w, gains, proj_w, up_w, down_w, sems,
):
    copies = []
    for source, target in (
        (cot_in, cot),
        (table_in.at[0:1], table),
        (spread_in, spread),
        (tokens_in, tokens),
        (qkv_in.at[0:1], qkv_w),
        (gains_in, gains),
        (proj_in.at[0:1], proj_w),
        (up_in.at[0:1], up_w),
        (down_in.at[0:1], down_w),
    ):
        copies.append(pltpu.make_async_copy(source, target, sems.at[len(copies)]))
    for copy in copies:
        copy.start()
    lat = lax.axis_index("lat")
    width = tokens.shape[-1]
    lons = tokens.shape[2]
    cut = CHUNK * (WLON // 2)
    copies[0].wait()
    lon_major(cot, cot_scr)
    g = jnp.concatenate([lon_column(cot_scr, lon, lons, width) for lon in range(lons)], axis=0)
    head_out[1] = g[0:cut, :].astype(BF16)
    tail_out[1] = g[cut:, :].astype(BF16)
    copies[1].wait()
    copies[2].wait()
    expand_bias(
        table.at[0], spread, tab_scr, rows_scr, wide_scr, bias_scr, lat, False, lat_total
    )
    copies[3].wait()
    lon_major(tokens, scr)
    x = jnp.concatenate([lon_column(scr, lon, lons, width) for lon in range(lons)], axis=0)
    x_out[...] = x.astype(BF16)
    for copy in copies[4:]:
        copy.wait()
    resid, _ = forward_core(
        x, 0, lat, lat_total, (qkv_w, proj_w, gains), qkv_out, bias_scr, mixed_out, probs_out
    )
    resid_out[...] = resid.astype(BF16)
    stand, _ = standardize(resid)
    normed = (stand * gains[0, 1:2, :]).astype(BF16)
    active, slope = gelu_parts(dot(normed, up_w[0]))
    active = active.astype(BF16)
    active_out[...] = active
    slope_out[...] = slope.astype(BF16)
    result = resid + dot_nt(active, down_w[0])
    head_out[0] = result[0:cut, :].astype(BF16)
    tail_out[0] = result[cut:, :].astype(BF16)


def bias_kernel(lat_total, table, spread, bias_out, tab_scr, rows_scr, wide_scr):
    lat = lax.axis_index("lat")
    expand_bias(
        table.at[1], spread, tab_scr, rows_scr, wide_scr, bias_out, lat, True, lat_total
    )


def merge_ahead(scr_own, scr_oth, rows):
    half = WLAT // 2
    n = lax.broadcasted_iota(jnp.int32, (rows, 1), 0)
    return jnp.where(
        lat_inside(n) < half,
        pltpu.roll(scr_own[...], rows - half, axis=0),
        pltpu.roll(scr_oth[...], half, axis=0),
    )


def merge_behind(scr_own, scr_oth, rows):
    half = WLAT // 2
    n = lax.broadcasted_iota(jnp.int32, (rows, 1), 0)
    return jnp.where(
        lat_inside(n) >= half,
        pltpu.roll(scr_own[...], half, axis=0),
        pltpu.roll(scr_oth[...], rows - half, axis=0),
    )


def second_kernel(
    lat_total,
    tail, lon_head, lat_tail, diag_head, bias, qkv_w, proj_w, up_w, down_w, gains,
    head_out, tail_out, n1_out, field_out, mixed_out, low_out, n2_out, hg_out, active_out, g_out,
    sums_out, gain_out,
    scr_own, scr_oth, qkv_scr, probs_scr, dmix_scr,
):
    lat = lax.axis_index("lat")
    rows, width = scr_own.shape
    cut = CHUNK * (WLON // 2)

    def rolled(which):
        scr_own[0 : rows - cut, :] = tail[which].astype(F32)
        scr_own[rows - cut :, :] = lon_head[which].astype(F32)
        scr_oth[0 : rows - cut, :] = lat_tail[which].astype(F32)
        scr_oth[rows - cut :, :] = diag_head[which].astype(F32)
        return merge_ahead(scr_own, scr_oth, rows)

    g = rolled(1)
    n = lax.broadcasted_iota(jnp.int32, (rows, 1), 0)
    keep = lat_row(n, lat, True, lat_total) < lat_total - PAD
    g = jnp.where(keep, g, 0.0)
    g_out[...] = g.astype(BF16)

    x = rolled(0)

    resid, normed = forward_core(
        x, 1, lat, lat_total, (qkv_w, proj_w, gains), qkv_scr, bias, mixed_out, probs_scr
    )
    n1_out[...] = normed
    stand2, inv2 = standardize(resid)
    normed2 = (stand2 * gains[1, 1:2, :]).astype(BF16)
    n2_out[...] = normed2
    active, slope = gelu_parts(dot(normed2, up_w[1]))
    active_out[...] = active.astype(BF16)

    hg = (dot(g_out[...], down_w[1]) * slope).astype(BF16)
    hg_out[...] = hg
    part, gain_two = norm_back(dot_nt(hg, up_w[1]), gains[1, 1:2, :], stand2, inv2)
    rg = g + part
    low = rg.astype(BF16)
    low_out[...] = low
    dmix_scr[...] = dot_nt(low, proj_w[1]).astype(BF16)
    sums_out[...] = jnp.zeros(sums_out.shape, F32)
    attend_back(
        qkv_scr, probs_scr, dmix_scr, field_out, sums_out, width, 0, probs_scr.shape[0]
    )
    ng = dot_nt(field_out[...], qkv_w[1]).astype(BF16).astype(F32)
    stand1, inv1 = standardize(x)
    part, gain_one = norm_back(ng, gains[1, 0:1, :], stand1, inv1)
    dx = rg + part
    head_out[...] = dx[0 : rows - cut, :].astype(BF16)
    tail_out[...] = dx[rows - cut :, :].astype(BF16)
    gain_out[0:1, :] = gain_one
    gain_out[1:2, :] = gain_two


def outer_kernel(
    n1, field, mixed, low, n2, hg, active, g, sums,
    keep, give, bias_out,
    m576, m192, m768, mdown, flat_scr,
):
    put(m576, slice(None), dot_tn(n1[...], field[...]))
    at = flat_store(flat_scr, 0, m576, field.shape[1])
    put(m192, slice(None), dot_tn(mixed[...], low[...]))
    at += flat_store(flat_scr, at, m192, mixed.shape[1])
    put(m768, slice(None), dot_tn(n2[...], hg[...]))
    at += flat_store(flat_scr, at, m768, active.shape[1])
    put(mdown, slice(None), dot_tn(active[...], g[...]))
    at += flat_store(flat_scr, at, mdown, mixed.shape[1])
    halves(flat_scr, lax.axis_index("lat"), keep, give)
    bias_units(sums, bias_out)


def lat_sum(keep_a, got_a, bias_a, keep_b, got_b, out):
    one, two = keep_a.shape[1], bias_a.shape[1]
    out[:, 0:one] = (keep_a[...].astype(F32) + got_a[...].astype(F32)).astype(BF16)
    out[:, one : one + two] = bias_a[...]
    out[:, one + two :] = (keep_b[...].astype(F32) + got_b[...].astype(F32)).astype(BF16)


def sum_pieces(pieces, out):
    total = pieces[0].astype(F32)
    for k in range(1, pieces.shape[0]):
        total = total + pieces[k].astype(F32)
    out[...] = total.astype(BF16)


def sum_direct(extra, pieces, out):
    lat = lax.axis_index("lat")
    units = out.shape[0] - extra
    total = pieces[0, 0:units].astype(F32)
    for k in range(1, pieces.shape[0]):
        total = total + pieces[k, 0:units].astype(F32)
    out[0:units] = total.astype(BF16)
    total = pieces[lat, units:].astype(F32)
    for k in range(1, pieces.shape[0] // 2):
        total = total + pieces[2 * k + lat, units:].astype(F32)
    out[units:] = total.astype(BF16)


def third_kernel(
    head, lon_tail, lat_head, diag_tail, resid_in, slope, active, mixed,
    proj_w, up_w, down_w, gains, keep_a,
    keep_out, give_out, rg_out, dmix_out, gain_out,
    scr_own, scr_oth, m192, m768, mdown, flat_scr,
):
    rows, width = scr_own.shape
    cut = CHUNK * (WLON // 2)
    scr_own[0:cut, :] = lon_tail[...].astype(F32)
    scr_own[cut:, :] = head[...].astype(F32)
    scr_oth[0:cut, :] = diag_tail[...].astype(F32)
    scr_oth[cut:, :] = lat_head[...].astype(F32)
    g = merge_behind(scr_own, scr_oth, rows)
    g_low = g.astype(BF16)
    hg = (dot(g_low, down_w[0]) * slope[...].astype(F32)).astype(BF16)
    stand2, inv2 = standardize(resid_in[...].astype(F32))
    normed2 = (stand2 * gains[0, 1:2, :]).astype(BF16)
    part, gain_two = norm_back(dot_nt(hg, up_w[0]), gains[0, 1:2, :], stand2, inv2)
    rg = g + part
    rg_out[...] = rg
    low = rg.astype(BF16)
    dmix_out[...] = dot_nt(low, proj_w[0]).astype(BF16)
    gain_out[...] = gain_two
    put(m192, slice(None), dot_tn(mixed[...], low))
    at = flat_store(flat_scr, 0, m192, mixed.shape[1])
    put(m768, slice(None), dot_tn(normed2, hg))
    at += flat_store(flat_scr, at, m768, active.shape[1])
    put(mdown, slice(None), dot_tn(active[...], g_low))
    at += flat_store(flat_scr, at, mdown, mixed.shape[1])
    flat_scr[at:, :] = jnp.zeros((flat_scr.shape[0] - at, 128), F32)
    halves(flat_scr, lax.axis_index("lat"), keep_out, give_out)


def gain_rows(one, two):
    return jnp.concatenate(
        [
            one[:, 0:128],
            jnp.concatenate([one[:, 128:192], two[:, 0:64]], axis=1),
            two[:, 64:192],
        ],
        axis=0,
    )


def fourth_kernel(
    x_in, qkv, probs, dmix, rg, gain_two, gains_late, order, qkv_w, gains,
    tokens_out, pieces_out,
    field, sums, m576, flat_scr, dx_scr, bias_scr,
):
    width = x_in.shape[-1]
    levels, lats, lons = tokens_out.shape[:3]
    sums[...] = jnp.zeros(sums.shape, F32)
    attend_back(qkv, probs, dmix, field, sums, width, 0, probs.shape[0])
    stand1, inv1 = standardize(x_in[...].astype(F32))
    normed = (stand1 * gains[0, 0:1, :]).astype(BF16)
    ng = dot_nt(field[...], qkv_w[0]).astype(BF16).astype(F32)
    part, gain_one = norm_back(ng, gains[0, 0:1, :], stand1, inv1)
    put(m576, slice(None), dot_tn(normed, field[...]))
    at = flat_store(flat_scr, 0, m576, field.shape[1])
    flat_scr[at:, :] = jnp.zeros((flat_scr.shape[0] - at, 128), F32)
    flat_scr[at : at + 3, :] = gain_rows(gain_one, gain_two[...])
    flat_scr[at + 3 : at + 6, :] = gain_rows(gains_late[0:1, :], gains_late[1:2, :])
    bias_units(sums, bias_scr)
    count, extra = bias_scr.shape[:2]
    units = pieces_out.shape[1] - extra
    for lon in range(count):
        for lat in range(2):
            base = (lat * count + lon) * units * UNIT
            for u in range(units):
                at = base + u * UNIT
                pieces_out[2 * lon + lat, u] = flat_scr[at : at + UNIT, :].astype(BF16)
            pieces_out[2 * lon + lat, units:] = bias_scr[lon]
    put(dx_scr, slice(None), rg[...] + part)
    for z in range(levels):
        for a in range(lats):
            tokens_out[z, a] = get(
                dx_scr, pl.ds(z * lats + a, lons, stride=CHUNK), width
            ).astype(BF16)


def last_kernel(
    units_a, units_c, extra, spread, pieces_ab, pieces_c, update_out, bias_out,
    scr, rows_scr, wide_scr,
):
    lat = lax.axis_index("lat")
    lons = pieces_ab.shape[0] // 2

    def place(pieces, first, last, dests):
        total = jnp.zeros((UNIT, 128), F32)
        per = last - first
        k = 0
        for where, room in dests:
            for at in range(where, where + room, UNIT):
                half, j, u = k // (per * lons), k // per % lons, k % per
                value = pieces[2 * j + half, first + u].astype(F32)
                scr[at : at + UNIT, :] = value
                total = total + value * value
                k += 1
        return total

    total = place(
        pieces_ab, 0, units_a, [(864, 864), (2016, 288), (3456, 1152), (5760, 1152)]
    )
    total = total + place(
        pieces_ab, units_a + extra, pieces_ab.shape[1], [(1728, 288), (2304, 1152), (4608, 1152)]
    )
    total = total + place(pieces_c, 0, units_c, [(0, 864), (6912, 8)])
    count = update_out.shape[0]
    mean = jnp.sum(total) * (1.0 / (count * 128))
    scale = lax.rsqrt(mean + 1e-06)
    update_out[...] = (scr[0:count, :] * scale).astype(BF16)

    for b, (piece, base) in enumerate(((pieces_c, units_c), (pieces_ab, units_a))):

        def read(at):
            parts = []
            for r in range(CHUNK // UNIT):
                k = at * (CHUNK // UNIT) + r
                parts.append(piece[k // extra * 2 + lat, base + k % extra].astype(F32))
            return jnp.concatenate(parts, axis=0)

        rest = read(2 * HEADS)
        for h in range(HEADS):
            rows = pl.ds(h, CHUNK, stride=8)
            wide_scr[0, rows, :] = read(h)
            wide_scr[1, rows, :] = read(HEADS + h)
            wide_scr[2, rows, :] = rest if h == 0 else pltpu.roll(rest, 128 - 8 * h, axis=1)
        low = get(wide_scr, slice(None), WIDE).astype(BF16)
        for zj in range(LEVELS):
            rows_scr[...] = dot_nt(low, spread[zj])
            for zi in range(LEVELS):
                for ai in range(WLAT):
                    at = ((zi * LEVELS + zj) * WLAT + ai) * PAIR
                    row = (zi * WLAT + ai) * 8
                    bias_out[b, 0, :, at : at + PAIR] = rows_scr[row : row + HEADS, 0:PAIR]


def call(kernel, outs, scratch, args, micros, mib, space=pltpu.VMEM):
    return pl.pallas_call(
        kernel,
        out_shape=[jax.ShapeDtypeStruct(shape, dtype) for shape, dtype in outs],
        in_specs=[pl.BlockSpec(memory_space=space)] * len(args),
        out_specs=[pl.BlockSpec(memory_space=pltpu.VMEM)] * len(outs),
        scratch_shapes=[
            pltpu.VMEM(*entry) if isinstance(entry, tuple) else entry for entry in scratch
        ],
        compiler_params=pltpu.CompilerParams(vmem_limit_bytes=mib * MIB),
        cost_estimate=pl.CostEstimate(
            flops=int(micros * 1.1e9), bytes_accessed=10**5, transcendentals=0
        ),
    )(*args)


def lat_swap(value):
    return lax.ppermute(value, "lat", [(0, 1), (1, 0)])


def lon_send(value, step):
    count = lax.axis_size("lon")
    return lax.ppermute(value, "lon", [(s, (s + step) % count) for s in range(count)])


def diag_send(value, step):
    count = lax.axis_size("lon")
    pairs = []
    for s in range(count):
        for t in range(2):
            pairs.append((2 * s + t, 2 * ((s + step) % count) + 1 - t))
    return lax.ppermute(value, ("lon", "lat"), pairs)


def shards(
    tokens, cotangent, qkv_weight, proj_weight, up_weight, down_weight, norm_gain, bias_table
):
    levels, lats, lons, width = tokens.shape
    rows = levels * lats * lons
    wins = rows // WIN
    hid = up_weight.shape[-1]
    heads = bias_table.shape[2]
    lon_size = lax.axis_size("lon")
    zs = lon_size // 2
    lat_total = lats * lax.axis_size("lat")
    cut = CHUNK * (WLON // 2)
    spread = jnp.asarray(spread_matrices(), BF16)
    down_turned = jnp.swapaxes(down_weight, 1, 2)
    table = jnp.swapaxes(bias_table, 1, 2)
    token = (rows, width)
    field_shape = ((rows, 3 * width), BF16)
    probs_shape = ((wins, heads, WIN, WIN), F32)
    bias_shape = ((heads * WIN, WIN), F32)
    sums_shape = ((heads * WIN, WIDE), F32)
    tab_scr = ((8, table.shape[-1]), F32)
    rows_scr = ((LEVELS * CHUNK * 8, PAIR), F32)
    wide_scr = ((WIDE // 128, CHUNK * 8, 128), F32)
    tiles = -(-width // 128)
    token_scr = ((tiles, rows, 128), F32)
    m576 = ((-(-3 * width // 128), width, 128), F32)
    m192 = ((tiles, width, 128), F32)
    m768 = ((hid // 128, width, 128), F32)
    mdown = ((tiles, hid, 128), F32)

    block_rows = (qkv_weight[0].size + proj_weight[0].size + 2 * up_weight[0].size) // 128
    qkv_rows = qkv_weight[0].size // 128
    counts = (block_rows, block_rows - qkv_rows, qkv_rows + 8)
    units_a, units_b, units_c = [-(-count // (2 * lon_size * UNIT)) for count in counts]
    extra = -(-BIAS_UNITS // lon_size)

    def units(*lead):
        return (lead + (UNIT, 128), BF16)

    def flat_scr(per):
        return ((2 * lon_size * per * UNIT, 128), F32)

    x0, tail, head, qkv0, mixed0, probs0, resid0, slope0, active0 = call(
        functools.partial(first_kernel, lat_total),
        [
            (token, BF16),
            ((2, rows - cut, width), BF16),
            ((2, cut, width), BF16),
            field_shape,
            (token, BF16),
            probs_shape,
            (token, BF16),
            ((rows, hid), BF16),
            ((rows, hid), BF16),
        ],
        [
            token_scr,
            token_scr,
            tab_scr,
            rows_scr,
            wide_scr,
            bias_shape,
            (cotangent.shape, BF16),
            ((1,) + table.shape[1:], F32),
            (spread.shape, BF16),
            (tokens.shape, BF16),
            ((1,) + qkv_weight.shape[1:], BF16),
            (norm_gain.shape, F32),
            ((1,) + proj_weight.shape[1:], BF16),
            ((1,) + up_weight.shape[1:], BF16),
            ((1,) + down_turned.shape[1:], BF16),
            pltpu.SemaphoreType.DMA((9,)),
        ],
        (
            tokens, cotangent, table, spread, qkv_weight, proj_weight, up_weight, down_turned,
            norm_gain,
        ),
        8,
        28,
        pltpu.HBM,
    )
    lon_head = lon_send(head, -1)
    diag_head = diag_send(head, -1)
    lat_tail = lat_swap(tail)
    (bias1,) = call(
        functools.partial(bias_kernel, lat_total),
        [bias_shape],
        [tab_scr, rows_scr, wide_scr],
        (table, spread),
        2,
        10,
    )

    (
        dhead, dtail, n1, field1, mixed1, low1, n2, hg1, active1, g1, sums1, gains1,
    ) = call(
        functools.partial(second_kernel, lat_total),
        [
            ((rows - cut, width), BF16),
            ((cut, width), BF16),
            (token, BF16),
            field_shape,
            (token, BF16),
            (token, BF16),
            (token, BF16),
            ((rows, hid), BF16),
            ((rows, hid), BF16),
            (token, BF16),
            sums_shape,
            ((2, width), F32),
        ],
        [(token, F32), (token, F32), field_shape, probs_shape, (token, BF16)],
        (
            tail, lon_head, lat_tail, diag_head, bias1, qkv_weight, proj_weight, up_weight,
            down_turned, norm_gain,
        ),
        19,
        28,
    )
    lon_tail = lon_send(dtail, 1)
    diag_tail = diag_send(dtail, 1)
    lat_dhead = lat_swap(dhead)

    keep_a, give_a, bias_a = call(
        outer_kernel,
        [units(lon_size, units_a), units(lon_size, units_a), units(lon_size, extra)],
        [m576, m192, m768, mdown, flat_scr(units_a)],
        (n1, field1, mixed1, low1, n2, hg1, active1, g1, sums1),
        3,
        20,
    )
    got_a = lat_swap(give_a)

    keep_b, give_b, rg0, dmix0, gain_two = call(
        third_kernel,
        [
            units(lon_size, units_b),
            units(lon_size, units_b),
            (token, F32),
            (token, BF16),
            ((1, width), F32),
        ],
        [(token, F32), (token, F32), m192, m768, mdown, flat_scr(units_b)],
        (
            dhead, lon_tail, lat_dhead, diag_tail, resid0, slope0, active0, mixed0,
            proj_weight, up_weight, down_turned, norm_gain, keep_a,
        ),
        2,
        20,
    )
    got_b = lat_swap(give_b)
    (part_ab,) = call(
        lat_sum,
        [units(lon_size, units_a + extra + units_b)],
        [],
        (keep_a, got_a, bias_a, keep_b, got_b),
        1,
        10,
    )
    pieces_ab = lax.all_to_all(part_ab, "lon", 0, 0)

    tokens_grad, pieces_c = call(
        fourth_kernel,
        [(tokens.shape, BF16), units(2 * lon_size, units_c + extra)],
        [
            field_shape,
            sums_shape,
            m576,
            flat_scr(units_c),
            token_scr,
            units(lon_size, extra),
        ],
        (
            x0, qkv0, probs0, dmix0, rg0, gain_two, gains1, part_ab, qkv_weight, norm_gain,
        ),
        11,
        24,
    )
    got_c = lax.all_to_all(pieces_c, ("lon", "lat"), 0, 0)

    (sum_ab,) = call(sum_pieces, [units(units_a + extra + units_b)], [], (pieces_ab,), 1, 10)
    whole_ab = lax.all_gather(sum_ab, ("lon", "lat"))
    (sum_c,) = call(
        functools.partial(sum_direct, extra), [units(units_c + extra)], [], (got_c,), 1, 10
    )
    whole_c = lax.all_to_all(
        jnp.broadcast_to(sum_c[None], (2 * lon_size,) + sum_c.shape), ("lon", "lat"), 0, 0
    )

    flat_rows = (2 * block_rows * 128 + norm_gain.size) // 128
    update, bias_grad = call(
        functools.partial(last_kernel, units_a, units_c, extra),
        [((flat_rows, 128), BF16), (bias_table.shape, F32)],
        [((flat_rows + 2, 128), F32), ((CHUNK * 8, PAIR), F32), wide_scr],
        (spread, whole_ab, whole_c),
        3,
        20,
    )
    return (tokens_grad, update.reshape(-1), bias_grad)


def solution(mesh):
    return jax.shard_map(
        shards,
        mesh=mesh,
        in_specs=(
            P("grp", "lat", "lon", None),
            P("grp", "lat", "lon", None),
            P(),
            P(),
            P(),
            P(),
            P(),
            P(None, "lat", None, None),
        ),
        out_specs=(P("grp", "lat", "lon", None), P("grp"), P("grp", "lat", None, None)),
        check_vma=False,
    )
```

```python
import functools

import jax
import jax.numpy as jnp
import numpy as np
from jax import lax
from jax.experimental import pallas as pl
from jax.experimental.pallas import tpu as pltpu
from jax.sharding import PartitionSpec as P

WLAT = 12
WLON = 6
PAD = 5
LEVELS = 2
HEADS = 6
CHUNK = LEVELS * WLAT
WIN = CHUNK * WLON
SHIFTS = 2 * WLON - 1
PAIR = WLAT * SHIFTS
WIDE = 384

EPS = 1e-05
NEGATIVE = -1000000000.0
ROOT_HALF = 0.7071067811865476
INV_ROOT_TAU = 0.3989422804014327

F32 = jnp.float32
BF16 = jnp.bfloat16
UNIT = 8
BIAS_UNITS = (2 * HEADS + 1) * CHUNK // UNIT
MIB = 1024 * 1024


def dot(a, b):
    return lax.dot_general(a, b, (((1,), (0,)), ((), ())), preferred_element_type=F32)


def dot_nt(a, b):
    return lax.dot_general(a, b, (((1,), (1,)), ((), ())), preferred_element_type=F32)


def dot_tn(a, b):
    return lax.dot_general(a, b, (((0,), (0,)), ((), ())), preferred_element_type=F32)


def row_mean(v):
    return jnp.sum(v, axis=-1, keepdims=True) * (1.0 / v.shape[-1])


def standardize(x):
    centred = x - row_mean(x)
    inv = lax.rsqrt(row_mean(centred * centred) + EPS)
    return centred * inv, inv


def norm_back(d, gain, stand, inv):
    scaled = d * gain
    first = row_mean(scaled)
    second = row_mean(scaled * stand)
    gain_grad = jnp.sum(d * stand, axis=0, keepdims=True)
    return inv * (scaled - first - stand * second), gain_grad


def gelu_parts(hidden):
    half = 0.5 * (1.0 + lax.erf(hidden * ROOT_HALF))
    slope = half + hidden * jnp.exp(-0.5 * hidden * hidden) * INV_ROOT_TAU
    return hidden * half, slope


def split3(v):
    hi = v.astype(BF16)
    rest = v - hi.astype(F32)
    mid = rest.astype(BF16)
    low = (rest - mid.astype(F32)).astype(BF16)
    return hi, mid, low


def spread_matrices():
    out = np.zeros((LEVELS, PAIR, WIDE), np.float32)
    for zj in range(LEVELS):
        for aj in range(WLAT):
            for d in range(SHIFTS):
                out[zj, aj * SHIFTS + d, (SHIFTS - 1 - d) * CHUNK + zj * WLAT + aj] = 1.0
    return out


def put(scr, rows, value):
    width = value.shape[1]
    for tile in range(-(-width // 128)):
        lanes = min(128, width - tile * 128)
        scr[tile, rows, 0:lanes] = value[:, tile * 128 : tile * 128 + lanes]


def get(scr, rows, width):
    parts = [scr[tile, rows, :] for tile in range(-(-width // 128))]
    return jnp.concatenate(parts, axis=1)[:, 0:width]


def head_masks(width, dtype):
    lane = lax.broadcasted_iota(jnp.int32, (1, width), 1)
    size = width // HEADS
    return [((lane >= h * size) & (lane < (h + 1) * size)).astype(dtype) for h in range(HEADS)]


def lat_inside(n):
    return lax.rem(n, WLAT)


def lat_row(row_iota, lat, shifted, lat_total):
    row = lat * WLAT + lat_inside(row_iota)
    if shifted:
        row = row + WLAT // 2
        row = jnp.where(row >= lat_total, row - lat_total, row)
    return row


def expand_bias(table, spread, tab_scr, rows_scr, wide_scr, bias_scr, lat, shifted, lat_total):
    for h in range(HEADS):
        tab_scr[h : h + 1, :] = table[h]
    for zi in range(LEVELS):
        for zj in range(LEVELS):
            for ai in range(WLAT):
                at = ((zi * LEVELS + zj) * WLAT + ai) * PAIR
                row = zj * CHUNK * 8 + (zi * WLAT + ai) * 8
                rows_scr[row : row + HEADS, 0:PAIR] = tab_scr[0:HEADS, at : at + PAIR]
    count = CHUNK * 8
    total = jnp.zeros((count, WIDE), F32)
    for zj in range(LEVELS):
        parts = split3(rows_scr[zj * count : (zj + 1) * count, 0:PAIR])
        for part in parts:
            total = total + dot(part, spread[zj])
    put(wide_scr, slice(None), total)
    i = lax.broadcasted_iota(jnp.int32, (CHUNK, WIN), 0)
    j = lax.broadcasted_iota(jnp.int32, (CHUNK, WIN), 1)
    allowed = lat_row(j, lat, shifted, lat_total) < lat_total - PAD
    if shifted:
        last = lat_total - WLAT // 2
        region_i = (lat * WLAT + lat_inside(i)) >= last
        region_j = (lat * WLAT + lat_inside(j)) >= last
        allowed = allowed & (region_i == region_j)
    for h in range(HEADS):
        wide = get(wide_scr, pl.ds(h, CHUNK, stride=8), WIDE)
        for oi in range(WLON):
            back = (WLON - 1 - oi) * CHUNK
            moved = wide if back == 0 else pltpu.roll(wide, WIDE - back, axis=1)
            at = h * WIN + oi * CHUNK
            bias_scr[at : at + CHUNK, :] = jnp.where(allowed, moved[:, 0:WIN], NEGATIVE)


def fold_bias(sums, put_unit):
    rest = jnp.zeros((CHUNK, 128), F32)

    def emit(at, value):
        for r in range(CHUNK // UNIT):
            put_unit(at * (CHUNK // UNIT) + r, value[r * UNIT : (r + 1) * UNIT, :].astype(BF16))

    for h in range(HEADS):
        total = jnp.zeros((CHUNK, WIDE), F32)
        for oi in range(WLON):
            back = (WLON - 1 - oi) * CHUNK
            at = h * WIN + oi * CHUNK
            part = sums[at : at + CHUNK, :]
            total = total + (part if back == 0 else pltpu.roll(part, back, axis=1))
        emit(h, total[:, 0:128])
        emit(HEADS + h, total[:, 128:256])
        last = total[:, 256:384]
        rest = rest + (last if h == 0 else pltpu.roll(last, 8 * h, axis=1))
    emit(2 * HEADS, rest)

def attend(qkv, bias, mixed, probs, width):
    masks = head_masks(width, BF16)
    masks32 = head_masks(width, F32)
    scale = (width // HEADS) ** -0.5

    def window(w, carry):
        rows = pl.ds(pl.multiple_of(w * WIN, 16), WIN)
        q = qkv[rows, 0:width]
        k = qkv[rows, width : 2 * width]
        v = qkv[rows, 2 * width : 3 * width]
        total = jnp.zeros((WIN, width), F32)
        for h in range(HEADS):
            logits = dot_nt(q * masks[h], k) * scale + bias[h * WIN : (h + 1) * WIN, :]
            weights = jnp.exp(logits - jnp.max(logits, axis=-1, keepdims=True))
            p = weights * (1.0 / jnp.sum(weights, axis=-1, keepdims=True))
            probs[w, h] = p
            total = total + dot(p.astype(BF16), v) * masks32[h]
        mixed[rows, :] = total.astype(BF16)
        return carry

    lax.fori_loop(0, probs.shape[0], window, 0)


def attend_back(qkv, probs, dmix, field, sums, width, first, last):
    masks = head_masks(width, BF16)
    masks32 = head_masks(width, F32)
    scale = (width // HEADS) ** -0.5

    def window(w, carry):
        rows = pl.ds(pl.multiple_of(w * WIN, 16), WIN)
        q = qkv[rows, 0:width]
        k = qkv[rows, width : 2 * width]
        v = qkv[rows, 2 * width : 3 * width]
        up = dmix[rows, :]
        dq = jnp.zeros((WIN, width), F32)
        dk = jnp.zeros((WIN, width), F32)
        dv = jnp.zeros((WIN, width), F32)
        for h in range(HEADS):
            p = probs[w, h]
            up_h = up * masks[h]
            dp = dot_nt(up_h, v)
            ds = p * (dp - jnp.sum(p * dp, axis=-1, keepdims=True))
            sums[h * WIN : (h + 1) * WIN, 0:WIN] += ds
            low = ds.astype(BF16)
            dq = dq + dot(low, k) * masks32[h]
            dk = dk + dot_tn(low, q * masks[h])
            dv = dv + dot_tn(p.astype(BF16), up_h)
        field[rows, 0:width] = (dq * scale).astype(BF16)
        field[rows, width : 2 * width] = (dk * scale).astype(BF16)
        field[rows, 2 * width : 3 * width] = dv.astype(BF16)
        return carry

    lax.fori_loop(first, last, window, 0)


def lon_major(src, scr):
    levels, lats, lons, width = src.shape
    for z in range(levels):
        for a in range(lats):
            at = (z * lats + a) * lons
            put(scr, slice(at, at + lons), src[z, a].astype(F32))


def lon_column(scr, lon, lons, width):
    return get(scr, pl.ds(lon, CHUNK, stride=lons), width)


def flat_store(dst, at, mat, cols):
    rows = mat.shape[1]
    if cols % 128 == 0:
        per = cols // 128
        for c in range(per):
            dst[pl.ds(at + c, rows, stride=per), :] = mat[c]
        return rows * per
    per = 2 * cols // 128
    half = cols // 128
    even = get(mat, pl.ds(0, rows // 2, stride=2), cols)
    odd = get(mat, pl.ds(1, rows // 2, stride=2), cols)
    for c in range(half):
        dst[pl.ds(at + c, rows // 2, stride=per), :] = even[:, c * 128 : (c + 1) * 128]
    dst[pl.ds(at + half, rows // 2, stride=per), :] = jnp.concatenate(
        [even[:, half * 128 : half * 128 + 64], odd[:, 0:64]], axis=1
    )
    for c in range(half):
        dst[pl.ds(at + half + 1 + c, rows // 2, stride=per), :] = odd[
            :, 64 + c * 128 : 64 + (c + 1) * 128
        ]
    return rows * cols // 128


def send_units(scr, base, out):
    lons, units = out.shape[:2]
    for j in range(lons):
        for u in range(units):
            at = base + (j * units + u) * UNIT
            if not isinstance(at, int):
                at = pl.multiple_of(at, UNIT)
            out[j, u] = scr[pl.ds(at, UNIT), :].astype(BF16)


def halves(scr, lat, keep, give):
    half = keep.shape[0] * keep.shape[1] * UNIT
    send_units(scr, lat * half, keep)
    send_units(scr, (1 - lat) * half, give)


def bias_units(sums, out):
    lons, per = out.shape[:2]

    def put_unit(k, value):
        out[k // per, k % per] = value

    fold_bias(sums, put_unit)
    for k in range(BIAS_UNITS, lons * per):
        put_unit(k, jnp.zeros((UNIT, 128), BF16))

def forward_core(x, b, lat, lat_total, refs, qkv_scr, bias_scr, mixed, probs):
    qkv_w, proj_w, gains = refs
    width = x.shape[-1]
    stand, inv = standardize(x)
    normed = (stand * gains[b, 0:1, :]).astype(BF16)
    qkv_scr[...] = dot(normed, qkv_w[b]).astype(BF16)
    attend(qkv_scr, bias_scr, mixed, probs, width)
    att = dot(mixed[...], proj_w[b]).astype(BF16)
    resid = (x + att.astype(F32)).astype(BF16).astype(F32)
    return resid, normed


def first_kernel(
    lat_total, tokens_in, cot_in, table_in, spread_in, qkv_in, proj_in, up_in, down_in, gains_in,
    x_out, tail_out, head_out, qkv_out, mixed_out, probs_out, resid_out, slope_out, active_out,
    scr, cot_scr, tab_scr, rows_scr, wide_scr, bias_scr,
    cot, table, spread, tokens, qkv_w, gains, proj_w, up_w, down_w, sems,
):
    copies = []
    for source, target in (
        (cot_in, cot),
        (table_in.at[0:1], table),
        (spread_in, spread),
        (tokens_in, tokens),
        (qkv_in.at[0:1], qkv_w),
        (gains_in, gains),
        (proj_in.at[0:1], proj_w),
        (up_in.at[0:1], up_w),
        (down_in.at[0:1], down_w),
    ):
        copies.append(pltpu.make_async_copy(source, target, sems.at[len(copies)]))
    for copy in copies:
        copy.start()
    lat = lax.axis_index("lat")
    width = tokens.shape[-1]
    lons = tokens.shape[2]
    cut = CHUNK * (WLON // 2)
    copies[0].wait()
    lon_major(cot, cot_scr)
    g = jnp.concatenate([lon_column(cot_scr, lon, lons, width) for lon in range(lons)], axis=0)
    head_out[1] = g[0:cut, :].astype(BF16)
    tail_out[1] = g[cut:, :].astype(BF16)
    copies[1].wait()
    copies[2].wait()
    expand_bias(
        table.at[0], spread, tab_scr, rows_scr, wide_scr, bias_scr, lat, False, lat_total
    )
    copies[3].wait()
    lon_major(tokens, scr)
    x = jnp.concatenate([lon_column(scr, lon, lons, width) for lon in range(lons)], axis=0)
    x_out[...] = x.astype(BF16)
    for copy in copies[4:]:
        copy.wait()
    resid, _ = forward_core(
        x, 0, lat, lat_total, (qkv_w, proj_w, gains), qkv_out, bias_scr, mixed_out, probs_out
    )
    resid_out[...] = resid.astype(BF16)
    stand, _ = standardize(resid)
    normed = (stand * gains[0, 1:2, :]).astype(BF16)
    active, slope = gelu_parts(dot(normed, up_w[0]))
    active = active.astype(BF16)
    active_out[...] = active
    slope_out[...] = slope.astype(BF16)
    result = resid + dot_nt(active, down_w[0])
    head_out[0] = result[0:cut, :].astype(BF16)
    tail_out[0] = result[cut:, :].astype(BF16)


def bias_kernel(lat_total, table, spread, bias_out, tab_scr, rows_scr, wide_scr):
    lat = lax.axis_index("lat")
    expand_bias(
        table.at[1], spread, tab_scr, rows_scr, wide_scr, bias_out, lat, True, lat_total
    )


def merge_ahead(scr_own, scr_oth, rows):
    half = WLAT // 2
    n = lax.broadcasted_iota(jnp.int32, (rows, 1), 0)
    return jnp.where(
        lat_inside(n) < half,
        pltpu.roll(scr_own[...], rows - half, axis=0),
        pltpu.roll(scr_oth[...], half, axis=0),
    )


def merge_behind(scr_own, scr_oth, rows):
    half = WLAT // 2
    n = lax.broadcasted_iota(jnp.int32, (rows, 1), 0)
    return jnp.where(
        lat_inside(n) >= half,
        pltpu.roll(scr_own[...], half, axis=0),
        pltpu.roll(scr_oth[...], rows - half, axis=0),
    )


def second_kernel(
    lat_total,
    tail, lon_head, lat_tail, diag_head, bias, qkv_w, proj_w, up_w, down_w, gains,
    head_out, tail_out, n1_out, field_out, mixed_out, low_out, n2_out, hg_out, active_out, g_out,
    sums_out, gain_out,
    scr_own, scr_oth, qkv_scr, probs_scr, dmix_scr,
):
    lat = lax.axis_index("lat")
    rows, width = scr_own.shape
    cut = CHUNK * (WLON // 2)

    def rolled(which):
        scr_own[0 : rows - cut, :] = tail[which].astype(F32)
        scr_own[rows - cut :, :] = lon_head[which].astype(F32)
        scr_oth[0 : rows - cut, :] = lat_tail[which].astype(F32)
        scr_oth[rows - cut :, :] = diag_head[which].astype(F32)
        return merge_ahead(scr_own, scr_oth, rows)

    g = rolled(1)
    n = lax.broadcasted_iota(jnp.int32, (rows, 1), 0)
    keep = lat_row(n, lat, True, lat_total) < lat_total - PAD
    g = jnp.where(keep, g, 0.0)
    g_out[...] = g.astype(BF16)

    x = rolled(0)

    resid, normed = forward_core(
        x, 1, lat, lat_total, (qkv_w, proj_w, gains), qkv_scr, bias, mixed_out, probs_scr
    )
    n1_out[...] = normed
    stand2, inv2 = standardize(resid)
    normed2 = (stand2 * gains[1, 1:2, :]).astype(BF16)
    n2_out[...] = normed2
    active, slope = gelu_parts(dot(normed2, up_w[1]))
    active_out[...] = active.astype(BF16)

    hg = (dot(g_out[...], down_w[1]) * slope).astype(BF16)
    hg_out[...] = hg
    part, gain_two = norm_back(dot_nt(hg, up_w[1]), gains[1, 1:2, :], stand2, inv2)
    rg = g + part
    low = rg.astype(BF16)
    low_out[...] = low
    dmix_scr[...] = dot_nt(low, proj_w[1]).astype(BF16)
    sums_out[...] = jnp.zeros(sums_out.shape, F32)
    attend_back(
        qkv_scr, probs_scr, dmix_scr, field_out, sums_out, width, 0, probs_scr.shape[0]
    )
    ng = dot_nt(field_out[...], qkv_w[1]).astype(BF16).astype(F32)
    stand1, inv1 = standardize(x)
    part, gain_one = norm_back(ng, gains[1, 0:1, :], stand1, inv1)
    dx = rg + part
    head_out[...] = dx[0 : rows - cut, :].astype(BF16)
    tail_out[...] = dx[rows - cut :, :].astype(BF16)
    gain_out[0:1, :] = gain_one
    gain_out[1:2, :] = gain_two


def outer_kernel(
    n1, field, mixed, low, n2, hg, active, g, sums,
    keep, give, bias_out,
    m576, m192, m768, mdown, flat_scr,
):
    put(m576, slice(None), dot_tn(n1[...], field[...]))
    at = flat_store(flat_scr, 0, m576, field.shape[1])
    put(m192, slice(None), dot_tn(mixed[...], low[...]))
    at += flat_store(flat_scr, at, m192, mixed.shape[1])
    put(m768, slice(None), dot_tn(n2[...], hg[...]))
    at += flat_store(flat_scr, at, m768, active.shape[1])
    put(mdown, slice(None), dot_tn(active[...], g[...]))
    at += flat_store(flat_scr, at, mdown, mixed.shape[1])
    halves(flat_scr, lax.axis_index("lat"), keep, give)
    bias_units(sums, bias_out)


def lat_sum(keep_a, got_a, bias_a, keep_b, got_b, out):
    one, two = keep_a.shape[1], bias_a.shape[1]
    out[:, 0:one] = (keep_a[...].astype(F32) + got_a[...].astype(F32)).astype(BF16)
    out[:, one : one + two] = bias_a[...]
    out[:, one + two :] = (keep_b[...].astype(F32) + got_b[...].astype(F32)).astype(BF16)


def lat_sum_late(keep, got, bias, out):
    one = keep.shape[1]
    out[:, 0:one] = (keep[...].astype(F32) + got[...].astype(F32)).astype(BF16)
    out[:, one:] = bias[...]


def sum_pieces(pieces, order, out):
    total = pieces[0].astype(F32)
    for k in range(1, pieces.shape[0]):
        total = total + pieces[k].astype(F32)
    for k in range(out.shape[0]):
        out[k] = total.astype(BF16)


def third_kernel(
    head, lon_tail, lat_head, diag_tail, resid_in, slope, active, mixed,
    proj_w, up_w, down_w, gains, keep_a,
    keep_out, give_out, rg_out, dmix_out, gain_out,
    scr_own, scr_oth, m192, m768, mdown, flat_scr,
):
    rows, width = scr_own.shape
    cut = CHUNK * (WLON // 2)
    scr_own[0:cut, :] = lon_tail[...].astype(F32)
    scr_own[cut:, :] = head[...].astype(F32)
    scr_oth[0:cut, :] = diag_tail[...].astype(F32)
    scr_oth[cut:, :] = lat_head[...].astype(F32)
    g = merge_behind(scr_own, scr_oth, rows)
    g_low = g.astype(BF16)
    hg = (dot(g_low, down_w[0]) * slope[...].astype(F32)).astype(BF16)
    stand2, inv2 = standardize(resid_in[...].astype(F32))
    normed2 = (stand2 * gains[0, 1:2, :]).astype(BF16)
    part, gain_two = norm_back(dot_nt(hg, up_w[0]), gains[0, 1:2, :], stand2, inv2)
    rg = g + part
    rg_out[...] = rg
    low = rg.astype(BF16)
    dmix_out[...] = dot_nt(low, proj_w[0]).astype(BF16)
    gain_out[...] = gain_two
    put(m192, slice(None), dot_tn(mixed[...], low))
    at = flat_store(flat_scr, 0, m192, mixed.shape[1])
    put(m768, slice(None), dot_tn(normed2, hg))
    at += flat_store(flat_scr, at, m768, active.shape[1])
    put(mdown, slice(None), dot_tn(active[...], g_low))
    at += flat_store(flat_scr, at, mdown, mixed.shape[1])
    flat_scr[at:, :] = jnp.zeros((flat_scr.shape[0] - at, 128), F32)
    halves(flat_scr, lax.axis_index("lat"), keep_out, give_out)


def gain_rows(one, two):
    return jnp.concatenate(
        [
            one[:, 0:128],
            jnp.concatenate([one[:, 128:192], two[:, 0:64]], axis=1),
            two[:, 64:192],
        ],
        axis=0,
    )


def fourth_kernel(
    x_in, qkv, probs_in, dmix, rg, gain_two, gains_late, order, qkv_w, gains,
    tokens_out, keep, give, bias_out,
    field, sums, m576, flat_scr, dx_scr, probs, sems,
):
    copies = [
        pltpu.make_async_copy(probs_in.at[w], probs.at[w], sems.at[w])
        for w in range(probs.shape[0])
    ]
    for copy in copies:
        copy.start()
    width = x_in.shape[-1]
    levels, lats, lons = tokens_out.shape[:3]
    sums[...] = jnp.zeros(sums.shape, F32)
    for copy in copies:
        copy.wait()
    attend_back(qkv, probs, dmix, field, sums, width, 0, probs.shape[0])
    stand1, inv1 = standardize(x_in[...].astype(F32))
    normed = (stand1 * gains[0, 0:1, :]).astype(BF16)
    ng = dot_nt(field[...], qkv_w[0]).astype(BF16).astype(F32)
    part, gain_one = norm_back(ng, gains[0, 0:1, :], stand1, inv1)
    put(m576, slice(None), dot_tn(normed, field[...]))
    at = flat_store(flat_scr, 0, m576, field.shape[1])
    flat_scr[at:, :] = jnp.zeros((flat_scr.shape[0] - at, 128), F32)
    flat_scr[at : at + 3, :] = gain_rows(gain_one, gain_two[...])
    flat_scr[at + 3 : at + 6, :] = gain_rows(gains_late[0:1, :], gains_late[1:2, :])
    bias_units(sums, bias_out)
    halves(flat_scr, lax.axis_index("lat"), keep, give)
    put(dx_scr, slice(None), rg[...] + part)
    for z in range(levels):
        for a in range(lats):
            tokens_out[z, a] = get(
                dx_scr, pl.ds(z * lats + a, lons, stride=CHUNK), width
            ).astype(BF16)


def last_kernel(
    units_a, units_c, extra, spread, own_ab, oth_ab, own_c, oth_c, update_out, bias_out,
    scr, rows_scr, wide_scr, tab_scr,
):
    lat = lax.axis_index("lat")
    lons = own_ab.shape[0]

    def place(own, oth, first, last, dests):
        total = jnp.zeros((UNIT, 128), F32)
        per = last - first
        k = 0
        for where, room in dests:
            for at in range(where, where + room, UNIT):
                half, j, u = k // (per * lons), k // per % lons, k % per
                value = jnp.where(
                    lat == half, own[j, first + u].astype(F32), oth[j, first + u].astype(F32)
                )
                scr[at : at + UNIT, :] = value
                total = total + value * value
                k += 1
        return total

    total = place(
        own_ab, oth_ab, 0, units_a, [(864, 864), (2016, 288), (3456, 1152), (5760, 1152)]
    )
    total = total + place(
        own_ab, oth_ab, units_a + extra, own_ab.shape[1],
        [(1728, 288), (2304, 1152), (4608, 1152)],
    )
    total = total + place(own_c, oth_c, 0, units_c, [(0, 864), (6912, 8)])
    count = update_out.shape[0]
    mean = jnp.sum(total) * (1.0 / (count * 128))
    scale = lax.rsqrt(mean + 1e-06)
    update_out[...] = (scr[0:count, :] * scale).astype(BF16)

    for b, (piece, base) in enumerate(((own_c, units_c), (own_ab, units_a))):

        def read(at):
            parts = []
            for r in range(CHUNK // UNIT):
                k = at * (CHUNK // UNIT) + r
                parts.append(piece[k // extra, base + k % extra].astype(F32))
            return jnp.concatenate(parts, axis=0)

        rest = read(2 * HEADS)
        for h in range(HEADS):
            rows = pl.ds(h, CHUNK, stride=8)
            wide_scr[0, rows, :] = read(h)
            wide_scr[1, rows, :] = read(HEADS + h)
            wide_scr[2, rows, :] = rest if h == 0 else pltpu.roll(rest, 128 - 8 * h, axis=1)
        low = get(wide_scr, slice(None), WIDE).astype(BF16)
        for zj in range(LEVELS):
            rows_scr[...] = dot_nt(low, spread[zj])
            for zi in range(LEVELS):
                for ai in range(WLAT):
                    at = ((zi * LEVELS + zj) * WLAT + ai) * PAIR
                    row = (zi * WLAT + ai) * 8
                    tab_scr[0:HEADS, at : at + PAIR] = rows_scr[row : row + HEADS, 0:PAIR]
        for h in range(HEADS):
            bias_out[b, h] = tab_scr[h : h + 1, :]


def call(kernel, outs, scratch, args, micros, mib, spaces=None):
    spaces = spaces or [pltpu.VMEM] * len(args)
    return pl.pallas_call(
        kernel,
        out_shape=[jax.ShapeDtypeStruct(shape, dtype) for shape, dtype in outs],
        in_specs=[pl.BlockSpec(memory_space=space) for space in spaces],
        out_specs=[pl.BlockSpec(memory_space=pltpu.VMEM)] * len(outs),
        scratch_shapes=[
            pltpu.VMEM(*entry) if isinstance(entry, tuple) else entry for entry in scratch
        ],
        compiler_params=pltpu.CompilerParams(vmem_limit_bytes=mib * MIB),
        cost_estimate=pl.CostEstimate(
            flops=int(micros * 1.1e9), bytes_accessed=10**5, transcendentals=0
        ),
    )(*args)


def lat_swap(value):
    return lax.ppermute(value, "lat", [(0, 1), (1, 0)])


def lon_send(value, step):
    count = lax.axis_size("lon")
    return lax.ppermute(value, "lon", [(s, (s + step) % count) for s in range(count)])


def diag_send(value, step):
    count = lax.axis_size("lon")
    pairs = []
    for s in range(count):
        for t in range(2):
            pairs.append((2 * s + t, 2 * ((s + step) % count) + 1 - t))
    return lax.ppermute(value, ("lon", "lat"), pairs)


def shards(
    tokens, cotangent, qkv_weight, proj_weight, up_weight, down_weight, norm_gain, bias_table
):
    levels, lats, lons, width = tokens.shape
    rows = levels * lats * lons
    wins = rows // WIN
    hid = up_weight.shape[-1]
    heads = bias_table.shape[2]
    lon_size = lax.axis_size("lon")
    zs = lon_size // 2
    lat_total = lats * lax.axis_size("lat")
    cut = CHUNK * (WLON // 2)
    spread = jnp.asarray(spread_matrices(), BF16)
    down_turned = jnp.swapaxes(down_weight, 1, 2)
    table = jnp.swapaxes(bias_table, 1, 2)
    token = (rows, width)
    field_shape = ((rows, 3 * width), BF16)
    probs_shape = ((wins, heads, WIN, WIN), F32)
    bias_shape = ((heads * WIN, WIN), F32)
    sums_shape = ((heads * WIN, WIDE), F32)
    tab_scr = ((8, table.shape[-1]), F32)
    rows_scr = ((LEVELS * CHUNK * 8, PAIR), F32)
    wide_scr = ((WIDE // 128, CHUNK * 8, 128), F32)
    tiles = -(-width // 128)
    token_scr = ((tiles, rows, 128), F32)
    m576 = ((-(-3 * width // 128), width, 128), F32)
    m192 = ((tiles, width, 128), F32)
    m768 = ((hid // 128, width, 128), F32)
    mdown = ((tiles, hid, 128), F32)

    block_rows = (qkv_weight[0].size + proj_weight[0].size + 2 * up_weight[0].size) // 128
    qkv_rows = qkv_weight[0].size // 128
    counts = (block_rows, block_rows - qkv_rows, qkv_rows + 8)
    units_a, units_b, units_c = [-(-count // (2 * lon_size * UNIT)) for count in counts]
    extra = -(-BIAS_UNITS // lon_size)

    def units(*lead):
        return (lead + (UNIT, 128), BF16)

    def flat_scr(per):
        return ((2 * lon_size * per * UNIT, 128), F32)

    x0, tail, head, qkv0, mixed0, probs0, resid0, slope0, active0 = call(
        functools.partial(first_kernel, lat_total),
        [
            (token, BF16),
            ((2, rows - cut, width), BF16),
            ((2, cut, width), BF16),
            field_shape,
            (token, BF16),
            probs_shape,
            (token, BF16),
            ((rows, hid), BF16),
            ((rows, hid), BF16),
        ],
        [
            token_scr,
            token_scr,
            tab_scr,
            rows_scr,
            wide_scr,
            bias_shape,
            (cotangent.shape, BF16),
            ((1,) + table.shape[1:], F32),
            (spread.shape, BF16),
            (tokens.shape, BF16),
            ((1,) + qkv_weight.shape[1:], BF16),
            (norm_gain.shape, F32),
            ((1,) + proj_weight.shape[1:], BF16),
            ((1,) + up_weight.shape[1:], BF16),
            ((1,) + down_turned.shape[1:], BF16),
            pltpu.SemaphoreType.DMA((9,)),
        ],
        [
            pltpu.with_memory_space_constraint(arg, pltpu.HBM)
            for arg in (
                tokens, cotangent, table, spread, qkv_weight, proj_weight, up_weight, down_turned,
                norm_gain,
            )
        ],
        8,
        28,
        [pltpu.HBM] * 9,
    )
    lon_head = lon_send(head, -1)
    diag_head = diag_send(head, -1)
    lat_tail = lat_swap(tail)
    (bias1,) = call(
        functools.partial(bias_kernel, lat_total),
        [bias_shape],
        [tab_scr, rows_scr, wide_scr],
        (table, spread),
        2,
        10,
    )

    (
        dhead, dtail, n1, field1, mixed1, low1, n2, hg1, active1, g1, sums1, gains1,
    ) = call(
        functools.partial(second_kernel, lat_total),
        [
            ((rows - cut, width), BF16),
            ((cut, width), BF16),
            (token, BF16),
            field_shape,
            (token, BF16),
            (token, BF16),
            (token, BF16),
            ((rows, hid), BF16),
            ((rows, hid), BF16),
            (token, BF16),
            sums_shape,
            ((2, width), F32),
        ],
        [(token, F32), (token, F32), field_shape, probs_shape, (token, BF16)],
        (
            tail, lon_head, lat_tail, diag_head, bias1, qkv_weight, proj_weight, up_weight,
            down_turned, norm_gain,
        ),
        19,
        28,
    )
    lon_tail = lon_send(dtail, 1)
    diag_tail = diag_send(dtail, 1)
    lat_dhead = lat_swap(dhead)

    keep_a, give_a, bias_a = call(
        outer_kernel,
        [units(lon_size, units_a), units(lon_size, units_a), units(lon_size, extra)],
        [m576, m192, m768, mdown, flat_scr(units_a)],
        (n1, field1, mixed1, low1, n2, hg1, active1, g1, sums1),
        3,
        20,
    )
    got_a = lat_swap(give_a)

    keep_b, give_b, rg0, dmix0, gain_two = call(
        third_kernel,
        [
            units(lon_size, units_b),
            units(lon_size, units_b),
            (token, F32),
            (token, BF16),
            ((1, width), F32),
        ],
        [(token, F32), (token, F32), m192, m768, mdown, flat_scr(units_b)],
        (
            dhead, lon_tail, lat_dhead, diag_tail, resid0, slope0, active0, mixed0,
            proj_weight, up_weight, down_turned, norm_gain, keep_a,
        ),
        2,
        20,
    )
    got_b = lat_swap(give_b)
    (part_ab,) = call(
        lat_sum,
        [units(lon_size, units_a + extra + units_b)],
        [],
        (keep_a, got_a, bias_a, keep_b, got_b),
        1,
        10,
    )
    pieces_ab = lax.all_to_all(part_ab, "lon", 0, 0)

    tokens_grad, keep_c, give_c, bias_c = call(
        fourth_kernel,
        [
            (tokens.shape, BF16),
            units(lon_size, units_c),
            units(lon_size, units_c),
            units(lon_size, extra),
        ],
        [
            field_shape,
            sums_shape,
            m576,
            flat_scr(units_c),
            token_scr,
            probs_shape,
            pltpu.SemaphoreType.DMA((wins,)),
        ],
        (
            x0, qkv0, pltpu.with_memory_space_constraint(probs0, pltpu.HBM), dmix0, rg0, gain_two,
            gains1, part_ab, qkv_weight, norm_gain,
        ),
        11,
        24,
        [pltpu.VMEM] * 2 + [pltpu.HBM] + [pltpu.VMEM] * 7,
    )
    got_c = lat_swap(give_c)
    (part_c,) = call(
        lat_sum_late, [units(lon_size, units_c + extra)], [], (keep_c, got_c, bias_c), 1, 10
    )
    pieces_c = lax.all_to_all(part_c, "lon", 0, 0)

    (sum_ab,) = call(
        sum_pieces, [units(lon_size, units_a + extra + units_b)], [], (pieces_ab, part_c), 1, 10
    )
    whole_ab = lax.all_to_all(sum_ab, "lon", 0, 0)
    (sum_c,) = call(
        sum_pieces, [units(lon_size, units_c + extra)], [], (pieces_c, sum_ab), 1, 10
    )
    whole_c = lax.all_to_all(sum_c, "lon", 0, 0)
    oth_ab = lat_swap(whole_ab)
    oth_c = lat_swap(whole_c)

    flat_rows = (2 * block_rows * 128 + norm_gain.size) // 128
    update, bias_grad = call(
        functools.partial(last_kernel, units_a, units_c, extra),
        [((flat_rows, 128), BF16), (table.shape, F32)],
        [((flat_rows + 2, 128), F32), ((CHUNK * 8, PAIR), F32), wide_scr, tab_scr],
        (spread, whole_ab, oth_ab, whole_c, oth_c),
        3,
        20,
    )
    bias_grad = jnp.swapaxes(bias_grad, 1, 2)
    return (tokens_grad, update.reshape(-1), bias_grad)


def solution(mesh):
    return jax.shard_map(
        shards,
        mesh=mesh,
        in_specs=(
            P("grp", "lat", "lon", None),
            P("grp", "lat", "lon", None),
            P(),
            P(),
            P(),
            P(),
            P(),
            P(None, "lat", None, None),
        ),
        out_specs=(P("grp", "lat", "lon", None), P("grp"), P("grp", "lat", None, None)),
        check_vma=False,
    )
```

```python
import functools

import jax
import jax.numpy as jnp
import numpy as np
from jax import lax
from jax.experimental import pallas as pl
from jax.experimental.pallas import tpu as pltpu
from jax.sharding import PartitionSpec as P

WLAT = 12
WLON = 6
PAD = 5
LEVELS = 2
HEADS = 6
CHUNK = LEVELS * WLAT
WIN = CHUNK * WLON
SHIFTS = 2 * WLON - 1
PAIR = WLAT * SHIFTS
WIDE = 384

EPS = 1e-05
NEGATIVE = -1000000000.0
ROOT_HALF = 0.7071067811865476
INV_ROOT_TAU = 0.3989422804014327

F32 = jnp.float32
BF16 = jnp.bfloat16
UNIT = 8
BIAS_UNITS = (2 * HEADS + 1) * CHUNK // UNIT
MIB = 1024 * 1024


def dot(a, b):
    return lax.dot_general(a, b, (((1,), (0,)), ((), ())), preferred_element_type=F32)


def dot_nt(a, b):
    return lax.dot_general(a, b, (((1,), (1,)), ((), ())), preferred_element_type=F32)


def dot_tn(a, b):
    return lax.dot_general(a, b, (((0,), (0,)), ((), ())), preferred_element_type=F32)


def row_mean(v):
    return jnp.sum(v, axis=-1, keepdims=True) * (1.0 / v.shape[-1])


def standardize(x):
    centred = x - row_mean(x)
    inv = lax.rsqrt(row_mean(centred * centred) + EPS)
    return centred * inv, inv


def norm_back(d, gain, stand, inv):
    scaled = d * gain
    first = row_mean(scaled)
    second = row_mean(scaled * stand)
    gain_grad = jnp.sum(d * stand, axis=0, keepdims=True)
    return inv * (scaled - first - stand * second), gain_grad


def gelu_parts(hidden):
    half = 0.5 * (1.0 + lax.erf(hidden * ROOT_HALF))
    slope = half + hidden * jnp.exp(-0.5 * hidden * hidden) * INV_ROOT_TAU
    return hidden * half, slope


def split3(v):
    hi = v.astype(BF16)
    rest = v - hi.astype(F32)
    mid = rest.astype(BF16)
    low = (rest - mid.astype(F32)).astype(BF16)
    return hi, mid, low


def spread_matrices():
    out = np.zeros((LEVELS, PAIR, WIDE), np.float32)
    for zj in range(LEVELS):
        for aj in range(WLAT):
            for d in range(SHIFTS):
                out[zj, aj * SHIFTS + d, (SHIFTS - 1 - d) * CHUNK + zj * WLAT + aj] = 1.0
    return out


def put(scr, rows, value):
    width = value.shape[1]
    for tile in range(-(-width // 128)):
        lanes = min(128, width - tile * 128)
        scr[tile, rows, 0:lanes] = value[:, tile * 128 : tile * 128 + lanes]


def get(scr, rows, width):
    parts = [scr[tile, rows, :] for tile in range(-(-width // 128))]
    return jnp.concatenate(parts, axis=1)[:, 0:width]


def head_masks(width, dtype):
    lane = lax.broadcasted_iota(jnp.int32, (1, width), 1)
    size = width // HEADS
    return [((lane >= h * size) & (lane < (h + 1) * size)).astype(dtype) for h in range(HEADS)]


def lat_inside(n):
    return lax.rem(n, WLAT)


def lat_row(row_iota, lat, shifted, lat_total):
    row = lat * WLAT + lat_inside(row_iota)
    if shifted:
        row = row + WLAT // 2
        row = jnp.where(row >= lat_total, row - lat_total, row)
    return row


def expand_bias(table, spread, tab_scr, rows_scr, wide_scr, bias_scr, lat, shifted, lat_total):
    for h in range(HEADS):
        tab_scr[h : h + 1, :] = table[h]
    for zi in range(LEVELS):
        for zj in range(LEVELS):
            for ai in range(WLAT):
                at = ((zi * LEVELS + zj) * WLAT + ai) * PAIR
                row = zj * CHUNK * 8 + (zi * WLAT + ai) * 8
                rows_scr[row : row + HEADS, 0:PAIR] = tab_scr[0:HEADS, at : at + PAIR]
    count = CHUNK * 8
    total = jnp.zeros((count, WIDE), F32)
    for zj in range(LEVELS):
        parts = split3(rows_scr[zj * count : (zj + 1) * count, 0:PAIR])
        for part in parts:
            total = total + dot(part, spread[zj])
    put(wide_scr, slice(None), total)
    i = lax.broadcasted_iota(jnp.int32, (CHUNK, WIN), 0)
    j = lax.broadcasted_iota(jnp.int32, (CHUNK, WIN), 1)
    allowed = lat_row(j, lat, shifted, lat_total) < lat_total - PAD
    if shifted:
        last = lat_total - WLAT // 2
        region_i = (lat * WLAT + lat_inside(i)) >= last
        region_j = (lat * WLAT + lat_inside(j)) >= last
        allowed = allowed & (region_i == region_j)
    for h in range(HEADS):
        wide = get(wide_scr, pl.ds(h, CHUNK, stride=8), WIDE)
        for oi in range(WLON):
            back = (WLON - 1 - oi) * CHUNK
            moved = wide if back == 0 else pltpu.roll(wide, WIDE - back, axis=1)
            at = h * WIN + oi * CHUNK
            bias_scr[at : at + CHUNK, :] = jnp.where(allowed, moved[:, 0:WIN], NEGATIVE)


def fold_bias(sums, put_unit):
    rest = jnp.zeros((CHUNK, 128), F32)

    def emit(at, value):
        for r in range(CHUNK // UNIT):
            put_unit(at * (CHUNK // UNIT) + r, value[r * UNIT : (r + 1) * UNIT, :].astype(BF16))

    for h in range(HEADS):
        total = jnp.zeros((CHUNK, WIDE), F32)
        for oi in range(WLON):
            back = (WLON - 1 - oi) * CHUNK
            at = h * WIN + oi * CHUNK
            part = sums[at : at + CHUNK, :]
            total = total + (part if back == 0 else pltpu.roll(part, back, axis=1))
        emit(h, total[:, 0:128])
        emit(HEADS + h, total[:, 128:256])
        last = total[:, 256:384]
        rest = rest + (last if h == 0 else pltpu.roll(last, 8 * h, axis=1))
    emit(2 * HEADS, rest)

def stack_heads(v, masks):
    return jnp.concatenate([v * mask for mask in masks], axis=0)


def pick_heads(v, masks):
    total = v[0:WIN] * masks[0]
    for h in range(1, HEADS):
        total = total + v[h * WIN : (h + 1) * WIN] * masks[h]
    return total


def attend(qkv, bias, mixed, probs, stack_scr, width, finish=None):
    masks = head_masks(width, BF16)
    masks32 = head_masks(width, F32)
    scale = (width // HEADS) ** -0.5

    def window(w, carry):
        rows = pl.ds(pl.multiple_of(w * WIN, 16), WIN)
        q = qkv[rows, 0:width]
        k = qkv[rows, width : 2 * width]
        v = qkv[rows, 2 * width : 3 * width]
        scores = dot_nt(stack_heads(q, masks), k)
        for h in range(HEADS):
            part = slice(h * WIN, (h + 1) * WIN)
            logits = scores[part] * scale + bias[part, :]
            weights = jnp.exp(logits - jnp.max(logits, axis=-1, keepdims=True))
            p = weights * (1.0 / jnp.sum(weights, axis=-1, keepdims=True))
            probs[w, h] = p
            stack_scr[part, :] = p.astype(BF16)
        mixed[rows, :] = pick_heads(dot(stack_scr[...], v), masks32).astype(BF16)
        if finish is not None:
            finish(w)
        return carry

    lax.fori_loop(0, probs.shape[0], window, 0)


def attend_back(qkv, probs, dmix, field, sums, low_scr, prob_scr, width, begin=None):
    masks = head_masks(width, BF16)
    masks32 = head_masks(width, F32)
    scale = (width // HEADS) ** -0.5

    def window(w, carry):
        rows = pl.ds(pl.multiple_of(w * WIN, 16), WIN)
        q = qkv[rows, 0:width]
        k = qkv[rows, width : 2 * width]
        v = qkv[rows, 2 * width : 3 * width]
        up = stack_heads(dmix[rows, :], masks)
        prob_grad = dot_nt(up, v)
        if begin is not None:
            begin(w)
        for h in range(HEADS):
            part = slice(h * WIN, (h + 1) * WIN)
            p = probs[w, h]
            weighted = p * prob_grad[part]
            ds = weighted - p * jnp.sum(weighted, axis=-1, keepdims=True)
            sums[part, 0:WIN] += ds
            low_scr[part, :] = ds.astype(BF16)
            prob_scr[part, :] = p.astype(BF16)
        low = low_scr[...]
        dq = pick_heads(dot(low, k), masks32)
        dk = dot_tn(low, stack_heads(q, masks))
        dv = dot_tn(prob_scr[...], up)
        field[rows, 0:width] = (dq * scale).astype(BF16)
        field[rows, width : 2 * width] = (dk * scale).astype(BF16)
        field[rows, 2 * width : 3 * width] = dv.astype(BF16)
        return carry

    lax.fori_loop(0, probs.shape[0], window, 0)


def lon_major(src, scr):
    levels, lats, lons, width = src.shape
    for z in range(levels):
        for a in range(lats):
            at = (z * lats + a) * lons
            put(scr, slice(at, at + lons), src[z, a].astype(F32))


def lon_column(scr, lon, lons, width):
    return get(scr, pl.ds(lon, CHUNK, stride=lons), width)


def flat_store(dst, at, mat, cols):
    rows = mat.shape[1]
    if cols % 128 == 0:
        per = cols // 128
        for c in range(per):
            dst[pl.ds(at + c, rows, stride=per), :] = mat[c]
        return rows * per
    per = 2 * cols // 128
    half = cols // 128
    even = get(mat, pl.ds(0, rows // 2, stride=2), cols)
    odd = get(mat, pl.ds(1, rows // 2, stride=2), cols)
    for c in range(half):
        dst[pl.ds(at + c, rows // 2, stride=per), :] = even[:, c * 128 : (c + 1) * 128]
    dst[pl.ds(at + half, rows // 2, stride=per), :] = jnp.concatenate(
        [even[:, half * 128 : half * 128 + 64], odd[:, 0:64]], axis=1
    )
    for c in range(half):
        dst[pl.ds(at + half + 1 + c, rows // 2, stride=per), :] = odd[
            :, 64 + c * 128 : 64 + (c + 1) * 128
        ]
    return rows * cols // 128


def send_units(scr, base, out):
    lons, units = out.shape[:2]
    for j in range(lons):
        for u in range(units):
            at = base + (j * units + u) * UNIT
            if not isinstance(at, int):
                at = pl.multiple_of(at, UNIT)
            out[j, u] = scr[pl.ds(at, UNIT), :].astype(BF16)


def halves(scr, lat, keep, give):
    half = keep.shape[0] * keep.shape[1] * UNIT
    send_units(scr, lat * half, keep)
    send_units(scr, (1 - lat) * half, give)


def bias_units(sums, out):
    lons, per = out.shape[:2]

    def put_unit(k, value):
        out[k // per, k % per] = value

    fold_bias(sums, put_unit)
    for k in range(BIAS_UNITS, lons * per):
        put_unit(k, jnp.zeros((UNIT, 128), BF16))

def forward_core(x, b, refs, qkv_scr, bias_scr, mixed, probs, stack_scr, finish=None):
    qkv_w, proj_w, gains = refs
    width = x.shape[-1]
    stand, inv = standardize(x)
    normed = (stand * gains[b, 0:1, :]).astype(BF16)
    qkv_scr[...] = dot(normed, qkv_w[b]).astype(BF16)
    attend(qkv_scr, bias_scr, mixed, probs, stack_scr, width, finish)
    att = dot(mixed[...], proj_w[b]).astype(BF16)
    resid = (x + att.astype(F32)).astype(BF16).astype(F32)
    return resid, normed


def first_kernel(
    lat_total, tokens_in, cot_in, table_in, spread_in, qkv_in, proj_in, up_in, down_in, gains_in,
    x_out, tail_out, head_out, qkv_out, mixed_out, probs_out, resid_out, slope_out, active_out,
    scr, cot_scr, tab_scr, rows_scr, wide_scr, bias_scr,
    cot, table, spread, tokens, qkv_w, gains, proj_w, up_w, down_w, stack_scr,
    probs, slope_scr, active_scr, sems, out_sems,
):
    copies = []
    for source, target in (
        (cot_in, cot),
        (table_in.at[0:1], table),
        (spread_in, spread),
        (tokens_in, tokens),
        (qkv_in.at[0:1], qkv_w),
        (gains_in, gains),
        (proj_in.at[0:1], proj_w),
        (up_in.at[0:1], up_w),
        (down_in.at[0:1], down_w),
    ):
        copies.append(pltpu.make_async_copy(source, target, sems.at[len(copies)]))
    for copy in copies:
        copy.start()
    lat = lax.axis_index("lat")
    width = tokens.shape[-1]
    lons = tokens.shape[2]
    cut = CHUNK * (WLON // 2)
    copies[0].wait()
    lon_major(cot, cot_scr)
    g = jnp.concatenate([lon_column(cot_scr, lon, lons, width) for lon in range(lons)], axis=0)
    head_out[1] = g[0:cut, :].astype(BF16)
    tail_out[1] = g[cut:, :].astype(BF16)
    copies[1].wait()
    copies[2].wait()
    expand_bias(
        table.at[0], spread, tab_scr, rows_scr, wide_scr, bias_scr, lat, False, lat_total
    )
    copies[3].wait()
    lon_major(tokens, scr)
    x = jnp.concatenate([lon_column(scr, lon, lons, width) for lon in range(lons)], axis=0)
    x_out[...] = x.astype(BF16)
    for copy in copies[4:]:
        copy.wait()

    def probs_copy(w):
        return pltpu.make_async_copy(probs.at[w], probs_out.at[w], out_sems.at[w])

    resid, _ = forward_core(
        x, 0, (qkv_w, proj_w, gains), qkv_out, bias_scr, mixed_out, probs, stack_scr,
        lambda w: probs_copy(w).start(),
    )
    resid_out[...] = resid.astype(BF16)
    stand, _ = standardize(resid)
    normed = (stand * gains[0, 1:2, :]).astype(BF16)
    active, slope = gelu_parts(dot(normed, up_w[0]))
    active = active.astype(BF16)
    active_scr[...] = active
    slope_scr[...] = slope.astype(BF16)
    wins = probs.shape[0]
    last = [
        pltpu.make_async_copy(active_scr, active_out, out_sems.at[wins]),
        pltpu.make_async_copy(slope_scr, slope_out, out_sems.at[wins + 1]),
    ]
    for copy in last:
        copy.start()
    result = resid + dot_nt(active, down_w[0])
    head_out[0] = result[0:cut, :].astype(BF16)
    tail_out[0] = result[cut:, :].astype(BF16)
    for copy in [probs_copy(w) for w in range(wins)] + last:
        copy.wait()


def bias_kernel(lat_total, table, spread, bias_out, tab_scr, rows_scr, wide_scr):
    lat = lax.axis_index("lat")
    expand_bias(
        table.at[1], spread, tab_scr, rows_scr, wide_scr, bias_out, lat, True, lat_total
    )


def merge_ahead(scr_own, scr_oth, rows):
    half = WLAT // 2
    n = lax.broadcasted_iota(jnp.int32, (rows, 1), 0)
    return jnp.where(
        lat_inside(n) < half,
        pltpu.roll(scr_own[...], rows - half, axis=0),
        pltpu.roll(scr_oth[...], half, axis=0),
    )


def merge_behind(scr_own, scr_oth, rows):
    half = WLAT // 2
    n = lax.broadcasted_iota(jnp.int32, (rows, 1), 0)
    return jnp.where(
        lat_inside(n) >= half,
        pltpu.roll(scr_own[...], half, axis=0),
        pltpu.roll(scr_oth[...], rows - half, axis=0),
    )


def second_kernel(
    lat_total,
    tail, lon_head, lat_tail, diag_head, bias, qkv_w, proj_w, up_w, down_w, gains,
    head_out, tail_out, n1_out, field_out, mixed_out, low_out, n2_out, hg_out, active_out, g_out,
    sums_out, gain_out,
    scr_own, scr_oth, qkv_scr, probs_scr, dmix_scr, low_scr, prob_scr,
):
    lat = lax.axis_index("lat")
    rows, width = scr_own.shape
    cut = CHUNK * (WLON // 2)

    def rolled(which):
        scr_own[0 : rows - cut, :] = tail[which].astype(F32)
        scr_own[rows - cut :, :] = lon_head[which].astype(F32)
        scr_oth[0 : rows - cut, :] = lat_tail[which].astype(F32)
        scr_oth[rows - cut :, :] = diag_head[which].astype(F32)
        return merge_ahead(scr_own, scr_oth, rows)

    g = rolled(1)
    n = lax.broadcasted_iota(jnp.int32, (rows, 1), 0)
    keep = lat_row(n, lat, True, lat_total) < lat_total - PAD
    g = jnp.where(keep, g, 0.0)
    g_out[...] = g.astype(BF16)

    x = rolled(0)

    resid, normed = forward_core(
        x, 1, (qkv_w, proj_w, gains), qkv_scr, bias, mixed_out, probs_scr, low_scr
    )
    n1_out[...] = normed
    stand2, inv2 = standardize(resid)
    normed2 = (stand2 * gains[1, 1:2, :]).astype(BF16)
    n2_out[...] = normed2
    active, slope = gelu_parts(dot(normed2, up_w[1]))
    active_out[...] = active.astype(BF16)

    hg = (dot(g_out[...], down_w[1]) * slope).astype(BF16)
    hg_out[...] = hg
    part, gain_two = norm_back(dot_nt(hg, up_w[1]), gains[1, 1:2, :], stand2, inv2)
    rg = g + part
    low = rg.astype(BF16)
    low_out[...] = low
    dmix_scr[...] = dot_nt(low, proj_w[1]).astype(BF16)
    sums_out[...] = jnp.zeros(sums_out.shape, F32)
    attend_back(
        qkv_scr, probs_scr, dmix_scr, field_out, sums_out, low_scr, prob_scr, width
    )
    ng = dot_nt(field_out[...], qkv_w[1]).astype(BF16).astype(F32)
    stand1, inv1 = standardize(x)
    part, gain_one = norm_back(ng, gains[1, 0:1, :], stand1, inv1)
    dx = rg + part
    head_out[...] = dx[0 : rows - cut, :].astype(BF16)
    tail_out[...] = dx[rows - cut :, :].astype(BF16)
    gain_out[0:1, :] = gain_one
    gain_out[1:2, :] = gain_two


def outer_kernel(
    n1, field, mixed, low, n2, hg, active, g, sums,
    keep, give, bias_out,
    m576, m192, m768, mdown, flat_scr,
):
    put(m576, slice(None), dot_tn(n1[...], field[...]))
    at = flat_store(flat_scr, 0, m576, field.shape[1])
    put(m192, slice(None), dot_tn(mixed[...], low[...]))
    at += flat_store(flat_scr, at, m192, mixed.shape[1])
    put(m768, slice(None), dot_tn(n2[...], hg[...]))
    at += flat_store(flat_scr, at, m768, active.shape[1])
    put(mdown, slice(None), dot_tn(active[...], g[...]))
    at += flat_store(flat_scr, at, mdown, mixed.shape[1])
    halves(flat_scr, lax.axis_index("lat"), keep, give)
    bias_units(sums, bias_out)


def lat_sum(keep_a, got_a, bias_a, keep_b, got_b, out):
    one, two = keep_a.shape[1], bias_a.shape[1]
    out[:, 0:one] = (keep_a[...].astype(F32) + got_a[...].astype(F32)).astype(BF16)
    out[:, one : one + two] = bias_a[...]
    out[:, one + two :] = (keep_b[...].astype(F32) + got_b[...].astype(F32)).astype(BF16)


def lat_sum_late(keep, got, bias, out):
    one = keep.shape[1]
    out[:, 0:one] = (keep[...].astype(F32) + got[...].astype(F32)).astype(BF16)
    out[:, one:] = bias[...]


def sum_pieces(pieces, order, out):
    total = pieces[0].astype(F32)
    for k in range(1, pieces.shape[0]):
        total = total + pieces[k].astype(F32)
    total = total.astype(BF16)
    if len(out.shape) == len(pieces.shape):
        for k in range(out.shape[0]):
            out[k] = total
    else:
        out[...] = total


def join_z(*refs):
    out = refs[-1]
    count = out.shape[0]
    z = lax.div(lax.axis_index("lon"), 2)
    for k in range(count):
        out[lax.rem(z + count - k, count)] = refs[k][...]


def third_kernel(
    head, lon_tail, lat_head, diag_tail, resid_in, slope_in, active_in, mixed,
    proj_w, up_w, down_w, gains, keep_a,
    keep_out, give_out, rg_out, dmix_out, gain_out,
    scr_own, scr_oth, m192, m768, mdown, flat_scr, slope, active, sems,
):
    copies = [
        pltpu.make_async_copy(slope_in, slope, sems.at[0]),
        pltpu.make_async_copy(active_in, active, sems.at[1]),
    ]
    for copy in copies:
        copy.start()
    rows, width = scr_own.shape
    cut = CHUNK * (WLON // 2)
    scr_own[0:cut, :] = lon_tail[...].astype(F32)
    scr_own[cut:, :] = head[...].astype(F32)
    scr_oth[0:cut, :] = diag_tail[...].astype(F32)
    scr_oth[cut:, :] = lat_head[...].astype(F32)
    g = merge_behind(scr_own, scr_oth, rows)
    g_low = g.astype(BF16)
    for copy in copies:
        copy.wait()
    hg = (dot(g_low, down_w[0]) * slope[...].astype(F32)).astype(BF16)
    stand2, inv2 = standardize(resid_in[...].astype(F32))
    normed2 = (stand2 * gains[0, 1:2, :]).astype(BF16)
    part, gain_two = norm_back(dot_nt(hg, up_w[0]), gains[0, 1:2, :], stand2, inv2)
    rg = g + part
    rg_out[...] = rg
    low = rg.astype(BF16)
    dmix_out[...] = dot_nt(low, proj_w[0]).astype(BF16)
    gain_out[...] = gain_two
    put(m192, slice(None), dot_tn(mixed[...], low))
    at = flat_store(flat_scr, 0, m192, mixed.shape[1])
    put(m768, slice(None), dot_tn(normed2, hg))
    at += flat_store(flat_scr, at, m768, active.shape[1])
    put(mdown, slice(None), dot_tn(active[...], g_low))
    at += flat_store(flat_scr, at, mdown, mixed.shape[1])
    flat_scr[at:, :] = jnp.zeros((flat_scr.shape[0] - at, 128), F32)
    halves(flat_scr, lax.axis_index("lat"), keep_out, give_out)


def gain_rows(one, two):
    return jnp.concatenate(
        [
            one[:, 0:128],
            jnp.concatenate([one[:, 128:192], two[:, 0:64]], axis=1),
            two[:, 64:192],
        ],
        axis=0,
    )


def fourth_kernel(
    x_in, qkv, probs_in, dmix, rg, gain_two, gains_late, order, qkv_w, gains,
    tokens_out, keep, give, bias_out,
    field, sums, m576, flat_scr, dx_scr, low_scr, prob_scr, probs, sems,
):
    def probs_copy(w):
        return pltpu.make_async_copy(probs_in.at[w], probs.at[w], sems.at[w])

    for w in range(probs.shape[0]):
        probs_copy(w).start()
    width = x_in.shape[-1]
    levels, lats, lons = tokens_out.shape[:3]
    sums[...] = jnp.zeros(sums.shape, F32)
    attend_back(
        qkv, probs, dmix, field, sums, low_scr, prob_scr, width, lambda w: probs_copy(w).wait()
    )
    stand1, inv1 = standardize(x_in[...].astype(F32))
    normed = (stand1 * gains[0, 0:1, :]).astype(BF16)
    ng = dot_nt(field[...], qkv_w[0]).astype(BF16).astype(F32)
    part, gain_one = norm_back(ng, gains[0, 0:1, :], stand1, inv1)
    put(m576, slice(None), dot_tn(normed, field[...]))
    at = flat_store(flat_scr, 0, m576, field.shape[1])
    flat_scr[at:, :] = jnp.zeros((flat_scr.shape[0] - at, 128), F32)
    flat_scr[at : at + 3, :] = gain_rows(gain_one, gain_two[...])
    flat_scr[at + 3 : at + 6, :] = gain_rows(gains_late[0:1, :], gains_late[1:2, :])
    bias_units(sums, bias_out)
    halves(flat_scr, lax.axis_index("lat"), keep, give)
    put(dx_scr, slice(None), rg[...] + part)
    for z in range(levels):
        for a in range(lats):
            tokens_out[z, a] = get(
                dx_scr, pl.ds(z * lats + a, lons, stride=CHUNK), width
            ).astype(BF16)


def last_kernel(
    units_a, units_c, extra, spread, same, same_x, cross, cross_x, own_c, oth_c,
    update_out, bias_out, scr, rows_scr, wide_scr, tab_scr, ab, c,
):
    lat = lax.axis_index("lat")
    x = lax.rem(lax.axis_index("lon"), 2)
    lons = own_c.shape[0]
    for j in range(lons):
        c[lat, j] = own_c[j]
        c[1 - lat, j] = oth_c[j]
    for z in range(lons // 2):
        ab[lat, 2 * z + x] = same[z]
        ab[lat, 2 * z + 1 - x] = same_x[z]
        ab[1 - lat, 2 * z + x] = cross[z]
        ab[1 - lat, 2 * z + 1 - x] = cross_x[z]

    def place(pieces, first, last, dests):
        total = jnp.zeros((UNIT, 128), F32)
        per = last - first
        k = 0
        for where, room in dests:
            for at in range(where, where + room, UNIT):
                half, j, u = k // (per * lons), k // per % lons, k % per
                value = pieces[half, j, first + u].astype(F32)
                scr[at : at + UNIT, :] = value
                total = total + value * value
                k += 1
        return total

    total = place(
        ab, 0, units_a, [(864, 864), (2016, 288), (3456, 1152), (5760, 1152)]
    )
    total = total + place(
        ab, units_a + extra, ab.shape[2],
        [(1728, 288), (2304, 1152), (4608, 1152)],
    )
    total = total + place(c, 0, units_c, [(0, 864), (6912, 8)])
    count = update_out.shape[0]
    mean = jnp.sum(total) * (1.0 / (count * 128))
    scale = lax.rsqrt(mean + 1e-06)
    update_out[...] = (scr[0:count, :] * scale).astype(BF16)

    for b, (piece, base) in enumerate(((c, units_c), (ab, units_a))):

        def read(at):
            parts = []
            for r in range(CHUNK // UNIT):
                k = at * (CHUNK // UNIT) + r
                parts.append(piece[lat, k // extra, base + k % extra].astype(F32))
            return jnp.concatenate(parts, axis=0)

        rest = read(2 * HEADS)
        for h in range(HEADS):
            rows = pl.ds(h, CHUNK, stride=8)
            wide_scr[0, rows, :] = read(h)
            wide_scr[1, rows, :] = read(HEADS + h)
            wide_scr[2, rows, :] = rest if h == 0 else pltpu.roll(rest, 128 - 8 * h, axis=1)
        low = get(wide_scr, slice(None), WIDE).astype(BF16)
        for zj in range(LEVELS):
            rows_scr[...] = dot_nt(low, spread[zj])
            for zi in range(LEVELS):
                for ai in range(WLAT):
                    at = ((zi * LEVELS + zj) * WLAT + ai) * PAIR
                    row = (zi * WLAT + ai) * 8
                    tab_scr[0:HEADS, at : at + PAIR] = rows_scr[row : row + HEADS, 0:PAIR]
        for h in range(HEADS):
            bias_out[b, h] = tab_scr[h : h + 1, :]


def call(kernel, outs, scratch, args, micros, mib, spaces=None, out_spaces=None):
    spaces = spaces or [pltpu.VMEM] * len(args)
    out_spaces = out_spaces or [pltpu.VMEM] * len(outs)
    return pl.pallas_call(
        kernel,
        out_shape=[
            pltpu.HBM(*entry) if space == pltpu.HBM else jax.ShapeDtypeStruct(*entry)
            for entry, space in zip(outs, out_spaces)
        ],
        in_specs=[pl.BlockSpec(memory_space=space) for space in spaces],
        out_specs=[pl.BlockSpec(memory_space=space) for space in out_spaces],
        scratch_shapes=[
            pltpu.VMEM(*entry) if isinstance(entry, tuple) else entry for entry in scratch
        ],
        compiler_params=pltpu.CompilerParams(vmem_limit_bytes=mib * MIB),
        cost_estimate=pl.CostEstimate(
            flops=int(micros * 1.1e9), bytes_accessed=10**5, transcendentals=0
        ),
    )(*args)


def lat_swap(value):
    return lax.ppermute(value, "lat", [(0, 1), (1, 0)])


def lon_send(value, step):
    count = lax.axis_size("lon")
    return lax.ppermute(value, "lon", [(s, (s + step) % count) for s in range(count)])


def x_swap(value):
    count = lax.axis_size("lon")
    return lax.ppermute(value, "lon", [(s, s ^ 1) for s in range(count)])


def diag_send(value, step):
    count = lax.axis_size("lon")
    pairs = []
    for s in range(count):
        for t in range(2):
            pairs.append((2 * s + t, 2 * ((s + step) % count) + 1 - t))
    return lax.ppermute(value, ("lon", "lat"), pairs)


def shards(
    tokens, cotangent, qkv_weight, proj_weight, up_weight, down_weight, norm_gain, bias_table
):
    levels, lats, lons, width = tokens.shape
    rows = levels * lats * lons
    wins = rows // WIN
    hid = up_weight.shape[-1]
    heads = bias_table.shape[2]
    lon_size = lax.axis_size("lon")
    zs = lon_size // 2
    lat_total = lats * lax.axis_size("lat")
    cut = CHUNK * (WLON // 2)
    spread = jnp.asarray(spread_matrices(), BF16)
    down_turned = jnp.swapaxes(down_weight, 1, 2)
    table = jnp.swapaxes(bias_table, 1, 2)
    token = (rows, width)
    field_shape = ((rows, 3 * width), BF16)
    probs_shape = ((wins, heads, WIN, WIN), F32)
    stack_shape = ((heads * WIN, WIN), BF16)
    bias_shape = ((heads * WIN, WIN), F32)
    sums_shape = ((heads * WIN, WIDE), F32)
    tab_scr = ((8, table.shape[-1]), F32)
    rows_scr = ((LEVELS * CHUNK * 8, PAIR), F32)
    wide_scr = ((WIDE // 128, CHUNK * 8, 128), F32)
    tiles = -(-width // 128)
    token_scr = ((tiles, rows, 128), F32)
    m576 = ((-(-3 * width // 128), width, 128), F32)
    m192 = ((tiles, width, 128), F32)
    m768 = ((hid // 128, width, 128), F32)
    mdown = ((tiles, hid, 128), F32)

    block_rows = (qkv_weight[0].size + proj_weight[0].size + 2 * up_weight[0].size) // 128
    qkv_rows = qkv_weight[0].size // 128
    counts = (block_rows, block_rows - qkv_rows, qkv_rows + 8)
    units_a, units_b, units_c = [-(-count // (2 * lon_size * UNIT)) for count in counts]
    extra = -(-BIAS_UNITS // lon_size)

    def units(*lead):
        return (lead + (UNIT, 128), BF16)

    def flat_scr(per):
        return ((2 * lon_size * per * UNIT, 128), F32)

    x0, tail, head, qkv0, mixed0, probs0, resid0, slope0, active0 = call(
        functools.partial(first_kernel, lat_total),
        [
            (token, BF16),
            ((2, rows - cut, width), BF16),
            ((2, cut, width), BF16),
            field_shape,
            (token, BF16),
            probs_shape,
            (token, BF16),
            ((rows, hid), BF16),
            ((rows, hid), BF16),
        ],
        [
            token_scr,
            token_scr,
            tab_scr,
            rows_scr,
            wide_scr,
            bias_shape,
            (cotangent.shape, BF16),
            ((1,) + table.shape[1:], F32),
            (spread.shape, BF16),
            (tokens.shape, BF16),
            ((1,) + qkv_weight.shape[1:], BF16),
            (norm_gain.shape, F32),
            ((1,) + proj_weight.shape[1:], BF16),
            ((1,) + up_weight.shape[1:], BF16),
            ((1,) + down_turned.shape[1:], BF16),
            stack_shape,
            probs_shape,
            ((rows, hid), BF16),
            ((rows, hid), BF16),
            pltpu.SemaphoreType.DMA((9,)),
            pltpu.SemaphoreType.DMA((wins + 2,)),
        ],
        [
            pltpu.with_memory_space_constraint(arg, pltpu.HBM)
            for arg in (
                tokens, cotangent, table, spread, qkv_weight, proj_weight, up_weight, down_turned,
                norm_gain,
            )
        ],
        8,
        28,
        [pltpu.HBM] * 9,
        [pltpu.VMEM] * 5 + [pltpu.HBM, pltpu.VMEM, pltpu.HBM, pltpu.HBM],
    )
    lon_head = lon_send(head, -1)
    diag_head = diag_send(head, -1)
    lat_tail = lat_swap(tail)
    (bias1,) = call(
        functools.partial(bias_kernel, lat_total),
        [bias_shape],
        [tab_scr, rows_scr, wide_scr],
        (table, spread),
        2,
        10,
    )

    (
        dhead, dtail, n1, field1, mixed1, low1, n2, hg1, active1, g1, sums1, gains1,
    ) = call(
        functools.partial(second_kernel, lat_total),
        [
            ((rows - cut, width), BF16),
            ((cut, width), BF16),
            (token, BF16),
            field_shape,
            (token, BF16),
            (token, BF16),
            (token, BF16),
            ((rows, hid), BF16),
            ((rows, hid), BF16),
            (token, BF16),
            sums_shape,
            ((2, width), F32),
        ],
        [
            (token, F32),
            (token, F32),
            field_shape,
            probs_shape,
            (token, BF16),
            stack_shape,
            stack_shape,
        ],
        (
            tail, lon_head, lat_tail, diag_head, bias1, qkv_weight, proj_weight, up_weight,
            down_turned, norm_gain,
        ),
        19,
        28,
    )
    lon_tail = lon_send(dtail, 1)
    diag_tail = diag_send(dtail, 1)
    lat_dhead = lat_swap(dhead)

    keep_a, give_a, bias_a = call(
        outer_kernel,
        [units(lon_size, units_a), units(lon_size, units_a), units(lon_size, extra)],
        [m576, m192, m768, mdown, flat_scr(units_a)],
        (n1, field1, mixed1, low1, n2, hg1, active1, g1, sums1),
        3,
        20,
    )
    got_a = lat_swap(give_a)

    keep_b, give_b, rg0, dmix0, gain_two = call(
        third_kernel,
        [
            units(lon_size, units_b),
            units(lon_size, units_b),
            (token, F32),
            (token, BF16),
            ((1, width), F32),
        ],
        [
            (token, F32),
            (token, F32),
            m192,
            m768,
            mdown,
            flat_scr(units_b),
            ((rows, hid), BF16),
            ((rows, hid), BF16),
            pltpu.SemaphoreType.DMA((2,)),
        ],
        (
            dhead, lon_tail, lat_dhead, diag_tail, resid0,
            pltpu.with_memory_space_constraint(slope0, pltpu.HBM),
            pltpu.with_memory_space_constraint(active0, pltpu.HBM),
            mixed0, proj_weight, up_weight, down_turned, norm_gain, keep_a,
        ),
        2,
        20,
        [pltpu.VMEM] * 5 + [pltpu.HBM] * 2 + [pltpu.VMEM] * 6,
    )
    got_b = lat_swap(give_b)
    (part_ab,) = call(
        lat_sum,
        [units(lon_size, units_a + extra + units_b)],
        [],
        (keep_a, got_a, bias_a, keep_b, got_b),
        1,
        10,
    )
    pieces_ab = lax.all_to_all(part_ab, "lon", 0, 0)

    tokens_grad, keep_c, give_c, bias_c = call(
        fourth_kernel,
        [
            (tokens.shape, BF16),
            units(lon_size, units_c),
            units(lon_size, units_c),
            units(lon_size, extra),
        ],
        [
            field_shape,
            sums_shape,
            m576,
            flat_scr(units_c),
            token_scr,
            stack_shape,
            stack_shape,
            probs_shape,
            pltpu.SemaphoreType.DMA((wins,)),
        ],
        (
            x0, qkv0, pltpu.with_memory_space_constraint(probs0, pltpu.HBM), dmix0, rg0, gain_two,
            gains1, part_ab, qkv_weight, norm_gain,
        ),
        11,
        24,
        [pltpu.VMEM] * 2 + [pltpu.HBM] + [pltpu.VMEM] * 7,
    )
    got_c = lat_swap(give_c)
    (part_c,) = call(
        lat_sum_late, [units(lon_size, units_c + extra)], [], (keep_c, got_c, bias_c), 1, 10
    )
    pieces_c = lax.all_to_all(part_c, "lon", 0, 0)

    (sum_ab,) = call(
        sum_pieces, [units(units_a + extra + units_b)], [], (pieces_ab, part_c), 1, 10
    )
    (sum_c,) = call(
        sum_pieces, [units(lon_size, units_c + extra)], [], (pieces_c, sum_ab), 1, 10
    )
    (same_ab,) = call(
        join_z,
        [units(zs, units_a + extra + units_b)],
        [],
        [sum_ab] + [lon_send(sum_ab, 2 * k) for k in range(1, zs)] + [sum_c],
        1,
        10,
    )
    whole_c = lax.all_to_all(sum_c, "lon", 0, 0)
    same_x = x_swap(same_ab)
    cross = lat_swap(same_ab)
    cross_x = lat_swap(same_x)
    oth_c = lat_swap(whole_c)

    flat_rows = (2 * block_rows * 128 + norm_gain.size) // 128
    update, bias_grad = call(
        functools.partial(last_kernel, units_a, units_c, extra),
        [((flat_rows, 128), BF16), (table.shape, F32)],
        [
            ((flat_rows + 2, 128), F32),
            ((CHUNK * 8, PAIR), F32),
            wide_scr,
            tab_scr,
            units(2, lon_size, units_a + extra + units_b),
            units(2, lon_size, units_c + extra),
        ],
        (spread, same_ab, same_x, cross, cross_x, whole_c, oth_c),
        3,
        20,
    )
    bias_grad = jnp.swapaxes(bias_grad, 1, 2)
    return (tokens_grad, update.reshape(-1), bias_grad)


def solution(mesh):
    return jax.shard_map(
        shards,
        mesh=mesh,
        in_specs=(
            P("grp", "lat", "lon", None),
            P("grp", "lat", "lon", None),
            P(),
            P(),
            P(),
            P(),
            P(),
            P(None, "lat", None, None),
        ),
        out_specs=(P("grp", "lat", "lon", None), P("grp"), P("grp", "lat", None, None)),
        check_vma=False,
    )
```

```python
import functools

import jax
import jax.numpy as jnp
import numpy as np
from jax import lax
from jax.experimental import pallas as pl
from jax.experimental.pallas import tpu as pltpu
from jax.sharding import PartitionSpec as P

WLAT = 12
WLON = 6
PAD = 5
LEVELS = 2
HEADS = 6
CHUNK = LEVELS * WLAT
WIN = CHUNK * WLON
SHIFTS = 2 * WLON - 1
PAIR = WLAT * SHIFTS
WIDE = 384

EPS = 1e-05
NEGATIVE = -1000000000.0
ROOT_HALF = 0.7071067811865476
INV_ROOT_TAU = 0.3989422804014327

F32 = jnp.float32
BF16 = jnp.bfloat16
UNIT = 8
BIAS_UNITS = (2 * HEADS + 1) * CHUNK // UNIT
MIB = 1024 * 1024


def dot(a, b):
    return lax.dot_general(a, b, (((1,), (0,)), ((), ())), preferred_element_type=F32)


def dot_nt(a, b):
    return lax.dot_general(a, b, (((1,), (1,)), ((), ())), preferred_element_type=F32)


def dot_tn(a, b):
    return lax.dot_general(a, b, (((0,), (0,)), ((), ())), preferred_element_type=F32)


def row_mean(v):
    return jnp.sum(v, axis=-1, keepdims=True) * (1.0 / v.shape[-1])


def standardize(x):
    centred = x - row_mean(x)
    inv = lax.rsqrt(row_mean(centred * centred) + EPS)
    return centred * inv, inv


def norm_back(d, gain, stand, inv):
    scaled = d * gain
    first = row_mean(scaled)
    second = row_mean(scaled * stand)
    gain_grad = jnp.sum(d * stand, axis=0, keepdims=True)
    return inv * (scaled - first - stand * second), gain_grad


def gelu_value(hidden):
    return 0.5 * hidden * (1.0 + lax.erf(hidden * ROOT_HALF))


def gelu_parts(hidden):
    half = 0.5 * (1.0 + lax.erf(hidden * ROOT_HALF))
    slope = half + hidden * jnp.exp(-0.5 * hidden * hidden) * INV_ROOT_TAU
    return hidden * half, slope


def split3(v):
    hi = v.astype(BF16)
    rest = v - hi.astype(F32)
    mid = rest.astype(BF16)
    low = (rest - mid.astype(F32)).astype(BF16)
    return hi, mid, low


def spread_matrices():
    out = np.zeros((LEVELS, PAIR, WIDE), np.float32)
    for zj in range(LEVELS):
        for aj in range(WLAT):
            for d in range(SHIFTS):
                out[zj, aj * SHIFTS + d, (SHIFTS - 1 - d) * CHUNK + zj * WLAT + aj] = 1.0
    return out


def put(scr, rows, value):
    width = value.shape[1]
    for tile in range(-(-width // 128)):
        lanes = min(128, width - tile * 128)
        scr[tile, rows, 0:lanes] = value[:, tile * 128 : tile * 128 + lanes]


def get(scr, rows, width):
    parts = [scr[tile, rows, :] for tile in range(-(-width // 128))]
    return jnp.concatenate(parts, axis=1)[:, 0:width]


def head_masks(width, dtype):
    lane = lax.broadcasted_iota(jnp.int32, (1, width), 1)
    size = width // HEADS
    return [((lane >= h * size) & (lane < (h + 1) * size)).astype(dtype) for h in range(HEADS)]


def lat_inside(n):
    return lax.rem(n, WLAT)


def lat_row(row_iota, lat, shifted, lat_total):
    row = lat * WLAT + lat_inside(row_iota)
    if shifted:
        row = row + WLAT // 2
        row = jnp.where(row >= lat_total, row - lat_total, row)
    return row


def expand_bias(table, spread, tab_scr, rows_scr, wide_scr, bias_scr, lat, shifted, lat_total):
    for h in range(HEADS):
        tab_scr[h : h + 1, :] = table[h]
    for zi in range(LEVELS):
        for zj in range(LEVELS):
            for ai in range(WLAT):
                at = ((zi * LEVELS + zj) * WLAT + ai) * PAIR
                row = zj * CHUNK * 8 + (zi * WLAT + ai) * 8
                rows_scr[row : row + HEADS, 0:PAIR] = tab_scr[0:HEADS, at : at + PAIR]
    count = CHUNK * 8
    total = jnp.zeros((count, WIDE), F32)
    for zj in range(LEVELS):
        parts = split3(rows_scr[zj * count : (zj + 1) * count, 0:PAIR])
        for part in parts:
            total = total + dot(part, spread[zj])
    put(wide_scr, slice(None), total)
    i = lax.broadcasted_iota(jnp.int32, (CHUNK, WIN), 0)
    j = lax.broadcasted_iota(jnp.int32, (CHUNK, WIN), 1)
    allowed = lat_row(j, lat, shifted, lat_total) < lat_total - PAD
    if shifted:
        last = lat_total - WLAT // 2
        region_i = (lat * WLAT + lat_inside(i)) >= last
        region_j = (lat * WLAT + lat_inside(j)) >= last
        allowed = allowed & (region_i == region_j)
    for h in range(HEADS):
        wide = get(wide_scr, pl.ds(h, CHUNK, stride=8), WIDE)
        for oi in range(WLON):
            back = (WLON - 1 - oi) * CHUNK
            moved = wide if back == 0 else pltpu.roll(wide, WIDE - back, axis=1)
            at = h * WIN + oi * CHUNK
            bias_scr[at : at + CHUNK, :] = jnp.where(allowed, moved[:, 0:WIN], NEGATIVE)


def fold_bias(sums, put_unit):
    rest = jnp.zeros((CHUNK, 128), F32)

    def emit(at, value):
        for r in range(CHUNK // UNIT):
            put_unit(at * (CHUNK // UNIT) + r, value[r * UNIT : (r + 1) * UNIT, :].astype(BF16))

    for h in range(HEADS):
        total = jnp.zeros((CHUNK, WIDE), F32)
        for oi in range(WLON):
            back = (WLON - 1 - oi) * CHUNK
            at = h * WIN + oi * CHUNK
            part = sums[at : at + CHUNK, :]
            total = total + (part if back == 0 else pltpu.roll(part, back, axis=1))
        emit(h, total[:, 0:128])
        emit(HEADS + h, total[:, 128:256])
        last = total[:, 256:384]
        rest = rest + (last if h == 0 else pltpu.roll(last, 8 * h, axis=1))
    emit(2 * HEADS, rest)

def stack_heads(v, masks):
    return jnp.concatenate([v * mask for mask in masks], axis=0)


def pick_heads(v, masks):
    total = v[0:WIN] * masks[0]
    for h in range(1, HEADS):
        total = total + v[h * WIN : (h + 1) * WIN] * masks[h]
    return total


def attend(qkv, bias, mixed, probs, stack_scr, width, finish=None):
    masks = head_masks(width, BF16)
    masks32 = head_masks(width, F32)
    scale = (width // HEADS) ** -0.5

    def window(w, carry):
        rows = pl.ds(pl.multiple_of(w * WIN, 16), WIN)
        q = qkv[rows, 0:width]
        k = qkv[rows, width : 2 * width]
        v = qkv[rows, 2 * width : 3 * width]
        scores = dot_nt(stack_heads(q, masks), k)
        for h in range(HEADS):
            part = slice(h * WIN, (h + 1) * WIN)
            logits = scores[part] * scale + bias[part, :]
            weights = jnp.exp(logits - jnp.max(logits, axis=-1, keepdims=True))
            p = weights * (1.0 / jnp.sum(weights, axis=-1, keepdims=True))
            probs[w, h] = p
            stack_scr[part, :] = p.astype(BF16)
        mixed[rows, :] = pick_heads(dot(stack_scr[...], v), masks32).astype(BF16)
        if finish is not None:
            finish(w)
        return carry

    lax.fori_loop(0, probs.shape[0], window, 0)


def attend_back(qkv, probs, dmix, field, sums, low_scr, prob_scr, width, begin=None):
    masks = head_masks(width, BF16)
    masks32 = head_masks(width, F32)
    scale = (width // HEADS) ** -0.5

    def window(w, carry):
        rows = pl.ds(pl.multiple_of(w * WIN, 16), WIN)
        q = qkv[rows, 0:width]
        k = qkv[rows, width : 2 * width]
        v = qkv[rows, 2 * width : 3 * width]
        up = stack_heads(dmix[rows, :], masks)
        prob_grad = dot_nt(up, v)
        if begin is not None:
            begin(w)
        for h in range(HEADS):
            part = slice(h * WIN, (h + 1) * WIN)
            p = probs[w, h]
            weighted = p * prob_grad[part]
            ds = weighted - p * jnp.sum(weighted, axis=-1, keepdims=True)
            sums[part, 0:WIN] += ds
            low_scr[part, :] = ds.astype(BF16)
            prob_scr[part, :] = p.astype(BF16)
        low = low_scr[...]
        dq = pick_heads(dot(low, k), masks32)
        dk = dot_tn(low, stack_heads(q, masks))
        dv = dot_tn(prob_scr[...], up)
        field[rows, 0:width] = (dq * scale).astype(BF16)
        field[rows, width : 2 * width] = (dk * scale).astype(BF16)
        field[rows, 2 * width : 3 * width] = dv.astype(BF16)
        return carry

    lax.fori_loop(0, probs.shape[0], window, 0)


def lon_major(src, scr):
    levels, lats, lons, width = src.shape
    for z in range(levels):
        for a in range(lats):
            at = (z * lats + a) * lons
            put(scr, slice(at, at + lons), src[z, a].astype(F32))


def lon_column(scr, lon, lons, width):
    return get(scr, pl.ds(lon, CHUNK, stride=lons), width)


def flat_store(dst, at, mat, cols):
    rows = mat.shape[1]
    if cols % 128 == 0:
        per = cols // 128
        for c in range(per):
            dst[pl.ds(at + c, rows, stride=per), :] = mat[c]
        return rows * per
    per = 2 * cols // 128
    half = cols // 128
    even = get(mat, pl.ds(0, rows // 2, stride=2), cols)
    odd = get(mat, pl.ds(1, rows // 2, stride=2), cols)
    for c in range(half):
        dst[pl.ds(at + c, rows // 2, stride=per), :] = even[:, c * 128 : (c + 1) * 128]
    dst[pl.ds(at + half, rows // 2, stride=per), :] = jnp.concatenate(
        [even[:, half * 128 : half * 128 + 64], odd[:, 0:64]], axis=1
    )
    for c in range(half):
        dst[pl.ds(at + half + 1 + c, rows // 2, stride=per), :] = odd[
            :, 64 + c * 128 : 64 + (c + 1) * 128
        ]
    return rows * cols // 128


def send_units(scr, base, out):
    lons, units = out.shape[:2]
    for j in range(lons):
        for u in range(units):
            at = base + (j * units + u) * UNIT
            if not isinstance(at, int):
                at = pl.multiple_of(at, UNIT)
            out[j, u] = scr[pl.ds(at, UNIT), :].astype(BF16)


def halves(scr, lat, keep, give):
    half = keep.shape[0] * keep.shape[1] * UNIT
    send_units(scr, lat * half, keep)
    send_units(scr, (1 - lat) * half, give)


def bias_units(sums, out):
    lons, per = out.shape[:2]

    def put_unit(k, value):
        out[k // per, k % per] = value

    fold_bias(sums, put_unit)
    for k in range(BIAS_UNITS, lons * per):
        put_unit(k, jnp.zeros((UNIT, 128), BF16))

def forward_core(x, b, refs, qkv_scr, bias_scr, mixed, probs, stack_scr, finish=None):
    qkv_w, proj_w, gains = refs
    width = x.shape[-1]
    stand, inv = standardize(x)
    normed = (stand * gains[b, 0:1, :]).astype(BF16)
    qkv_scr[...] = dot(normed, qkv_w[b]).astype(BF16)
    attend(qkv_scr, bias_scr, mixed, probs, stack_scr, width, finish)
    att = dot(mixed[...], proj_w[b]).astype(BF16)
    resid = (x + att.astype(F32)).astype(BF16).astype(F32)
    return resid, normed


def first_kernel(
    lat_total, tokens_in, cot_in, table_in, spread_in, qkv_in, proj_in, up_in, down_in, gains_in,
    x_out, tail_out, head_out, qkv_out, mixed_out, probs_out, resid_out, hidden_out, active_out,
    scr, cot_scr, tab_scr, rows_scr, wide_scr, bias_scr,
    cot, table, spread, tokens, qkv_w, gains, proj_w, up_w, down_w, stack_scr,
    probs, active_scr, sems, out_sems,
):
    copies = []
    for source, target in (
        (cot_in, cot),
        (table_in.at[0:1], table),
        (spread_in, spread),
        (tokens_in, tokens),
        (qkv_in.at[0:1], qkv_w),
        (gains_in, gains),
        (proj_in.at[0:1], proj_w),
        (up_in.at[0:1], up_w),
        (down_in.at[0:1], down_w),
    ):
        copies.append(pltpu.make_async_copy(source, target, sems.at[len(copies)]))
    for copy in copies:
        copy.start()
    lat = lax.axis_index("lat")
    width = tokens.shape[-1]
    lons = tokens.shape[2]
    cut = CHUNK * (WLON // 2)
    copies[0].wait()
    lon_major(cot, cot_scr)
    g = jnp.concatenate([lon_column(cot_scr, lon, lons, width) for lon in range(lons)], axis=0)
    head_out[1] = g[0:cut, :].astype(BF16)
    tail_out[1] = g[cut:, :].astype(BF16)
    copies[1].wait()
    copies[2].wait()
    expand_bias(
        table.at[0], spread, tab_scr, rows_scr, wide_scr, bias_scr, lat, False, lat_total
    )
    copies[3].wait()
    lon_major(tokens, scr)
    x = jnp.concatenate([lon_column(scr, lon, lons, width) for lon in range(lons)], axis=0)
    x_out[...] = x.astype(BF16)
    for copy in copies[4:]:
        copy.wait()

    def probs_copy(w):
        return pltpu.make_async_copy(probs.at[w], probs_out.at[w], out_sems.at[w])

    resid, _ = forward_core(
        x, 0, (qkv_w, proj_w, gains), qkv_out, bias_scr, mixed_out, probs, stack_scr,
        lambda w: probs_copy(w).start(),
    )
    resid_out[...] = resid.astype(BF16)
    stand, _ = standardize(resid)
    normed = (stand * gains[0, 1:2, :]).astype(BF16)
    hidden = dot(normed, up_w[0])
    hidden_out[...] = hidden
    active = gelu_value(hidden).astype(BF16)
    active_scr[...] = active
    wins = probs.shape[0]
    last = pltpu.make_async_copy(active_scr, active_out, out_sems.at[wins])
    last.start()
    result = resid + dot_nt(active, down_w[0])
    head_out[0] = result[0:cut, :].astype(BF16)
    tail_out[0] = result[cut:, :].astype(BF16)
    for copy in [probs_copy(w) for w in range(wins)] + [last]:
        copy.wait()


def bias_kernel(
    lat_total, table, spread, hidden, bias_out, slope_out, tab_scr, rows_scr, wide_scr, slope_scr, sems
):
    half = hidden.shape[0] // 2
    copies = []
    for rows in (slice(0, half), slice(half, 2 * half)):
        slope_scr[rows, :] = gelu_parts(hidden[rows, :])[1].astype(BF16)
        copies.append(
            pltpu.make_async_copy(slope_scr.at[rows], slope_out.at[rows], sems.at[len(copies)])
        )
        copies[-1].start()
    lat = lax.axis_index("lat")
    expand_bias(
        table.at[1], spread, tab_scr, rows_scr, wide_scr, bias_out, lat, True, lat_total
    )
    for copy in copies:
        copy.wait()


def merge_ahead(scr_own, scr_oth, rows):
    half = WLAT // 2
    n = lax.broadcasted_iota(jnp.int32, (rows, 1), 0)
    return jnp.where(
        lat_inside(n) < half,
        pltpu.roll(scr_own[...], rows - half, axis=0),
        pltpu.roll(scr_oth[...], half, axis=0),
    )


def merge_behind(scr_own, scr_oth, rows):
    half = WLAT // 2
    n = lax.broadcasted_iota(jnp.int32, (rows, 1), 0)
    return jnp.where(
        lat_inside(n) >= half,
        pltpu.roll(scr_own[...], half, axis=0),
        pltpu.roll(scr_oth[...], rows - half, axis=0),
    )


def second_kernel(
    lat_total,
    tail, lon_head, lat_tail, diag_head, bias, qkv_w, proj_w, up_w, down_w, gains,
    x_out, n1_out, qkv_out, probs_out, mixed_out, low_out, n2_out, hg_out, active_out, g_out,
    rg_out, dmix_out, gain_out,
    scr_own, scr_oth, stack_scr,
):
    lat = lax.axis_index("lat")
    rows, width = scr_own.shape
    cut = CHUNK * (WLON // 2)

    def rolled(which):
        scr_own[0 : rows - cut, :] = tail[which].astype(F32)
        scr_own[rows - cut :, :] = lon_head[which].astype(F32)
        scr_oth[0 : rows - cut, :] = lat_tail[which].astype(F32)
        scr_oth[rows - cut :, :] = diag_head[which].astype(F32)
        return merge_ahead(scr_own, scr_oth, rows)

    g = rolled(1)
    n = lax.broadcasted_iota(jnp.int32, (rows, 1), 0)
    keep = lat_row(n, lat, True, lat_total) < lat_total - PAD
    g = jnp.where(keep, g, 0.0)
    g_out[...] = g.astype(BF16)

    x = rolled(0)
    x_out[...] = x.astype(BF16)
    resid, normed = forward_core(
        x, 1, (qkv_w, proj_w, gains), qkv_out, bias, mixed_out, probs_out, stack_scr
    )
    n1_out[...] = normed
    stand2, inv2 = standardize(resid)
    normed2 = (stand2 * gains[1, 1:2, :]).astype(BF16)
    n2_out[...] = normed2
    active, slope = gelu_parts(dot(normed2, up_w[1]))
    active_out[...] = active.astype(BF16)

    hg = (dot(g_out[...], down_w[1]) * slope).astype(BF16)
    hg_out[...] = hg
    part, gain_two = norm_back(dot_nt(hg, up_w[1]), gains[1, 1:2, :], stand2, inv2)
    rg = g + part
    rg_out[...] = rg
    low = rg.astype(BF16)
    low_out[...] = low
    dmix_out[...] = dot_nt(low, proj_w[1]).astype(BF16)
    gain_out[...] = gain_two


def middle_kernel(
    x_in, qkv, probs, dmix, rg, gain_two, order, qkv_w, gains,
    head_out, tail_out, field_out, sums_out, gain_out,
    low_scr, prob_scr,
):
    rows, width = x_in.shape
    cut = CHUNK * (WLON // 2)
    sums_out[...] = jnp.zeros(sums_out.shape, F32)
    attend_back(qkv, probs, dmix, field_out, sums_out, low_scr, prob_scr, width)
    ng = dot_nt(field_out[...], qkv_w[1]).astype(BF16).astype(F32)
    stand1, inv1 = standardize(x_in[...].astype(F32))
    part, gain_one = norm_back(ng, gains[1, 0:1, :], stand1, inv1)
    dx = rg[...] + part
    head_out[...] = dx[0 : rows - cut, :].astype(BF16)
    tail_out[...] = dx[rows - cut :, :].astype(BF16)
    gain_out[0:1, :] = gain_one
    gain_out[1:2, :] = gain_two[...]


def outer_wide(n2, hg, active, g, keep, give, m768, mdown, flat_scr):
    put(m768, slice(None), dot_tn(n2[...], hg[...]))
    at = flat_store(flat_scr, 0, m768, hg.shape[1])
    put(mdown, slice(None), dot_tn(active[...], g[...]))
    flat_store(flat_scr, at, mdown, g.shape[1])
    halves(flat_scr, lax.axis_index("lat"), keep, give)


def outer_attention(
    n1, field, mixed, low, sums, keep, give, bias_out, m576, m192, flat_scr
):
    put(m576, slice(None), dot_tn(n1[...], field[...]))
    at = flat_store(flat_scr, 0, m576, field.shape[1])
    put(m192, slice(None), dot_tn(mixed[...], low[...]))
    flat_store(flat_scr, at, m192, low.shape[1])
    halves(flat_scr, lax.axis_index("lat"), keep, give)
    bias_units(sums, bias_out)


def add_halves(keep, got, out):
    out[...] = (keep[...].astype(F32) + got[...].astype(F32)).astype(BF16)


def lat_sum(keep_a, got_a, bias_a, keep_b, got_b, out):
    one, two = keep_a.shape[1], bias_a.shape[1]
    out[:, 0:one] = (keep_a[...].astype(F32) + got_a[...].astype(F32)).astype(BF16)
    out[:, one : one + two] = bias_a[...]
    out[:, one + two :] = (keep_b[...].astype(F32) + got_b[...].astype(F32)).astype(BF16)


def lat_sum_late(keep, got, bias, out):
    one = keep.shape[1]
    out[:, 0:one] = (keep[...].astype(F32) + got[...].astype(F32)).astype(BF16)
    out[:, one:] = bias[...]


def sum_both(first, second, order, out):
    at = 0
    for pieces in (first, second):
        total = pieces[0].astype(F32)
        for k in range(1, pieces.shape[0]):
            total = total + pieces[k].astype(F32)
        out[at : at + pieces.shape[1]] = total.astype(BF16)
        at += pieces.shape[1]


def sum_pieces(pieces, order, out):
    total = pieces[0].astype(F32)
    for k in range(1, pieces.shape[0]):
        total = total + pieces[k].astype(F32)
    total = total.astype(BF16)
    if len(out.shape) == len(pieces.shape):
        for k in range(out.shape[0]):
            out[k] = total
    else:
        out[...] = total


def join_z(*refs):
    out = refs[-1]
    count = out.shape[0]
    z = lax.div(lax.axis_index("lon"), 2)
    for k in range(count):
        out[lax.rem(z + count - k, count)] = refs[k][...]


def third_kernel(
    head, lon_tail, lat_head, diag_tail, resid_in, slope_in, active_in, mixed,
    proj_w, up_w, down_w, gains, order, order_too,
    keep_out, give_out, rg_out, dmix_out, gain_out,
    scr_own, scr_oth, m192, m768, mdown, flat_scr, slope, active, sems,
):
    copies = [
        pltpu.make_async_copy(slope_in, slope, sems.at[0]),
        pltpu.make_async_copy(active_in, active, sems.at[1]),
    ]
    for copy in copies:
        copy.start()
    rows, width = scr_own.shape
    cut = CHUNK * (WLON // 2)
    scr_own[0:cut, :] = lon_tail[...].astype(F32)
    scr_own[cut:, :] = head[...].astype(F32)
    scr_oth[0:cut, :] = diag_tail[...].astype(F32)
    scr_oth[cut:, :] = lat_head[...].astype(F32)
    g = merge_behind(scr_own, scr_oth, rows)
    g_low = g.astype(BF16)
    stand2, inv2 = standardize(resid_in[...].astype(F32))
    normed2 = (stand2 * gains[0, 1:2, :]).astype(BF16)
    hg = dot(g_low, down_w[0])
    copies[0].wait()
    hg = (hg * slope[...].astype(F32)).astype(BF16)
    part, gain_two = norm_back(dot_nt(hg, up_w[0]), gains[0, 1:2, :], stand2, inv2)
    rg = g + part
    rg_out[...] = rg
    low = rg.astype(BF16)
    dmix_out[...] = dot_nt(low, proj_w[0]).astype(BF16)
    gain_out[...] = gain_two
    put(m192, slice(None), dot_tn(mixed[...], low))
    at = flat_store(flat_scr, 0, m192, mixed.shape[1])
    put(m768, slice(None), dot_tn(normed2, hg))
    at += flat_store(flat_scr, at, m768, active.shape[1])
    copies[1].wait()
    put(mdown, slice(None), dot_tn(active[...], g_low))
    at += flat_store(flat_scr, at, mdown, mixed.shape[1])
    flat_scr[at:, :] = jnp.zeros((flat_scr.shape[0] - at, 128), F32)
    halves(flat_scr, lax.axis_index("lat"), keep_out, give_out)


def gain_rows(one, two):
    return jnp.concatenate(
        [
            one[:, 0:128],
            jnp.concatenate([one[:, 128:192], two[:, 0:64]], axis=1),
            two[:, 64:192],
        ],
        axis=0,
    )


def fourth_kernel(
    x_in, qkv, probs_in, dmix, rg, gain_two, gains_late, order, qkv_w, gains,
    tokens_out, keep, give, bias_out,
    field, sums, m576, flat_scr, dx_scr, low_scr, prob_scr, probs, sems,
):
    def probs_copy(w):
        return pltpu.make_async_copy(probs_in.at[w], probs.at[w], sems.at[w])

    for w in range(probs.shape[0]):
        probs_copy(w).start()
    width = x_in.shape[-1]
    levels, lats, lons = tokens_out.shape[:3]
    sums[...] = jnp.zeros(sums.shape, F32)
    attend_back(
        qkv, probs, dmix, field, sums, low_scr, prob_scr, width, lambda w: probs_copy(w).wait()
    )
    stand1, inv1 = standardize(x_in[...].astype(F32))
    normed = (stand1 * gains[0, 0:1, :]).astype(BF16)
    ng = dot_nt(field[...], qkv_w[0]).astype(BF16).astype(F32)
    part, gain_one = norm_back(ng, gains[0, 0:1, :], stand1, inv1)
    put(m576, slice(None), dot_tn(normed, field[...]))
    at = flat_store(flat_scr, 0, m576, field.shape[1])
    flat_scr[at:, :] = jnp.zeros((flat_scr.shape[0] - at, 128), F32)
    flat_scr[at : at + 3, :] = gain_rows(gain_one, gain_two[...])
    flat_scr[at + 3 : at + 6, :] = gain_rows(gains_late[0:1, :], gains_late[1:2, :])
    bias_units(sums, bias_out)
    halves(flat_scr, lax.axis_index("lat"), keep, give)
    put(dx_scr, slice(None), rg[...] + part)
    for z in range(levels):
        for a in range(lats):
            tokens_out[z, a] = get(
                dx_scr, pl.ds(z * lats + a, lons, stride=CHUNK), width
            ).astype(BF16)


def last_kernel(
    units_a, units_b, units_c, extra, spread, same, same_x, cross, cross_x, own_c, oth_c,
    update_out, bias_out, scr, rows_scr, wide_scr, tab_scr, ab, c,
):
    lat = lax.axis_index("lat")
    x = lax.rem(lax.axis_index("lon"), 2)
    lons = own_c.shape[0]
    for j in range(lons):
        c[lat, j] = own_c[j]
        c[1 - lat, j] = oth_c[j]
    for z in range(lons // 2):
        ab[lat, 2 * z + x] = same[z]
        ab[lat, 2 * z + 1 - x] = same_x[z]
        ab[1 - lat, 2 * z + x] = cross[z]
        ab[1 - lat, 2 * z + 1 - x] = cross_x[z]

    def place(pieces, first, last, dests):
        total = jnp.zeros((UNIT, 128), F32)
        per = last - first
        k = 0
        for where, room in dests:
            for at in range(where, where + room, UNIT):
                half, j, u = k // (per * lons), k // per % lons, k % per
                value = pieces[half, j, first + u].astype(F32)
                scr[at : at + UNIT, :] = value
                total = total + value * value
                k += 1
        return total

    at = units_a + extra
    total = place(ab, 0, units_a, [(864, 864), (2016, 288)])
    total = total + place(ab, at, at + units_b, [(1728, 288), (2304, 1152), (4608, 1152)])
    total = total + place(ab, at + units_b, ab.shape[2], [(3456, 1152), (5760, 1152)])
    total = total + place(c, 0, units_c, [(0, 864), (6912, 8)])
    count = update_out.shape[0]
    mean = jnp.sum(total) * (1.0 / (count * 128))
    scale = lax.rsqrt(mean + 1e-06)
    update_out[...] = (scr[0:count, :] * scale).astype(BF16)

    for b, (piece, base) in enumerate(((c, units_c), (ab, units_a))):

        def read(at):
            parts = []
            for r in range(CHUNK // UNIT):
                k = at * (CHUNK // UNIT) + r
                parts.append(piece[lat, k // extra, base + k % extra].astype(F32))
            return jnp.concatenate(parts, axis=0)

        rest = read(2 * HEADS)
        for h in range(HEADS):
            rows = pl.ds(h, CHUNK, stride=8)
            wide_scr[0, rows, :] = read(h)
            wide_scr[1, rows, :] = read(HEADS + h)
            wide_scr[2, rows, :] = rest if h == 0 else pltpu.roll(rest, 128 - 8 * h, axis=1)
        low = get(wide_scr, slice(None), WIDE).astype(BF16)
        for zj in range(LEVELS):
            rows_scr[...] = dot_nt(low, spread[zj])
            for zi in range(LEVELS):
                for ai in range(WLAT):
                    at = ((zi * LEVELS + zj) * WLAT + ai) * PAIR
                    row = (zi * WLAT + ai) * 8
                    tab_scr[0:HEADS, at : at + PAIR] = rows_scr[row : row + HEADS, 0:PAIR]
        for h in range(HEADS):
            bias_out[b, h] = tab_scr[h : h + 1, :]


def call(kernel, outs, scratch, args, micros, mib, spaces=None, out_spaces=None):
    spaces = spaces or [pltpu.VMEM] * len(args)
    out_spaces = out_spaces or [pltpu.VMEM] * len(outs)
    return pl.pallas_call(
        kernel,
        out_shape=[
            pltpu.HBM(*entry) if space == pltpu.HBM else jax.ShapeDtypeStruct(*entry)
            for entry, space in zip(outs, out_spaces)
        ],
        in_specs=[pl.BlockSpec(memory_space=space) for space in spaces],
        out_specs=[pl.BlockSpec(memory_space=space) for space in out_spaces],
        scratch_shapes=[
            pltpu.VMEM(*entry) if isinstance(entry, tuple) else entry for entry in scratch
        ],
        compiler_params=pltpu.CompilerParams(vmem_limit_bytes=mib * MIB),
        cost_estimate=pl.CostEstimate(
            flops=int(micros * 1.1e9), bytes_accessed=10**5, transcendentals=0
        ),
    )(*args)


def lat_swap(value):
    return lax.ppermute(value, "lat", [(0, 1), (1, 0)])


def lon_send(value, step):
    count = lax.axis_size("lon")
    return lax.ppermute(value, "lon", [(s, (s + step) % count) for s in range(count)])


def x_swap(value):
    count = lax.axis_size("lon")
    return lax.ppermute(value, "lon", [(s, s ^ 1) for s in range(count)])


def diag_send(value, step):
    count = lax.axis_size("lon")
    pairs = []
    for s in range(count):
        for t in range(2):
            pairs.append((2 * s + t, 2 * ((s + step) % count) + 1 - t))
    return lax.ppermute(value, ("lon", "lat"), pairs)


def shards(
    tokens, cotangent, qkv_weight, proj_weight, up_weight, down_weight, norm_gain, bias_table
):
    levels, lats, lons, width = tokens.shape
    rows = levels * lats * lons
    wins = rows // WIN
    hid = up_weight.shape[-1]
    heads = bias_table.shape[2]
    lon_size = lax.axis_size("lon")
    zs = lon_size // 2
    lat_total = lats * lax.axis_size("lat")
    cut = CHUNK * (WLON // 2)
    spread = jnp.asarray(spread_matrices(), BF16)
    down_turned = jnp.swapaxes(down_weight, 1, 2)
    table = jnp.swapaxes(bias_table, 1, 2)
    token = (rows, width)
    field_shape = ((rows, 3 * width), BF16)
    probs_shape = ((wins, heads, WIN, WIN), F32)
    stack_shape = ((heads * WIN, WIN), BF16)
    bias_shape = ((heads * WIN, WIN), F32)
    sums_shape = ((heads * WIN, WIDE), F32)
    tab_scr = ((8, table.shape[-1]), F32)
    rows_scr = ((LEVELS * CHUNK * 8, PAIR), F32)
    wide_scr = ((WIDE // 128, CHUNK * 8, 128), F32)
    tiles = -(-width // 128)
    token_scr = ((tiles, rows, 128), F32)
    m576 = ((-(-3 * width // 128), width, 128), F32)
    m192 = ((tiles, width, 128), F32)
    m768 = ((hid // 128, width, 128), F32)
    mdown = ((tiles, hid, 128), F32)

    block_rows = (qkv_weight[0].size + proj_weight[0].size + 2 * up_weight[0].size) // 128
    qkv_rows = qkv_weight[0].size // 128
    wide_rows = 2 * up_weight[0].size // 128
    counts = (wide_rows, block_rows - wide_rows, block_rows - qkv_rows, qkv_rows + 8)
    units_wide, units_a, units_b, units_c = [
        -(-count // (2 * lon_size * UNIT)) for count in counts
    ]
    extra = -(-BIAS_UNITS // lon_size)

    def units(*lead):
        return (lead + (UNIT, 128), BF16)

    def flat_scr(per):
        return ((2 * lon_size * per * UNIT, 128), F32)

    x0, tail, head, qkv0, mixed0, probs0, resid0, hidden0, active0 = call(
        functools.partial(first_kernel, lat_total),
        [
            (token, BF16),
            ((2, rows - cut, width), BF16),
            ((2, cut, width), BF16),
            field_shape,
            (token, BF16),
            probs_shape,
            (token, BF16),
            ((rows, hid), F32),
            ((rows, hid), BF16),
        ],
        [
            token_scr,
            token_scr,
            tab_scr,
            rows_scr,
            wide_scr,
            bias_shape,
            (cotangent.shape, BF16),
            ((1,) + table.shape[1:], F32),
            (spread.shape, BF16),
            (tokens.shape, BF16),
            ((1,) + qkv_weight.shape[1:], BF16),
            (norm_gain.shape, F32),
            ((1,) + proj_weight.shape[1:], BF16),
            ((1,) + up_weight.shape[1:], BF16),
            ((1,) + down_turned.shape[1:], BF16),
            stack_shape,
            probs_shape,
            ((rows, hid), BF16),
            pltpu.SemaphoreType.DMA((9,)),
            pltpu.SemaphoreType.DMA((wins + 1,)),
        ],
        [
            pltpu.with_memory_space_constraint(arg, pltpu.HBM)
            for arg in (
                tokens, cotangent, table, spread, qkv_weight, proj_weight, up_weight, down_turned,
                norm_gain,
            )
        ],
        8,
        28,
        [pltpu.HBM] * 9,
        [pltpu.VMEM] * 5 + [pltpu.HBM, pltpu.VMEM, pltpu.VMEM, pltpu.HBM],
    )
    lon_head = lon_send(head, -1)
    diag_head = diag_send(head, -1)
    lat_tail = lat_swap(tail)
    bias1, slope0 = call(
        functools.partial(bias_kernel, lat_total),
        [bias_shape, ((rows, hid), BF16)],
        [tab_scr, rows_scr, wide_scr, ((rows, hid), BF16), pltpu.SemaphoreType.DMA((2,))],
        (table, spread, hidden0),
        3,
        10,
        None,
        [pltpu.VMEM, pltpu.HBM],
    )

    x1, n1, qkv1, probs1, mixed1, low1, n2, hg1, active1, g1, rg1, dmix1, gain_late = call(
        functools.partial(second_kernel, lat_total),
        [
            (token, BF16),
            (token, BF16),
            field_shape,
            probs_shape,
            (token, BF16),
            (token, BF16),
            (token, BF16),
            ((rows, hid), BF16),
            ((rows, hid), BF16),
            (token, BF16),
            (token, F32),
            (token, BF16),
            ((1, width), F32),
        ],
        [(token, F32), (token, F32), stack_shape],
        (
            tail, lon_head, lat_tail, diag_head, bias1, qkv_weight, proj_weight, up_weight,
            down_turned, norm_gain,
        ),
        7,
        24,
    )
    keep_w, give_w = call(
        outer_wide,
        [units(lon_size, units_wide), units(lon_size, units_wide)],
        [m768, mdown, flat_scr(units_wide)],
        (n2, hg1, active1, g1),
        1,
        16,
    )
    got_w = lat_swap(give_w)
    dhead, dtail, field1, sums1, gains1 = call(
        middle_kernel,
        [
            ((rows - cut, width), BF16),
            ((cut, width), BF16),
            field_shape,
            sums_shape,
            ((2, width), F32),
        ],
        [stack_shape, stack_shape],
        (x1, qkv1, probs1, dmix1, rg1, gain_late, keep_w, qkv_weight, norm_gain),
        5,
        20,
    )
    lon_tail = lon_send(dtail, 1)
    diag_tail = diag_send(dtail, 1)
    lat_dhead = lat_swap(dhead)

    keep_a, give_a, bias_a = call(
        outer_attention,
        [units(lon_size, units_a), units(lon_size, units_a), units(lon_size, extra)],
        [m576, m192, flat_scr(units_a)],
        (n1, field1, mixed1, low1, sums1),
        1,
        16,
    )
    got_a = lat_swap(give_a)
    (part_w,) = call(add_halves, [units(lon_size, units_wide)], [], (keep_w, got_w), 1, 10)
    pieces_w = lax.all_to_all(part_w, "lon", 0, 0)

    keep_b, give_b, rg0, dmix0, gain_two = call(
        third_kernel,
        [
            units(lon_size, units_b),
            units(lon_size, units_b),
            (token, F32),
            (token, BF16),
            ((1, width), F32),
        ],
        [
            (token, F32),
            (token, F32),
            m192,
            m768,
            mdown,
            flat_scr(units_b),
            ((rows, hid), BF16),
            ((rows, hid), BF16),
            pltpu.SemaphoreType.DMA((2,)),
        ],
        (
            dhead, lon_tail, lat_dhead, diag_tail, resid0,
            pltpu.with_memory_space_constraint(slope0, pltpu.HBM),
            pltpu.with_memory_space_constraint(active0, pltpu.HBM),
            mixed0, proj_weight, up_weight, down_turned, norm_gain, keep_a, part_w,
        ),
        2,
        20,
        [pltpu.VMEM] * 5 + [pltpu.HBM] * 2 + [pltpu.VMEM] * 7,
    )
    got_b = lat_swap(give_b)
    (part_ab,) = call(
        lat_sum,
        [units(lon_size, units_a + extra + units_b)],
        [],
        (keep_a, got_a, bias_a, keep_b, got_b),
        1,
        10,
    )
    pieces_ab = lax.all_to_all(part_ab, "lon", 0, 0)

    tokens_grad, keep_c, give_c, bias_c = call(
        fourth_kernel,
        [
            (tokens.shape, BF16),
            units(lon_size, units_c),
            units(lon_size, units_c),
            units(lon_size, extra),
        ],
        [
            field_shape,
            sums_shape,
            m576,
            flat_scr(units_c),
            token_scr,
            stack_shape,
            stack_shape,
            probs_shape,
            pltpu.SemaphoreType.DMA((wins,)),
        ],
        (
            x0, qkv0, pltpu.with_memory_space_constraint(probs0, pltpu.HBM), dmix0, rg0, gain_two,
            gains1, part_ab, qkv_weight, norm_gain,
        ),
        11,
        24,
        [pltpu.VMEM] * 2 + [pltpu.HBM] + [pltpu.VMEM] * 7,
    )
    got_c = lat_swap(give_c)
    (part_c,) = call(
        lat_sum_late, [units(lon_size, units_c + extra)], [], (keep_c, got_c, bias_c), 1, 10
    )
    pieces_c = lax.all_to_all(part_c, "lon", 0, 0)

    units_ab = units_a + extra + units_b + units_wide
    (sum_ab,) = call(
        sum_both, [units(units_ab)], [], (pieces_ab, pieces_w, part_c), 1, 10
    )
    (sum_c,) = call(
        sum_pieces, [units(lon_size, units_c + extra)], [], (pieces_c, sum_ab), 1, 10
    )
    (same_ab,) = call(
        join_z,
        [units(zs, units_ab)],
        [],
        [sum_ab] + [lon_send(sum_ab, 2 * k) for k in range(1, zs)] + [sum_c],
        1,
        10,
    )
    whole_c = lax.all_to_all(sum_c, "lon", 0, 0)
    same_x = x_swap(same_ab)
    cross = lat_swap(same_ab)
    cross_x = lat_swap(same_x)
    oth_c = lat_swap(whole_c)

    flat_rows = (2 * block_rows * 128 + norm_gain.size) // 128
    update, bias_grad = call(
        functools.partial(last_kernel, units_a, units_b, units_c, extra),
        [((flat_rows, 128), BF16), (table.shape, F32)],
        [
            ((flat_rows + 2, 128), F32),
            ((CHUNK * 8, PAIR), F32),
            wide_scr,
            tab_scr,
            units(2, lon_size, units_ab),
            units(2, lon_size, units_c + extra),
        ],
        (spread, same_ab, same_x, cross, cross_x, whole_c, oth_c),
        3,
        20,
    )
    bias_grad = jnp.swapaxes(bias_grad, 1, 2)
    return (tokens_grad, update.reshape(-1), bias_grad)


def solution(mesh):
    return jax.shard_map(
        shards,
        mesh=mesh,
        in_specs=(
            P("grp", "lat", "lon", None),
            P("grp", "lat", "lon", None),
            P(),
            P(),
            P(),
            P(),
            P(),
            P(None, "lat", None, None),
        ),
        out_specs=(P("grp", "lat", "lon", None), P("grp"), P("grp", "lat", None, None)),
        check_vma=False,
    )
```

```python
import functools

import jax
import jax.numpy as jnp
import numpy as np
from jax import lax
from jax.experimental import pallas as pl
from jax.experimental.pallas import tpu as pltpu
from jax.sharding import PartitionSpec as P

WLAT = 12
WLON = 6
PAD = 5
LEVELS = 2
HEADS = 6
CHUNK = LEVELS * WLAT
WIN = CHUNK * WLON
SHIFTS = 2 * WLON - 1
PAIR = WLAT * SHIFTS
WIDE = 384

EPS = 1e-05
NEGATIVE = -1000000000.0
ROOT_HALF = 0.7071067811865476
INV_ROOT_TAU = 0.3989422804014327

F32 = jnp.float32
BF16 = jnp.bfloat16
UNIT = 8
BIAS_UNITS = (2 * HEADS + 1) * CHUNK // UNIT
MIB = 1024 * 1024


def dot(a, b):
    return lax.dot_general(a, b, (((1,), (0,)), ((), ())), preferred_element_type=F32)


def dot_nt(a, b):
    return lax.dot_general(a, b, (((1,), (1,)), ((), ())), preferred_element_type=F32)


def dot_tn(a, b):
    return lax.dot_general(a, b, (((0,), (0,)), ((), ())), preferred_element_type=F32)


def row_mean(v):
    return jnp.sum(v, axis=-1, keepdims=True) * (1.0 / v.shape[-1])


def standardize(x):
    centred = x - row_mean(x)
    inv = lax.rsqrt(row_mean(centred * centred) + EPS)
    return centred * inv, inv


def norm_back(d, gain, stand, inv):
    scaled = d * gain
    first = row_mean(scaled)
    second = row_mean(scaled * stand)
    gain_grad = jnp.sum(d * stand, axis=0, keepdims=True)
    return inv * (scaled - first - stand * second), gain_grad


def gelu_value(hidden):
    return 0.5 * hidden * (1.0 + lax.erf(hidden * ROOT_HALF))


def gelu_parts(hidden):
    half = 0.5 * (1.0 + lax.erf(hidden * ROOT_HALF))
    slope = half + hidden * jnp.exp(-0.5 * hidden * hidden) * INV_ROOT_TAU
    return hidden * half, slope


def split3(v):
    hi = v.astype(BF16)
    rest = v - hi.astype(F32)
    mid = rest.astype(BF16)
    low = (rest - mid.astype(F32)).astype(BF16)
    return hi, mid, low


def spread_matrices():
    out = np.zeros((LEVELS, PAIR, WIDE), np.float32)
    for zj in range(LEVELS):
        for aj in range(WLAT):
            for d in range(SHIFTS):
                out[zj, aj * SHIFTS + d, (SHIFTS - 1 - d) * CHUNK + zj * WLAT + aj] = 1.0
    return out


def put(scr, rows, value):
    width = value.shape[1]
    for tile in range(-(-width // 128)):
        lanes = min(128, width - tile * 128)
        scr[tile, rows, 0:lanes] = value[:, tile * 128 : tile * 128 + lanes]


def get(scr, rows, width):
    parts = [scr[tile, rows, :] for tile in range(-(-width // 128))]
    return jnp.concatenate(parts, axis=1)[:, 0:width]


def head_masks(width, dtype):
    lane = lax.broadcasted_iota(jnp.int32, (1, width), 1)
    size = width // HEADS
    return [((lane >= h * size) & (lane < (h + 1) * size)).astype(dtype) for h in range(HEADS)]


def lat_inside(n):
    return lax.rem(n, WLAT)


def lat_row(row_iota, lat, shifted, lat_total):
    row = lat * WLAT + lat_inside(row_iota)
    if shifted:
        row = row + WLAT // 2
        row = jnp.where(row >= lat_total, row - lat_total, row)
    return row


def expand_bias(table, spread, tab_scr, rows_scr, wide_scr, bias_scr, lat, shifted, lat_total):
    for h in range(HEADS):
        tab_scr[h : h + 1, :] = table[h]
    for zi in range(LEVELS):
        for zj in range(LEVELS):
            for ai in range(WLAT):
                at = ((zi * LEVELS + zj) * WLAT + ai) * PAIR
                row = zj * CHUNK * 8 + (zi * WLAT + ai) * 8
                rows_scr[row : row + HEADS, 0:PAIR] = tab_scr[0:HEADS, at : at + PAIR]
    count = CHUNK * 8
    total = jnp.zeros((count, WIDE), F32)
    for zj in range(LEVELS):
        parts = split3(rows_scr[zj * count : (zj + 1) * count, 0:PAIR])
        for part in parts:
            total = total + dot(part, spread[zj])
    put(wide_scr, slice(None), total)
    i = lax.broadcasted_iota(jnp.int32, (CHUNK, WIN), 0)
    j = lax.broadcasted_iota(jnp.int32, (CHUNK, WIN), 1)
    allowed = lat_row(j, lat, shifted, lat_total) < lat_total - PAD
    if shifted:
        last = lat_total - WLAT // 2
        region_i = (lat * WLAT + lat_inside(i)) >= last
        region_j = (lat * WLAT + lat_inside(j)) >= last
        allowed = allowed & (region_i == region_j)
    for h in range(HEADS):
        wide = get(wide_scr, pl.ds(h, CHUNK, stride=8), WIDE)
        for oi in range(WLON):
            back = (WLON - 1 - oi) * CHUNK
            moved = wide if back == 0 else pltpu.roll(wide, WIDE - back, axis=1)
            at = h * WIN + oi * CHUNK
            bias_scr[at : at + CHUNK, :] = jnp.where(allowed, moved[:, 0:WIN], NEGATIVE)


def fold_bias(sums, put_unit):
    rest = jnp.zeros((CHUNK, 128), F32)

    def emit(at, value):
        for r in range(CHUNK // UNIT):
            put_unit(at * (CHUNK // UNIT) + r, value[r * UNIT : (r + 1) * UNIT, :].astype(BF16))

    for h in range(HEADS):
        total = jnp.zeros((CHUNK, WIDE), F32)
        for oi in range(WLON):
            back = (WLON - 1 - oi) * CHUNK
            at = h * WIN + oi * CHUNK
            part = sums[at : at + CHUNK, :]
            total = total + (part if back == 0 else pltpu.roll(part, back, axis=1))
        emit(h, total[:, 0:128])
        emit(HEADS + h, total[:, 128:256])
        last = total[:, 256:384]
        rest = rest + (last if h == 0 else pltpu.roll(last, 8 * h, axis=1))
    emit(2 * HEADS, rest)

def stack_heads(v, masks):
    return jnp.concatenate([v * mask for mask in masks], axis=0)


def pick_heads(v, masks):
    total = v[0:WIN] * masks[0]
    for h in range(1, HEADS):
        total = total + v[h * WIN : (h + 1) * WIN] * masks[h]
    return total


def attend(qkv, bias, mixed, probs, stack_scr, width):
    masks = head_masks(width, BF16)
    masks32 = head_masks(width, F32)
    scale = (width // HEADS) ** -0.5

    def window(w, carry):
        rows = pl.ds(pl.multiple_of(w * WIN, 16), WIN)
        q = qkv[rows, 0:width]
        k = qkv[rows, width : 2 * width]
        v = qkv[rows, 2 * width : 3 * width]
        scores = dot_nt(stack_heads(q, masks), k)
        for h in range(HEADS):
            part = slice(h * WIN, (h + 1) * WIN)
            logits = scores[part] * scale + bias[part, :]
            weights = jnp.exp(logits - jnp.max(logits, axis=-1, keepdims=True))
            p = weights * (1.0 / jnp.sum(weights, axis=-1, keepdims=True))
            probs[w, h] = p
            stack_scr[part, :] = p.astype(BF16)
        mixed[rows, :] = pick_heads(dot(stack_scr[...], v), masks32).astype(BF16)
        return carry

    lax.fori_loop(0, probs.shape[0], window, 0)


def attend_back(qkv, probs, dmix, field, sums, low_scr, prob_scr, width):
    masks = head_masks(width, BF16)
    masks32 = head_masks(width, F32)
    scale = (width // HEADS) ** -0.5

    def window(w, carry):
        rows = pl.ds(pl.multiple_of(w * WIN, 16), WIN)
        q = qkv[rows, 0:width]
        k = qkv[rows, width : 2 * width]
        v = qkv[rows, 2 * width : 3 * width]
        up = stack_heads(dmix[rows, :], masks)
        prob_grad = dot_nt(up, v)
        for h in range(HEADS):
            part = slice(h * WIN, (h + 1) * WIN)
            p = probs[w, h]
            weighted = p * prob_grad[part]
            ds = weighted - p * jnp.sum(weighted, axis=-1, keepdims=True)
            sums[part, 0:WIN] += ds
            low_scr[part, :] = ds.astype(BF16)
            prob_scr[part, :] = p.astype(BF16)
        low = low_scr[...]
        dq = pick_heads(dot(low, k), masks32)
        dk = dot_tn(low, stack_heads(q, masks))
        dv = dot_tn(prob_scr[...], up)
        field[rows, 0:width] = (dq * scale).astype(BF16)
        field[rows, width : 2 * width] = (dk * scale).astype(BF16)
        field[rows, 2 * width : 3 * width] = dv.astype(BF16)
        return carry

    lax.fori_loop(0, probs.shape[0], window, 0)


def lon_major(src, scr):
    levels, lats, lons, width = src.shape
    for z in range(levels):
        for a in range(lats):
            at = (z * lats + a) * lons
            put(scr, slice(at, at + lons), src[z, a].astype(F32))


def lon_column(scr, lon, lons, width):
    return get(scr, pl.ds(lon, CHUNK, stride=lons), width)


def flat_store(dst, at, mat, cols):
    rows = mat.shape[1]
    if cols % 128 == 0:
        per = cols // 128
        for c in range(per):
            dst[pl.ds(at + c, rows, stride=per), :] = mat[c]
        return rows * per
    per = 2 * cols // 128
    half = cols // 128
    even = get(mat, pl.ds(0, rows // 2, stride=2), cols)
    odd = get(mat, pl.ds(1, rows // 2, stride=2), cols)
    for c in range(half):
        dst[pl.ds(at + c, rows // 2, stride=per), :] = even[:, c * 128 : (c + 1) * 128]
    dst[pl.ds(at + half, rows // 2, stride=per), :] = jnp.concatenate(
        [even[:, half * 128 : half * 128 + 64], odd[:, 0:64]], axis=1
    )
    for c in range(half):
        dst[pl.ds(at + half + 1 + c, rows // 2, stride=per), :] = odd[
            :, 64 + c * 128 : 64 + (c + 1) * 128
        ]
    return rows * cols // 128


def send_units(scr, base, out):
    lons, units = out.shape[:2]
    for j in range(lons):
        for u in range(units):
            at = base + (j * units + u) * UNIT
            if not isinstance(at, int):
                at = pl.multiple_of(at, UNIT)
            out[j, u] = scr[pl.ds(at, UNIT), :].astype(BF16)


def halves(scr, lat, keep, give):
    half = keep.shape[0] * keep.shape[1] * UNIT
    send_units(scr, lat * half, keep)
    send_units(scr, (1 - lat) * half, give)


def bias_units(sums, out):
    lons, per = out.shape[:2]

    def put_unit(k, value):
        out[k // per, k % per] = value

    fold_bias(sums, put_unit)
    for k in range(BIAS_UNITS, lons * per):
        put_unit(k, jnp.zeros((UNIT, 128), BF16))

def forward_core(x, b, refs, qkv_scr, bias_scr, mixed, probs, stack_scr):
    qkv_w, proj_w, gains = refs
    width = x.shape[-1]
    stand, inv = standardize(x)
    normed = (stand * gains[b, 0:1, :]).astype(BF16)
    qkv_scr[...] = dot(normed, qkv_w[b]).astype(BF16)
    attend(qkv_scr, bias_scr, mixed, probs, stack_scr, width)
    att = dot(mixed[...], proj_w[b]).astype(BF16)
    resid = (x + att.astype(F32)).astype(BF16).astype(F32)
    return resid, normed


def first_kernel(
    lat_total, tokens_in, cot_in, table_in, spread_in, qkv_in, proj_in, up_in, down_in, gains_in,
    x_out, tail_out, head_out, qkv_out, mixed_out, probs_out, resid_out, hidden_out, active_out,
    scr, cot_scr, tab_scr, rows_scr, wide_scr, bias_scr,
    cot, table, spread, tokens, qkv_w, gains, proj_w, up_w, down_w, stack_scr, sems,
):
    copies = []
    for source, target in (
        (cot_in, cot),
        (table_in.at[0:1], table),
        (spread_in, spread),
        (tokens_in, tokens),
        (qkv_in.at[0:1], qkv_w),
        (gains_in, gains),
        (proj_in.at[0:1], proj_w),
        (up_in.at[0:1], up_w),
        (down_in.at[0:1], down_w),
    ):
        copies.append(pltpu.make_async_copy(source, target, sems.at[len(copies)]))
    for copy in copies:
        copy.start()
    lat = lax.axis_index("lat")
    width = tokens.shape[-1]
    lons = tokens.shape[2]
    cut = CHUNK * (WLON // 2)
    copies[0].wait()
    lon_major(cot, cot_scr)
    g = jnp.concatenate([lon_column(cot_scr, lon, lons, width) for lon in range(lons)], axis=0)
    head_out[1] = g[0:cut, :].astype(BF16)
    tail_out[1] = g[cut:, :].astype(BF16)
    copies[1].wait()
    copies[2].wait()
    expand_bias(
        table.at[0], spread, tab_scr, rows_scr, wide_scr, bias_scr, lat, False, lat_total
    )
    copies[3].wait()
    lon_major(tokens, scr)
    x = jnp.concatenate([lon_column(scr, lon, lons, width) for lon in range(lons)], axis=0)
    x_out[...] = x.astype(BF16)
    for copy in copies[4:]:
        copy.wait()

    resid, _ = forward_core(
        x, 0, (qkv_w, proj_w, gains), qkv_out, bias_scr, mixed_out, probs_out, stack_scr
    )
    resid_out[...] = resid.astype(BF16)
    stand, _ = standardize(resid)
    normed = (stand * gains[0, 1:2, :]).astype(BF16)
    hidden = dot(normed, up_w[0])
    hidden_out[...] = hidden
    active = gelu_value(hidden).astype(BF16)
    active_out[...] = active
    result = resid + dot_nt(active, down_w[0])
    head_out[0] = result[0:cut, :].astype(BF16)
    tail_out[0] = result[cut:, :].astype(BF16)


def bias_kernel(
    lat_total, table, spread, hidden, bias_out, slope_out, tab_scr, rows_scr, wide_scr
):
    lat = lax.axis_index("lat")
    expand_bias(
        table.at[1], spread, tab_scr, rows_scr, wide_scr, bias_out, lat, True, lat_total
    )
    slope_out[...] = gelu_parts(hidden[...])[1].astype(BF16)


def merge_ahead(scr_own, scr_oth, rows):
    half = WLAT // 2
    n = lax.broadcasted_iota(jnp.int32, (rows, 1), 0)
    return jnp.where(
        lat_inside(n) < half,
        pltpu.roll(scr_own[...], rows - half, axis=0),
        pltpu.roll(scr_oth[...], half, axis=0),
    )


def merge_behind(scr_own, scr_oth, rows):
    half = WLAT // 2
    n = lax.broadcasted_iota(jnp.int32, (rows, 1), 0)
    return jnp.where(
        lat_inside(n) >= half,
        pltpu.roll(scr_own[...], half, axis=0),
        pltpu.roll(scr_oth[...], rows - half, axis=0),
    )


def second_kernel(
    lat_total,
    tail, lon_head, lat_tail, diag_head, bias, qkv_w, proj_w, up_w, down_w, gains,
    head_out, tail_out, n1_out, field_out, mixed_out, low_out, n2_out, hg_out, active_out, g_out,
    sums_out, gain_out,
    scr_own, scr_oth, qkv_scr, probs_scr, dmix_scr, low_scr, prob_scr,
):
    lat = lax.axis_index("lat")
    rows, width = scr_own.shape
    cut = CHUNK * (WLON // 2)

    def rolled(which):
        scr_own[0 : rows - cut, :] = tail[which].astype(F32)
        scr_own[rows - cut :, :] = lon_head[which].astype(F32)
        scr_oth[0 : rows - cut, :] = lat_tail[which].astype(F32)
        scr_oth[rows - cut :, :] = diag_head[which].astype(F32)
        return merge_ahead(scr_own, scr_oth, rows)

    g = rolled(1)
    n = lax.broadcasted_iota(jnp.int32, (rows, 1), 0)
    keep = lat_row(n, lat, True, lat_total) < lat_total - PAD
    g = jnp.where(keep, g, 0.0)
    g_out[...] = g.astype(BF16)

    x = rolled(0)

    resid, normed = forward_core(
        x, 1, (qkv_w, proj_w, gains), qkv_scr, bias, mixed_out, probs_scr, low_scr
    )
    n1_out[...] = normed
    stand2, inv2 = standardize(resid)
    normed2 = (stand2 * gains[1, 1:2, :]).astype(BF16)
    n2_out[...] = normed2
    active, slope = gelu_parts(dot(normed2, up_w[1]))
    active_out[...] = active.astype(BF16)

    hg = (dot(g_out[...], down_w[1]) * slope).astype(BF16)
    hg_out[...] = hg
    part, gain_two = norm_back(dot_nt(hg, up_w[1]), gains[1, 1:2, :], stand2, inv2)
    rg = g + part
    low = rg.astype(BF16)
    low_out[...] = low
    dmix_scr[...] = dot_nt(low, proj_w[1]).astype(BF16)
    sums_out[...] = jnp.zeros(sums_out.shape, F32)
    attend_back(
        qkv_scr, probs_scr, dmix_scr, field_out, sums_out, low_scr, prob_scr, width
    )
    ng = dot_nt(field_out[...], qkv_w[1]).astype(BF16).astype(F32)
    stand1, inv1 = standardize(x)
    part, gain_one = norm_back(ng, gains[1, 0:1, :], stand1, inv1)
    dx = rg + part
    head_out[...] = dx[0 : rows - cut, :].astype(BF16)
    tail_out[...] = dx[rows - cut :, :].astype(BF16)
    gain_out[0:1, :] = gain_one
    gain_out[1:2, :] = gain_two


def outer_kernel(
    n1, field, mixed, low, n2, hg, active, g, sums,
    keep, give, bias_out,
    m576, m192, m768, mdown, flat_scr,
):
    put(m576, slice(None), dot_tn(n1[...], field[...]))
    at = flat_store(flat_scr, 0, m576, field.shape[1])
    put(m192, slice(None), dot_tn(mixed[...], low[...]))
    at += flat_store(flat_scr, at, m192, mixed.shape[1])
    put(m768, slice(None), dot_tn(n2[...], hg[...]))
    at += flat_store(flat_scr, at, m768, active.shape[1])
    put(mdown, slice(None), dot_tn(active[...], g[...]))
    at += flat_store(flat_scr, at, mdown, mixed.shape[1])
    halves(flat_scr, lax.axis_index("lat"), keep, give)
    bias_units(sums, bias_out)


def lat_sums(*refs):
    out = refs[-1]
    at = 0
    for k in range(0, len(refs) - 2, 2):
        keep, got = refs[k], refs[k + 1]
        count = keep.shape[1]
        out[:, at : at + count] = (keep[...].astype(F32) + got[...].astype(F32)).astype(BF16)
        at += count
    out[:, at:] = refs[-2][...]


def sum_pieces(pieces, order, out):
    total = pieces[0].astype(F32)
    for k in range(1, pieces.shape[0]):
        total = total + pieces[k].astype(F32)
    total = total.astype(BF16)
    if len(out.shape) == len(pieces.shape):
        for k in range(out.shape[0]):
            out[k] = total
    else:
        out[...] = total


def join_z(*refs):
    out = refs[-1]
    count = out.shape[0]
    z = lax.div(lax.axis_index("lon"), 2)
    for k in range(count):
        out[lax.rem(z + count - k, count)] = refs[k][...]


def third_kernel(
    head, lon_tail, lat_head, diag_tail, resid_in, slope, active, mixed,
    proj_w, up_w, down_w, gains, order,
    keep_out, give_out, rg_out, dmix_out, gain_out,
    scr_own, scr_oth, m192, m768, mdown, flat_scr,
):
    rows, width = scr_own.shape
    cut = CHUNK * (WLON // 2)
    scr_own[0:cut, :] = lon_tail[...].astype(F32)
    scr_own[cut:, :] = head[...].astype(F32)
    scr_oth[0:cut, :] = diag_tail[...].astype(F32)
    scr_oth[cut:, :] = lat_head[...].astype(F32)
    g = merge_behind(scr_own, scr_oth, rows)
    g_low = g.astype(BF16)
    stand2, inv2 = standardize(resid_in[...].astype(F32))
    normed2 = (stand2 * gains[0, 1:2, :]).astype(BF16)
    hg = dot(g_low, down_w[0])
    hg = (hg * slope[...].astype(F32)).astype(BF16)
    part, gain_two = norm_back(dot_nt(hg, up_w[0]), gains[0, 1:2, :], stand2, inv2)
    rg = g + part
    rg_out[...] = rg
    low = rg.astype(BF16)
    dmix_out[...] = dot_nt(low, proj_w[0]).astype(BF16)
    gain_out[...] = gain_two
    put(m192, slice(None), dot_tn(mixed[...], low))
    at = flat_store(flat_scr, 0, m192, mixed.shape[1])
    put(m768, slice(None), dot_tn(normed2, hg))
    at += flat_store(flat_scr, at, m768, active.shape[1])
    put(mdown, slice(None), dot_tn(active[...], g_low))
    at += flat_store(flat_scr, at, mdown, mixed.shape[1])
    flat_scr[at:, :] = jnp.zeros((flat_scr.shape[0] - at, 128), F32)
    halves(flat_scr, lax.axis_index("lat"), keep_out, give_out)


def gain_rows(one, two):
    return jnp.concatenate(
        [
            one[:, 0:128],
            jnp.concatenate([one[:, 128:192], two[:, 0:64]], axis=1),
            two[:, 64:192],
        ],
        axis=0,
    )


def fourth_kernel(
    x_in, qkv, probs, dmix, rg, gain_two, gains_late, order, qkv_w, gains,
    tokens_out, keep, give, bias_out,
    field, sums, m576, flat_scr, dx_scr, low_scr, prob_scr,
):
    width = x_in.shape[-1]
    levels, lats, lons = tokens_out.shape[:3]
    sums[...] = jnp.zeros(sums.shape, F32)
    attend_back(qkv, probs, dmix, field, sums, low_scr, prob_scr, width)
    stand1, inv1 = standardize(x_in[...].astype(F32))
    normed = (stand1 * gains[0, 0:1, :]).astype(BF16)
    ng = dot_nt(field[...], qkv_w[0]).astype(BF16).astype(F32)
    part, gain_one = norm_back(ng, gains[0, 0:1, :], stand1, inv1)
    put(m576, slice(None), dot_tn(normed, field[...]))
    at = flat_store(flat_scr, 0, m576, field.shape[1])
    flat_scr[at:, :] = jnp.zeros((flat_scr.shape[0] - at, 128), F32)
    flat_scr[at : at + 3, :] = gain_rows(gain_one, gain_two[...])
    flat_scr[at + 3 : at + 6, :] = gain_rows(gains_late[0:1, :], gains_late[1:2, :])
    bias_units(sums, bias_out)
    halves(flat_scr, lax.axis_index("lat"), keep, give)
    put(dx_scr, slice(None), rg[...] + part)
    for z in range(levels):
        for a in range(lats):
            tokens_out[z, a] = get(
                dx_scr, pl.ds(z * lats + a, lons, stride=CHUNK), width
            ).astype(BF16)


def last_kernel(
    units_a, units_b, units_c, spread, same, same_x, cross, cross_x, own_bc, oth_bc,
    update_out, bias_out, scr, rows_scr, wide_scr, tab_scr, a, bc,
):
    lat = lax.axis_index("lat")
    x = lax.rem(lax.axis_index("lon"), 2)
    lons = own_bc.shape[0]
    extra = bc.shape[2] - units_b - units_c
    for j in range(lons):
        bc[lat, j] = own_bc[j]
        bc[1 - lat, j] = oth_bc[j]
    for z in range(lons // 2):
        a[lat, 2 * z + x] = same[z]
        a[lat, 2 * z + 1 - x] = same_x[z]
        a[1 - lat, 2 * z + x] = cross[z]
        a[1 - lat, 2 * z + 1 - x] = cross_x[z]

    def place(pieces, first, last, dests):
        total = jnp.zeros((UNIT, 128), F32)
        per = last - first
        k = 0
        for where, room in dests:
            for at in range(where, where + room, UNIT):
                half, j, u = k // (per * lons), k // per % lons, k % per
                value = pieces[half, j, first + u].astype(F32)
                scr[at : at + UNIT, :] = value
                total = total + value * value
                k += 1
        return total

    total = place(a, 0, units_a, [(864, 864), (2016, 288), (3456, 1152), (5760, 1152)])
    total = total + place(bc, 0, units_b, [(1728, 288), (2304, 1152), (4608, 1152)])
    total = total + place(bc, units_b, units_b + units_c, [(0, 864), (6912, 8)])
    count = update_out.shape[0]
    mean = jnp.sum(total) * (1.0 / (count * 128))
    scale = lax.rsqrt(mean + 1e-06)
    update_out[...] = (scr[0:count, :] * scale).astype(BF16)

    for b, (piece, base) in enumerate(((bc, units_b + units_c), (a, units_a))):

        def read(at):
            parts = []
            for r in range(CHUNK // UNIT):
                k = at * (CHUNK // UNIT) + r
                parts.append(piece[lat, k // extra, base + k % extra].astype(F32))
            return jnp.concatenate(parts, axis=0)

        rest = read(2 * HEADS)
        for h in range(HEADS):
            rows = pl.ds(h, CHUNK, stride=8)
            wide_scr[0, rows, :] = read(h)
            wide_scr[1, rows, :] = read(HEADS + h)
            wide_scr[2, rows, :] = rest if h == 0 else pltpu.roll(rest, 128 - 8 * h, axis=1)
        low = get(wide_scr, slice(None), WIDE).astype(BF16)
        for zj in range(LEVELS):
            rows_scr[...] = dot_nt(low, spread[zj])
            for zi in range(LEVELS):
                for ai in range(WLAT):
                    at = ((zi * LEVELS + zj) * WLAT + ai) * PAIR
                    row = (zi * WLAT + ai) * 8
                    tab_scr[0:HEADS, at : at + PAIR] = rows_scr[row : row + HEADS, 0:PAIR]
        for h in range(HEADS):
            bias_out[b, h] = tab_scr[h : h + 1, :]


def call(kernel, outs, scratch, args, micros, mib, spaces=None, pinned=()):
    spaces = spaces or [pltpu.VMEM] * len(args)
    return pl.pallas_call(
        kernel,
        out_shape=[
            pltpu.VMEM(*entry) if at in pinned else jax.ShapeDtypeStruct(*entry)
            for at, entry in enumerate(outs)
        ],
        in_specs=[pl.BlockSpec(memory_space=space) for space in spaces],
        out_specs=[pl.BlockSpec(memory_space=pltpu.VMEM)] * len(outs),
        scratch_shapes=[
            pltpu.VMEM(*entry) if isinstance(entry, tuple) else entry for entry in scratch
        ],
        compiler_params=pltpu.CompilerParams(vmem_limit_bytes=mib * MIB),
        cost_estimate=pl.CostEstimate(
            flops=int(micros * 1.1e9), bytes_accessed=10**5, transcendentals=0
        ),
    )(*args)


def lat_swap(value):
    return lax.ppermute(value, "lat", [(0, 1), (1, 0)])


def lon_send(value, step):
    count = lax.axis_size("lon")
    return lax.ppermute(value, "lon", [(s, (s + step) % count) for s in range(count)])


def x_swap(value):
    count = lax.axis_size("lon")
    return lax.ppermute(value, "lon", [(s, s ^ 1) for s in range(count)])


def diag_send(value, step):
    count = lax.axis_size("lon")
    pairs = []
    for s in range(count):
        for t in range(2):
            pairs.append((2 * s + t, 2 * ((s + step) % count) + 1 - t))
    return lax.ppermute(value, ("lon", "lat"), pairs)


def shards(
    tokens, cotangent, qkv_weight, proj_weight, up_weight, down_weight, norm_gain, bias_table
):
    levels, lats, lons, width = tokens.shape
    rows = levels * lats * lons
    wins = rows // WIN
    hid = up_weight.shape[-1]
    heads = bias_table.shape[2]
    lon_size = lax.axis_size("lon")
    zs = lon_size // 2
    lat_total = lats * lax.axis_size("lat")
    cut = CHUNK * (WLON // 2)
    spread = jnp.asarray(spread_matrices(), BF16)
    down_turned = jnp.swapaxes(down_weight, 1, 2)
    table = jnp.swapaxes(bias_table, 1, 2)
    token = (rows, width)
    field_shape = ((rows, 3 * width), BF16)
    probs_shape = ((wins, heads, WIN, WIN), F32)
    stack_shape = ((heads * WIN, WIN), BF16)
    bias_shape = ((heads * WIN, WIN), F32)
    sums_shape = ((heads * WIN, WIDE), F32)
    tab_scr = ((8, table.shape[-1]), F32)
    rows_scr = ((LEVELS * CHUNK * 8, PAIR), F32)
    wide_scr = ((WIDE // 128, CHUNK * 8, 128), F32)
    tiles = -(-width // 128)
    token_scr = ((tiles, rows, 128), F32)
    m576 = ((-(-3 * width // 128), width, 128), F32)
    m192 = ((tiles, width, 128), F32)
    m768 = ((hid // 128, width, 128), F32)
    mdown = ((tiles, hid, 128), F32)

    block_rows = (qkv_weight[0].size + proj_weight[0].size + 2 * up_weight[0].size) // 128
    qkv_rows = qkv_weight[0].size // 128
    counts = (block_rows, block_rows - qkv_rows, qkv_rows + 8)
    units_a, units_b, units_c = [-(-count // (2 * lon_size * UNIT)) for count in counts]
    extra = -(-BIAS_UNITS // lon_size)

    def units(*lead):
        return (lead + (UNIT, 128), BF16)

    def flat_scr(per):
        return ((2 * lon_size * per * UNIT, 128), F32)

    x0, tail, head, qkv0, mixed0, probs0, resid0, hidden0, active0 = call(
        functools.partial(first_kernel, lat_total),
        [
            (token, BF16),
            ((2, rows - cut, width), BF16),
            ((2, cut, width), BF16),
            field_shape,
            (token, BF16),
            probs_shape,
            (token, BF16),
            ((rows, hid), F32),
            ((rows, hid), BF16),
        ],
        [
            token_scr,
            token_scr,
            tab_scr,
            rows_scr,
            wide_scr,
            bias_shape,
            (cotangent.shape, BF16),
            ((1,) + table.shape[1:], F32),
            (spread.shape, BF16),
            (tokens.shape, BF16),
            ((1,) + qkv_weight.shape[1:], BF16),
            (norm_gain.shape, F32),
            ((1,) + proj_weight.shape[1:], BF16),
            ((1,) + up_weight.shape[1:], BF16),
            ((1,) + down_turned.shape[1:], BF16),
            stack_shape,
            pltpu.SemaphoreType.DMA((9,)),
        ],
        [
            pltpu.with_memory_space_constraint(arg, pltpu.HBM)
            for arg in (
                tokens, cotangent, table, spread, qkv_weight, proj_weight, up_weight, down_turned,
                norm_gain,
            )
        ],
        8,
        28,
        [pltpu.HBM] * 9,
        (0, 3, 4, 5, 6, 8),
    )
    lon_head = lon_send(head, -1)
    diag_head = diag_send(head, -1)
    lat_tail = lat_swap(tail)
    bias1, slope0 = call(
        functools.partial(bias_kernel, lat_total),
        [bias_shape, ((rows, hid), BF16)],
        [tab_scr, rows_scr, wide_scr],
        (table, spread, hidden0),
        3,
        10,
        None,
        (1,),
    )

    (
        dhead, dtail, n1, field1, mixed1, low1, n2, hg1, active1, g1, sums1, gains1,
    ) = call(
        functools.partial(second_kernel, lat_total),
        [
            ((rows - cut, width), BF16),
            ((cut, width), BF16),
            (token, BF16),
            field_shape,
            (token, BF16),
            (token, BF16),
            (token, BF16),
            ((rows, hid), BF16),
            ((rows, hid), BF16),
            (token, BF16),
            sums_shape,
            ((2, width), F32),
        ],
        [
            (token, F32),
            (token, F32),
            field_shape,
            probs_shape,
            (token, BF16),
            stack_shape,
            stack_shape,
        ],
        (
            tail, lon_head, lat_tail, diag_head, bias1, qkv_weight, proj_weight, up_weight,
            down_turned, norm_gain,
        ),
        19,
        28,
    )
    lon_tail = lon_send(dtail, 1)
    diag_tail = diag_send(dtail, 1)
    lat_dhead = lat_swap(dhead)

    keep_a, give_a, bias_a = call(
        outer_kernel,
        [units(lon_size, units_a), units(lon_size, units_a), units(lon_size, extra)],
        [m576, m192, m768, mdown, flat_scr(units_a)],
        (n1, field1, mixed1, low1, n2, hg1, active1, g1, sums1),
        3,
        20,
    )
    got_a = lat_swap(give_a)

    keep_b, give_b, rg0, dmix0, gain_two = call(
        third_kernel,
        [
            units(lon_size, units_b),
            units(lon_size, units_b),
            (token, F32),
            (token, BF16),
            ((1, width), F32),
        ],
        [(token, F32), (token, F32), m192, m768, mdown, flat_scr(units_b)],
        (
            dhead, lon_tail, lat_dhead, diag_tail, resid0, slope0, active0, mixed0, proj_weight,
            up_weight, down_turned, norm_gain, keep_a,
        ),
        3,
        20,
    )
    got_b = lat_swap(give_b)
    (part_a,) = call(
        lat_sums, [units(lon_size, units_a + extra)], [], (keep_a, got_a, bias_a), 1, 10
    )
    pieces_a = lax.all_to_all(part_a, "lon", 0, 0)

    tokens_grad, keep_c, give_c, bias_c = call(
        fourth_kernel,
        [
            (tokens.shape, BF16),
            units(lon_size, units_c),
            units(lon_size, units_c),
            units(lon_size, extra),
        ],
        [
            field_shape,
            sums_shape,
            m576,
            flat_scr(units_c),
            token_scr,
            stack_shape,
            stack_shape,
        ],
        (
            x0, qkv0, probs0, dmix0, rg0, gain_two, gains1, part_a, qkv_weight, norm_gain,
        ),
        9,
        20,
    )
    got_c = lat_swap(give_c)
    (part_bc,) = call(
        lat_sums,
        [units(lon_size, units_b + units_c + extra)],
        [],
        (keep_b, got_b, keep_c, got_c, bias_c),
        1,
        10,
    )
    pieces_bc = lax.all_to_all(part_bc, "lon", 0, 0)

    (sum_a,) = call(
        sum_pieces, [units(units_a + extra)], [], (pieces_a, part_bc), 1, 10
    )
    (sum_bc,) = call(
        sum_pieces,
        [units(lon_size, units_b + units_c + extra)],
        [],
        (pieces_bc, sum_a),
        1,
        10,
    )
    whole_bc = lax.all_to_all(sum_bc, "lon", 0, 0)
    (same,) = call(
        join_z,
        [units(zs, units_a + extra)],
        [],
        [sum_a] + [lon_send(sum_a, 2 * k) for k in range(1, zs)],
        1,
        10,
    )
    same_x = x_swap(same)
    cross = lat_swap(same)
    cross_x = lat_swap(same_x)
    oth_bc = lat_swap(whole_bc)

    flat_rows = (2 * block_rows * 128 + norm_gain.size) // 128
    update, bias_grad = call(
        functools.partial(last_kernel, units_a, units_b, units_c),
        [((flat_rows, 128), BF16), (table.shape, F32)],
        [
            ((flat_rows + 2, 128), F32),
            ((CHUNK * 8, PAIR), F32),
            wide_scr,
            tab_scr,
            units(2, lon_size, units_a + extra),
            units(2, lon_size, units_b + units_c + extra),
        ],
        (spread, same, same_x, cross, cross_x, whole_bc, oth_bc),
        3,
        20,
    )
    bias_grad = jnp.swapaxes(bias_grad, 1, 2)
    return (tokens_grad, update.reshape(-1), bias_grad)


def solution(mesh):
    return jax.shard_map(
        shards,
        mesh=mesh,
        in_specs=(
            P("grp", "lat", "lon", None),
            P("grp", "lat", "lon", None),
            P(),
            P(),
            P(),
            P(),
            P(),
            P(None, "lat", None, None),
        ),
        out_specs=(P("grp", "lat", "lon", None), P("grp"), P("grp", "lat", None, None)),
        check_vma=False,
    )
```

```python
import functools

import jax
import jax.numpy as jnp
import numpy as np
from jax import lax
from jax.experimental import pallas as pl
from jax.experimental.pallas import tpu as pltpu
from jax.sharding import PartitionSpec as P

WLAT = 12
WLON = 6
PAD = 5
LEVELS = 2
HEADS = 6
CHUNK = LEVELS * WLAT
WIN = CHUNK * WLON
SHIFTS = 2 * WLON - 1
PAIR = WLAT * SHIFTS
WIDE = 384

EPS = 1e-05
NEGATIVE = -1000000000.0
ROOT_HALF = 0.7071067811865476
INV_ROOT_TAU = 0.3989422804014327

F32 = jnp.float32
BF16 = jnp.bfloat16
UNIT = 8
BIAS_UNITS = (2 * HEADS + 1) * CHUNK // UNIT
MIB = 1024 * 1024


def dot(a, b):
    return lax.dot_general(a, b, (((1,), (0,)), ((), ())), preferred_element_type=F32)


def dot_nt(a, b):
    return lax.dot_general(a, b, (((1,), (1,)), ((), ())), preferred_element_type=F32)


def dot_tn(a, b):
    return lax.dot_general(a, b, (((0,), (0,)), ((), ())), preferred_element_type=F32)


def row_mean(v):
    return jnp.sum(v, axis=-1, keepdims=True) * (1.0 / v.shape[-1])


def standardize(x):
    centred = x - row_mean(x)
    inv = lax.rsqrt(row_mean(centred * centred) + EPS)
    return centred * inv, inv


def norm_back(d, gain, stand, inv):
    scaled = d * gain
    first = row_mean(scaled)
    second = row_mean(scaled * stand)
    gain_grad = jnp.sum(d * stand, axis=0, keepdims=True)
    return inv * (scaled - first - stand * second), gain_grad


def gelu_value(hidden):
    return 0.5 * hidden * (1.0 + lax.erf(hidden * ROOT_HALF))


def gelu_parts(hidden):
    half = 0.5 * (1.0 + lax.erf(hidden * ROOT_HALF))
    slope = half + hidden * jnp.exp(-0.5 * hidden * hidden) * INV_ROOT_TAU
    return hidden * half, slope


def split3(v):
    hi = v.astype(BF16)
    rest = v - hi.astype(F32)
    mid = rest.astype(BF16)
    low = (rest - mid.astype(F32)).astype(BF16)
    return hi, mid, low


def spread_matrices():
    out = np.zeros((LEVELS, PAIR, WIDE), np.float32)
    for zj in range(LEVELS):
        for aj in range(WLAT):
            for d in range(SHIFTS):
                out[zj, aj * SHIFTS + d, (SHIFTS - 1 - d) * CHUNK + zj * WLAT + aj] = 1.0
    return out


def put(scr, rows, value):
    width = value.shape[1]
    for tile in range(-(-width // 128)):
        lanes = min(128, width - tile * 128)
        scr[tile, rows, 0:lanes] = value[:, tile * 128 : tile * 128 + lanes]


def get(scr, rows, width):
    parts = [scr[tile, rows, :] for tile in range(-(-width // 128))]
    return jnp.concatenate(parts, axis=1)[:, 0:width]


def head_masks(width, dtype):
    lane = lax.broadcasted_iota(jnp.int32, (1, width), 1)
    size = width // HEADS
    return [((lane >= h * size) & (lane < (h + 1) * size)).astype(dtype) for h in range(HEADS)]


def lat_inside(n):
    return lax.rem(n, WLAT)


def lat_row(row_iota, lat, shifted, lat_total):
    row = lat * WLAT + lat_inside(row_iota)
    if shifted:
        row = row + WLAT // 2
        row = jnp.where(row >= lat_total, row - lat_total, row)
    return row


def expand_bias(table, spread, tab_scr, rows_scr, wide_scr, bias_scr, lat, shifted, lat_total):
    for h in range(HEADS):
        tab_scr[h : h + 1, :] = table[h]
    for zi in range(LEVELS):
        for zj in range(LEVELS):
            for ai in range(WLAT):
                at = ((zi * LEVELS + zj) * WLAT + ai) * PAIR
                row = zj * CHUNK * 8 + (zi * WLAT + ai) * 8
                rows_scr[row : row + HEADS, 0:PAIR] = tab_scr[0:HEADS, at : at + PAIR]
    count = CHUNK * 8
    total = jnp.zeros((count, WIDE), F32)
    for zj in range(LEVELS):
        parts = split3(rows_scr[zj * count : (zj + 1) * count, 0:PAIR])
        for part in parts:
            total = total + dot(part, spread[zj])
    put(wide_scr, slice(None), total)
    i = lax.broadcasted_iota(jnp.int32, (CHUNK, WIN), 0)
    j = lax.broadcasted_iota(jnp.int32, (CHUNK, WIN), 1)
    allowed = lat_row(j, lat, shifted, lat_total) < lat_total - PAD
    if shifted:
        last = lat_total - WLAT // 2
        region_i = (lat * WLAT + lat_inside(i)) >= last
        region_j = (lat * WLAT + lat_inside(j)) >= last
        allowed = allowed & (region_i == region_j)
    for h in range(HEADS):
        wide = get(wide_scr, pl.ds(h, CHUNK, stride=8), WIDE)
        for oi in range(WLON):
            back = (WLON - 1 - oi) * CHUNK
            moved = wide if back == 0 else pltpu.roll(wide, WIDE - back, axis=1)
            at = h * WIN + oi * CHUNK
            bias_scr[at : at + CHUNK, :] = jnp.where(allowed, moved[:, 0:WIN], NEGATIVE)


def fold_bias(sums, put_unit):
    rest = jnp.zeros((CHUNK, 128), F32)

    def emit(at, value):
        for r in range(CHUNK // UNIT):
            put_unit(at * (CHUNK // UNIT) + r, value[r * UNIT : (r + 1) * UNIT, :].astype(BF16))

    for h in range(HEADS):
        total = jnp.zeros((CHUNK, WIDE), F32)
        for oi in range(WLON):
            back = (WLON - 1 - oi) * CHUNK
            at = h * WIN + oi * CHUNK
            part = sums[at : at + CHUNK, :]
            total = total + (part if back == 0 else pltpu.roll(part, back, axis=1))
        emit(h, total[:, 0:128])
        emit(HEADS + h, total[:, 128:256])
        last = total[:, 256:384]
        rest = rest + (last if h == 0 else pltpu.roll(last, 8 * h, axis=1))
    emit(2 * HEADS, rest)

def stack_heads(v, masks):
    return jnp.concatenate([v * mask for mask in masks], axis=0)


def pick_heads(v, masks):
    total = v[0:WIN] * masks[0]
    for h in range(1, HEADS):
        total = total + v[h * WIN : (h + 1) * WIN] * masks[h]
    return total


def attend(qkv, bias, mixed, probs, stack_scr, width, finish=None):
    masks = head_masks(width, BF16)
    masks32 = head_masks(width, F32)
    scale = (width // HEADS) ** -0.5

    def window(w, carry):
        rows = pl.ds(pl.multiple_of(w * WIN, 16), WIN)
        q = qkv[rows, 0:width]
        k = qkv[rows, width : 2 * width]
        v = qkv[rows, 2 * width : 3 * width]
        scores = dot_nt(stack_heads(q, masks), k)
        for h in range(HEADS):
            part = slice(h * WIN, (h + 1) * WIN)
            logits = scores[part] * scale + bias[part, :]
            weights = jnp.exp(logits - jnp.max(logits, axis=-1, keepdims=True))
            p = weights * (1.0 / jnp.sum(weights, axis=-1, keepdims=True))
            probs[w, h] = p
            stack_scr[part, :] = p.astype(BF16)
        mixed[rows, :] = pick_heads(dot(stack_scr[...], v), masks32).astype(BF16)
        if finish is not None:
            finish(w)
        return carry

    lax.fori_loop(0, probs.shape[0], window, 0, unroll=True)


def attend_back(qkv, probs, dmix, field, sums, low_scr, prob_scr, width, first=0):
    masks = head_masks(width, BF16)
    masks32 = head_masks(width, F32)
    scale = (width // HEADS) ** -0.5

    def window(w, carry):
        rows = pl.ds(pl.multiple_of(w * WIN, 16), WIN)
        q = qkv[rows, 0:width]
        k = qkv[rows, width : 2 * width]
        v = qkv[rows, 2 * width : 3 * width]
        up = stack_heads(dmix[rows, :], masks)
        prob_grad = dot_nt(up, v)
        for h in range(HEADS):
            part = slice(h * WIN, (h + 1) * WIN)
            p = probs[w - first, h]
            weighted = p * prob_grad[part]
            ds = weighted - p * jnp.sum(weighted, axis=-1, keepdims=True)
            sums[part, 0:WIN] += ds
            low_scr[part, :] = ds.astype(BF16)
            prob_scr[part, :] = p.astype(BF16)
        low = low_scr[...]
        dq = pick_heads(dot(low, k), masks32)
        dk = dot_tn(low, stack_heads(q, masks))
        dv = dot_tn(prob_scr[...], up)
        field[rows, 0:width] = (dq * scale).astype(BF16)
        field[rows, width : 2 * width] = (dk * scale).astype(BF16)
        field[rows, 2 * width : 3 * width] = dv.astype(BF16)
        return carry

    lax.fori_loop(first, first + probs.shape[0], window, 0, unroll=True)


def lon_major(src, scr):
    levels, lats, lons, width = src.shape
    for z in range(levels):
        for a in range(lats):
            at = (z * lats + a) * lons
            put(scr, slice(at, at + lons), src[z, a].astype(F32))


def lon_column(scr, lon, lons, width):
    return get(scr, pl.ds(lon, CHUNK, stride=lons), width)


def flat_store(dst, at, mat, cols):
    rows = mat.shape[1]
    if cols % 128 == 0:
        per = cols // 128
        for c in range(per):
            dst[pl.ds(at + c, rows, stride=per), :] = mat[c]
        return rows * per
    per = 2 * cols // 128
    half = cols // 128
    even = get(mat, pl.ds(0, rows // 2, stride=2), cols)
    odd = get(mat, pl.ds(1, rows // 2, stride=2), cols)
    for c in range(half):
        dst[pl.ds(at + c, rows // 2, stride=per), :] = even[:, c * 128 : (c + 1) * 128]
    dst[pl.ds(at + half, rows // 2, stride=per), :] = jnp.concatenate(
        [even[:, half * 128 : half * 128 + 64], odd[:, 0:64]], axis=1
    )
    for c in range(half):
        dst[pl.ds(at + half + 1 + c, rows // 2, stride=per), :] = odd[
            :, 64 + c * 128 : 64 + (c + 1) * 128
        ]
    return rows * cols // 128


def send_units(scr, base, out):
    lons, units = out.shape[:2]
    for j in range(lons):
        for u in range(units):
            at = base + (j * units + u) * UNIT
            if not isinstance(at, int):
                at = pl.multiple_of(at, UNIT)
            out[j, u] = scr[pl.ds(at, UNIT), :].astype(BF16)


def halves(scr, lat, keep, give):
    half = keep.shape[0] * keep.shape[1] * UNIT
    send_units(scr, lat * half, keep)
    send_units(scr, (1 - lat) * half, give)


def bias_units(sums, out):
    lons, per = out.shape[:2]

    def put_unit(k, value):
        out[k // per, k % per] = value

    fold_bias(sums, put_unit)
    for k in range(BIAS_UNITS, lons * per):
        put_unit(k, jnp.zeros((UNIT, 128), BF16))

def forward_core(x, b, refs, qkv_scr, bias_scr, mixed, probs, stack_scr, finish=None):
    qkv_w, proj_w, gains = refs
    width = x.shape[-1]
    stand, inv = standardize(x)
    normed = (stand * gains[b, 0:1, :]).astype(BF16)
    qkv_scr[...] = dot(normed, qkv_w[b]).astype(BF16)
    attend(qkv_scr, bias_scr, mixed, probs, stack_scr, width, finish)
    att = dot(mixed[...], proj_w[b]).astype(BF16)
    resid = (x + att.astype(F32)).astype(BF16).astype(F32)
    return resid, normed


def first_kernel(
    lat_total, tokens_in, cot_in, table_in, spread_in, qkv_in, proj_in, up_in, down_in, gains_in,
    x_out, tail_out, head_out, qkv_out, mixed_out, probs_out, resid_out, hidden_out, active_out,
    scr, cot_scr, tab_scr, rows_scr, wide_scr, bias_scr,
    cot, table, spread, tokens, qkv_w, gains, proj_w, up_w, down_w, stack_scr, probs, sems, out_sems,
):
    copies = []
    for source, target in (
        (cot_in, cot),
        (table_in.at[0:1], table),
        (spread_in, spread),
        (tokens_in, tokens),
        (qkv_in.at[0:1], qkv_w),
        (gains_in, gains),
        (proj_in.at[0:1], proj_w),
        (up_in.at[0:1], up_w),
        (down_in.at[0:1], down_w),
    ):
        copies.append(pltpu.make_async_copy(source, target, sems.at[len(copies)]))
    for copy in copies:
        copy.start()
    lat = lax.axis_index("lat")
    width = tokens.shape[-1]
    lons = tokens.shape[2]
    cut = CHUNK * (WLON // 2)
    copies[0].wait()
    lon_major(cot, cot_scr)
    g = jnp.concatenate([lon_column(cot_scr, lon, lons, width) for lon in range(lons)], axis=0)
    head_out[1] = g[0:cut, :].astype(BF16)
    tail_out[1] = g[cut:, :].astype(BF16)
    copies[1].wait()
    copies[2].wait()
    expand_bias(
        table.at[0], spread, tab_scr, rows_scr, wide_scr, bias_scr, lat, False, lat_total
    )
    copies[3].wait()
    lon_major(tokens, scr)
    x = jnp.concatenate([lon_column(scr, lon, lons, width) for lon in range(lons)], axis=0)
    x_out[...] = x.astype(BF16)
    for copy in copies[4:]:
        copy.wait()

    def probs_copy(w):
        return pltpu.make_async_copy(probs.at[w], probs_out.at[w], out_sems.at[w])

    resid, _ = forward_core(
        x, 0, (qkv_w, proj_w, gains), qkv_out, bias_scr, mixed_out, probs, stack_scr,
        lambda w: probs_copy(w).start(),
    )
    resid_out[...] = resid.astype(BF16)
    stand, _ = standardize(resid)
    normed = (stand * gains[0, 1:2, :]).astype(BF16)
    hidden = dot(normed, up_w[0])
    hidden_out[...] = hidden
    active = gelu_value(hidden).astype(BF16)
    active_out[...] = active
    result = resid + dot_nt(active, down_w[0])
    head_out[0] = result[0:cut, :].astype(BF16)
    tail_out[0] = result[cut:, :].astype(BF16)
    for w in range(probs.shape[0]):
        probs_copy(w).wait()


def bias_kernel(
    lat_total, table, spread, hidden, bias_out, slope_out, tab_scr, rows_scr, wide_scr
):
    lat = lax.axis_index("lat")
    expand_bias(
        table.at[1], spread, tab_scr, rows_scr, wide_scr, bias_out, lat, True, lat_total
    )
    slope_out[...] = gelu_parts(hidden[...])[1].astype(BF16)


def merge_ahead(scr_own, scr_oth, rows):
    half = WLAT // 2
    n = lax.broadcasted_iota(jnp.int32, (rows, 1), 0)
    return jnp.where(
        lat_inside(n) < half,
        pltpu.roll(scr_own[...], rows - half, axis=0),
        pltpu.roll(scr_oth[...], half, axis=0),
    )


def merge_behind(scr_own, scr_oth, rows):
    half = WLAT // 2
    n = lax.broadcasted_iota(jnp.int32, (rows, 1), 0)
    return jnp.where(
        lat_inside(n) >= half,
        pltpu.roll(scr_own[...], half, axis=0),
        pltpu.roll(scr_oth[...], rows - half, axis=0),
    )


def second_kernel(
    lat_total,
    tail, lon_head, lat_tail, diag_head, bias, qkv_w, proj_w, up_w, down_w, gains,
    head_out, tail_out, n1_out, field_out, mixed_out, low_out, n2_out, hg_out, active_out, g_out,
    sums_out, gain_out,
    scr_own, scr_oth, qkv_scr, probs_scr, dmix_scr, low_scr, prob_scr,
):
    lat = lax.axis_index("lat")
    rows, width = scr_own.shape
    cut = CHUNK * (WLON // 2)

    def rolled(which):
        scr_own[0 : rows - cut, :] = tail[which].astype(F32)
        scr_own[rows - cut :, :] = lon_head[which].astype(F32)
        scr_oth[0 : rows - cut, :] = lat_tail[which].astype(F32)
        scr_oth[rows - cut :, :] = diag_head[which].astype(F32)
        return merge_ahead(scr_own, scr_oth, rows)

    g = rolled(1)
    n = lax.broadcasted_iota(jnp.int32, (rows, 1), 0)
    keep = lat_row(n, lat, True, lat_total) < lat_total - PAD
    g = jnp.where(keep, g, 0.0)
    g_out[...] = g.astype(BF16)

    x = rolled(0)

    resid, normed = forward_core(
        x, 1, (qkv_w, proj_w, gains), qkv_scr, bias, mixed_out, probs_scr, low_scr
    )
    n1_out[...] = normed
    stand2, inv2 = standardize(resid)
    normed2 = (stand2 * gains[1, 1:2, :]).astype(BF16)
    n2_out[...] = normed2
    active, slope = gelu_parts(dot(normed2, up_w[1]))
    active_out[...] = active.astype(BF16)

    hg = (dot(g_out[...], down_w[1]) * slope).astype(BF16)
    hg_out[...] = hg
    part, gain_two = norm_back(dot_nt(hg, up_w[1]), gains[1, 1:2, :], stand2, inv2)
    rg = g + part
    low = rg.astype(BF16)
    low_out[...] = low
    dmix_scr[...] = dot_nt(low, proj_w[1]).astype(BF16)
    sums_out[...] = jnp.zeros(sums_out.shape, F32)
    attend_back(
        qkv_scr, probs_scr, dmix_scr, field_out, sums_out, low_scr, prob_scr, width
    )
    ng = dot_nt(field_out[...], qkv_w[1]).astype(BF16).astype(F32)
    stand1, inv1 = standardize(x)
    part, gain_one = norm_back(ng, gains[1, 0:1, :], stand1, inv1)
    dx = rg + part
    head_out[...] = dx[0 : rows - cut, :].astype(BF16)
    tail_out[...] = dx[rows - cut :, :].astype(BF16)
    gain_out[0:1, :] = gain_one
    gain_out[1:2, :] = gain_two


def outer_kernel(
    n1, field, mixed, low, n2, hg, active, g, sums,
    keep, give, bias_out,
    m576, m192, m768, mdown, flat_scr,
):
    put(m576, slice(None), dot_tn(n1[...], field[...]))
    at = flat_store(flat_scr, 0, m576, field.shape[1])
    put(m192, slice(None), dot_tn(mixed[...], low[...]))
    at += flat_store(flat_scr, at, m192, mixed.shape[1])
    put(m768, slice(None), dot_tn(n2[...], hg[...]))
    at += flat_store(flat_scr, at, m768, active.shape[1])
    put(mdown, slice(None), dot_tn(active[...], g[...]))
    at += flat_store(flat_scr, at, mdown, mixed.shape[1])
    halves(flat_scr, lax.axis_index("lat"), keep, give)
    bias_units(sums, bias_out)


def lat_sums(*refs):
    out = refs[-1]
    at = 0
    for k in range(0, len(refs) - 2, 2):
        keep, got = refs[k], refs[k + 1]
        count = keep.shape[1]
        out[:, at : at + count] = (keep[...].astype(F32) + got[...].astype(F32)).astype(BF16)
        at += count
    out[:, at:] = refs[-2][...]


def sum_pieces(pieces, order, out):
    total = pieces[0].astype(F32)
    for k in range(1, pieces.shape[0]):
        total = total + pieces[k].astype(F32)
    total = total.astype(BF16)
    if len(out.shape) == len(pieces.shape):
        for k in range(out.shape[0]):
            out[k] = total
    else:
        out[...] = total


def join_z(*refs):
    out = refs[-1]
    count = out.shape[0]
    z = lax.div(lax.axis_index("lon"), 2)
    for k in range(count):
        out[lax.rem(z + count - k, count)] = refs[k][...]


def third_kernel(
    head, lon_tail, lat_head, diag_tail, resid_in, slope, active, mixed,
    proj_w, up_w, down_w, gains, probs_in, qkv_in, order,
    keep_out, give_out, rg_out, dmix_out, gain_out, probs_out, qkv_out,
    scr_own, scr_oth, m192, m768, mdown, flat_scr, sems,
):
    copies = [
        pltpu.make_async_copy(qkv_in, qkv_out, sems.at[0]),
        pltpu.make_async_copy(probs_in.at[0 : probs_out.shape[0]], probs_out, sems.at[1]),
    ]
    for copy in copies:
        copy.start()
    rows, width = scr_own.shape
    cut = CHUNK * (WLON // 2)
    scr_own[0:cut, :] = lon_tail[...].astype(F32)
    scr_own[cut:, :] = head[...].astype(F32)
    scr_oth[0:cut, :] = diag_tail[...].astype(F32)
    scr_oth[cut:, :] = lat_head[...].astype(F32)
    g = merge_behind(scr_own, scr_oth, rows)
    g_low = g.astype(BF16)
    stand2, inv2 = standardize(resid_in[...].astype(F32))
    normed2 = (stand2 * gains[0, 1:2, :]).astype(BF16)
    hg = dot(g_low, down_w[0])
    hg = (hg * slope[...].astype(F32)).astype(BF16)
    part, gain_two = norm_back(dot_nt(hg, up_w[0]), gains[0, 1:2, :], stand2, inv2)
    rg = g + part
    rg_out[...] = rg
    low = rg.astype(BF16)
    dmix_out[...] = dot_nt(low, proj_w[0]).astype(BF16)
    gain_out[...] = gain_two
    put(m192, slice(None), dot_tn(mixed[...], low))
    at = flat_store(flat_scr, 0, m192, mixed.shape[1])
    put(m768, slice(None), dot_tn(normed2, hg))
    at += flat_store(flat_scr, at, m768, active.shape[1])
    put(mdown, slice(None), dot_tn(active[...], g_low))
    at += flat_store(flat_scr, at, mdown, mixed.shape[1])
    flat_scr[at:, :] = jnp.zeros((flat_scr.shape[0] - at, 128), F32)
    halves(flat_scr, lax.axis_index("lat"), keep_out, give_out)
    for copy in copies:
        copy.wait()


def gain_rows(one, two):
    return jnp.concatenate(
        [
            one[:, 0:128],
            jnp.concatenate([one[:, 128:192], two[:, 0:64]], axis=1),
            two[:, 64:192],
        ],
        axis=0,
    )


def fourth_kernel(
    x_in, qkv, probs_near, probs_in, dmix, rg, gain_two, gains_late, qkv_w, gains,
    tokens_out, keep, give, bias_out,
    field, sums, m576, flat_scr, dx_scr, low_scr, prob_scr, probs, sem,
):
    near = probs_near.shape[0]
    copy = pltpu.make_async_copy(probs_in.at[near : probs_in.shape[0]], probs, sem)
    copy.start()
    width = x_in.shape[-1]
    levels, lats, lons = tokens_out.shape[:3]
    sums[...] = jnp.zeros(sums.shape, F32)
    attend_back(qkv, probs_near, dmix, field, sums, low_scr, prob_scr, width)
    copy.wait()
    attend_back(qkv, probs, dmix, field, sums, low_scr, prob_scr, width, near)
    stand1, inv1 = standardize(x_in[...].astype(F32))
    normed = (stand1 * gains[0, 0:1, :]).astype(BF16)
    ng = dot_nt(field[...], qkv_w[0]).astype(BF16).astype(F32)
    part, gain_one = norm_back(ng, gains[0, 0:1, :], stand1, inv1)
    put(m576, slice(None), dot_tn(normed, field[...]))
    at = flat_store(flat_scr, 0, m576, field.shape[1])
    flat_scr[at:, :] = jnp.zeros((flat_scr.shape[0] - at, 128), F32)
    flat_scr[at : at + 3, :] = gain_rows(gain_one, gain_two[...])
    flat_scr[at + 3 : at + 6, :] = gain_rows(gains_late[0:1, :], gains_late[1:2, :])
    bias_units(sums, bias_out)
    halves(flat_scr, lax.axis_index("lat"), keep, give)
    put(dx_scr, slice(None), rg[...] + part)
    for z in range(levels):
        for a in range(lats):
            tokens_out[z, a] = get(
                dx_scr, pl.ds(z * lats + a, lons, stride=CHUNK), width
            ).astype(BF16)


def last_kernel(
    units_a, units_b, units_c, spread, same, same_x, cross, cross_x, own_bc, oth_bc,
    update_out, bias_out, scr, rows_scr, wide_scr, tab_scr, a, bc,
):
    lat = lax.axis_index("lat")
    x = lax.rem(lax.axis_index("lon"), 2)
    lons = own_bc.shape[0]
    extra = bc.shape[2] - units_b - units_c
    for j in range(lons):
        bc[lat, j] = own_bc[j]
        bc[1 - lat, j] = oth_bc[j]
    for z in range(lons // 2):
        a[lat, 2 * z + x] = same[z]
        a[lat, 2 * z + 1 - x] = same_x[z]
        a[1 - lat, 2 * z + x] = cross[z]
        a[1 - lat, 2 * z + 1 - x] = cross_x[z]

    def place(pieces, first, last, dests):
        total = jnp.zeros((UNIT, 128), F32)
        per = last - first
        k = 0
        for where, room in dests:
            for at in range(where, where + room, UNIT):
                half, j, u = k // (per * lons), k // per % lons, k % per
                value = pieces[half, j, first + u].astype(F32)
                scr[at : at + UNIT, :] = value
                total = total + value * value
                k += 1
        return total

    total = place(a, 0, units_a, [(864, 864), (2016, 288), (3456, 1152), (5760, 1152)])
    total = total + place(bc, 0, units_b, [(1728, 288), (2304, 1152), (4608, 1152)])
    total = total + place(bc, units_b, units_b + units_c, [(0, 864), (6912, 8)])
    count = update_out.shape[0]
    mean = jnp.sum(total) * (1.0 / (count * 128))
    scale = lax.rsqrt(mean + 1e-06)
    update_out[...] = (scr[0:count, :] * scale).astype(BF16)

    for b, (piece, base) in enumerate(((bc, units_b + units_c), (a, units_a))):

        def read(at):
            parts = []
            for r in range(CHUNK // UNIT):
                k = at * (CHUNK // UNIT) + r
                parts.append(piece[lat, k // extra, base + k % extra].astype(F32))
            return jnp.concatenate(parts, axis=0)

        rest = read(2 * HEADS)
        for h in range(HEADS):
            rows = pl.ds(h, CHUNK, stride=8)
            wide_scr[0, rows, :] = read(h)
            wide_scr[1, rows, :] = read(HEADS + h)
            wide_scr[2, rows, :] = rest if h == 0 else pltpu.roll(rest, 128 - 8 * h, axis=1)
        low = get(wide_scr, slice(None), WIDE).astype(BF16)
        for zj in range(LEVELS):
            rows_scr[...] = dot_nt(low, spread[zj])
            for zi in range(LEVELS):
                for ai in range(WLAT):
                    at = ((zi * LEVELS + zj) * WLAT + ai) * PAIR
                    row = (zi * WLAT + ai) * 8
                    tab_scr[0:HEADS, at : at + PAIR] = rows_scr[row : row + HEADS, 0:PAIR]
        for h in range(HEADS):
            bias_out[b, h] = tab_scr[h : h + 1, :]


def call(kernel, outs, scratch, args, micros, mib, spaces=None, far=()):
    spaces = spaces or [pltpu.VMEM] * len(args)
    return pl.pallas_call(
        kernel,
        out_shape=[
            pltpu.HBM(*entry) if at in far else jax.ShapeDtypeStruct(*entry)
            for at, entry in enumerate(outs)
        ],
        in_specs=[pl.BlockSpec(memory_space=space) for space in spaces],
        out_specs=[
            pl.BlockSpec(memory_space=pltpu.HBM if at in far else pltpu.VMEM)
            for at in range(len(outs))
        ],
        scratch_shapes=[
            pltpu.VMEM(*entry) if isinstance(entry, tuple) else entry for entry in scratch
        ],
        compiler_params=pltpu.CompilerParams(vmem_limit_bytes=mib * MIB),
        cost_estimate=pl.CostEstimate(
            flops=int(micros * 1.1e9), bytes_accessed=10**5, transcendentals=0
        ),
    )(*args)


def lat_swap(value):
    return lax.ppermute(value, "lat", [(0, 1), (1, 0)])


def lon_send(value, step):
    count = lax.axis_size("lon")
    return lax.ppermute(value, "lon", [(s, (s + step) % count) for s in range(count)])


def x_swap(value):
    count = lax.axis_size("lon")
    return lax.ppermute(value, "lon", [(s, s ^ 1) for s in range(count)])


def diag_send(value, step):
    count = lax.axis_size("lon")
    pairs = []
    for s in range(count):
        for t in range(2):
            pairs.append((2 * s + t, 2 * ((s + step) % count) + 1 - t))
    return lax.ppermute(value, ("lon", "lat"), pairs)


def shards(
    tokens, cotangent, qkv_weight, proj_weight, up_weight, down_weight, norm_gain, bias_table
):
    levels, lats, lons, width = tokens.shape
    rows = levels * lats * lons
    wins = rows // WIN
    hid = up_weight.shape[-1]
    heads = bias_table.shape[2]
    lon_size = lax.axis_size("lon")
    zs = lon_size // 2
    lat_total = lats * lax.axis_size("lat")
    cut = CHUNK * (WLON // 2)
    spread = jnp.asarray(spread_matrices(), BF16)
    down_turned = jnp.swapaxes(down_weight, 1, 2)
    table = jnp.swapaxes(bias_table, 1, 2)
    token = (rows, width)
    field_shape = ((rows, 3 * width), BF16)
    probs_shape = ((wins, heads, WIN, WIN), F32)
    stack_shape = ((heads * WIN, WIN), BF16)
    bias_shape = ((heads * WIN, WIN), F32)
    sums_shape = ((heads * WIN, WIDE), F32)
    tab_scr = ((8, table.shape[-1]), F32)
    rows_scr = ((LEVELS * CHUNK * 8, PAIR), F32)
    wide_scr = ((WIDE // 128, CHUNK * 8, 128), F32)
    tiles = -(-width // 128)
    token_scr = ((tiles, rows, 128), F32)
    m576 = ((-(-3 * width // 128), width, 128), F32)
    m192 = ((tiles, width, 128), F32)
    m768 = ((hid // 128, width, 128), F32)
    mdown = ((tiles, hid, 128), F32)

    block_rows = (qkv_weight[0].size + proj_weight[0].size + 2 * up_weight[0].size) // 128
    qkv_rows = qkv_weight[0].size // 128
    counts = (block_rows, block_rows - qkv_rows, qkv_rows + 8)
    units_a, units_b, units_c = [-(-count // (2 * lon_size * UNIT)) for count in counts]
    extra = -(-BIAS_UNITS // lon_size)

    def units(*lead):
        return (lead + (UNIT, 128), BF16)

    def flat_scr(per):
        return ((2 * lon_size * per * UNIT, 128), F32)

    x0, tail, head, qkv0, mixed0, probs0, resid0, hidden0, active0 = call(
        functools.partial(first_kernel, lat_total),
        [
            (token, BF16),
            ((2, rows - cut, width), BF16),
            ((2, cut, width), BF16),
            field_shape,
            (token, BF16),
            probs_shape,
            (token, BF16),
            ((rows, hid), F32),
            ((rows, hid), BF16),
        ],
        [
            token_scr,
            token_scr,
            tab_scr,
            rows_scr,
            wide_scr,
            bias_shape,
            (cotangent.shape, BF16),
            ((1,) + table.shape[1:], F32),
            (spread.shape, BF16),
            (tokens.shape, BF16),
            ((1,) + qkv_weight.shape[1:], BF16),
            (norm_gain.shape, F32),
            ((1,) + proj_weight.shape[1:], BF16),
            ((1,) + up_weight.shape[1:], BF16),
            ((1,) + down_turned.shape[1:], BF16),
            stack_shape,
            probs_shape,
            pltpu.SemaphoreType.DMA((9,)),
            pltpu.SemaphoreType.DMA((wins,)),
        ],
        [
            pltpu.with_memory_space_constraint(arg, pltpu.HBM)
            for arg in (
                tokens, cotangent, table, spread, qkv_weight, proj_weight, up_weight, down_turned,
                norm_gain,
            )
        ],
        8,
        28,
        [pltpu.HBM] * 9,
        (5,),
    )
    lon_head = lon_send(head, -1)
    diag_head = diag_send(head, -1)
    lat_tail = lat_swap(tail)
    bias1, slope0 = call(
        functools.partial(bias_kernel, lat_total),
        [bias_shape, ((rows, hid), BF16)],
        [tab_scr, rows_scr, wide_scr],
        (table, spread, hidden0),
        3,
        10,
    )

    (
        dhead, dtail, n1, field1, mixed1, low1, n2, hg1, active1, g1, sums1, gains1,
    ) = call(
        functools.partial(second_kernel, lat_total),
        [
            ((rows - cut, width), BF16),
            ((cut, width), BF16),
            (token, BF16),
            field_shape,
            (token, BF16),
            (token, BF16),
            (token, BF16),
            ((rows, hid), BF16),
            ((rows, hid), BF16),
            (token, BF16),
            sums_shape,
            ((2, width), F32),
        ],
        [
            (token, F32),
            (token, F32),
            field_shape,
            probs_shape,
            (token, BF16),
            stack_shape,
            stack_shape,
        ],
        (
            tail, lon_head, lat_tail, diag_head, bias1, qkv_weight, proj_weight, up_weight,
            down_turned, norm_gain,
        ),
        19,
        28,
    )
    lon_tail = lon_send(dtail, 1)
    diag_tail = diag_send(dtail, 1)
    lat_dhead = lat_swap(dhead)

    keep_a, give_a, bias_a = call(
        outer_kernel,
        [units(lon_size, units_a), units(lon_size, units_a), units(lon_size, extra)],
        [m576, m192, m768, mdown, flat_scr(units_a)],
        (n1, field1, mixed1, low1, n2, hg1, active1, g1, sums1),
        3,
        20,
    )
    got_a = lat_swap(give_a)

    (part_a,) = call(
        lat_sums, [units(lon_size, units_a + extra)], [], (keep_a, got_a, bias_a), 1, 10
    )
    pieces_a = lax.all_to_all(part_a, "lon", 0, 0)

    near = wins // 2
    probs_far = pltpu.with_memory_space_constraint(probs0, pltpu.HBM)
    keep_b, give_b, rg0, dmix0, gain_two, probs_near, qkv_near = call(
        third_kernel,
        [
            units(lon_size, units_b),
            units(lon_size, units_b),
            (token, F32),
            (token, BF16),
            ((1, width), F32),
            ((near,) + probs_shape[0][1:], F32),
            field_shape,
        ],
        [
            (token, F32),
            (token, F32),
            m192,
            m768,
            mdown,
            flat_scr(units_b),
            pltpu.SemaphoreType.DMA((2,)),
        ],
        (
            dhead, lon_tail, lat_dhead, diag_tail, resid0, slope0, active0, mixed0, proj_weight,
            up_weight, down_turned, norm_gain, probs_far,
            pltpu.with_memory_space_constraint(qkv0, pltpu.HBM), part_a,
        ),
        3,
        20,
        [pltpu.VMEM] * 12 + [pltpu.HBM] * 2 + [pltpu.VMEM],
    )
    got_b = lat_swap(give_b)

    tokens_grad, keep_c, give_c, bias_c = call(
        fourth_kernel,
        [
            (tokens.shape, BF16),
            units(lon_size, units_c),
            units(lon_size, units_c),
            units(lon_size, extra),
        ],
        [
            field_shape,
            sums_shape,
            m576,
            flat_scr(units_c),
            token_scr,
            stack_shape,
            stack_shape,
            ((wins - near,) + probs_shape[0][1:], F32),
            pltpu.SemaphoreType.DMA,
        ],
        (
            x0, qkv_near, probs_near, probs_far, dmix0, rg0, gain_two, gains1, qkv_weight,
            norm_gain,
        ),
        8,
        20,
        [pltpu.VMEM] * 3 + [pltpu.HBM] + [pltpu.VMEM] * 6,
    )
    got_c = lat_swap(give_c)
    (part_bc,) = call(
        lat_sums,
        [units(lon_size, units_b + units_c + extra)],
        [],
        (keep_b, got_b, keep_c, got_c, bias_c),
        1,
        10,
    )
    pieces_bc = lax.all_to_all(part_bc, "lon", 0, 0)

    (sum_a,) = call(
        sum_pieces, [units(units_a + extra)], [], (pieces_a, part_bc), 1, 10
    )
    (same,) = call(
        join_z,
        [units(zs, units_a + extra)],
        [],
        [sum_a] + [lon_send(sum_a, 2 * k) for k in range(1, zs)],
        1,
        10,
    )
    (sum_bc,) = call(
        sum_pieces,
        [units(lon_size, units_b + units_c + extra)],
        [],
        (pieces_bc, same),
        1,
        10,
    )
    whole_bc = lax.all_to_all(sum_bc, "lon", 0, 0)
    same_x = x_swap(same)
    cross = lat_swap(same)
    cross_x = lat_swap(same_x)
    oth_bc = lat_swap(whole_bc)

    flat_rows = (2 * block_rows * 128 + norm_gain.size) // 128
    update, bias_grad = call(
        functools.partial(last_kernel, units_a, units_b, units_c),
        [((flat_rows, 128), BF16), (table.shape, F32)],
        [
            ((flat_rows + 2, 128), F32),
            ((CHUNK * 8, PAIR), F32),
            wide_scr,
            tab_scr,
            units(2, lon_size, units_a + extra),
            units(2, lon_size, units_b + units_c + extra),
        ],
        (spread, same, same_x, cross, cross_x, whole_bc, oth_bc),
        3,
        20,
    )
    bias_grad = jnp.swapaxes(bias_grad, 1, 2)
    return (tokens_grad, update.reshape(-1), bias_grad)


def solution(mesh):
    return jax.shard_map(
        shards,
        mesh=mesh,
        in_specs=(
            P("grp", "lat", "lon", None),
            P("grp", "lat", "lon", None),
            P(),
            P(),
            P(),
            P(),
            P(),
            P(None, "lat", None, None),
        ),
        out_specs=(P("grp", "lat", "lon", None), P("grp"), P("grp", "lat", None, None)),
        check_vma=False,
    )
```

```python
import functools

import jax
import jax.numpy as jnp
import numpy as np
from jax import lax
from jax.experimental import pallas as pl
from jax.experimental.pallas import tpu as pltpu
from jax.sharding import PartitionSpec as P

WLAT = 12
WLON = 6
PAD = 5
LEVELS = 2
HEADS = 6
CHUNK = LEVELS * WLAT
WIN = CHUNK * WLON
SHIFTS = 2 * WLON - 1
PAIR = WLAT * SHIFTS
WIDE = 384

EPS = 1e-05
NEGATIVE = -1000000000.0
ROOT_HALF = 0.7071067811865476
INV_ROOT_TAU = 0.3989422804014327

F32 = jnp.float32
BF16 = jnp.bfloat16
UNIT = 8
BIAS_UNITS = (2 * HEADS + 1) * CHUNK // UNIT
MIB = 1024 * 1024


def dot(a, b):
    return lax.dot_general(a, b, (((1,), (0,)), ((), ())), preferred_element_type=F32)


def dot_nt(a, b):
    return lax.dot_general(a, b, (((1,), (1,)), ((), ())), preferred_element_type=F32)


def dot_tn(a, b):
    return lax.dot_general(a, b, (((0,), (0,)), ((), ())), preferred_element_type=F32)


def row_mean(v):
    return jnp.sum(v, axis=-1, keepdims=True) * (1.0 / v.shape[-1])


def standardize(x):
    centred = x - row_mean(x)
    inv = lax.rsqrt(row_mean(centred * centred) + EPS)
    return centred * inv, inv


def norm_back(d, gain, stand, inv):
    scaled = d * gain
    first = row_mean(scaled)
    second = row_mean(scaled * stand)
    gain_grad = jnp.sum(d * stand, axis=0, keepdims=True)
    return inv * (scaled - first - stand * second), gain_grad


def gelu_value(hidden):
    return 0.5 * hidden * (1.0 + lax.erf(hidden * ROOT_HALF))


def gelu_parts(hidden):
    half = 0.5 * (1.0 + lax.erf(hidden * ROOT_HALF))
    slope = half + hidden * jnp.exp(-0.5 * hidden * hidden) * INV_ROOT_TAU
    return hidden * half, slope


def split3(v):
    hi = v.astype(BF16)
    rest = v - hi.astype(F32)
    mid = rest.astype(BF16)
    low = (rest - mid.astype(F32)).astype(BF16)
    return hi, mid, low


def spread_matrices():
    out = np.zeros((LEVELS, PAIR, WIDE), np.float32)
    for zj in range(LEVELS):
        for aj in range(WLAT):
            for d in range(SHIFTS):
                out[zj, aj * SHIFTS + d, (SHIFTS - 1 - d) * CHUNK + zj * WLAT + aj] = 1.0
    return out


def put(scr, rows, value):
    width = value.shape[1]
    for tile in range(-(-width // 128)):
        lanes = min(128, width - tile * 128)
        scr[tile, rows, 0:lanes] = value[:, tile * 128 : tile * 128 + lanes]


def get(scr, rows, width):
    parts = [scr[tile, rows, :] for tile in range(-(-width // 128))]
    return jnp.concatenate(parts, axis=1)[:, 0:width]


def head_masks(width, dtype):
    lane = lax.broadcasted_iota(jnp.int32, (1, width), 1)
    size = width // HEADS
    return [((lane >= h * size) & (lane < (h + 1) * size)).astype(dtype) for h in range(HEADS)]


def lat_inside(n):
    return lax.rem(n, WLAT)


def lat_row(row_iota, lat, shifted, lat_total):
    row = lat * WLAT + lat_inside(row_iota)
    if shifted:
        row = row + WLAT // 2
        row = jnp.where(row >= lat_total, row - lat_total, row)
    return row


def expand_bias(table, spread, tab_scr, rows_scr, wide_scr, bias_scr, lat, shifted, lat_total):
    for h in range(HEADS):
        tab_scr[h : h + 1, :] = table[h]
    for zi in range(LEVELS):
        for zj in range(LEVELS):
            for ai in range(WLAT):
                at = ((zi * LEVELS + zj) * WLAT + ai) * PAIR
                row = zj * CHUNK * 8 + (zi * WLAT + ai) * 8
                rows_scr[row : row + HEADS, 0:PAIR] = tab_scr[0:HEADS, at : at + PAIR]
    count = CHUNK * 8
    total = jnp.zeros((count, WIDE), F32)
    for zj in range(LEVELS):
        parts = split3(rows_scr[zj * count : (zj + 1) * count, 0:PAIR])
        for part in parts:
            total = total + dot(part, spread[zj])
    put(wide_scr, slice(None), total)
    i = lax.broadcasted_iota(jnp.int32, (CHUNK, WIN), 0)
    j = lax.broadcasted_iota(jnp.int32, (CHUNK, WIN), 1)
    allowed = lat_row(j, lat, shifted, lat_total) < lat_total - PAD
    if shifted:
        last = lat_total - WLAT // 2
        region_i = (lat * WLAT + lat_inside(i)) >= last
        region_j = (lat * WLAT + lat_inside(j)) >= last
        allowed = allowed & (region_i == region_j)
    for h in range(HEADS):
        wide = get(wide_scr, pl.ds(h, CHUNK, stride=8), WIDE)
        for oi in range(WLON):
            back = (WLON - 1 - oi) * CHUNK
            moved = wide if back == 0 else pltpu.roll(wide, WIDE - back, axis=1)
            at = h * WIN + oi * CHUNK
            bias_scr[at : at + CHUNK, :] = jnp.where(allowed, moved[:, 0:WIN], NEGATIVE)


def fold_bias(sums, put_unit):
    rest = jnp.zeros((CHUNK, 128), F32)

    def emit(at, value):
        for r in range(CHUNK // UNIT):
            put_unit(at * (CHUNK // UNIT) + r, value[r * UNIT : (r + 1) * UNIT, :].astype(BF16))

    for h in range(HEADS):
        total = jnp.zeros((CHUNK, WIDE), F32)
        for oi in range(WLON):
            back = (WLON - 1 - oi) * CHUNK
            at = h * WIN + oi * CHUNK
            part = sums[at : at + CHUNK, :]
            total = total + (part if back == 0 else pltpu.roll(part, back, axis=1))
        emit(h, total[:, 0:128])
        emit(HEADS + h, total[:, 128:256])
        last = total[:, 256:384]
        rest = rest + (last if h == 0 else pltpu.roll(last, 8 * h, axis=1))
    emit(2 * HEADS, rest)

def stack_heads(v, masks):
    return jnp.concatenate([v * mask for mask in masks], axis=0)


def pick_heads(v, masks):
    total = v[0:WIN] * masks[0]
    for h in range(1, HEADS):
        total = total + v[h * WIN : (h + 1) * WIN] * masks[h]
    return total


def attend(qkv, bias, mixed, probs, stack_scr, width, finish=None):
    masks = head_masks(width, BF16)
    masks32 = head_masks(width, F32)
    scale = (width // HEADS) ** -0.5

    def window(w, carry):
        rows = pl.ds(pl.multiple_of(w * WIN, 16), WIN)
        q = qkv[rows, 0:width]
        k = qkv[rows, width : 2 * width]
        v = qkv[rows, 2 * width : 3 * width]
        scores = dot_nt(stack_heads(q, masks), k)
        for h in range(HEADS):
            part = slice(h * WIN, (h + 1) * WIN)
            logits = scores[part] * scale + bias[part, :]
            weights = jnp.exp(logits - jnp.max(logits, axis=-1, keepdims=True))
            p = weights * (1.0 / jnp.sum(weights, axis=-1, keepdims=True))
            probs[w, h] = p
            stack_scr[part, :] = p.astype(BF16)
        mixed[rows, :] = pick_heads(dot(stack_scr[...], v), masks32).astype(BF16)
        if finish is not None:
            finish(w)
        return carry

    lax.fori_loop(0, probs.shape[0], window, 0, unroll=True)


def attend_back(qkv, probs, dmix, field, sums, low_scr, prob_scr, width, first=0):
    masks = head_masks(width, BF16)
    masks32 = head_masks(width, F32)
    scale = (width // HEADS) ** -0.5

    def window(w, carry):
        rows = pl.ds(pl.multiple_of(w * WIN, 16), WIN)
        q = qkv[rows, 0:width]
        k = qkv[rows, width : 2 * width]
        v = qkv[rows, 2 * width : 3 * width]
        up = stack_heads(dmix[rows, :], masks)
        prob_grad = dot_nt(up, v)
        for h in range(HEADS):
            part = slice(h * WIN, (h + 1) * WIN)
            p = probs[w - first, h]
            weighted = p * prob_grad[part]
            ds = weighted - p * jnp.sum(weighted, axis=-1, keepdims=True)
            sums[part, 0:WIN] += ds
            low_scr[part, :] = ds.astype(BF16)
            prob_scr[part, :] = p.astype(BF16)
        low = low_scr[...]
        dq = pick_heads(dot(low, k), masks32)
        dk = dot_tn(low, stack_heads(q, masks))
        dv = dot_tn(prob_scr[...], up)
        field[rows, 0:width] = (dq * scale).astype(BF16)
        field[rows, width : 2 * width] = (dk * scale).astype(BF16)
        field[rows, 2 * width : 3 * width] = dv.astype(BF16)
        return carry

    lax.fori_loop(first, first + probs.shape[0], window, 0, unroll=True)


def lon_major(src, scr):
    levels, lats, lons, width = src.shape
    for z in range(levels):
        for a in range(lats):
            at = (z * lats + a) * lons
            put(scr, slice(at, at + lons), src[z, a].astype(F32))


def lon_column(scr, lon, lons, width):
    return get(scr, pl.ds(lon, CHUNK, stride=lons), width)


def flat_store(dst, at, mat, cols):
    rows = mat.shape[1]
    if cols % 128 == 0:
        per = cols // 128
        for c in range(per):
            dst[pl.ds(at + c, rows, stride=per), :] = mat[c]
        return rows * per
    per = 2 * cols // 128
    half = cols // 128
    even = get(mat, pl.ds(0, rows // 2, stride=2), cols)
    odd = get(mat, pl.ds(1, rows // 2, stride=2), cols)
    for c in range(half):
        dst[pl.ds(at + c, rows // 2, stride=per), :] = even[:, c * 128 : (c + 1) * 128]
    dst[pl.ds(at + half, rows // 2, stride=per), :] = jnp.concatenate(
        [even[:, half * 128 : half * 128 + 64], odd[:, 0:64]], axis=1
    )
    for c in range(half):
        dst[pl.ds(at + half + 1 + c, rows // 2, stride=per), :] = odd[
            :, 64 + c * 128 : 64 + (c + 1) * 128
        ]
    return rows * cols // 128


def send_units(scr, base, out):
    lons, units = out.shape[:2]
    for j in range(lons):
        for u in range(units):
            at = base + (j * units + u) * UNIT
            if not isinstance(at, int):
                at = pl.multiple_of(at, UNIT)
            out[j, u] = scr[pl.ds(at, UNIT), :].astype(BF16)


def halves(scr, lat, keep, give):
    half = keep.shape[0] * keep.shape[1] * UNIT
    send_units(scr, lat * half, keep)
    send_units(scr, (1 - lat) * half, give)


def bias_units(sums, out):
    lons, per = out.shape[:2]

    def put_unit(k, value):
        out[k // per, k % per] = value

    fold_bias(sums, put_unit)
    for k in range(BIAS_UNITS, lons * per):
        put_unit(k, jnp.zeros((UNIT, 128), BF16))

def forward_core(x, b, refs, qkv_scr, bias_scr, mixed, probs, stack_scr, finish=None):
    qkv_w, proj_w, gains = refs
    width = x.shape[-1]
    stand, inv = standardize(x)
    normed = (stand * gains[b, 0:1, :]).astype(BF16)
    qkv_scr[...] = dot(normed, qkv_w[b]).astype(BF16)
    attend(qkv_scr, bias_scr, mixed, probs, stack_scr, width, finish)
    att = dot(mixed[...], proj_w[b]).astype(BF16)
    resid = (x + att.astype(F32)).astype(BF16).astype(F32)
    return resid, normed


def first_kernel(
    lat_total, tokens_in, cot_in, table_in, spread_in, qkv_in, proj_in, up_in, down_in, gains_in,
    x_out, tail_out, head_out, qkv_out, mixed_out, probs_out, resid_out, hidden_out, active_out,
    scr, cot_scr, tab_scr, rows_scr, wide_scr, bias_scr,
    cot, table, spread, tokens, qkv_w, gains, proj_w, up_w, down_w, stack_scr, probs, sems, out_sems,
):
    copies = []
    for source, target in (
        (cot_in, cot),
        (table_in.at[0:1], table),
        (spread_in, spread),
        (tokens_in, tokens),
        (qkv_in.at[0:1], qkv_w),
        (gains_in, gains),
        (proj_in.at[0:1], proj_w),
        (up_in.at[0:1], up_w),
        (down_in.at[0:1], down_w),
    ):
        copies.append(pltpu.make_async_copy(source, target, sems.at[len(copies)]))
    for copy in copies:
        copy.start()
    lat = lax.axis_index("lat")
    width = tokens.shape[-1]
    lons = tokens.shape[2]
    cut = CHUNK * (WLON // 2)
    copies[0].wait()
    lon_major(cot, cot_scr)
    g = jnp.concatenate([lon_column(cot_scr, lon, lons, width) for lon in range(lons)], axis=0)
    head_out[1] = g[0:cut, :].astype(BF16)
    tail_out[1] = g[cut:, :].astype(BF16)
    copies[1].wait()
    copies[2].wait()
    expand_bias(
        table.at[0], spread, tab_scr, rows_scr, wide_scr, bias_scr, lat, False, lat_total
    )
    copies[3].wait()
    lon_major(tokens, scr)
    x = jnp.concatenate([lon_column(scr, lon, lons, width) for lon in range(lons)], axis=0)
    x_out[...] = x.astype(BF16)
    for copy in copies[4:]:
        copy.wait()

    def probs_copy(w):
        return pltpu.make_async_copy(probs.at[w], probs_out.at[w], out_sems.at[w])

    resid, _ = forward_core(
        x, 0, (qkv_w, proj_w, gains), qkv_out, bias_scr, mixed_out, probs, stack_scr,
        lambda w: probs_copy(w).start(),
    )
    resid_out[...] = resid.astype(BF16)
    stand, _ = standardize(resid)
    normed = (stand * gains[0, 1:2, :]).astype(BF16)
    hidden = dot(normed, up_w[0])
    hidden_out[...] = hidden
    active = gelu_value(hidden).astype(BF16)
    active_out[...] = active
    result = resid + dot_nt(active, down_w[0])
    head_out[0] = result[0:cut, :].astype(BF16)
    tail_out[0] = result[cut:, :].astype(BF16)
    for w in range(probs.shape[0]):
        probs_copy(w).wait()


def bias_kernel(
    lat_total, table, spread, hidden, bias_out, slope_out, tab_scr, rows_scr, wide_scr
):
    lat = lax.axis_index("lat")
    expand_bias(
        table.at[1], spread, tab_scr, rows_scr, wide_scr, bias_out, lat, True, lat_total
    )
    slope_out[...] = gelu_parts(hidden[...])[1].astype(BF16)


def merge_ahead(scr_own, scr_oth, rows):
    half = WLAT // 2
    n = lax.broadcasted_iota(jnp.int32, (rows, 1), 0)
    return jnp.where(
        lat_inside(n) < half,
        pltpu.roll(scr_own[...], rows - half, axis=0),
        pltpu.roll(scr_oth[...], half, axis=0),
    )


def merge_behind(scr_own, scr_oth, rows):
    half = WLAT // 2
    n = lax.broadcasted_iota(jnp.int32, (rows, 1), 0)
    return jnp.where(
        lat_inside(n) >= half,
        pltpu.roll(scr_own[...], half, axis=0),
        pltpu.roll(scr_oth[...], rows - half, axis=0),
    )


def second_kernel(
    lat_total,
    tail, lon_head, lat_tail, diag_head, bias, qkv_w, proj_w, up_w, down_w, gains,
    head_out, tail_out, n1_out, field_out, mixed_out, low_out, n2_out, hg_out, active_out, g_out,
    sums_out, gain_out,
    scr_own, scr_oth, qkv_scr, probs_scr, dmix_scr, low_scr, prob_scr,
):
    lat = lax.axis_index("lat")
    rows, width = scr_own.shape
    cut = CHUNK * (WLON // 2)

    def rolled(which):
        scr_own[0 : rows - cut, :] = tail[which].astype(F32)
        scr_own[rows - cut :, :] = lon_head[which].astype(F32)
        scr_oth[0 : rows - cut, :] = lat_tail[which].astype(F32)
        scr_oth[rows - cut :, :] = diag_head[which].astype(F32)
        return merge_ahead(scr_own, scr_oth, rows)

    g = rolled(1)
    n = lax.broadcasted_iota(jnp.int32, (rows, 1), 0)
    keep = lat_row(n, lat, True, lat_total) < lat_total - PAD
    g = jnp.where(keep, g, 0.0)
    g_out[...] = g.astype(BF16)

    x = rolled(0)

    resid, normed = forward_core(
        x, 1, (qkv_w, proj_w, gains), qkv_scr, bias, mixed_out, probs_scr, low_scr
    )
    n1_out[...] = normed
    stand2, inv2 = standardize(resid)
    normed2 = (stand2 * gains[1, 1:2, :]).astype(BF16)
    n2_out[...] = normed2
    active, slope = gelu_parts(dot(normed2, up_w[1]))
    active_out[...] = active.astype(BF16)

    hg = (dot(g_out[...], down_w[1]) * slope).astype(BF16)
    hg_out[...] = hg
    part, gain_two = norm_back(dot_nt(hg, up_w[1]), gains[1, 1:2, :], stand2, inv2)
    rg = g + part
    low = rg.astype(BF16)
    low_out[...] = low
    dmix_scr[...] = dot_nt(low, proj_w[1]).astype(BF16)
    sums_out[...] = jnp.zeros(sums_out.shape, F32)
    attend_back(
        qkv_scr, probs_scr, dmix_scr, field_out, sums_out, low_scr, prob_scr, width
    )
    ng = dot_nt(field_out[...], qkv_w[1]).astype(BF16).astype(F32)
    stand1, inv1 = standardize(x)
    part, gain_one = norm_back(ng, gains[1, 0:1, :], stand1, inv1)
    dx = rg + part
    head_out[...] = dx[0 : rows - cut, :].astype(BF16)
    tail_out[...] = dx[rows - cut :, :].astype(BF16)
    gain_out[0:1, :] = gain_one
    gain_out[1:2, :] = gain_two


def outer_kernel(
    n1, field, mixed, low, n2, hg, active, g, sums,
    keep, give, bias_out,
    m576, m192, m768, mdown, flat_scr,
):
    put(m576, slice(None), dot_tn(n1[...], field[...]))
    at = flat_store(flat_scr, 0, m576, field.shape[1])
    put(m192, slice(None), dot_tn(mixed[...], low[...]))
    at += flat_store(flat_scr, at, m192, mixed.shape[1])
    put(m768, slice(None), dot_tn(n2[...], hg[...]))
    at += flat_store(flat_scr, at, m768, active.shape[1])
    put(mdown, slice(None), dot_tn(active[...], g[...]))
    at += flat_store(flat_scr, at, mdown, mixed.shape[1])
    halves(flat_scr, lax.axis_index("lat"), keep, give)
    bias_units(sums, bias_out)


def lat_sums(*refs):
    out = refs[-1]
    at = 0
    for k in range(0, len(refs) - 2, 2):
        keep, got = refs[k], refs[k + 1]
        count = keep.shape[1]
        out[:, at : at + count] = (keep[...].astype(F32) + got[...].astype(F32)).astype(BF16)
        at += count
    out[:, at:] = refs[-2][...]


def sum_pieces(pieces, order, out):
    total = pieces[0].astype(F32)
    for k in range(1, pieces.shape[0]):
        total = total + pieces[k].astype(F32)
    total = total.astype(BF16)
    if len(out.shape) == len(pieces.shape):
        for k in range(out.shape[0]):
            out[k] = total
    else:
        out[...] = total


def join_z(*refs):
    out = refs[-1]
    count = out.shape[0]
    z = lax.div(lax.axis_index("lon"), 2)
    for k in range(count):
        out[lax.rem(z + count - k, count)] = refs[k][...]


def third_kernel(
    head, lon_tail, lat_head, diag_tail, resid_in, slope, active, mixed,
    proj_w, up_w, down_w, gains, probs_in, order,
    keep_out, give_out, rg_out, dmix_out, gain_out, probs_out,
    scr_own, scr_oth, m192, m768, mdown, flat_scr, sem,
):
    copy = pltpu.make_async_copy(probs_in.at[0 : probs_out.shape[0]], probs_out, sem)
    copy.start()
    rows, width = scr_own.shape
    cut = CHUNK * (WLON // 2)
    scr_own[0:cut, :] = lon_tail[...].astype(F32)
    scr_own[cut:, :] = head[...].astype(F32)
    scr_oth[0:cut, :] = diag_tail[...].astype(F32)
    scr_oth[cut:, :] = lat_head[...].astype(F32)
    g = merge_behind(scr_own, scr_oth, rows)
    g_low = g.astype(BF16)
    stand2, inv2 = standardize(resid_in[...].astype(F32))
    normed2 = (stand2 * gains[0, 1:2, :]).astype(BF16)
    hg = dot(g_low, down_w[0])
    hg = (hg * slope[...].astype(F32)).astype(BF16)
    part, gain_two = norm_back(dot_nt(hg, up_w[0]), gains[0, 1:2, :], stand2, inv2)
    rg = g + part
    rg_out[...] = rg
    low = rg.astype(BF16)
    dmix_out[...] = dot_nt(low, proj_w[0]).astype(BF16)
    gain_out[...] = gain_two
    put(m192, slice(None), dot_tn(mixed[...], low))
    at = flat_store(flat_scr, 0, m192, mixed.shape[1])
    put(m768, slice(None), dot_tn(normed2, hg))
    at += flat_store(flat_scr, at, m768, active.shape[1])
    put(mdown, slice(None), dot_tn(active[...], g_low))
    at += flat_store(flat_scr, at, mdown, mixed.shape[1])
    flat_scr[at:, :] = jnp.zeros((flat_scr.shape[0] - at, 128), F32)
    halves(flat_scr, lax.axis_index("lat"), keep_out, give_out)
    copy.wait()


def gain_rows(one, two):
    return jnp.concatenate(
        [
            one[:, 0:128],
            jnp.concatenate([one[:, 128:192], two[:, 0:64]], axis=1),
            two[:, 64:192],
        ],
        axis=0,
    )


def fourth_kernel(
    x_in, qkv, probs_near, probs_in, dmix, rg, gain_two, gains_late, qkv_w, gains,
    tokens_out, keep, give, bias_out,
    field, sums, m576, flat_scr, dx_scr, low_scr, prob_scr, probs, sem,
):
    near = probs_near.shape[0]
    copy = pltpu.make_async_copy(probs_in.at[near : probs_in.shape[0]], probs, sem)
    copy.start()
    width = x_in.shape[-1]
    levels, lats, lons = tokens_out.shape[:3]
    sums[...] = jnp.zeros(sums.shape, F32)
    attend_back(qkv, probs_near, dmix, field, sums, low_scr, prob_scr, width)
    copy.wait()
    attend_back(qkv, probs, dmix, field, sums, low_scr, prob_scr, width, near)
    stand1, inv1 = standardize(x_in[...].astype(F32))
    normed = (stand1 * gains[0, 0:1, :]).astype(BF16)
    ng = dot_nt(field[...], qkv_w[0]).astype(BF16).astype(F32)
    part, gain_one = norm_back(ng, gains[0, 0:1, :], stand1, inv1)
    put(m576, slice(None), dot_tn(normed, field[...]))
    at = flat_store(flat_scr, 0, m576, field.shape[1])
    flat_scr[at:, :] = jnp.zeros((flat_scr.shape[0] - at, 128), F32)
    flat_scr[at : at + 3, :] = gain_rows(gain_one, gain_two[...])
    flat_scr[at + 3 : at + 6, :] = gain_rows(gains_late[0:1, :], gains_late[1:2, :])
    bias_units(sums, bias_out)
    halves(flat_scr, lax.axis_index("lat"), keep, give)
    put(dx_scr, slice(None), rg[...] + part)
    for z in range(levels):
        for a in range(lats):
            tokens_out[z, a] = get(
                dx_scr, pl.ds(z * lats + a, lons, stride=CHUNK), width
            ).astype(BF16)


def place(pieces, first, last, dests, scr):
    total = jnp.zeros((UNIT, 128), F32)
    lons = pieces.shape[1]
    per = last - first
    k = 0
    for where, room in dests:
        for at in range(where, where + room, UNIT):
            half, j, u = k // (per * lons), k // per % lons, k % per
            value = pieces[half, j, first + u].astype(F32)
            scr[at : at + UNIT, :] = value
            total = total + value * value
            k += 1
    return total


def bias_rows(piece, base, spread, out, rows_scr, wide_scr, tab_scr):
    lat = lax.axis_index("lat")
    extra = -(-BIAS_UNITS // piece.shape[1])

    def read(at):
        parts = []
        for r in range(CHUNK // UNIT):
            k = at * (CHUNK // UNIT) + r
            parts.append(piece[lat, k // extra, base + k % extra].astype(F32))
        return jnp.concatenate(parts, axis=0)

    rest = read(2 * HEADS)
    for h in range(HEADS):
        rows = pl.ds(h, CHUNK, stride=8)
        wide_scr[0, rows, :] = read(h)
        wide_scr[1, rows, :] = read(HEADS + h)
        wide_scr[2, rows, :] = rest if h == 0 else pltpu.roll(rest, 128 - 8 * h, axis=1)
    low = get(wide_scr, slice(None), WIDE).astype(BF16)
    for zj in range(LEVELS):
        rows_scr[...] = dot_nt(low, spread[zj])
        for zi in range(LEVELS):
            for ai in range(WLAT):
                at = ((zi * LEVELS + zj) * WLAT + ai) * PAIR
                row = (zi * WLAT + ai) * 8
                tab_scr[0:HEADS, at : at + PAIR] = rows_scr[row : row + HEADS, 0:PAIR]
    for h in range(HEADS):
        out[h] = tab_scr[h : h + 1, :]


def late_kernel(
    units_a, spread, same, same_x, cross, cross_x, flat_out, squares_out, bias_out,
    rows_scr, wide_scr, tab_scr, a,
):
    lat = lax.axis_index("lat")
    x = lax.rem(lax.axis_index("lon"), 2)
    for z in range(same.shape[0]):
        a[lat, 2 * z + x] = same[z]
        a[lat, 2 * z + 1 - x] = same_x[z]
        a[1 - lat, 2 * z + x] = cross[z]
        a[1 - lat, 2 * z + 1 - x] = cross_x[z]
    squares_out[...] = place(a, 0, units_a, [(0, flat_out.shape[0])], flat_out)
    bias_rows(a, units_a, spread, bias_out, rows_scr, wide_scr, tab_scr)


def last_kernel(
    units_b, units_c, spread, flat_a, squares, bias_late, own_bc, oth_bc, update_out, bias_out,
    scr, rows_scr, wide_scr, tab_scr, bc,
):
    lat = lax.axis_index("lat")
    for j in range(own_bc.shape[0]):
        bc[lat, j] = own_bc[j]
        bc[1 - lat, j] = oth_bc[j]
    total = squares[...]
    total = total + place(bc, 0, units_b, [(864, 288), (1152, 1152), (2304, 1152)], scr)
    total = total + place(bc, units_b, units_b + units_c, [(0, 864), (3456, 8)], scr)
    count = update_out.shape[0]
    mean = jnp.sum(total) * (1.0 / (count * 128))
    scale = lax.rsqrt(mean + 1e-06)
    early, late = (0, 1728, 2304, 4608), (864, 2016, 3456, 5760)
    at = 0
    for first, second, rows in zip(early, late, (864, 288, 1152, 1152)):
        update_out[first : first + rows, :] = (scr[at : at + rows, :] * scale).astype(BF16)
        update_out[second : second + rows, :] = (flat_a[at : at + rows, :] * scale).astype(BF16)
        at += rows
    update_out[6912:count, :] = (scr[at : at + count - 6912, :] * scale).astype(BF16)
    bias_rows(bc, units_b + units_c, spread, bias_out.at[0], rows_scr, wide_scr, tab_scr)
    bias_out[1] = bias_late[...]


def call(kernel, outs, scratch, args, micros, mib, spaces=None, far=()):
    spaces = spaces or [pltpu.VMEM] * len(args)
    return pl.pallas_call(
        kernel,
        out_shape=[
            pltpu.HBM(*entry) if at in far else jax.ShapeDtypeStruct(*entry)
            for at, entry in enumerate(outs)
        ],
        in_specs=[pl.BlockSpec(memory_space=space) for space in spaces],
        out_specs=[
            pl.BlockSpec(memory_space=pltpu.HBM if at in far else pltpu.VMEM)
            for at in range(len(outs))
        ],
        scratch_shapes=[
            pltpu.VMEM(*entry) if isinstance(entry, tuple) else entry for entry in scratch
        ],
        compiler_params=pltpu.CompilerParams(vmem_limit_bytes=mib * MIB),
        cost_estimate=pl.CostEstimate(
            flops=int(micros * 1.1e9), bytes_accessed=10**5, transcendentals=0
        ),
    )(*args)


def lat_swap(value):
    return lax.ppermute(value, "lat", [(0, 1), (1, 0)])


def lon_send(value, step):
    count = lax.axis_size("lon")
    return lax.ppermute(value, "lon", [(s, (s + step) % count) for s in range(count)])


def x_swap(value):
    count = lax.axis_size("lon")
    return lax.ppermute(value, "lon", [(s, s ^ 1) for s in range(count)])


def diag_send(value, step):
    count = lax.axis_size("lon")
    pairs = []
    for s in range(count):
        for t in range(2):
            pairs.append((2 * s + t, 2 * ((s + step) % count) + 1 - t))
    return lax.ppermute(value, ("lon", "lat"), pairs)


def shards(
    tokens, cotangent, qkv_weight, proj_weight, up_weight, down_weight, norm_gain, bias_table
):
    levels, lats, lons, width = tokens.shape
    rows = levels * lats * lons
    wins = rows // WIN
    hid = up_weight.shape[-1]
    heads = bias_table.shape[2]
    lon_size = lax.axis_size("lon")
    zs = lon_size // 2
    lat_total = lats * lax.axis_size("lat")
    cut = CHUNK * (WLON // 2)
    spread = jnp.asarray(spread_matrices(), BF16)
    down_turned = jnp.swapaxes(down_weight, 1, 2)
    table = jnp.swapaxes(bias_table, 1, 2)
    token = (rows, width)
    field_shape = ((rows, 3 * width), BF16)
    probs_shape = ((wins, heads, WIN, WIN), F32)
    stack_shape = ((heads * WIN, WIN), BF16)
    bias_shape = ((heads * WIN, WIN), F32)
    sums_shape = ((heads * WIN, WIDE), F32)
    tab_scr = ((8, table.shape[-1]), F32)
    rows_scr = ((LEVELS * CHUNK * 8, PAIR), F32)
    wide_scr = ((WIDE // 128, CHUNK * 8, 128), F32)
    tiles = -(-width // 128)
    token_scr = ((tiles, rows, 128), F32)
    m576 = ((-(-3 * width // 128), width, 128), F32)
    m192 = ((tiles, width, 128), F32)
    m768 = ((hid // 128, width, 128), F32)
    mdown = ((tiles, hid, 128), F32)

    block_rows = (qkv_weight[0].size + proj_weight[0].size + 2 * up_weight[0].size) // 128
    qkv_rows = qkv_weight[0].size // 128
    counts = (block_rows, block_rows - qkv_rows, qkv_rows + 8)
    units_a, units_b, units_c = [-(-count // (2 * lon_size * UNIT)) for count in counts]
    extra = -(-BIAS_UNITS // lon_size)

    def units(*lead):
        return (lead + (UNIT, 128), BF16)

    def flat_scr(per):
        return ((2 * lon_size * per * UNIT, 128), F32)

    x0, tail, head, qkv0, mixed0, probs0, resid0, hidden0, active0 = call(
        functools.partial(first_kernel, lat_total),
        [
            (token, BF16),
            ((2, rows - cut, width), BF16),
            ((2, cut, width), BF16),
            field_shape,
            (token, BF16),
            probs_shape,
            (token, BF16),
            ((rows, hid), F32),
            ((rows, hid), BF16),
        ],
        [
            token_scr,
            token_scr,
            tab_scr,
            rows_scr,
            wide_scr,
            bias_shape,
            (cotangent.shape, BF16),
            ((1,) + table.shape[1:], F32),
            (spread.shape, BF16),
            (tokens.shape, BF16),
            ((1,) + qkv_weight.shape[1:], BF16),
            (norm_gain.shape, F32),
            ((1,) + proj_weight.shape[1:], BF16),
            ((1,) + up_weight.shape[1:], BF16),
            ((1,) + down_turned.shape[1:], BF16),
            stack_shape,
            probs_shape,
            pltpu.SemaphoreType.DMA((9,)),
            pltpu.SemaphoreType.DMA((wins,)),
        ],
        [
            pltpu.with_memory_space_constraint(arg, pltpu.HBM)
            for arg in (
                tokens, cotangent, table, spread, qkv_weight, proj_weight, up_weight, down_turned,
                norm_gain,
            )
        ],
        8,
        16,
        [pltpu.HBM] * 9,
        (5,),
    )
    lon_head = lon_send(head, -1)
    diag_head = diag_send(head, -1)
    lat_tail = lat_swap(tail)
    bias1, slope0 = call(
        functools.partial(bias_kernel, lat_total),
        [bias_shape, ((rows, hid), BF16)],
        [tab_scr, rows_scr, wide_scr],
        (table, spread, hidden0),
        3,
        10,
    )

    (
        dhead, dtail, n1, field1, mixed1, low1, n2, hg1, active1, g1, sums1, gains1,
    ) = call(
        functools.partial(second_kernel, lat_total),
        [
            ((rows - cut, width), BF16),
            ((cut, width), BF16),
            (token, BF16),
            field_shape,
            (token, BF16),
            (token, BF16),
            (token, BF16),
            ((rows, hid), BF16),
            ((rows, hid), BF16),
            (token, BF16),
            sums_shape,
            ((2, width), F32),
        ],
        [
            (token, F32),
            (token, F32),
            field_shape,
            probs_shape,
            (token, BF16),
            stack_shape,
            stack_shape,
        ],
        (
            tail, lon_head, lat_tail, diag_head, bias1, qkv_weight, proj_weight, up_weight,
            down_turned, norm_gain,
        ),
        19,
        16,
    )
    lon_tail = lon_send(dtail, 1)
    diag_tail = diag_send(dtail, 1)
    lat_dhead = lat_swap(dhead)

    keep_a, give_a, bias_a = call(
        outer_kernel,
        [units(lon_size, units_a), units(lon_size, units_a), units(lon_size, extra)],
        [m576, m192, m768, mdown, flat_scr(units_a)],
        (n1, field1, mixed1, low1, n2, hg1, active1, g1, sums1),
        3,
        14,
    )
    got_a = lat_swap(give_a)

    (part_a,) = call(
        lat_sums, [units(lon_size, units_a + extra)], [], (keep_a, got_a, bias_a), 1, 10
    )
    pieces_a = lax.all_to_all(part_a, "lon", 0, 0)

    near = wins // 2
    probs_far = pltpu.with_memory_space_constraint(probs0, pltpu.HBM)
    keep_b, give_b, rg0, dmix0, gain_two, probs_near = call(
        third_kernel,
        [
            units(lon_size, units_b),
            units(lon_size, units_b),
            (token, F32),
            (token, BF16),
            ((1, width), F32),
            ((near,) + probs_shape[0][1:], F32),
        ],
        [
            (token, F32),
            (token, F32),
            m192,
            m768,
            mdown,
            flat_scr(units_b),
            pltpu.SemaphoreType.DMA,
        ],
        (
            dhead, lon_tail, lat_dhead, diag_tail, resid0, slope0, active0, mixed0, proj_weight,
            up_weight, down_turned, norm_gain, probs_far, part_a,
        ),
        3,
        14,
        [pltpu.VMEM] * 12 + [pltpu.HBM, pltpu.VMEM],
    )
    got_b = lat_swap(give_b)

    tokens_grad, keep_c, give_c, bias_c = call(
        fourth_kernel,
        [
            (tokens.shape, BF16),
            units(lon_size, units_c),
            units(lon_size, units_c),
            units(lon_size, extra),
        ],
        [
            field_shape,
            sums_shape,
            m576,
            flat_scr(units_c),
            token_scr,
            stack_shape,
            stack_shape,
            ((wins - near,) + probs_shape[0][1:], F32),
            pltpu.SemaphoreType.DMA,
        ],
        (
            x0, qkv0, probs_near, probs_far, dmix0, rg0, gain_two, gains1, qkv_weight,
            norm_gain,
        ),
        8,
        14,
        [pltpu.VMEM] * 3 + [pltpu.HBM] + [pltpu.VMEM] * 6,
    )
    got_c = lat_swap(give_c)
    (part_bc,) = call(
        lat_sums,
        [units(lon_size, units_b + units_c + extra)],
        [],
        (keep_b, got_b, keep_c, got_c, bias_c),
        1,
        10,
    )
    pieces_bc = lax.all_to_all(part_bc, "lon", 0, 0)

    (sum_a,) = call(
        sum_pieces, [units(units_a + extra)], [], (pieces_a, part_bc), 1, 10
    )
    (same,) = call(
        join_z,
        [units(zs, units_a + extra)],
        [],
        [sum_a] + [lon_send(sum_a, 2 * k) for k in range(1, zs)],
        1,
        10,
    )
    (sum_bc,) = call(
        sum_pieces,
        [units(lon_size, units_b + units_c + extra)],
        [],
        (pieces_bc, same),
        1,
        10,
    )
    whole_bc = lax.all_to_all(sum_bc, "lon", 0, 0)
    same_x = x_swap(same)
    cross = lat_swap(same)
    cross_x = lat_swap(same_x)
    oth_bc = lat_swap(whole_bc)

    flat_rows = (2 * block_rows * 128 + norm_gain.size) // 128
    fold_scr = [((CHUNK * 8, PAIR), F32), wide_scr, tab_scr]
    flat_a, squares, bias_late = call(
        functools.partial(late_kernel, units_a),
        [((block_rows, 128), F32), ((UNIT, 128), F32), (table.shape[1:], F32)],
        [*fold_scr, units(2, lon_size, units_a + extra)],
        (spread, same, same_x, cross, cross_x),
        2,
        14,
    )
    update, bias_grad = call(
        functools.partial(last_kernel, units_b, units_c),
        [((flat_rows, 128), BF16), (table.shape, F32)],
        [
            ((block_rows + 8, 128), F32),
            *fold_scr,
            units(2, lon_size, units_b + units_c + extra),
        ],
        (spread, flat_a, squares, bias_late, whole_bc, oth_bc),
        2,
        14,
    )
    bias_grad = jnp.swapaxes(bias_grad, 1, 2)
    return (tokens_grad, update.reshape(-1), bias_grad)


def solution(mesh):
    return jax.shard_map(
        shards,
        mesh=mesh,
        in_specs=(
            P("grp", "lat", "lon", None),
            P("grp", "lat", "lon", None),
            P(),
            P(),
            P(),
            P(),
            P(),
            P(None, "lat", None, None),
        ),
        out_specs=(P("grp", "lat", "lon", None), P("grp"), P("grp", "lat", None, None)),
        check_vma=False,
    )
```

```python
import functools

import jax
import jax.numpy as jnp
import numpy as np
from jax import lax
from jax.experimental import pallas as pl
from jax.experimental.pallas import tpu as pltpu
from jax.sharding import PartitionSpec as P

WLAT = 12
WLON = 6
PAD = 5
LEVELS = 2
HEADS = 6
CHUNK = LEVELS * WLAT
WIN = CHUNK * WLON
SHIFTS = 2 * WLON - 1
PAIR = WLAT * SHIFTS
WIDE = 384

EPS = 1e-05
NEGATIVE = -1000000000.0
ROOT_HALF = 0.7071067811865476
INV_ROOT_TAU = 0.3989422804014327

F32 = jnp.float32
BF16 = jnp.bfloat16
UNIT = 8
BIAS_UNITS = (2 * HEADS + 1) * CHUNK // UNIT
MIB = 1024 * 1024


def dot(a, b):
    return lax.dot_general(a, b, (((1,), (0,)), ((), ())), preferred_element_type=F32)


def dot_nt(a, b):
    return lax.dot_general(a, b, (((1,), (1,)), ((), ())), preferred_element_type=F32)


def dot_tn(a, b):
    return lax.dot_general(a, b, (((0,), (0,)), ((), ())), preferred_element_type=F32)


def row_mean(v):
    return jnp.sum(v, axis=-1, keepdims=True) * (1.0 / v.shape[-1])


def standardize(x):
    centred = x - row_mean(x)
    inv = lax.rsqrt(row_mean(centred * centred) + EPS)
    return centred * inv, inv


def norm_back(d, gain, stand, inv):
    scaled = d * gain
    first = row_mean(scaled)
    second = row_mean(scaled * stand)
    gain_grad = jnp.sum(d * stand, axis=0, keepdims=True)
    return inv * (scaled - first - stand * second), gain_grad


def gelu_value(hidden):
    return 0.5 * hidden * (1.0 + lax.erf(hidden * ROOT_HALF))


def gelu_parts(hidden):
    half = 0.5 * (1.0 + lax.erf(hidden * ROOT_HALF))
    slope = half + hidden * jnp.exp(-0.5 * hidden * hidden) * INV_ROOT_TAU
    return hidden * half, slope


def split3(v):
    hi = v.astype(BF16)
    rest = v - hi.astype(F32)
    mid = rest.astype(BF16)
    low = (rest - mid.astype(F32)).astype(BF16)
    return hi, mid, low


def spread_matrices():
    out = np.zeros((LEVELS, PAIR, WIDE), np.float32)
    for zj in range(LEVELS):
        for aj in range(WLAT):
            for d in range(SHIFTS):
                out[zj, aj * SHIFTS + d, (SHIFTS - 1 - d) * CHUNK + zj * WLAT + aj] = 1.0
    return out


def put(scr, rows, value):
    width = value.shape[1]
    for tile in range(-(-width // 128)):
        lanes = min(128, width - tile * 128)
        scr[tile, rows, 0:lanes] = value[:, tile * 128 : tile * 128 + lanes]


def get(scr, rows, width):
    parts = [scr[tile, rows, :] for tile in range(-(-width // 128))]
    return jnp.concatenate(parts, axis=1)[:, 0:width]


def head_masks(width, dtype):
    lane = lax.broadcasted_iota(jnp.int32, (1, width), 1)
    size = width // HEADS
    return [((lane >= h * size) & (lane < (h + 1) * size)).astype(dtype) for h in range(HEADS)]


def lat_inside(n):
    return lax.rem(n, WLAT)


def lat_row(row_iota, lat, shifted, lat_total):
    row = lat * WLAT + lat_inside(row_iota)
    if shifted:
        row = row + WLAT // 2
        row = jnp.where(row >= lat_total, row - lat_total, row)
    return row


def expand_bias(table, spread, tab_scr, rows_scr, wide_scr, bias_scr, lat, shifted, lat_total):
    for h in range(HEADS):
        tab_scr[h : h + 1, :] = table[h]
    for zi in range(LEVELS):
        for zj in range(LEVELS):
            for ai in range(WLAT):
                at = ((zi * LEVELS + zj) * WLAT + ai) * PAIR
                row = zj * CHUNK * 8 + (zi * WLAT + ai) * 8
                rows_scr[row : row + HEADS, 0:PAIR] = tab_scr[0:HEADS, at : at + PAIR]
    count = CHUNK * 8
    total = jnp.zeros((count, WIDE), F32)
    for zj in range(LEVELS):
        parts = split3(rows_scr[zj * count : (zj + 1) * count, 0:PAIR])
        for part in parts:
            total = total + dot(part, spread[zj])
    put(wide_scr, slice(None), total)
    i = lax.broadcasted_iota(jnp.int32, (CHUNK, WIN), 0)
    j = lax.broadcasted_iota(jnp.int32, (CHUNK, WIN), 1)
    allowed = lat_row(j, lat, shifted, lat_total) < lat_total - PAD
    if shifted:
        last = lat_total - WLAT // 2
        region_i = (lat * WLAT + lat_inside(i)) >= last
        region_j = (lat * WLAT + lat_inside(j)) >= last
        allowed = allowed & (region_i == region_j)
    for h in range(HEADS):
        wide = get(wide_scr, pl.ds(h, CHUNK, stride=8), WIDE)
        for oi in range(WLON):
            back = (WLON - 1 - oi) * CHUNK
            moved = wide if back == 0 else pltpu.roll(wide, WIDE - back, axis=1)
            at = h * WIN + oi * CHUNK
            bias_scr[at : at + CHUNK, :] = jnp.where(allowed, moved[:, 0:WIN], NEGATIVE)


def fold_bias(sums, put_unit):
    rest = jnp.zeros((CHUNK, 128), F32)

    def emit(at, value):
        for r in range(CHUNK // UNIT):
            put_unit(at * (CHUNK // UNIT) + r, value[r * UNIT : (r + 1) * UNIT, :].astype(BF16))

    for h in range(HEADS):
        total = jnp.zeros((CHUNK, WIDE), F32)
        for oi in range(WLON):
            back = (WLON - 1 - oi) * CHUNK
            at = h * WIN + oi * CHUNK
            part = sums[at : at + CHUNK, :]
            total = total + (part if back == 0 else pltpu.roll(part, back, axis=1))
        emit(h, total[:, 0:128])
        emit(HEADS + h, total[:, 128:256])
        last = total[:, 256:384]
        rest = rest + (last if h == 0 else pltpu.roll(last, 8 * h, axis=1))
    emit(2 * HEADS, rest)

def stack_heads(v, masks):
    return jnp.concatenate([v * mask for mask in masks], axis=0)


def pick_heads(v, masks):
    total = v[0:WIN] * masks[0]
    for h in range(1, HEADS):
        total = total + v[h * WIN : (h + 1) * WIN] * masks[h]
    return total


def attend(qkv, bias, mixed, probs, stack_scr, width, finish=None):
    masks = head_masks(width, BF16)
    masks32 = head_masks(width, F32)
    scale = (width // HEADS) ** -0.5

    def window(w, carry):
        rows = pl.ds(pl.multiple_of(w * WIN, 16), WIN)
        q = qkv[rows, 0:width]
        k = qkv[rows, width : 2 * width]
        v = qkv[rows, 2 * width : 3 * width]
        scores = dot_nt(stack_heads(q, masks), k)
        for h in range(HEADS):
            part = slice(h * WIN, (h + 1) * WIN)
            logits = scores[part] * scale + bias[part, :]
            weights = jnp.exp(logits - jnp.max(logits, axis=-1, keepdims=True))
            p = weights * (1.0 / jnp.sum(weights, axis=-1, keepdims=True))
            probs[w, h] = p
            stack_scr[part, :] = p.astype(BF16)
        mixed[rows, :] = pick_heads(dot(stack_scr[...], v), masks32).astype(BF16)
        if finish is not None:
            finish(w)
        return carry

    lax.fori_loop(0, probs.shape[0], window, 0, unroll=True)


def attend_back(qkv, probs, dmix, field, sums, low_scr, prob_scr, width, first=0, begin=None):
    masks = head_masks(width, BF16)
    masks32 = head_masks(width, F32)
    scale = (width // HEADS) ** -0.5

    def window(w, carry):
        rows = pl.ds(pl.multiple_of(w * WIN, 16), WIN)
        q = qkv[rows, 0:width]
        k = qkv[rows, width : 2 * width]
        v = qkv[rows, 2 * width : 3 * width]
        up = stack_heads(dmix[rows, :], masks)
        prob_grad = dot_nt(up, v)
        if begin is not None:
            begin(w)
        for h in range(HEADS):
            part = slice(h * WIN, (h + 1) * WIN)
            p = probs[w - first, h]
            weighted = p * prob_grad[part]
            ds = weighted - p * jnp.sum(weighted, axis=-1, keepdims=True)
            sums[part, 0:WIN] += ds
            low_scr[part, :] = ds.astype(BF16)
            prob_scr[part, :] = p.astype(BF16)
        low = low_scr[...]
        dq = pick_heads(dot(low, k), masks32)
        dk = dot_tn(low, stack_heads(q, masks))
        dv = dot_tn(prob_scr[...], up)
        field[rows, 0:width] = (dq * scale).astype(BF16)
        field[rows, width : 2 * width] = (dk * scale).astype(BF16)
        field[rows, 2 * width : 3 * width] = dv.astype(BF16)
        return carry

    lax.fori_loop(first, first + probs.shape[0], window, 0, unroll=True)


def lon_major(src, scr):
    levels, lats, lons, width = src.shape
    for z in range(levels):
        for a in range(lats):
            at = (z * lats + a) * lons
            put(scr, slice(at, at + lons), src[z, a].astype(F32))


def lon_column(scr, lon, lons, width):
    return get(scr, pl.ds(lon, CHUNK, stride=lons), width)


def flat_store(dst, at, mat, cols):
    rows = mat.shape[1]
    if cols % 128 == 0:
        per = cols // 128
        for c in range(per):
            dst[pl.ds(at + c, rows, stride=per), :] = mat[c]
        return rows * per
    per = 2 * cols // 128
    half = cols // 128
    even = get(mat, pl.ds(0, rows // 2, stride=2), cols)
    odd = get(mat, pl.ds(1, rows // 2, stride=2), cols)
    for c in range(half):
        dst[pl.ds(at + c, rows // 2, stride=per), :] = even[:, c * 128 : (c + 1) * 128]
    dst[pl.ds(at + half, rows // 2, stride=per), :] = jnp.concatenate(
        [even[:, half * 128 : half * 128 + 64], odd[:, 0:64]], axis=1
    )
    for c in range(half):
        dst[pl.ds(at + half + 1 + c, rows // 2, stride=per), :] = odd[
            :, 64 + c * 128 : 64 + (c + 1) * 128
        ]
    return rows * cols // 128


def send_units(scr, base, out):
    lons, units = out.shape[:2]
    for j in range(lons):
        for u in range(units):
            at = base + (j * units + u) * UNIT
            if not isinstance(at, int):
                at = pl.multiple_of(at, UNIT)
            out[j, u] = scr[pl.ds(at, UNIT), :].astype(BF16)


def halves(scr, lat, keep, give):
    half = keep.shape[0] * keep.shape[1] * UNIT
    send_units(scr, lat * half, keep)
    send_units(scr, (1 - lat) * half, give)


def bias_units(sums, out):
    lons, per = out.shape[:2]

    def put_unit(k, value):
        out[k // per, k % per] = value

    fold_bias(sums, put_unit)
    for k in range(BIAS_UNITS, lons * per):
        put_unit(k, jnp.zeros((UNIT, 128), BF16))

def forward_core(x, b, refs, qkv_scr, bias_scr, mixed, probs, stack_scr, finish=None):
    qkv_w, proj_w, gains = refs
    width = x.shape[-1]
    stand, inv = standardize(x)
    normed = (stand * gains[b, 0:1, :]).astype(BF16)
    qkv_scr[...] = dot(normed, qkv_w[b]).astype(BF16)
    attend(qkv_scr, bias_scr, mixed, probs, stack_scr, width, finish)
    att = dot(mixed[...], proj_w[b]).astype(BF16)
    resid = (x + att.astype(F32)).astype(BF16).astype(F32)
    return resid, normed


def first_kernel(
    lat_total, tokens_in, cot_in, table_in, spread_in, qkv_in, proj_in, up_in, down_in, gains_in,
    x_out, tail_out, head_out, qkv_out, mixed_out, probs_out, resid_out, hidden_out, active_out,
    scr, cot_scr, tab_scr, rows_scr, wide_scr, bias_scr,
    cot, table, spread, tokens, qkv_w, gains, proj_w, up_w, down_w, stack_scr, probs, sems, out_sems,
):
    copies = []
    for source, target in (
        (cot_in, cot),
        (table_in.at[0:1], table),
        (spread_in, spread),
        (tokens_in, tokens),
        (qkv_in.at[0:1], qkv_w),
        (gains_in, gains),
        (proj_in.at[0:1], proj_w),
        (up_in.at[0:1], up_w),
        (down_in.at[0:1], down_w),
    ):
        copies.append(pltpu.make_async_copy(source, target, sems.at[len(copies)]))
    for copy in copies:
        copy.start()
    lat = lax.axis_index("lat")
    width = tokens.shape[-1]
    lons = tokens.shape[2]
    cut = CHUNK * (WLON // 2)
    copies[0].wait()
    lon_major(cot, cot_scr)
    g = jnp.concatenate([lon_column(cot_scr, lon, lons, width) for lon in range(lons)], axis=0)
    head_out[1] = g[0:cut, :].astype(BF16)
    tail_out[1] = g[cut:, :].astype(BF16)
    copies[1].wait()
    copies[2].wait()
    expand_bias(
        table.at[0], spread, tab_scr, rows_scr, wide_scr, bias_scr, lat, False, lat_total
    )
    copies[3].wait()
    lon_major(tokens, scr)
    x = jnp.concatenate([lon_column(scr, lon, lons, width) for lon in range(lons)], axis=0)
    x_out[...] = x.astype(BF16)
    for copy in copies[4:]:
        copy.wait()

    def probs_copy(w):
        return pltpu.make_async_copy(probs.at[w], probs_out.at[w], out_sems.at[w])

    resid, _ = forward_core(
        x, 0, (qkv_w, proj_w, gains), qkv_out, bias_scr, mixed_out, probs, stack_scr,
        lambda w: probs_copy(w).start(),
    )
    resid_out[...] = resid.astype(BF16)
    stand, _ = standardize(resid)
    normed = (stand * gains[0, 1:2, :]).astype(BF16)
    hidden = dot(normed, up_w[0])
    hidden_out[...] = hidden
    active = gelu_value(hidden).astype(BF16)
    active_out[...] = active
    result = resid + dot_nt(active, down_w[0])
    head_out[0] = result[0:cut, :].astype(BF16)
    tail_out[0] = result[cut:, :].astype(BF16)
    for w in range(probs.shape[0]):
        probs_copy(w).wait()


def bias_kernel(
    lat_total, table, spread, hidden, bias_out, slope_out, tab_scr, rows_scr, wide_scr
):
    lat = lax.axis_index("lat")
    expand_bias(
        table.at[1], spread, tab_scr, rows_scr, wide_scr, bias_out, lat, True, lat_total
    )
    slope_out[...] = gelu_parts(hidden[...])[1].astype(BF16)


def merge_ahead(scr_own, scr_oth, rows):
    half = WLAT // 2
    n = lax.broadcasted_iota(jnp.int32, (rows, 1), 0)
    return jnp.where(
        lat_inside(n) < half,
        pltpu.roll(scr_own[...], rows - half, axis=0),
        pltpu.roll(scr_oth[...], half, axis=0),
    )


def merge_behind(scr_own, scr_oth, rows):
    half = WLAT // 2
    n = lax.broadcasted_iota(jnp.int32, (rows, 1), 0)
    return jnp.where(
        lat_inside(n) >= half,
        pltpu.roll(scr_own[...], half, axis=0),
        pltpu.roll(scr_oth[...], rows - half, axis=0),
    )


def second_kernel(
    lat_total,
    tail, lon_head, lat_tail, diag_head, bias, qkv_w, proj_w, up_w, down_w, gains,
    head_out, tail_out, n1_out, field_out, mixed_out, low_out, n2_out, hg_out, active_out, g_out,
    sums_out, gain_out,
    scr_own, scr_oth, qkv_scr, probs_scr, dmix_scr, low_scr, prob_scr,
):
    lat = lax.axis_index("lat")
    rows, width = scr_own.shape
    cut = CHUNK * (WLON // 2)

    def rolled(which):
        scr_own[0 : rows - cut, :] = tail[which].astype(F32)
        scr_own[rows - cut :, :] = lon_head[which].astype(F32)
        scr_oth[0 : rows - cut, :] = lat_tail[which].astype(F32)
        scr_oth[rows - cut :, :] = diag_head[which].astype(F32)
        return merge_ahead(scr_own, scr_oth, rows)

    g = rolled(1)
    n = lax.broadcasted_iota(jnp.int32, (rows, 1), 0)
    keep = lat_row(n, lat, True, lat_total) < lat_total - PAD
    g = jnp.where(keep, g, 0.0)
    g_out[...] = g.astype(BF16)

    x = rolled(0)

    resid, normed = forward_core(
        x, 1, (qkv_w, proj_w, gains), qkv_scr, bias, mixed_out, probs_scr, low_scr
    )
    n1_out[...] = normed
    stand2, inv2 = standardize(resid)
    normed2 = (stand2 * gains[1, 1:2, :]).astype(BF16)
    n2_out[...] = normed2
    active, slope = gelu_parts(dot(normed2, up_w[1]))
    active_out[...] = active.astype(BF16)

    hg = (dot(g_out[...], down_w[1]) * slope).astype(BF16)
    hg_out[...] = hg
    part, gain_two = norm_back(dot_nt(hg, up_w[1]), gains[1, 1:2, :], stand2, inv2)
    rg = g + part
    low = rg.astype(BF16)
    low_out[...] = low
    dmix_scr[...] = dot_nt(low, proj_w[1]).astype(BF16)
    sums_out[...] = jnp.zeros(sums_out.shape, F32)
    attend_back(
        qkv_scr, probs_scr, dmix_scr, field_out, sums_out, low_scr, prob_scr, width
    )
    ng = dot_nt(field_out[...], qkv_w[1]).astype(BF16).astype(F32)
    stand1, inv1 = standardize(x)
    part, gain_one = norm_back(ng, gains[1, 0:1, :], stand1, inv1)
    dx = rg + part
    head_out[...] = dx[0 : rows - cut, :].astype(BF16)
    tail_out[...] = dx[rows - cut :, :].astype(BF16)
    gain_out[0:1, :] = gain_one
    gain_out[1:2, :] = gain_two


def outer_kernel(
    n1, field, mixed, low, n2, hg, active, g, sums,
    keep, give, bias_out,
    m576, m192, m768, mdown, flat_scr,
):
    put(m576, slice(None), dot_tn(n1[...], field[...]))
    at = flat_store(flat_scr, 0, m576, field.shape[1])
    put(m192, slice(None), dot_tn(mixed[...], low[...]))
    at += flat_store(flat_scr, at, m192, mixed.shape[1])
    put(m768, slice(None), dot_tn(n2[...], hg[...]))
    at += flat_store(flat_scr, at, m768, active.shape[1])
    put(mdown, slice(None), dot_tn(active[...], g[...]))
    at += flat_store(flat_scr, at, mdown, mixed.shape[1])
    halves(flat_scr, lax.axis_index("lat"), keep, give)
    bias_units(sums, bias_out)


def lat_sums(*refs):
    out = refs[-1]
    at = 0
    for k in range(0, len(refs) - 2, 2):
        keep, got = refs[k], refs[k + 1]
        count = keep.shape[1]
        out[:, at : at + count] = (keep[...].astype(F32) + got[...].astype(F32)).astype(BF16)
        at += count
    out[:, at:] = refs[-2][...]


def lat_sums_split(*refs):
    keep_out, give_out = refs[-2:]
    x = lax.rem(lax.axis_index("lon"), 2)
    for out, side in ((keep_out, x), (give_out, 1 - x)):
        for z in range(out.shape[0]):
            j = 2 * z + side
            at = 0
            for k in range(0, len(refs) - 3, 2):
                keep, got = refs[k], refs[k + 1]
                count = keep.shape[1]
                total = keep[j].astype(F32) + got[j].astype(F32)
                out[z, at : at + count] = total.astype(BF16)
                at += count
            out[z, at:] = refs[-3][j]


def add_pair(keep, got, out):
    out[...] = (keep[...].astype(F32) + got[...].astype(F32)).astype(BF16)


def sum_pieces(pieces, order, out):
    total = pieces[0].astype(F32)
    for k in range(1, pieces.shape[0]):
        total = total + pieces[k].astype(F32)
    total = total.astype(BF16)
    if len(out.shape) == len(pieces.shape):
        for k in range(out.shape[0]):
            out[k] = total
    else:
        out[...] = total


def join_z(*refs):
    out = refs[-1]
    count = out.shape[0]
    z = lax.div(lax.axis_index("lon"), 2)
    for k in range(count):
        out[lax.rem(z + count - k, count)] = refs[k][...]


def third_kernel(
    head, lon_tail, lat_head, diag_tail, resid_in, slope, active, mixed,
    proj_w, up_w, down_w, gains, probs_in, order,
    keep_out, give_out, rg_out, dmix_out, gain_out, probs_out,
    scr_own, scr_oth, m192, m768, mdown, flat_scr, sem,
):
    copy = pltpu.make_async_copy(probs_in.at[0 : probs_out.shape[0]], probs_out, sem)
    copy.start()
    rows, width = scr_own.shape
    cut = CHUNK * (WLON // 2)
    scr_own[0:cut, :] = lon_tail[...].astype(F32)
    scr_own[cut:, :] = head[...].astype(F32)
    scr_oth[0:cut, :] = diag_tail[...].astype(F32)
    scr_oth[cut:, :] = lat_head[...].astype(F32)
    g = merge_behind(scr_own, scr_oth, rows)
    g_low = g.astype(BF16)
    stand2, inv2 = standardize(resid_in[...].astype(F32))
    normed2 = (stand2 * gains[0, 1:2, :]).astype(BF16)
    hg = dot(g_low, down_w[0])
    hg = (hg * slope[...].astype(F32)).astype(BF16)
    part, gain_two = norm_back(dot_nt(hg, up_w[0]), gains[0, 1:2, :], stand2, inv2)
    rg = g + part
    rg_out[...] = rg
    low = rg.astype(BF16)
    dmix_out[...] = dot_nt(low, proj_w[0]).astype(BF16)
    gain_out[...] = gain_two
    put(m192, slice(None), dot_tn(mixed[...], low))
    at = flat_store(flat_scr, 0, m192, mixed.shape[1])
    put(m768, slice(None), dot_tn(normed2, hg))
    at += flat_store(flat_scr, at, m768, active.shape[1])
    put(mdown, slice(None), dot_tn(active[...], g_low))
    at += flat_store(flat_scr, at, mdown, mixed.shape[1])
    flat_scr[at:, :] = jnp.zeros((flat_scr.shape[0] - at, 128), F32)
    halves(flat_scr, lax.axis_index("lat"), keep_out, give_out)
    copy.wait()


def gain_rows(one, two):
    return jnp.concatenate(
        [
            one[:, 0:128],
            jnp.concatenate([one[:, 128:192], two[:, 0:64]], axis=1),
            two[:, 64:192],
        ],
        axis=0,
    )


def fourth_kernel(
    x_in, qkv, probs_near, probs_in, dmix, rg, gain_two, gains_late, qkv_w, gains,
    tokens_out, keep, give, bias_out,
    field, sums, m576, flat_scr, dx_scr, low_scr, prob_scr, probs, sems,
):
    near = probs_near.shape[0]

    def probs_copy(w):
        return pltpu.make_async_copy(probs_in.at[w], probs.at[w - near], sems.at[w - near])

    for w in range(near, probs_in.shape[0]):
        probs_copy(w).start()
    width = x_in.shape[-1]
    levels, lats, lons = tokens_out.shape[:3]
    sums[...] = jnp.zeros(sums.shape, F32)
    attend_back(qkv, probs_near, dmix, field, sums, low_scr, prob_scr, width)
    attend_back(
        qkv, probs, dmix, field, sums, low_scr, prob_scr, width, near,
        lambda w: probs_copy(w).wait(),
    )
    stand1, inv1 = standardize(x_in[...].astype(F32))
    normed = (stand1 * gains[0, 0:1, :]).astype(BF16)
    ng = dot_nt(field[...], qkv_w[0]).astype(BF16).astype(F32)
    part, gain_one = norm_back(ng, gains[0, 0:1, :], stand1, inv1)
    put(m576, slice(None), dot_tn(normed, field[...]))
    at = flat_store(flat_scr, 0, m576, field.shape[1])
    flat_scr[at:, :] = jnp.zeros((flat_scr.shape[0] - at, 128), F32)
    flat_scr[at : at + 3, :] = gain_rows(gain_one, gain_two[...])
    flat_scr[at + 3 : at + 6, :] = gain_rows(gains_late[0:1, :], gains_late[1:2, :])
    bias_units(sums, bias_out)
    halves(flat_scr, lax.axis_index("lat"), keep, give)
    put(dx_scr, slice(None), rg[...] + part)
    for z in range(levels):
        for a in range(lats):
            tokens_out[z, a] = get(
                dx_scr, pl.ds(z * lats + a, lons, stride=CHUNK), width
            ).astype(BF16)


def place(pieces, first, last, dests, scr):
    total = jnp.zeros((UNIT, 128), F32)
    lons = pieces.shape[1]
    per = last - first
    k = 0
    for where, room in dests:
        for at in range(where, where + room, UNIT):
            half, j, u = k // (per * lons), k // per % lons, k % per
            value = pieces[half, j, first + u].astype(F32)
            scr[at : at + UNIT, :] = value
            total = total + value * value
            k += 1
    return total


def bias_rows(piece, base, spread, out, rows_scr, wide_scr, tab_scr):
    lat = lax.axis_index("lat")
    extra = -(-BIAS_UNITS // piece.shape[1])

    def read(at):
        parts = []
        for r in range(CHUNK // UNIT):
            k = at * (CHUNK // UNIT) + r
            parts.append(piece[lat, k // extra, base + k % extra].astype(F32))
        return jnp.concatenate(parts, axis=0)

    rest = read(2 * HEADS)
    for h in range(HEADS):
        rows = pl.ds(h, CHUNK, stride=8)
        wide_scr[0, rows, :] = read(h)
        wide_scr[1, rows, :] = read(HEADS + h)
        wide_scr[2, rows, :] = rest if h == 0 else pltpu.roll(rest, 128 - 8 * h, axis=1)
    low = get(wide_scr, slice(None), WIDE).astype(BF16)
    for zj in range(LEVELS):
        rows_scr[...] = dot_nt(low, spread[zj])
        for zi in range(LEVELS):
            for ai in range(WLAT):
                at = ((zi * LEVELS + zj) * WLAT + ai) * PAIR
                row = (zi * WLAT + ai) * 8
                tab_scr[0:HEADS, at : at + PAIR] = rows_scr[row : row + HEADS, 0:PAIR]
    for h in range(HEADS):
        out[h] = tab_scr[h : h + 1, :]


def late_kernel(
    units_a, spread, same, same_x, cross, cross_x, flat_out, squares_out, bias_out,
    rows_scr, wide_scr, tab_scr, a,
):
    lat = lax.axis_index("lat")
    x = lax.rem(lax.axis_index("lon"), 2)
    for z in range(same.shape[0]):
        a[lat, 2 * z + x] = same[z]
        a[lat, 2 * z + 1 - x] = same_x[z]
        a[1 - lat, 2 * z + x] = cross[z]
        a[1 - lat, 2 * z + 1 - x] = cross_x[z]
    squares_out[...] = place(a, 0, units_a, [(0, flat_out.shape[0])], flat_out)
    bias_rows(a, units_a, spread, bias_out, rows_scr, wide_scr, tab_scr)


def last_kernel(
    units_b, units_c, spread, flat_a, squares, bias_late, own_bc, oth_bc, update_out, bias_out,
    scr, rows_scr, wide_scr, tab_scr, bc,
):
    lat = lax.axis_index("lat")
    for j in range(own_bc.shape[0]):
        bc[lat, j] = own_bc[j]
        bc[1 - lat, j] = oth_bc[j]
    total = squares[...]
    total = total + place(bc, 0, units_b, [(864, 288), (1152, 1152), (2304, 1152)], scr)
    total = total + place(bc, units_b, units_b + units_c, [(0, 864), (3456, 8)], scr)
    count = update_out.shape[0]
    mean = jnp.sum(total) * (1.0 / (count * 128))
    scale = lax.rsqrt(mean + 1e-06)
    early, late = (0, 1728, 2304, 4608), (864, 2016, 3456, 5760)
    at = 0
    for first, second, rows in zip(early, late, (864, 288, 1152, 1152)):
        update_out[first : first + rows, :] = (scr[at : at + rows, :] * scale).astype(BF16)
        update_out[second : second + rows, :] = (flat_a[at : at + rows, :] * scale).astype(BF16)
        at += rows
    update_out[6912:count, :] = (scr[at : at + count - 6912, :] * scale).astype(BF16)
    bias_rows(bc, units_b + units_c, spread, bias_out.at[0], rows_scr, wide_scr, tab_scr)
    bias_out[1] = bias_late[...]


def call(kernel, outs, scratch, args, micros, mib, spaces=None, far=(), near=()):
    spaces = spaces or [pltpu.VMEM] * len(args)
    return pl.pallas_call(
        kernel,
        out_shape=[
            pltpu.HBM(*entry)
            if at in far
            else (pltpu.VMEM if at in near else jax.ShapeDtypeStruct)(*entry)
            for at, entry in enumerate(outs)
        ],
        in_specs=[pl.BlockSpec(memory_space=space) for space in spaces],
        out_specs=[
            pl.BlockSpec(memory_space=pltpu.HBM if at in far else pltpu.VMEM)
            for at in range(len(outs))
        ],
        scratch_shapes=[
            pltpu.VMEM(*entry) if isinstance(entry, tuple) else entry for entry in scratch
        ],
        compiler_params=pltpu.CompilerParams(vmem_limit_bytes=mib * MIB),
        cost_estimate=pl.CostEstimate(
            flops=int(micros * 1.1e9), bytes_accessed=10**5, transcendentals=0
        ),
    )(*args)


def lat_swap(value):
    return lax.ppermute(value, "lat", [(0, 1), (1, 0)])


def lon_send(value, step):
    count = lax.axis_size("lon")
    return lax.ppermute(value, "lon", [(s, (s + step) % count) for s in range(count)])


def x_swap(value):
    count = lax.axis_size("lon")
    return lax.ppermute(value, "lon", [(s, s ^ 1) for s in range(count)])


def diag_send(value, step):
    count = lax.axis_size("lon")
    pairs = []
    for s in range(count):
        for t in range(2):
            pairs.append((2 * s + t, 2 * ((s + step) % count) + 1 - t))
    return lax.ppermute(value, ("lon", "lat"), pairs)


def shards(
    tokens, cotangent, qkv_weight, proj_weight, up_weight, down_weight, norm_gain, bias_table
):
    levels, lats, lons, width = tokens.shape
    rows = levels * lats * lons
    wins = rows // WIN
    hid = up_weight.shape[-1]
    heads = bias_table.shape[2]
    lon_size = lax.axis_size("lon")
    zs = lon_size // 2
    lat_total = lats * lax.axis_size("lat")
    cut = CHUNK * (WLON // 2)
    spread = jnp.asarray(spread_matrices(), BF16)
    down_turned = jnp.swapaxes(down_weight, 1, 2)
    table = jnp.swapaxes(bias_table, 1, 2)
    token = (rows, width)
    field_shape = ((rows, 3 * width), BF16)
    probs_shape = ((wins, heads, WIN, WIN), F32)
    stack_shape = ((heads * WIN, WIN), BF16)
    bias_shape = ((heads * WIN, WIN), F32)
    sums_shape = ((heads * WIN, WIDE), F32)
    tab_scr = ((8, table.shape[-1]), F32)
    rows_scr = ((LEVELS * CHUNK * 8, PAIR), F32)
    wide_scr = ((WIDE // 128, CHUNK * 8, 128), F32)
    tiles = -(-width // 128)
    token_scr = ((tiles, rows, 128), F32)
    m576 = ((-(-3 * width // 128), width, 128), F32)
    m192 = ((tiles, width, 128), F32)
    m768 = ((hid // 128, width, 128), F32)
    mdown = ((tiles, hid, 128), F32)

    block_rows = (qkv_weight[0].size + proj_weight[0].size + 2 * up_weight[0].size) // 128
    qkv_rows = qkv_weight[0].size // 128
    counts = (block_rows, block_rows - qkv_rows, qkv_rows + 8)
    units_a, units_b, units_c = [-(-count // (2 * lon_size * UNIT)) for count in counts]
    extra = -(-BIAS_UNITS // lon_size)

    def units(*lead):
        return (lead + (UNIT, 128), BF16)

    def flat_scr(per):
        return ((2 * lon_size * per * UNIT, 128), F32)

    x0, tail, head, qkv0, mixed0, probs0, resid0, hidden0, active0 = call(
        functools.partial(first_kernel, lat_total),
        [
            (token, BF16),
            ((2, rows - cut, width), BF16),
            ((2, cut, width), BF16),
            field_shape,
            (token, BF16),
            probs_shape,
            (token, BF16),
            ((rows, hid), F32),
            ((rows, hid), BF16),
        ],
        [
            token_scr,
            token_scr,
            tab_scr,
            rows_scr,
            wide_scr,
            bias_shape,
            (cotangent.shape, BF16),
            ((1,) + table.shape[1:], F32),
            (spread.shape, BF16),
            (tokens.shape, BF16),
            ((1,) + qkv_weight.shape[1:], BF16),
            (norm_gain.shape, F32),
            ((1,) + proj_weight.shape[1:], BF16),
            ((1,) + up_weight.shape[1:], BF16),
            ((1,) + down_turned.shape[1:], BF16),
            stack_shape,
            probs_shape,
            pltpu.SemaphoreType.DMA((9,)),
            pltpu.SemaphoreType.DMA((wins,)),
        ],
        [
            pltpu.with_memory_space_constraint(arg, pltpu.HBM)
            for arg in (
                tokens, cotangent, table, spread, qkv_weight, proj_weight, up_weight, down_turned,
                norm_gain,
            )
        ],
        8,
        16,
        [pltpu.HBM] * 9,
        (5,),
        (0, 3, 4, 6, 8),
    )
    lon_head = lon_send(head, -1)
    diag_head = diag_send(head, -1)
    lat_tail = lat_swap(tail)
    bias1, slope0 = call(
        functools.partial(bias_kernel, lat_total),
        [bias_shape, ((rows, hid), BF16)],
        [tab_scr, rows_scr, wide_scr],
        (table, spread, hidden0),
        3,
        10,
        near=(1,),
    )

    (
        dhead, dtail, n1, field1, mixed1, low1, n2, hg1, active1, g1, sums1, gains1,
    ) = call(
        functools.partial(second_kernel, lat_total),
        [
            ((rows - cut, width), BF16),
            ((cut, width), BF16),
            (token, BF16),
            field_shape,
            (token, BF16),
            (token, BF16),
            (token, BF16),
            ((rows, hid), BF16),
            ((rows, hid), BF16),
            (token, BF16),
            sums_shape,
            ((2, width), F32),
        ],
        [
            (token, F32),
            (token, F32),
            field_shape,
            probs_shape,
            (token, BF16),
            stack_shape,
            stack_shape,
        ],
        (
            tail, lon_head, lat_tail, diag_head, bias1, qkv_weight, proj_weight, up_weight,
            down_turned, norm_gain,
        ),
        19,
        16,
    )
    lon_tail = lon_send(dtail, 1)
    diag_tail = diag_send(dtail, 1)
    lat_dhead = lat_swap(dhead)

    keep_a, give_a, bias_a = call(
        outer_kernel,
        [units(lon_size, units_a), units(lon_size, units_a), units(lon_size, extra)],
        [m576, m192, m768, mdown, flat_scr(units_a)],
        (n1, field1, mixed1, low1, n2, hg1, active1, g1, sums1),
        3,
        14,
    )
    got_a = lat_swap(give_a)

    (part_a,) = call(
        lat_sums, [units(lon_size, units_a + extra)], [], (keep_a, got_a, bias_a), 1, 10
    )
    pieces_a = lax.all_to_all(part_a, "lon", 0, 0)

    near = 1
    probs_far = pltpu.with_memory_space_constraint(probs0, pltpu.HBM)
    keep_b, give_b, rg0, dmix0, gain_two, probs_near = call(
        third_kernel,
        [
            units(lon_size, units_b),
            units(lon_size, units_b),
            (token, F32),
            (token, BF16),
            ((1, width), F32),
            ((near,) + probs_shape[0][1:], F32),
        ],
        [
            (token, F32),
            (token, F32),
            m192,
            m768,
            mdown,
            flat_scr(units_b),
            pltpu.SemaphoreType.DMA,
        ],
        (
            dhead, lon_tail, lat_dhead, diag_tail, resid0, slope0, active0, mixed0, proj_weight,
            up_weight, down_turned, norm_gain, probs_far, part_a,
        ),
        3,
        14,
        [pltpu.VMEM] * 12 + [pltpu.HBM, pltpu.VMEM],
    )
    got_b = lat_swap(give_b)

    tokens_grad, keep_c, give_c, bias_c = call(
        fourth_kernel,
        [
            (tokens.shape, BF16),
            units(lon_size, units_c),
            units(lon_size, units_c),
            units(lon_size, extra),
        ],
        [
            field_shape,
            sums_shape,
            m576,
            flat_scr(units_c),
            token_scr,
            stack_shape,
            stack_shape,
            ((wins - near,) + probs_shape[0][1:], F32),
            pltpu.SemaphoreType.DMA((wins - near,)),
        ],
        (
            x0, qkv0, probs_near, probs_far, dmix0, rg0, gain_two, gains1, qkv_weight,
            norm_gain,
        ),
        8,
        14,
        [pltpu.VMEM] * 3 + [pltpu.HBM] + [pltpu.VMEM] * 6,
    )
    got_c = lat_swap(give_c)
    units_bc = units_b + units_c + extra
    keep_x, give_x = call(
        lat_sums_split,
        [units(zs, units_bc)] * 2,
        [],
        (keep_b, got_b, keep_c, got_c, bias_c),
        1,
        10,
    )
    got_x = x_swap(give_x)
    (sum_a,) = call(sum_pieces, [units(units_a + extra)], [], (pieces_a, keep_x), 1, 10)
    (part_z,) = call(add_pair, [units(zs, units_bc)], [], (keep_x, got_x), 1, 10)
    pieces_bc = lax.all_to_all(
        part_z,
        "lon",
        0,
        0,
        axis_index_groups=[[2 * z + x for z in range(zs)] for x in range(2)],
    )

    (same,) = call(
        join_z,
        [units(zs, units_a + extra)],
        [],
        [sum_a] + [lon_send(sum_a, 2 * k) for k in range(1, zs)] + [part_z],
        1,
        10,
    )
    (sum_bc,) = call(
        sum_pieces,
        [units(lon_size, units_bc)],
        [],
        (pieces_bc, same),
        1,
        10,
    )
    whole_bc = lax.all_to_all(sum_bc, "lon", 0, 0)
    same_x = x_swap(same)
    cross = lat_swap(same)
    cross_x = lat_swap(same_x)
    oth_bc = lat_swap(whole_bc)

    flat_rows = (2 * block_rows * 128 + norm_gain.size) // 128
    fold_scr = [((CHUNK * 8, PAIR), F32), wide_scr, tab_scr]
    flat_a, squares, bias_late = call(
        functools.partial(late_kernel, units_a),
        [((block_rows, 128), F32), ((UNIT, 128), F32), (table.shape[1:], F32)],
        [*fold_scr, units(2, lon_size, units_a + extra)],
        (spread, same, same_x, cross, cross_x),
        2,
        14,
    )
    update, bias_grad = call(
        functools.partial(last_kernel, units_b, units_c),
        [((flat_rows, 128), BF16), (table.shape, F32)],
        [
            ((block_rows + 8, 128), F32),
            *fold_scr,
            units(2, lon_size, units_b + units_c + extra),
        ],
        (spread, flat_a, squares, bias_late, whole_bc, oth_bc),
        2,
        14,
    )
    bias_grad = jnp.swapaxes(bias_grad, 1, 2)
    return (tokens_grad, update.reshape(-1), bias_grad)


def solution(mesh):
    return jax.shard_map(
        shards,
        mesh=mesh,
        in_specs=(
            P("grp", "lat", "lon", None),
            P("grp", "lat", "lon", None),
            P(),
            P(),
            P(),
            P(),
            P(),
            P(None, "lat", None, None),
        ),
        out_specs=(P("grp", "lat", "lon", None), P("grp"), P("grp", "lat", None, None)),
        check_vma=False,
    )
```

```python
import functools

import jax
import jax.numpy as jnp
import numpy as np
from jax import lax
from jax.experimental import pallas as pl
from jax.experimental.pallas import tpu as pltpu
from jax.sharding import PartitionSpec as P

WLAT = 12
WLON = 6
PAD = 5
LEVELS = 2
HEADS = 6
CHUNK = LEVELS * WLAT
WIN = CHUNK * WLON
SHIFTS = 2 * WLON - 1
PAIR = WLAT * SHIFTS
WIDE = 384

EPS = 1e-05
NEGATIVE = -1000000000.0
ROOT_HALF = 0.7071067811865476
INV_ROOT_TAU = 0.3989422804014327

F32 = jnp.float32
BF16 = jnp.bfloat16
UNIT = 8
BIAS_UNITS = (2 * HEADS + 1) * CHUNK // UNIT
MIB = 1024 * 1024


def dot(a, b):
    return lax.dot_general(a, b, (((1,), (0,)), ((), ())), preferred_element_type=F32)


def dot_nt(a, b):
    return lax.dot_general(a, b, (((1,), (1,)), ((), ())), preferred_element_type=F32)


def dot_tn(a, b):
    return lax.dot_general(a, b, (((0,), (0,)), ((), ())), preferred_element_type=F32)


def row_mean(v):
    return jnp.sum(v, axis=-1, keepdims=True) * (1.0 / v.shape[-1])


def standardize(x):
    centred = x - row_mean(x)
    inv = lax.rsqrt(row_mean(centred * centred) + EPS)
    return centred * inv, inv


def norm_back(d, gain, stand, inv):
    scaled = d * gain
    first = row_mean(scaled)
    second = row_mean(scaled * stand)
    gain_grad = jnp.sum(d * stand, axis=0, keepdims=True)
    return inv * (scaled - first - stand * second), gain_grad


def gelu_value(hidden):
    return 0.5 * hidden * (1.0 + lax.erf(hidden * ROOT_HALF))


def gelu_parts(hidden):
    half = 0.5 * (1.0 + lax.erf(hidden * ROOT_HALF))
    slope = half + hidden * jnp.exp(-0.5 * hidden * hidden) * INV_ROOT_TAU
    return hidden * half, slope


def split3(v):
    hi = v.astype(BF16)
    rest = v - hi.astype(F32)
    mid = rest.astype(BF16)
    low = (rest - mid.astype(F32)).astype(BF16)
    return hi, mid, low


def spread_matrices():
    out = np.zeros((LEVELS, PAIR, WIDE), np.float32)
    for zj in range(LEVELS):
        for aj in range(WLAT):
            for d in range(SHIFTS):
                out[zj, aj * SHIFTS + d, (SHIFTS - 1 - d) * CHUNK + zj * WLAT + aj] = 1.0
    return out


def put(scr, rows, value):
    width = value.shape[1]
    for tile in range(-(-width // 128)):
        lanes = min(128, width - tile * 128)
        scr[tile, rows, 0:lanes] = value[:, tile * 128 : tile * 128 + lanes]


def get(scr, rows, width):
    parts = [scr[tile, rows, :] for tile in range(-(-width // 128))]
    return jnp.concatenate(parts, axis=1)[:, 0:width]


def head_masks(width, dtype):
    lane = lax.broadcasted_iota(jnp.int32, (1, width), 1)
    size = width // HEADS
    return [((lane >= h * size) & (lane < (h + 1) * size)).astype(dtype) for h in range(HEADS)]


def lat_inside(n):
    return lax.rem(n, WLAT)


def lat_row(row_iota, lat, shifted, lat_total):
    row = lat * WLAT + lat_inside(row_iota)
    if shifted:
        row = row + WLAT // 2
        row = jnp.where(row >= lat_total, row - lat_total, row)
    return row


def expand_bias(table, spread, tab_scr, rows_scr, wide_scr, bias_scr, lat, shifted, lat_total):
    for h in range(HEADS):
        tab_scr[h : h + 1, :] = table[h]
    for zi in range(LEVELS):
        for zj in range(LEVELS):
            for ai in range(WLAT):
                at = ((zi * LEVELS + zj) * WLAT + ai) * PAIR
                row = zj * CHUNK * 8 + (zi * WLAT + ai) * 8
                rows_scr[row : row + HEADS, 0:PAIR] = tab_scr[0:HEADS, at : at + PAIR]
    count = CHUNK * 8
    total = jnp.zeros((count, WIDE), F32)
    for zj in range(LEVELS):
        parts = split3(rows_scr[zj * count : (zj + 1) * count, 0:PAIR])
        for part in parts:
            total = total + dot(part, spread[zj])
    put(wide_scr, slice(None), total)
    i = lax.broadcasted_iota(jnp.int32, (CHUNK, WIN), 0)
    j = lax.broadcasted_iota(jnp.int32, (CHUNK, WIN), 1)
    allowed = lat_row(j, lat, shifted, lat_total) < lat_total - PAD
    if shifted:
        last = lat_total - WLAT // 2
        region_i = (lat * WLAT + lat_inside(i)) >= last
        region_j = (lat * WLAT + lat_inside(j)) >= last
        allowed = allowed & (region_i == region_j)
    for h in range(HEADS):
        wide = get(wide_scr, pl.ds(h, CHUNK, stride=8), WIDE)
        for oi in range(WLON):
            back = (WLON - 1 - oi) * CHUNK
            moved = wide if back == 0 else pltpu.roll(wide, WIDE - back, axis=1)
            at = h * WIN + oi * CHUNK
            bias_scr[at : at + CHUNK, :] = jnp.where(allowed, moved[:, 0:WIN], NEGATIVE)


def fold_bias(sums, put_unit):
    rest = jnp.zeros((CHUNK, 128), F32)

    def emit(at, value):
        for r in range(CHUNK // UNIT):
            put_unit(at * (CHUNK // UNIT) + r, value[r * UNIT : (r + 1) * UNIT, :].astype(BF16))

    for h in range(HEADS):
        total = jnp.zeros((CHUNK, WIDE), F32)
        for oi in range(WLON):
            back = (WLON - 1 - oi) * CHUNK
            at = h * WIN + oi * CHUNK
            part = sums[at : at + CHUNK, :]
            total = total + (part if back == 0 else pltpu.roll(part, back, axis=1))
        emit(h, total[:, 0:128])
        emit(HEADS + h, total[:, 128:256])
        last = total[:, 256:384]
        rest = rest + (last if h == 0 else pltpu.roll(last, 8 * h, axis=1))
    emit(2 * HEADS, rest)

def stack_heads(v, masks):
    return jnp.concatenate([v * mask for mask in masks], axis=0)


def pick_heads(v, masks):
    total = v[0:WIN] * masks[0]
    for h in range(1, HEADS):
        total = total + v[h * WIN : (h + 1) * WIN] * masks[h]
    return total


def attend(qkv, bias, mixed, probs, stack_scr, width, finish=None):
    masks = head_masks(width, BF16)
    masks32 = head_masks(width, F32)
    scale = (width // HEADS) ** -0.5

    def window(w, carry):
        rows = pl.ds(pl.multiple_of(w * WIN, 16), WIN)
        q = qkv[rows, 0:width]
        k = qkv[rows, width : 2 * width]
        v = qkv[rows, 2 * width : 3 * width]
        scores = dot_nt(stack_heads(q, masks), k)
        for h in range(HEADS):
            part = slice(h * WIN, (h + 1) * WIN)
            logits = scores[part] * scale + bias[part, :]
            weights = jnp.exp(logits - jnp.max(logits, axis=-1, keepdims=True))
            p = weights * (1.0 / jnp.sum(weights, axis=-1, keepdims=True))
            probs[w, h] = p
            stack_scr[part, :] = p.astype(BF16)
        mixed[rows, :] = pick_heads(dot(stack_scr[...], v), masks32).astype(BF16)
        if finish is not None:
            finish(w)
        return carry

    lax.fori_loop(0, probs.shape[0], window, 0, unroll=True)


def attend_back(qkv, probs, dmix, field, sums, low_scr, prob_scr, width, first=0, begin=None):
    masks = head_masks(width, BF16)
    masks32 = head_masks(width, F32)
    scale = (width // HEADS) ** -0.5

    def window(w, carry):
        rows = pl.ds(pl.multiple_of(w * WIN, 16), WIN)
        q = qkv[rows, 0:width]
        k = qkv[rows, width : 2 * width]
        v = qkv[rows, 2 * width : 3 * width]
        up = stack_heads(dmix[rows, :], masks)
        prob_grad = dot_nt(up, v)
        if begin is not None:
            begin(w)
        for h in range(HEADS):
            part = slice(h * WIN, (h + 1) * WIN)
            p = probs[w - first, h]
            weighted = p * prob_grad[part]
            ds = weighted - p * jnp.sum(weighted, axis=-1, keepdims=True)
            sums[part, 0:WIN] += ds
            low_scr[part, :] = ds.astype(BF16)
            prob_scr[part, :] = p.astype(BF16)
        low = low_scr[...]
        dq = pick_heads(dot(low, k), masks32)
        dk = dot_tn(low, stack_heads(q, masks))
        dv = dot_tn(prob_scr[...], up)
        field[rows, 0:width] = (dq * scale).astype(BF16)
        field[rows, width : 2 * width] = (dk * scale).astype(BF16)
        field[rows, 2 * width : 3 * width] = dv.astype(BF16)
        return carry

    lax.fori_loop(first, first + probs.shape[0], window, 0, unroll=True)


def lon_major(src, scr):
    levels, lats, lons, width = src.shape
    for z in range(levels):
        for a in range(lats):
            at = (z * lats + a) * lons
            put(scr, slice(at, at + lons), src[z, a].astype(F32))


def lon_column(scr, lon, lons, width):
    return get(scr, pl.ds(lon, CHUNK, stride=lons), width)


def flat_store(dst, at, mat, cols):
    rows = mat.shape[1]
    if cols % 128 == 0:
        per = cols // 128
        for c in range(per):
            dst[pl.ds(at + c, rows, stride=per), :] = mat[c]
        return rows * per
    per = 2 * cols // 128
    half = cols // 128
    even = get(mat, pl.ds(0, rows // 2, stride=2), cols)
    odd = get(mat, pl.ds(1, rows // 2, stride=2), cols)
    for c in range(half):
        dst[pl.ds(at + c, rows // 2, stride=per), :] = even[:, c * 128 : (c + 1) * 128]
    dst[pl.ds(at + half, rows // 2, stride=per), :] = jnp.concatenate(
        [even[:, half * 128 : half * 128 + 64], odd[:, 0:64]], axis=1
    )
    for c in range(half):
        dst[pl.ds(at + half + 1 + c, rows // 2, stride=per), :] = odd[
            :, 64 + c * 128 : 64 + (c + 1) * 128
        ]
    return rows * cols // 128


def send_units(scr, base, out):
    lons, units = out.shape[:2]
    for j in range(lons):
        for u in range(units):
            at = base + (j * units + u) * UNIT
            if not isinstance(at, int):
                at = pl.multiple_of(at, UNIT)
            out[j, u] = scr[pl.ds(at, UNIT), :].astype(BF16)


def halves(scr, lat, keep, give):
    half = keep.shape[0] * keep.shape[1] * UNIT
    send_units(scr, lat * half, keep)
    send_units(scr, (1 - lat) * half, give)


def bias_units(sums, out):
    lons, per = out.shape[:2]

    def put_unit(k, value):
        out[k // per, k % per] = value

    fold_bias(sums, put_unit)
    for k in range(BIAS_UNITS, lons * per):
        put_unit(k, jnp.zeros((UNIT, 128), BF16))

def forward_core(x, b, refs, qkv_scr, bias_scr, mixed, probs, stack_scr, finish=None):
    qkv_w, proj_w, gains = refs
    width = x.shape[-1]
    stand, inv = standardize(x)
    normed = (stand * gains[b, 0:1, :]).astype(BF16)
    qkv_scr[...] = dot(normed, qkv_w[b]).astype(BF16)
    attend(qkv_scr, bias_scr, mixed, probs, stack_scr, width, finish)
    att = dot(mixed[...], proj_w[b]).astype(BF16)
    resid = (x + att.astype(F32)).astype(BF16).astype(F32)
    return resid, normed


def first_kernel(
    lat_total, tokens_in, cot_in, table_in, spread_in, qkv_in, proj_in, up_in, down_in, gains_in,
    x_out, tail_out, head_out, qkv_out, mixed_out, probs_out, resid_out, hidden_out, active_out,
    scr, cot_scr, tab_scr, rows_scr, wide_scr, bias_scr,
    cot, table, spread, tokens, qkv_w, gains, proj_w, up_w, down_w, stack_scr, probs,
    mixed, resid_scr, active_scr, sems, out_sems,
):
    copies = []
    for source, target in (
        (cot_in, cot),
        (table_in.at[0:1], table),
        (spread_in, spread),
        (tokens_in, tokens),
        (qkv_in.at[0:1], qkv_w),
        (gains_in, gains),
        (proj_in.at[0:1], proj_w),
        (up_in.at[0:1], up_w),
        (down_in.at[0:1], down_w),
    ):
        copies.append(pltpu.make_async_copy(source, target, sems.at[len(copies)]))
    for copy in copies:
        copy.start()
    lat = lax.axis_index("lat")
    width = tokens.shape[-1]
    lons = tokens.shape[2]
    cut = CHUNK * (WLON // 2)
    copies[0].wait()
    lon_major(cot, cot_scr)
    g = jnp.concatenate([lon_column(cot_scr, lon, lons, width) for lon in range(lons)], axis=0)
    head_out[1] = g[0:cut, :].astype(BF16)
    tail_out[1] = g[cut:, :].astype(BF16)
    copies[1].wait()
    copies[2].wait()
    expand_bias(
        table.at[0], spread, tab_scr, rows_scr, wide_scr, bias_scr, lat, False, lat_total
    )
    copies[3].wait()
    lon_major(tokens, scr)
    x = jnp.concatenate([lon_column(scr, lon, lons, width) for lon in range(lons)], axis=0)
    x_out[...] = x.astype(BF16)
    for copy in copies[4:]:
        copy.wait()

    def probs_copy(w):
        return pltpu.make_async_copy(probs.at[w], probs_out.at[w], out_sems.at[w])

    resid, _ = forward_core(
        x, 0, (qkv_w, proj_w, gains), qkv_out, bias_scr, mixed, probs, stack_scr,
        lambda w: probs_copy(w).start(),
    )
    resid_scr[...] = resid.astype(BF16)
    wins = probs.shape[0]
    saved = [
        pltpu.make_async_copy(source, target, out_sems.at[wins + k])
        for k, (source, target) in enumerate(
            ((mixed, mixed_out), (resid_scr, resid_out), (active_scr, active_out))
        )
    ]
    saved[0].start()
    saved[1].start()
    stand, _ = standardize(resid)
    normed = (stand * gains[0, 1:2, :]).astype(BF16)
    hidden = dot(normed, up_w[0])
    hidden_out[...] = hidden
    active = gelu_value(hidden).astype(BF16)
    active_scr[...] = active
    saved[2].start()
    result = resid + dot_nt(active, down_w[0])
    head_out[0] = result[0:cut, :].astype(BF16)
    tail_out[0] = result[cut:, :].astype(BF16)
    for copy in [probs_copy(w) for w in range(wins)] + saved:
        copy.wait()


def bias_kernel(
    lat_total, table, spread, hidden, bias_out, slope_out, tab_scr, rows_scr, wide_scr, slope, sem
):
    lat = lax.axis_index("lat")
    slope[...] = gelu_parts(hidden[...])[1].astype(BF16)
    copy = pltpu.make_async_copy(slope, slope_out, sem)
    copy.start()
    expand_bias(
        table.at[1], spread, tab_scr, rows_scr, wide_scr, bias_out, lat, True, lat_total
    )
    copy.wait()


def merge_ahead(scr_own, scr_oth, rows):
    half = WLAT // 2
    n = lax.broadcasted_iota(jnp.int32, (rows, 1), 0)
    return jnp.where(
        lat_inside(n) < half,
        pltpu.roll(scr_own[...], rows - half, axis=0),
        pltpu.roll(scr_oth[...], half, axis=0),
    )


def merge_behind(scr_own, scr_oth, rows):
    half = WLAT // 2
    n = lax.broadcasted_iota(jnp.int32, (rows, 1), 0)
    return jnp.where(
        lat_inside(n) >= half,
        pltpu.roll(scr_own[...], half, axis=0),
        pltpu.roll(scr_oth[...], rows - half, axis=0),
    )


def second_kernel(
    lat_total,
    tail, lon_head, lat_tail, diag_head, bias, qkv_w, proj_w, up_w, down_w, gains,
    head_out, tail_out, n1_out, field_out, mixed_out, low_out, n2_out, hg_out, active_out, g_out,
    sums_out, gain_out,
    scr_own, scr_oth, qkv_scr, probs_scr, dmix_scr, low_scr, prob_scr,
):
    lat = lax.axis_index("lat")
    rows, width = scr_own.shape
    cut = CHUNK * (WLON // 2)

    def rolled(which):
        scr_own[0 : rows - cut, :] = tail[which].astype(F32)
        scr_own[rows - cut :, :] = lon_head[which].astype(F32)
        scr_oth[0 : rows - cut, :] = lat_tail[which].astype(F32)
        scr_oth[rows - cut :, :] = diag_head[which].astype(F32)
        return merge_ahead(scr_own, scr_oth, rows)

    g = rolled(1)
    n = lax.broadcasted_iota(jnp.int32, (rows, 1), 0)
    keep = lat_row(n, lat, True, lat_total) < lat_total - PAD
    g = jnp.where(keep, g, 0.0)
    g_out[...] = g.astype(BF16)

    x = rolled(0)

    resid, normed = forward_core(
        x, 1, (qkv_w, proj_w, gains), qkv_scr, bias, mixed_out, probs_scr, low_scr
    )
    n1_out[...] = normed
    stand2, inv2 = standardize(resid)
    normed2 = (stand2 * gains[1, 1:2, :]).astype(BF16)
    n2_out[...] = normed2
    active, slope = gelu_parts(dot(normed2, up_w[1]))
    active_out[...] = active.astype(BF16)

    hg = (dot(g_out[...], down_w[1]) * slope).astype(BF16)
    hg_out[...] = hg
    part, gain_two = norm_back(dot_nt(hg, up_w[1]), gains[1, 1:2, :], stand2, inv2)
    rg = g + part
    low = rg.astype(BF16)
    low_out[...] = low
    dmix_scr[...] = dot_nt(low, proj_w[1]).astype(BF16)
    sums_out[...] = jnp.zeros(sums_out.shape, F32)
    attend_back(
        qkv_scr, probs_scr, dmix_scr, field_out, sums_out, low_scr, prob_scr, width
    )
    ng = dot_nt(field_out[...], qkv_w[1]).astype(BF16).astype(F32)
    stand1, inv1 = standardize(x)
    part, gain_one = norm_back(ng, gains[1, 0:1, :], stand1, inv1)
    dx = rg + part
    head_out[...] = dx[0 : rows - cut, :].astype(BF16)
    tail_out[...] = dx[rows - cut :, :].astype(BF16)
    gain_out[0:1, :] = gain_one
    gain_out[1:2, :] = gain_two


def outer_kernel(
    n1, field, mixed, low, n2, hg, active, g, sums,
    keep, give, bias_out,
    m576, m192, m768, mdown, flat_scr,
):
    put(m576, slice(None), dot_tn(n1[...], field[...]))
    at = flat_store(flat_scr, 0, m576, field.shape[1])
    put(m192, slice(None), dot_tn(mixed[...], low[...]))
    at += flat_store(flat_scr, at, m192, mixed.shape[1])
    put(m768, slice(None), dot_tn(n2[...], hg[...]))
    at += flat_store(flat_scr, at, m768, active.shape[1])
    put(mdown, slice(None), dot_tn(active[...], g[...]))
    at += flat_store(flat_scr, at, mdown, mixed.shape[1])
    halves(flat_scr, lax.axis_index("lat"), keep, give)
    bias_units(sums, bias_out)


def lat_sums(*refs):
    out = refs[-1]
    at = 0
    for k in range(0, len(refs) - 2, 2):
        keep, got = refs[k], refs[k + 1]
        count = keep.shape[1]
        out[:, at : at + count] = (keep[...].astype(F32) + got[...].astype(F32)).astype(BF16)
        at += count
    out[:, at:] = refs[-2][...]


def lat_sums_split(*refs):
    keep_out, give_out = refs[-2:]
    x = lax.rem(lax.axis_index("lon"), 2)
    for out, side in ((keep_out, x), (give_out, 1 - x)):
        for z in range(out.shape[0]):
            j = 2 * z + side
            at = 0
            for k in range(0, len(refs) - 3, 2):
                keep, got = refs[k], refs[k + 1]
                count = keep.shape[1]
                total = keep[j].astype(F32) + got[j].astype(F32)
                out[z, at : at + count] = total.astype(BF16)
                at += count
            out[z, at:] = refs[-3][j]


def add_pair(keep, got, order, out):
    out[...] = (keep[...].astype(F32) + got[...].astype(F32)).astype(BF16)


def sum_pieces(pieces, order, out):
    total = pieces[0].astype(F32)
    for k in range(1, pieces.shape[0]):
        total = total + pieces[k].astype(F32)
    total = total.astype(BF16)
    if len(out.shape) == len(pieces.shape):
        for k in range(out.shape[0]):
            out[k] = total
    else:
        out[...] = total


def join_z(*refs):
    out = refs[-1]
    count = out.shape[0]
    z = lax.div(lax.axis_index("lon"), 2)
    for k in range(count):
        out[lax.rem(z + count - k, count)] = refs[k][...]


def third_kernel(
    head, lon_tail, lat_head, diag_tail, resid_in, slope_in, active_in, mixed_in,
    proj_w, up_w, down_w, gains, probs_in, order,
    keep_out, give_out, rg_out, dmix_out, gain_out, probs_out,
    scr_own, scr_oth, m192, m768, mdown, flat_scr,
    resid, slope, active, mixed, sems,
):
    copies = [
        pltpu.make_async_copy(source, target, sems.at[k])
        for k, (source, target) in enumerate(
            (
                (resid_in, resid),
                (slope_in, slope),
                (mixed_in, mixed),
                (active_in, active),
                (probs_in.at[0 : probs_out.shape[0]], probs_out),
            )
        )
    ]
    for copy in copies:
        copy.start()
    rows, width = scr_own.shape
    cut = CHUNK * (WLON // 2)
    scr_own[0:cut, :] = lon_tail[...].astype(F32)
    scr_own[cut:, :] = head[...].astype(F32)
    scr_oth[0:cut, :] = diag_tail[...].astype(F32)
    scr_oth[cut:, :] = lat_head[...].astype(F32)
    g = merge_behind(scr_own, scr_oth, rows)
    g_low = g.astype(BF16)
    hg = dot(g_low, down_w[0])
    copies[0].wait()
    stand2, inv2 = standardize(resid[...].astype(F32))
    normed2 = (stand2 * gains[0, 1:2, :]).astype(BF16)
    copies[1].wait()
    hg = (hg * slope[...].astype(F32)).astype(BF16)
    part, gain_two = norm_back(dot_nt(hg, up_w[0]), gains[0, 1:2, :], stand2, inv2)
    rg = g + part
    rg_out[...] = rg
    low = rg.astype(BF16)
    dmix_out[...] = dot_nt(low, proj_w[0]).astype(BF16)
    gain_out[...] = gain_two
    copies[2].wait()
    put(m192, slice(None), dot_tn(mixed[...], low))
    at = flat_store(flat_scr, 0, m192, mixed.shape[1])
    put(m768, slice(None), dot_tn(normed2, hg))
    at += flat_store(flat_scr, at, m768, active.shape[1])
    copies[3].wait()
    put(mdown, slice(None), dot_tn(active[...], g_low))
    at += flat_store(flat_scr, at, mdown, mixed.shape[1])
    flat_scr[at:, :] = jnp.zeros((flat_scr.shape[0] - at, 128), F32)
    halves(flat_scr, lax.axis_index("lat"), keep_out, give_out)
    copies[4].wait()


def gain_rows(one, two):
    return jnp.concatenate(
        [
            one[:, 0:128],
            jnp.concatenate([one[:, 128:192], two[:, 0:64]], axis=1),
            two[:, 64:192],
        ],
        axis=0,
    )


def fourth_kernel(
    x_in, qkv, probs_near, probs_in, dmix, rg, gain_two, gains_late, qkv_w, gains,
    tokens_out, keep, give, bias_out,
    field, sums, m576, flat_scr, dx_scr, low_scr, prob_scr, probs, sems,
):
    near = probs_near.shape[0]

    def probs_copy(w):
        return pltpu.make_async_copy(probs_in.at[w], probs.at[w - near], sems.at[w - near])

    for w in range(near, probs_in.shape[0]):
        probs_copy(w).start()
    width = x_in.shape[-1]
    levels, lats, lons = tokens_out.shape[:3]
    sums[...] = jnp.zeros(sums.shape, F32)
    attend_back(qkv, probs_near, dmix, field, sums, low_scr, prob_scr, width)
    attend_back(
        qkv, probs, dmix, field, sums, low_scr, prob_scr, width, near,
        lambda w: probs_copy(w).wait(),
    )
    stand1, inv1 = standardize(x_in[...].astype(F32))
    normed = (stand1 * gains[0, 0:1, :]).astype(BF16)
    ng = dot_nt(field[...], qkv_w[0]).astype(BF16).astype(F32)
    part, gain_one = norm_back(ng, gains[0, 0:1, :], stand1, inv1)
    put(m576, slice(None), dot_tn(normed, field[...]))
    at = flat_store(flat_scr, 0, m576, field.shape[1])
    flat_scr[at:, :] = jnp.zeros((flat_scr.shape[0] - at, 128), F32)
    flat_scr[at : at + 3, :] = gain_rows(gain_one, gain_two[...])
    flat_scr[at + 3 : at + 6, :] = gain_rows(gains_late[0:1, :], gains_late[1:2, :])
    bias_units(sums, bias_out)
    halves(flat_scr, lax.axis_index("lat"), keep, give)
    put(dx_scr, slice(None), rg[...] + part)
    for z in range(levels):
        for a in range(lats):
            tokens_out[z, a] = get(
                dx_scr, pl.ds(z * lats + a, lons, stride=CHUNK), width
            ).astype(BF16)


def place(pieces, first, last, dests, scr):
    total = jnp.zeros((UNIT, 128), F32)
    lons = pieces.shape[1]
    per = last - first
    k = 0
    for where, room in dests:
        for at in range(where, where + room, UNIT):
            half, j, u = k // (per * lons), k // per % lons, k % per
            value = pieces[half, j, first + u].astype(F32)
            scr[at : at + UNIT, :] = value
            total = total + value * value
            k += 1
    return total


def bias_rows(piece, base, spread, out, rows_scr, wide_scr, tab_scr):
    lat = lax.axis_index("lat")
    extra = -(-BIAS_UNITS // piece.shape[1])

    def read(at):
        parts = []
        for r in range(CHUNK // UNIT):
            k = at * (CHUNK // UNIT) + r
            parts.append(piece[lat, k // extra, base + k % extra].astype(F32))
        return jnp.concatenate(parts, axis=0)

    rest = read(2 * HEADS)
    for h in range(HEADS):
        rows = pl.ds(h, CHUNK, stride=8)
        wide_scr[0, rows, :] = read(h)
        wide_scr[1, rows, :] = read(HEADS + h)
        wide_scr[2, rows, :] = rest if h == 0 else pltpu.roll(rest, 128 - 8 * h, axis=1)
    low = get(wide_scr, slice(None), WIDE).astype(BF16)
    for zj in range(LEVELS):
        rows_scr[...] = dot_nt(low, spread[zj])
        for zi in range(LEVELS):
            for ai in range(WLAT):
                at = ((zi * LEVELS + zj) * WLAT + ai) * PAIR
                row = (zi * WLAT + ai) * 8
                tab_scr[0:HEADS, at : at + PAIR] = rows_scr[row : row + HEADS, 0:PAIR]
    for h in range(HEADS):
        out[h] = tab_scr[h : h + 1, :]


def late_kernel(
    units_a, spread, same, same_x, cross, cross_x, flat_out, squares_out, bias_out,
    rows_scr, wide_scr, tab_scr, a,
):
    lat = lax.axis_index("lat")
    x = lax.rem(lax.axis_index("lon"), 2)
    for z in range(same.shape[0]):
        a[lat, 2 * z + x] = same[z]
        a[lat, 2 * z + 1 - x] = same_x[z]
        a[1 - lat, 2 * z + x] = cross[z]
        a[1 - lat, 2 * z + 1 - x] = cross_x[z]
    squares_out[...] = place(a, 0, units_a, [(0, flat_out.shape[0])], flat_out)
    bias_rows(a, units_a, spread, bias_out, rows_scr, wide_scr, tab_scr)


def last_kernel(
    units_b, units_c, spread, flat_a, squares, bias_late, own_bc, oth_bc, update_out, bias_out,
    scr, rows_scr, wide_scr, tab_scr, bc,
):
    lat = lax.axis_index("lat")
    for j in range(own_bc.shape[0]):
        bc[lat, j] = own_bc[j]
        bc[1 - lat, j] = oth_bc[j]
    total = squares[...]
    total = total + place(bc, 0, units_b, [(864, 288), (1152, 1152), (2304, 1152)], scr)
    total = total + place(bc, units_b, units_b + units_c, [(0, 864), (3456, 8)], scr)
    count = update_out.shape[0]
    mean = jnp.sum(total) * (1.0 / (count * 128))
    scale = lax.rsqrt(mean + 1e-06)
    early, late = (0, 1728, 2304, 4608), (864, 2016, 3456, 5760)
    at = 0
    for first, second, rows in zip(early, late, (864, 288, 1152, 1152)):
        update_out[first : first + rows, :] = (scr[at : at + rows, :] * scale).astype(BF16)
        update_out[second : second + rows, :] = (flat_a[at : at + rows, :] * scale).astype(BF16)
        at += rows
    update_out[6912:count, :] = (scr[at : at + count - 6912, :] * scale).astype(BF16)
    bias_rows(bc, units_b + units_c, spread, bias_out.at[0], rows_scr, wide_scr, tab_scr)
    bias_out[1] = bias_late[...]


def call(kernel, outs, scratch, args, micros, mib, spaces=None, far=(), near=()):
    spaces = spaces or [pltpu.VMEM] * len(args)
    return pl.pallas_call(
        kernel,
        out_shape=[
            pltpu.HBM(*entry)
            if at in far
            else (pltpu.VMEM if at in near else jax.ShapeDtypeStruct)(*entry)
            for at, entry in enumerate(outs)
        ],
        in_specs=[pl.BlockSpec(memory_space=space) for space in spaces],
        out_specs=[
            pl.BlockSpec(memory_space=pltpu.HBM if at in far else pltpu.VMEM)
            for at in range(len(outs))
        ],
        scratch_shapes=[
            pltpu.VMEM(*entry) if isinstance(entry, tuple) else entry for entry in scratch
        ],
        compiler_params=pltpu.CompilerParams(vmem_limit_bytes=mib * MIB),
        cost_estimate=pl.CostEstimate(
            flops=int(micros * 1.1e9), bytes_accessed=10**5, transcendentals=0
        ),
    )(*args)


def lat_swap(value):
    return lax.ppermute(value, "lat", [(0, 1), (1, 0)])


def lon_send(value, step):
    count = lax.axis_size("lon")
    return lax.ppermute(value, "lon", [(s, (s + step) % count) for s in range(count)])


def x_swap(value):
    count = lax.axis_size("lon")
    return lax.ppermute(value, "lon", [(s, s ^ 1) for s in range(count)])


def diag_send(value, step):
    count = lax.axis_size("lon")
    pairs = []
    for s in range(count):
        for t in range(2):
            pairs.append((2 * s + t, 2 * ((s + step) % count) + 1 - t))
    return lax.ppermute(value, ("lon", "lat"), pairs)


def shards(
    tokens, cotangent, qkv_weight, proj_weight, up_weight, down_weight, norm_gain, bias_table
):
    levels, lats, lons, width = tokens.shape
    rows = levels * lats * lons
    wins = rows // WIN
    hid = up_weight.shape[-1]
    heads = bias_table.shape[2]
    lon_size = lax.axis_size("lon")
    zs = lon_size // 2
    lat_total = lats * lax.axis_size("lat")
    cut = CHUNK * (WLON // 2)
    spread = jnp.asarray(spread_matrices(), BF16)
    down_turned = jnp.swapaxes(down_weight, 1, 2)
    table = jnp.swapaxes(bias_table, 1, 2)
    token = (rows, width)
    field_shape = ((rows, 3 * width), BF16)
    probs_shape = ((wins, heads, WIN, WIN), F32)
    stack_shape = ((heads * WIN, WIN), BF16)
    bias_shape = ((heads * WIN, WIN), F32)
    sums_shape = ((heads * WIN, WIDE), F32)
    tab_scr = ((8, table.shape[-1]), F32)
    rows_scr = ((LEVELS * CHUNK * 8, PAIR), F32)
    wide_scr = ((WIDE // 128, CHUNK * 8, 128), F32)
    tiles = -(-width // 128)
    token_scr = ((tiles, rows, 128), F32)
    m576 = ((-(-3 * width // 128), width, 128), F32)
    m192 = ((tiles, width, 128), F32)
    m768 = ((hid // 128, width, 128), F32)
    mdown = ((tiles, hid, 128), F32)

    block_rows = (qkv_weight[0].size + proj_weight[0].size + 2 * up_weight[0].size) // 128
    qkv_rows = qkv_weight[0].size // 128
    counts = (block_rows, block_rows - qkv_rows, qkv_rows + 8)
    units_a, units_b, units_c = [-(-count // (2 * lon_size * UNIT)) for count in counts]
    extra = -(-BIAS_UNITS // lon_size)

    def units(*lead):
        return (lead + (UNIT, 128), BF16)

    def flat_scr(per):
        return ((2 * lon_size * per * UNIT, 128), F32)

    x0, tail, head, qkv0, mixed0, probs0, resid0, hidden0, active0 = call(
        functools.partial(first_kernel, lat_total),
        [
            (token, BF16),
            ((2, rows - cut, width), BF16),
            ((2, cut, width), BF16),
            field_shape,
            (token, BF16),
            probs_shape,
            (token, BF16),
            ((rows, hid), F32),
            ((rows, hid), BF16),
        ],
        [
            token_scr,
            token_scr,
            tab_scr,
            rows_scr,
            wide_scr,
            bias_shape,
            (cotangent.shape, BF16),
            ((1,) + table.shape[1:], F32),
            (spread.shape, BF16),
            (tokens.shape, BF16),
            ((1,) + qkv_weight.shape[1:], BF16),
            (norm_gain.shape, F32),
            ((1,) + proj_weight.shape[1:], BF16),
            ((1,) + up_weight.shape[1:], BF16),
            ((1,) + down_turned.shape[1:], BF16),
            stack_shape,
            probs_shape,
            (token, BF16),
            (token, BF16),
            ((rows, hid), BF16),
            pltpu.SemaphoreType.DMA((9,)),
            pltpu.SemaphoreType.DMA((wins + 3,)),
        ],
        [
            pltpu.with_memory_space_constraint(arg, pltpu.HBM)
            for arg in (
                tokens, cotangent, table, spread, qkv_weight, proj_weight, up_weight, down_turned,
                norm_gain,
            )
        ],
        8,
        16,
        [pltpu.HBM] * 9,
        (4, 5, 6, 8),
        (0, 3),
    )
    lon_head = lon_send(head, -1)
    diag_head = diag_send(head, -1)
    lat_tail = lat_swap(tail)
    bias1, slope0 = call(
        functools.partial(bias_kernel, lat_total),
        [bias_shape, ((rows, hid), BF16)],
        [tab_scr, rows_scr, wide_scr, ((rows, hid), BF16), pltpu.SemaphoreType.DMA],
        (table, spread, hidden0),
        3,
        12,
        far=(1,),
    )

    (
        dhead, dtail, n1, field1, mixed1, low1, n2, hg1, active1, g1, sums1, gains1,
    ) = call(
        functools.partial(second_kernel, lat_total),
        [
            ((rows - cut, width), BF16),
            ((cut, width), BF16),
            (token, BF16),
            field_shape,
            (token, BF16),
            (token, BF16),
            (token, BF16),
            ((rows, hid), BF16),
            ((rows, hid), BF16),
            (token, BF16),
            sums_shape,
            ((2, width), F32),
        ],
        [
            (token, F32),
            (token, F32),
            field_shape,
            probs_shape,
            (token, BF16),
            stack_shape,
            stack_shape,
        ],
        (
            tail, lon_head, lat_tail, diag_head, bias1, qkv_weight, proj_weight, up_weight,
            down_turned, norm_gain,
        ),
        19,
        16,
    )
    lon_tail = lon_send(dtail, 1)
    diag_tail = diag_send(dtail, 1)
    lat_dhead = lat_swap(dhead)

    keep_a, give_a, bias_a = call(
        outer_kernel,
        [units(lon_size, units_a), units(lon_size, units_a), units(lon_size, extra)],
        [m576, m192, m768, mdown, flat_scr(units_a)],
        (n1, field1, mixed1, low1, n2, hg1, active1, g1, sums1),
        3,
        14,
    )
    got_a = lat_swap(give_a)

    (part_a,) = call(
        lat_sums, [units(lon_size, units_a + extra)], [], (keep_a, got_a, bias_a), 1, 10
    )
    pieces_a = lax.all_to_all(part_a, "lon", 0, 0)

    near = 1
    probs_far = pltpu.with_memory_space_constraint(probs0, pltpu.HBM)
    keep_b, give_b, rg0, dmix0, gain_two, probs_near = call(
        third_kernel,
        [
            units(lon_size, units_b),
            units(lon_size, units_b),
            (token, F32),
            (token, BF16),
            ((1, width), F32),
            ((near,) + probs_shape[0][1:], F32),
        ],
        [
            (token, F32),
            (token, F32),
            m192,
            m768,
            mdown,
            flat_scr(units_b),
            (token, BF16),
            ((rows, hid), BF16),
            ((rows, hid), BF16),
            (token, BF16),
            pltpu.SemaphoreType.DMA((5,)),
        ],
        (
            dhead, lon_tail, lat_dhead, diag_tail,
            *[
                pltpu.with_memory_space_constraint(saved, pltpu.HBM)
                for saved in (resid0, slope0, active0, mixed0)
            ],
            proj_weight, up_weight, down_turned, norm_gain, probs_far, part_a,
        ),
        3,
        14,
        [pltpu.VMEM] * 4 + [pltpu.HBM] * 4 + [pltpu.VMEM] * 4 + [pltpu.HBM, pltpu.VMEM],
    )
    got_b = lat_swap(give_b)

    tokens_grad, keep_c, give_c, bias_c = call(
        fourth_kernel,
        [
            (tokens.shape, BF16),
            units(lon_size, units_c),
            units(lon_size, units_c),
            units(lon_size, extra),
        ],
        [
            field_shape,
            sums_shape,
            m576,
            flat_scr(units_c),
            token_scr,
            stack_shape,
            stack_shape,
            ((wins - near,) + probs_shape[0][1:], F32),
            pltpu.SemaphoreType.DMA((wins - near,)),
        ],
        (
            x0, qkv0, probs_near, probs_far, dmix0, rg0, gain_two, gains1, qkv_weight,
            norm_gain,
        ),
        8,
        14,
        [pltpu.VMEM] * 3 + [pltpu.HBM] + [pltpu.VMEM] * 6,
    )
    got_c = lat_swap(give_c)
    units_bc = units_b + units_c + extra
    keep_x, give_x = call(
        lat_sums_split,
        [units(zs, units_bc)] * 2,
        [],
        (keep_b, got_b, keep_c, got_c, bias_c),
        1,
        10,
    )
    got_x = x_swap(give_x)
    (sum_a,) = call(sum_pieces, [units(units_a + extra)], [], (pieces_a, keep_x), 1, 10)
    (same,) = call(
        join_z,
        [units(zs, units_a + extra)],
        [],
        [sum_a] + [lon_send(sum_a, 2 * k) for k in range(1, zs)],
        1,
        10,
    )
    (part_z,) = call(add_pair, [units(zs, units_bc)], [], (keep_x, got_x, same), 1, 10)
    pieces_bc = lax.all_to_all(
        part_z,
        "lon",
        0,
        0,
        axis_index_groups=[[2 * z + x for z in range(zs)] for x in range(2)],
    )

    same_x = x_swap(same)
    cross = lat_swap(same)
    cross_x = lat_swap(same_x)
    (sum_bc,) = call(
        sum_pieces,
        [units(lon_size, units_bc)],
        [],
        (pieces_bc, cross_x),
        1,
        10,
    )
    whole_bc = lax.all_to_all(sum_bc, "lon", 0, 0)
    oth_bc = lat_swap(whole_bc)

    flat_rows = (2 * block_rows * 128 + norm_gain.size) // 128
    fold_scr = [((CHUNK * 8, PAIR), F32), wide_scr, tab_scr]
    flat_a, squares, bias_late = call(
        functools.partial(late_kernel, units_a),
        [((block_rows, 128), F32), ((UNIT, 128), F32), (table.shape[1:], F32)],
        [*fold_scr, units(2, lon_size, units_a + extra)],
        (spread, same, same_x, cross, cross_x),
        2,
        14,
    )
    update, bias_grad = call(
        functools.partial(last_kernel, units_b, units_c),
        [((flat_rows, 128), BF16), (table.shape, F32)],
        [
            ((block_rows + 8, 128), F32),
            *fold_scr,
            units(2, lon_size, units_b + units_c + extra),
        ],
        (spread, flat_a, squares, bias_late, whole_bc, oth_bc),
        2,
        14,
    )
    bias_grad = jnp.swapaxes(bias_grad, 1, 2)
    return (tokens_grad, update.reshape(-1), bias_grad)


def solution(mesh):
    return jax.shard_map(
        shards,
        mesh=mesh,
        in_specs=(
            P("grp", "lat", "lon", None),
            P("grp", "lat", "lon", None),
            P(),
            P(),
            P(),
            P(),
            P(),
            P(None, "lat", None, None),
        ),
        out_specs=(P("grp", "lat", "lon", None), P("grp"), P("grp", "lat", None, None)),
        check_vma=False,
    )
```

```python
import functools

import jax
import jax.numpy as jnp
import numpy as np
from jax import lax
from jax.experimental import pallas as pl
from jax.experimental.pallas import tpu as pltpu
from jax.sharding import PartitionSpec as P

WLAT = 12
WLON = 6
PAD = 5
LEVELS = 2
HEADS = 6
CHUNK = LEVELS * WLAT
WIN = CHUNK * WLON
SHIFTS = 2 * WLON - 1
PAIR = WLAT * SHIFTS
WIDE = 384

EPS = 1e-05
NEGATIVE = -1000000000.0
ROOT_HALF = 0.7071067811865476
INV_ROOT_TAU = 0.3989422804014327

F32 = jnp.float32
BF16 = jnp.bfloat16
UNIT = 8
BIAS_UNITS = (2 * HEADS + 1) * CHUNK // UNIT
MIB = 1024 * 1024


def dot(a, b):
    return lax.dot_general(a, b, (((1,), (0,)), ((), ())), preferred_element_type=F32)


def dot_nt(a, b):
    return lax.dot_general(a, b, (((1,), (1,)), ((), ())), preferred_element_type=F32)


def dot_tn(a, b):
    return lax.dot_general(a, b, (((0,), (0,)), ((), ())), preferred_element_type=F32)


def row_mean(v):
    return jnp.sum(v, axis=-1, keepdims=True) * (1.0 / v.shape[-1])


def standardize(x):
    centred = x - row_mean(x)
    inv = lax.rsqrt(row_mean(centred * centred) + EPS)
    return centred * inv, inv


def norm_back(d, gain, stand, inv):
    scaled = d * gain
    first = row_mean(scaled)
    second = row_mean(scaled * stand)
    gain_grad = jnp.sum(d * stand, axis=0, keepdims=True)
    return inv * (scaled - first - stand * second), gain_grad


def gelu_value(hidden):
    return 0.5 * hidden * (1.0 + lax.erf(hidden * ROOT_HALF))


def gelu_parts(hidden):
    half = 0.5 * (1.0 + lax.erf(hidden * ROOT_HALF))
    slope = half + hidden * jnp.exp(-0.5 * hidden * hidden) * INV_ROOT_TAU
    return hidden * half, slope


def split3(v):
    hi = v.astype(BF16)
    rest = v - hi.astype(F32)
    mid = rest.astype(BF16)
    low = (rest - mid.astype(F32)).astype(BF16)
    return hi, mid, low


def spread_matrices():
    out = np.zeros((LEVELS, PAIR, WIDE), np.float32)
    for zj in range(LEVELS):
        for aj in range(WLAT):
            for d in range(SHIFTS):
                out[zj, aj * SHIFTS + d, (SHIFTS - 1 - d) * CHUNK + zj * WLAT + aj] = 1.0
    return out


def put(scr, rows, value):
    width = value.shape[1]
    for tile in range(-(-width // 128)):
        lanes = min(128, width - tile * 128)
        scr[tile, rows, 0:lanes] = value[:, tile * 128 : tile * 128 + lanes]


def get(scr, rows, width):
    parts = [scr[tile, rows, :] for tile in range(-(-width // 128))]
    return jnp.concatenate(parts, axis=1)[:, 0:width]


def head_masks(width, dtype):
    lane = lax.broadcasted_iota(jnp.int32, (1, width), 1)
    size = width // HEADS
    return [((lane >= h * size) & (lane < (h + 1) * size)).astype(dtype) for h in range(HEADS)]


def lat_inside(n):
    return lax.rem(n, WLAT)


def lat_row(row_iota, lat, shifted, lat_total):
    row = lat * WLAT + lat_inside(row_iota)
    if shifted:
        row = row + WLAT // 2
        row = jnp.where(row >= lat_total, row - lat_total, row)
    return row


def expand_bias(table, spread, tab_scr, rows_scr, wide_scr, bias_scr, lat, shifted, lat_total):
    for h in range(HEADS):
        tab_scr[h : h + 1, :] = table[h]
    for zi in range(LEVELS):
        for zj in range(LEVELS):
            for ai in range(WLAT):
                at = ((zi * LEVELS + zj) * WLAT + ai) * PAIR
                row = zj * CHUNK * 8 + (zi * WLAT + ai) * 8
                rows_scr[row : row + HEADS, 0:PAIR] = tab_scr[0:HEADS, at : at + PAIR]
    count = CHUNK * 8
    total = jnp.zeros((count, WIDE), F32)
    for zj in range(LEVELS):
        parts = split3(rows_scr[zj * count : (zj + 1) * count, 0:PAIR])
        for part in parts:
            total = total + dot(part, spread[zj])
    put(wide_scr, slice(None), total)
    i = lax.broadcasted_iota(jnp.int32, (CHUNK, WIN), 0)
    j = lax.broadcasted_iota(jnp.int32, (CHUNK, WIN), 1)
    allowed = lat_row(j, lat, shifted, lat_total) < lat_total - PAD
    if shifted:
        last = lat_total - WLAT // 2
        region_i = (lat * WLAT + lat_inside(i)) >= last
        region_j = (lat * WLAT + lat_inside(j)) >= last
        allowed = allowed & (region_i == region_j)
    for h in range(HEADS):
        wide = get(wide_scr, pl.ds(h, CHUNK, stride=8), WIDE)
        for oi in range(WLON):
            back = (WLON - 1 - oi) * CHUNK
            moved = wide if back == 0 else pltpu.roll(wide, WIDE - back, axis=1)
            at = h * WIN + oi * CHUNK
            bias_scr[at : at + CHUNK, :] = jnp.where(allowed, moved[:, 0:WIN], NEGATIVE)


def fold_bias(sums, put_unit):
    rest = jnp.zeros((CHUNK, 128), F32)

    def emit(at, value):
        for r in range(CHUNK // UNIT):
            put_unit(at * (CHUNK // UNIT) + r, value[r * UNIT : (r + 1) * UNIT, :].astype(BF16))

    for h in range(HEADS):
        total = jnp.zeros((CHUNK, WIDE), F32)
        for oi in range(WLON):
            back = (WLON - 1 - oi) * CHUNK
            at = h * WIN + oi * CHUNK
            part = sums[at : at + CHUNK, :]
            total = total + (part if back == 0 else pltpu.roll(part, back, axis=1))
        emit(h, total[:, 0:128])
        emit(HEADS + h, total[:, 128:256])
        last = total[:, 256:384]
        rest = rest + (last if h == 0 else pltpu.roll(last, 8 * h, axis=1))
    emit(2 * HEADS, rest)

def stack_heads(v, masks):
    return jnp.concatenate([v * mask for mask in masks], axis=0)


def pick_heads(v, masks):
    total = v[0:WIN] * masks[0]
    for h in range(1, HEADS):
        total = total + v[h * WIN : (h + 1) * WIN] * masks[h]
    return total


def attend(qkv, bias, mixed, probs, stack_scr, width):
    masks = head_masks(width, BF16)
    masks32 = head_masks(width, F32)
    scale = (width // HEADS) ** -0.5

    def window(w, carry):
        rows = pl.ds(pl.multiple_of(w * WIN, 16), WIN)
        q = qkv[rows, 0:width]
        k = qkv[rows, width : 2 * width]
        v = qkv[rows, 2 * width : 3 * width]
        scores = dot_nt(stack_heads(q, masks), k)
        for h in range(HEADS):
            part = slice(h * WIN, (h + 1) * WIN)
            logits = scores[part] * scale + bias[part, :]
            weights = jnp.exp(logits - jnp.max(logits, axis=-1, keepdims=True))
            p = weights * (1.0 / jnp.sum(weights, axis=-1, keepdims=True))
            probs[w, h] = p
            stack_scr[part, :] = p.astype(BF16)
        mixed[rows, :] = pick_heads(dot(stack_scr[...], v), masks32).astype(BF16)
        return carry

    lax.fori_loop(0, probs.shape[0], window, 0, unroll=True)


def attend_back(qkv, probs, dmix, field, sums, low_scr, prob_scr, width):
    masks = head_masks(width, BF16)
    masks32 = head_masks(width, F32)
    scale = (width // HEADS) ** -0.5

    def window(w, carry):
        rows = pl.ds(pl.multiple_of(w * WIN, 16), WIN)
        q = qkv[rows, 0:width]
        k = qkv[rows, width : 2 * width]
        v = qkv[rows, 2 * width : 3 * width]
        up = stack_heads(dmix[rows, :], masks)
        prob_grad = dot_nt(up, v)
        for h in range(HEADS):
            part = slice(h * WIN, (h + 1) * WIN)
            p = probs[w, h]
            weighted = p * prob_grad[part]
            ds = weighted - p * jnp.sum(weighted, axis=-1, keepdims=True)
            sums[part, 0:WIN] += ds
            low_scr[part, :] = ds.astype(BF16)
            prob_scr[part, :] = p.astype(BF16)
        low = low_scr[...]
        dq = pick_heads(dot(low, k), masks32)
        dk = dot_tn(low, stack_heads(q, masks))
        dv = dot_tn(prob_scr[...], up)
        field[rows, 0:width] = (dq * scale).astype(BF16)
        field[rows, width : 2 * width] = (dk * scale).astype(BF16)
        field[rows, 2 * width : 3 * width] = dv.astype(BF16)
        return carry

    lax.fori_loop(0, probs.shape[0], window, 0, unroll=True)


def lon_major(src, scr):
    levels, lats, lons, width = src.shape
    for z in range(levels):
        for a in range(lats):
            at = (z * lats + a) * lons
            put(scr, slice(at, at + lons), src[z, a].astype(F32))


def lon_column(scr, lon, lons, width):
    return get(scr, pl.ds(lon, CHUNK, stride=lons), width)


def flat_store(dst, at, mat, cols):
    rows = mat.shape[1]
    if cols % 128 == 0:
        per = cols // 128
        for c in range(per):
            dst[pl.ds(at + c, rows, stride=per), :] = mat[c]
        return rows * per
    per = 2 * cols // 128
    half = cols // 128
    even = get(mat, pl.ds(0, rows // 2, stride=2), cols)
    odd = get(mat, pl.ds(1, rows // 2, stride=2), cols)
    for c in range(half):
        dst[pl.ds(at + c, rows // 2, stride=per), :] = even[:, c * 128 : (c + 1) * 128]
    dst[pl.ds(at + half, rows // 2, stride=per), :] = jnp.concatenate(
        [even[:, half * 128 : half * 128 + 64], odd[:, 0:64]], axis=1
    )
    for c in range(half):
        dst[pl.ds(at + half + 1 + c, rows // 2, stride=per), :] = odd[
            :, 64 + c * 128 : 64 + (c + 1) * 128
        ]
    return rows * cols // 128


def send_units(scr, base, out):
    lons, units = out.shape[:2]
    for j in range(lons):
        for u in range(units):
            at = base + (j * units + u) * UNIT
            if not isinstance(at, int):
                at = pl.multiple_of(at, UNIT)
            out[j, u] = scr[pl.ds(at, UNIT), :].astype(BF16)


def halves(scr, lat, keep, give):
    half = keep.shape[0] * keep.shape[1] * UNIT
    send_units(scr, lat * half, keep)
    send_units(scr, (1 - lat) * half, give)


def bias_units(sums, out):
    lons, per = out.shape[:2]

    def put_unit(k, value):
        out[k // per, k % per] = value

    fold_bias(sums, put_unit)
    for k in range(BIAS_UNITS, lons * per):
        put_unit(k, jnp.zeros((UNIT, 128), BF16))

def forward_core(x, b, refs, qkv_scr, bias_scr, mixed, probs, stack_scr):
    qkv_w, proj_w, gains = refs
    width = x.shape[-1]
    stand, inv = standardize(x)
    normed = (stand * gains[b, 0:1, :]).astype(BF16)
    qkv_scr[...] = dot(normed, qkv_w[b]).astype(BF16)
    attend(qkv_scr, bias_scr, mixed, probs, stack_scr, width)
    att = dot(mixed[...], proj_w[b]).astype(BF16)
    resid = (x + att.astype(F32)).astype(BF16).astype(F32)
    return resid, normed


def first_kernel(
    lat_total, tokens_in, cot_in, table_in, spread_in, qkv_in, proj_in, up_in, down_in, gains_in,
    x_out, tail_out, head_out, qkv_out, mixed_out, probs_out, resid_out, hidden_out, active_out,
    scr, cot_scr, tab_scr, rows_scr, wide_scr, bias_scr,
    cot, table, spread, tokens, qkv_w, gains, proj_w, up_w, down_w, stack_scr, sems,
):
    copies = []
    for source, target in (
        (cot_in, cot),
        (table_in.at[0:1], table),
        (spread_in, spread),
        (tokens_in, tokens),
        (qkv_in.at[0:1], qkv_w),
        (gains_in, gains),
        (proj_in.at[0:1], proj_w),
        (up_in.at[0:1], up_w),
        (down_in.at[0:1], down_w),
    ):
        copies.append(pltpu.make_async_copy(source, target, sems.at[len(copies)]))
    for copy in copies:
        copy.start()
    lat = lax.axis_index("lat")
    width = tokens.shape[-1]
    lons = tokens.shape[2]
    cut = CHUNK * (WLON // 2)
    copies[0].wait()
    lon_major(cot, cot_scr)
    g = jnp.concatenate([lon_column(cot_scr, lon, lons, width) for lon in range(lons)], axis=0)
    head_out[1] = g[0:cut, :].astype(BF16)
    tail_out[1] = g[cut:, :].astype(BF16)
    copies[1].wait()
    copies[2].wait()
    expand_bias(
        table.at[0], spread, tab_scr, rows_scr, wide_scr, bias_scr, lat, False, lat_total
    )
    copies[3].wait()
    lon_major(tokens, scr)
    x = jnp.concatenate([lon_column(scr, lon, lons, width) for lon in range(lons)], axis=0)
    x_out[...] = x.astype(BF16)
    for copy in copies[4:]:
        copy.wait()

    resid, _ = forward_core(
        x, 0, (qkv_w, proj_w, gains), qkv_out, bias_scr, mixed_out, probs_out, stack_scr
    )
    resid_out[...] = resid.astype(BF16)
    stand, _ = standardize(resid)
    normed = (stand * gains[0, 1:2, :]).astype(BF16)
    hidden = dot(normed, up_w[0])
    hidden_out[...] = hidden
    active = gelu_value(hidden).astype(BF16)
    active_out[...] = active
    result = resid + dot_nt(active, down_w[0])
    head_out[0] = result[0:cut, :].astype(BF16)
    tail_out[0] = result[cut:, :].astype(BF16)


def bias_kernel(
    lat_total, table, spread, hidden, bias_out, slope_out, tab_scr, rows_scr, wide_scr
):
    lat = lax.axis_index("lat")
    slope_out[...] = gelu_parts(hidden[...])[1].astype(BF16)
    expand_bias(
        table.at[1], spread, tab_scr, rows_scr, wide_scr, bias_out, lat, True, lat_total
    )


def merge_ahead(scr_own, scr_oth, rows):
    half = WLAT // 2
    n = lax.broadcasted_iota(jnp.int32, (rows, 1), 0)
    return jnp.where(
        lat_inside(n) < half,
        pltpu.roll(scr_own[...], rows - half, axis=0),
        pltpu.roll(scr_oth[...], half, axis=0),
    )


def merge_behind(scr_own, scr_oth, rows):
    half = WLAT // 2
    n = lax.broadcasted_iota(jnp.int32, (rows, 1), 0)
    return jnp.where(
        lat_inside(n) >= half,
        pltpu.roll(scr_own[...], half, axis=0),
        pltpu.roll(scr_oth[...], rows - half, axis=0),
    )


def second_kernel(
    lat_total,
    kept, tail, lon_head, lat_tail, diag_head, bias, qkv_w, proj_w, up_w, down_w, gains, *rest
):
    run_second(
        lat_total, tail, lon_head, lat_tail, diag_head, bias, qkv_w, proj_w, up_w, down_w, gains,
        *rest[kept:kept + 12], *rest[2 * kept + 12 :]
    )


def run_second(
    lat_total,
    tail, lon_head, lat_tail, diag_head, bias, qkv_w, proj_w, up_w, down_w, gains,
    head_out, tail_out, n1_out, field_out, mixed_out, low_out, n2_out, hg_out, active_out, g_out,
    sums_out, gain_out,
    scr_own, scr_oth, qkv_scr, probs_scr, dmix_scr, low_scr, prob_scr,
):
    lat = lax.axis_index("lat")
    rows, width = scr_own.shape
    cut = CHUNK * (WLON // 2)

    def rolled(which):
        scr_own[0 : rows - cut, :] = tail[which].astype(F32)
        scr_own[rows - cut :, :] = lon_head[which].astype(F32)
        scr_oth[0 : rows - cut, :] = lat_tail[which].astype(F32)
        scr_oth[rows - cut :, :] = diag_head[which].astype(F32)
        return merge_ahead(scr_own, scr_oth, rows)

    g = rolled(1)
    n = lax.broadcasted_iota(jnp.int32, (rows, 1), 0)
    keep = lat_row(n, lat, True, lat_total) < lat_total - PAD
    g = jnp.where(keep, g, 0.0)
    g_out[...] = g.astype(BF16)

    x = rolled(0)

    resid, normed = forward_core(
        x, 1, (qkv_w, proj_w, gains), qkv_scr, bias, mixed_out, probs_scr, low_scr
    )
    n1_out[...] = normed
    stand2, inv2 = standardize(resid)
    normed2 = (stand2 * gains[1, 1:2, :]).astype(BF16)
    n2_out[...] = normed2
    active, slope = gelu_parts(dot(normed2, up_w[1]))
    active_out[...] = active.astype(BF16)

    hg = (dot(g_out[...], down_w[1]) * slope).astype(BF16)
    hg_out[...] = hg
    part, gain_two = norm_back(dot_nt(hg, up_w[1]), gains[1, 1:2, :], stand2, inv2)
    rg = g + part
    low = rg.astype(BF16)
    low_out[...] = low
    dmix_scr[...] = dot_nt(low, proj_w[1]).astype(BF16)
    sums_out[...] = jnp.zeros(sums_out.shape, F32)
    attend_back(
        qkv_scr, probs_scr, dmix_scr, field_out, sums_out, low_scr, prob_scr, width
    )
    ng = dot_nt(field_out[...], qkv_w[1]).astype(BF16).astype(F32)
    stand1, inv1 = standardize(x)
    part, gain_one = norm_back(ng, gains[1, 0:1, :], stand1, inv1)
    dx = rg + part
    head_out[...] = dx[0 : rows - cut, :].astype(BF16)
    tail_out[...] = dx[rows - cut :, :].astype(BF16)
    gain_out[0:1, :] = gain_one
    gain_out[1:2, :] = gain_two


def outer_kernel(
    n1, field, mixed, low, n2, hg, active, g, sums,
    keep, give, bias_out,
    m576, m192, m768, mdown, flat_scr,
):
    put(m576, slice(None), dot_tn(n1[...], field[...]))
    at = flat_store(flat_scr, 0, m576, field.shape[1])
    put(m192, slice(None), dot_tn(mixed[...], low[...]))
    at += flat_store(flat_scr, at, m192, mixed.shape[1])
    put(m768, slice(None), dot_tn(n2[...], hg[...]))
    at += flat_store(flat_scr, at, m768, active.shape[1])
    put(mdown, slice(None), dot_tn(active[...], g[...]))
    at += flat_store(flat_scr, at, mdown, mixed.shape[1])
    halves(flat_scr, lax.axis_index("lat"), keep, give)
    bias_units(sums, bias_out)


def lat_sums(*refs):
    out = refs[-1]
    at = 0
    for k in range(0, len(refs) - 2, 2):
        keep, got = refs[k], refs[k + 1]
        count = keep.shape[1]
        out[:, at : at + count] = (keep[...].astype(F32) + got[...].astype(F32)).astype(BF16)
        at += count
    out[:, at:] = refs[-2][...]


def lat_sums_split(*refs):
    keep_out, give_out = refs[-2:]
    x = lax.rem(lax.axis_index("lon"), 2)
    for out, side in ((keep_out, x), (give_out, 1 - x)):
        for z in range(out.shape[0]):
            j = 2 * z + side
            at = 0
            for k in range(0, len(refs) - 3, 2):
                keep, got = refs[k], refs[k + 1]
                count = keep.shape[1]
                total = keep[j].astype(F32) + got[j].astype(F32)
                out[z, at : at + count] = total.astype(BF16)
                at += count
            out[z, at:] = refs[-3][j]


def add_pair(keep, got, order, out):
    out[...] = (keep[...].astype(F32) + got[...].astype(F32)).astype(BF16)


def sum_pieces(pieces, order, out):
    total = pieces[0].astype(F32)
    for k in range(1, pieces.shape[0]):
        total = total + pieces[k].astype(F32)
    total = total.astype(BF16)
    if len(out.shape) == len(pieces.shape):
        for k in range(out.shape[0]):
            out[k] = total
    else:
        out[...] = total


def join_z(*refs):
    out = refs[-1]
    count = out.shape[0]
    z = lax.div(lax.axis_index("lon"), 2)
    for k in range(count):
        out[lax.rem(z + count - k, count)] = refs[k][...]


def third_kernel(
    head, lon_tail, lat_head, diag_tail, resid, slope, active, mixed,
    proj_w, up_w, down_w, gains, order,
    keep_out, give_out, rg_out, dmix_out, gain_out,
    scr_own, scr_oth, m192, m768, mdown, flat_scr,
):
    rows, width = scr_own.shape
    cut = CHUNK * (WLON // 2)
    scr_own[0:cut, :] = lon_tail[...].astype(F32)
    scr_own[cut:, :] = head[...].astype(F32)
    scr_oth[0:cut, :] = diag_tail[...].astype(F32)
    scr_oth[cut:, :] = lat_head[...].astype(F32)
    g = merge_behind(scr_own, scr_oth, rows)
    g_low = g.astype(BF16)
    hg = dot(g_low, down_w[0])
    stand2, inv2 = standardize(resid[...].astype(F32))
    normed2 = (stand2 * gains[0, 1:2, :]).astype(BF16)
    hg = (hg * slope[...].astype(F32)).astype(BF16)
    part, gain_two = norm_back(dot_nt(hg, up_w[0]), gains[0, 1:2, :], stand2, inv2)
    rg = g + part
    rg_out[...] = rg
    low = rg.astype(BF16)
    dmix_out[...] = dot_nt(low, proj_w[0]).astype(BF16)
    gain_out[...] = gain_two
    put(m192, slice(None), dot_tn(mixed[...], low))
    at = flat_store(flat_scr, 0, m192, mixed.shape[1])
    put(m768, slice(None), dot_tn(normed2, hg))
    at += flat_store(flat_scr, at, m768, active.shape[1])
    put(mdown, slice(None), dot_tn(active[...], g_low))
    at += flat_store(flat_scr, at, mdown, mixed.shape[1])
    flat_scr[at:, :] = jnp.zeros((flat_scr.shape[0] - at, 128), F32)
    halves(flat_scr, lax.axis_index("lat"), keep_out, give_out)


def gain_rows(one, two):
    return jnp.concatenate(
        [
            one[:, 0:128],
            jnp.concatenate([one[:, 128:192], two[:, 0:64]], axis=1),
            two[:, 64:192],
        ],
        axis=0,
    )


def fourth_kernel(
    x_in, qkv, probs, dmix, rg, gain_two, gains_late, qkv_w, gains,
    tokens_out, keep, give, bias_out,
    field, sums, m576, flat_scr, dx_scr, low_scr, prob_scr,
):
    width = x_in.shape[-1]
    levels, lats, lons = tokens_out.shape[:3]
    sums[...] = jnp.zeros(sums.shape, F32)
    attend_back(qkv, probs, dmix, field, sums, low_scr, prob_scr, width)
    stand1, inv1 = standardize(x_in[...].astype(F32))
    normed = (stand1 * gains[0, 0:1, :]).astype(BF16)
    ng = dot_nt(field[...], qkv_w[0]).astype(BF16).astype(F32)
    part, gain_one = norm_back(ng, gains[0, 0:1, :], stand1, inv1)
    put(m576, slice(None), dot_tn(normed, field[...]))
    at = flat_store(flat_scr, 0, m576, field.shape[1])
    flat_scr[at:, :] = jnp.zeros((flat_scr.shape[0] - at, 128), F32)
    flat_scr[at : at + 3, :] = gain_rows(gain_one, gain_two[...])
    flat_scr[at + 3 : at + 6, :] = gain_rows(gains_late[0:1, :], gains_late[1:2, :])
    bias_units(sums, bias_out)
    halves(flat_scr, lax.axis_index("lat"), keep, give)
    put(dx_scr, slice(None), rg[...] + part)
    for z in range(levels):
        for a in range(lats):
            tokens_out[z, a] = get(
                dx_scr, pl.ds(z * lats + a, lons, stride=CHUNK), width
            ).astype(BF16)


def place(pieces, first, last, dests, scr):
    total = jnp.zeros((UNIT, 128), F32)
    lons = pieces.shape[1]
    per = last - first
    k = 0
    for where, room in dests:
        for at in range(where, where + room, UNIT):
            half, j, u = k // (per * lons), k // per % lons, k % per
            value = pieces[half, j, first + u].astype(F32)
            scr[at : at + UNIT, :] = value
            total = total + value * value
            k += 1
    return total


def bias_rows(piece, base, spread, out, rows_scr, wide_scr, tab_scr):
    lat = lax.axis_index("lat")
    extra = -(-BIAS_UNITS // piece.shape[1])

    def read(at):
        parts = []
        for r in range(CHUNK // UNIT):
            k = at * (CHUNK // UNIT) + r
            parts.append(piece[lat, k // extra, base + k % extra].astype(F32))
        return jnp.concatenate(parts, axis=0)

    rest = read(2 * HEADS)
    for h in range(HEADS):
        rows = pl.ds(h, CHUNK, stride=8)
        wide_scr[0, rows, :] = read(h)
        wide_scr[1, rows, :] = read(HEADS + h)
        wide_scr[2, rows, :] = rest if h == 0 else pltpu.roll(rest, 128 - 8 * h, axis=1)
    low = get(wide_scr, slice(None), WIDE).astype(BF16)
    for zj in range(LEVELS):
        rows_scr[...] = dot_nt(low, spread[zj])
        for zi in range(LEVELS):
            for ai in range(WLAT):
                at = ((zi * LEVELS + zj) * WLAT + ai) * PAIR
                row = (zi * WLAT + ai) * 8
                tab_scr[0:HEADS, at : at + PAIR] = rows_scr[row : row + HEADS, 0:PAIR]
    for h in range(HEADS):
        out[h] = tab_scr[h : h + 1, :]


def late_kernel(
    units_a, spread, same, same_x, cross, cross_x, flat_out, squares_out, bias_out,
    rows_scr, wide_scr, tab_scr, a,
):
    lat = lax.axis_index("lat")
    x = lax.rem(lax.axis_index("lon"), 2)
    for z in range(same.shape[0]):
        a[lat, 2 * z + x] = same[z]
        a[lat, 2 * z + 1 - x] = same_x[z]
        a[1 - lat, 2 * z + x] = cross[z]
        a[1 - lat, 2 * z + 1 - x] = cross_x[z]
    squares_out[...] = place(a, 0, units_a, [(0, flat_out.shape[0])], flat_out)
    bias_rows(a, units_a, spread, bias_out, rows_scr, wide_scr, tab_scr)


def last_kernel(
    units_b, units_c, spread, flat_a, squares, bias_late, own_bc, oth_bc, update_out, bias_out,
    scr, rows_scr, wide_scr, tab_scr, bc,
):
    lat = lax.axis_index("lat")
    for j in range(own_bc.shape[0]):
        bc[lat, j] = own_bc[j]
        bc[1 - lat, j] = oth_bc[j]
    total = squares[...]
    total = total + place(bc, 0, units_b, [(864, 288), (1152, 1152), (2304, 1152)], scr)
    total = total + place(bc, units_b, units_b + units_c, [(0, 864), (3456, 8)], scr)
    count = update_out.shape[0]
    mean = jnp.sum(total) * (1.0 / (count * 128))
    scale = lax.rsqrt(mean + 1e-06)
    early, late = (0, 1728, 2304, 4608), (864, 2016, 3456, 5760)
    at = 0
    for first, second, rows in zip(early, late, (864, 288, 1152, 1152)):
        update_out[first : first + rows, :] = (scr[at : at + rows, :] * scale).astype(BF16)
        update_out[second : second + rows, :] = (flat_a[at : at + rows, :] * scale).astype(BF16)
        at += rows
    update_out[6912:count, :] = (scr[at : at + count - 6912, :] * scale).astype(BF16)
    bias_rows(bc, units_b + units_c, spread, bias_out.at[0], rows_scr, wide_scr, tab_scr)
    bias_out[1] = bias_late[...]


def call(kernel, outs, scratch, args, micros, mib, spaces=None, near=(), kept=0):
    spaces = spaces or [pltpu.VMEM] * len(args)
    return pl.pallas_call(
        kernel,
        out_shape=[
            (pltpu.VMEM if at in near else jax.ShapeDtypeStruct)(*entry)
            for at, entry in enumerate(outs)
        ],
        in_specs=[pl.BlockSpec(memory_space=space) for space in spaces],
        out_specs=[
            pl.BlockSpec(memory_space=pltpu.VMEM if at < len(outs) - kept else pl.ANY)
            for at in range(len(outs))
        ],
        input_output_aliases={
            len(args) - kept + k: len(outs) - kept + k for k in range(kept)
        },
        scratch_shapes=[
            pltpu.VMEM(*entry) if isinstance(entry, tuple) else entry for entry in scratch
        ],
        compiler_params=pltpu.CompilerParams(vmem_limit_bytes=mib * MIB),
        cost_estimate=pl.CostEstimate(
            flops=int(micros * 1.1e9), bytes_accessed=10**5, transcendentals=0
        ),
    )(*args)


def lat_swap(value):
    return lax.ppermute(value, "lat", [(0, 1), (1, 0)])


def lon_send(value, step):
    count = lax.axis_size("lon")
    return lax.ppermute(value, "lon", [(s, (s + step) % count) for s in range(count)])


def x_swap(value):
    count = lax.axis_size("lon")
    return lax.ppermute(value, "lon", [(s, s ^ 1) for s in range(count)])


def diag_send(value, step):
    count = lax.axis_size("lon")
    pairs = []
    for s in range(count):
        for t in range(2):
            pairs.append((2 * s + t, 2 * ((s + step) % count) + 1 - t))
    return lax.ppermute(value, ("lon", "lat"), pairs)


def shards(
    tokens, cotangent, qkv_weight, proj_weight, up_weight, down_weight, norm_gain, bias_table
):
    levels, lats, lons, width = tokens.shape
    rows = levels * lats * lons
    wins = rows // WIN
    hid = up_weight.shape[-1]
    heads = bias_table.shape[2]
    lon_size = lax.axis_size("lon")
    zs = lon_size // 2
    lat_total = lats * lax.axis_size("lat")
    cut = CHUNK * (WLON // 2)
    spread = jnp.asarray(spread_matrices(), BF16)
    down_turned = jnp.swapaxes(down_weight, 1, 2)
    table = jnp.swapaxes(bias_table, 1, 2)
    token = (rows, width)
    field_shape = ((rows, 3 * width), BF16)
    probs_shape = ((wins, heads, WIN, WIN), F32)
    stack_shape = ((heads * WIN, WIN), BF16)
    bias_shape = ((heads * WIN, WIN), F32)
    sums_shape = ((heads * WIN, WIDE), F32)
    tab_scr = ((8, table.shape[-1]), F32)
    rows_scr = ((LEVELS * CHUNK * 8, PAIR), F32)
    wide_scr = ((WIDE // 128, CHUNK * 8, 128), F32)
    tiles = -(-width // 128)
    token_scr = ((tiles, rows, 128), F32)
    m576 = ((-(-3 * width // 128), width, 128), F32)
    m192 = ((tiles, width, 128), F32)
    m768 = ((hid // 128, width, 128), F32)
    mdown = ((tiles, hid, 128), F32)

    block_rows = (qkv_weight[0].size + proj_weight[0].size + 2 * up_weight[0].size) // 128
    qkv_rows = qkv_weight[0].size // 128
    counts = (block_rows, block_rows - qkv_rows, qkv_rows + 8)
    units_a, units_b, units_c = [-(-count // (2 * lon_size * UNIT)) for count in counts]
    extra = -(-BIAS_UNITS // lon_size)

    def units(*lead):
        return (lead + (UNIT, 128), BF16)

    def flat_scr(per):
        return ((2 * lon_size * per * UNIT, 128), F32)

    x0, tail, head, qkv0, mixed0, probs0, resid0, hidden0, active0 = call(
        functools.partial(first_kernel, lat_total),
        [
            (token, BF16),
            ((2, rows - cut, width), BF16),
            ((2, cut, width), BF16),
            field_shape,
            (token, BF16),
            probs_shape,
            (token, BF16),
            ((rows, hid), F32),
            ((rows, hid), BF16),
        ],
        [
            token_scr,
            token_scr,
            tab_scr,
            rows_scr,
            wide_scr,
            bias_shape,
            (cotangent.shape, BF16),
            ((1,) + table.shape[1:], F32),
            (spread.shape, BF16),
            (tokens.shape, BF16),
            ((1,) + qkv_weight.shape[1:], BF16),
            (norm_gain.shape, F32),
            ((1,) + proj_weight.shape[1:], BF16),
            ((1,) + up_weight.shape[1:], BF16),
            ((1,) + down_turned.shape[1:], BF16),
            stack_shape,
            pltpu.SemaphoreType.DMA((9,)),
        ],
        [
            pltpu.with_memory_space_constraint(arg, pltpu.HBM)
            for arg in (
                tokens, cotangent, table, spread, qkv_weight, proj_weight, up_weight, down_turned,
                norm_gain,
            )
        ],
        8,
        16,
        [pltpu.HBM] * 9,
        near=(0, 3, 4, 5, 6, 8),
    )
    lon_head = lon_send(head, -1)
    diag_head = diag_send(head, -1)
    lat_tail = lat_swap(tail)
    bias1, slope0 = call(
        functools.partial(bias_kernel, lat_total),
        [bias_shape, ((rows, hid), BF16)],
        [tab_scr, rows_scr, wide_scr],
        (table, spread, hidden0),
        3,
        12,
        near=(1,),
    )

    saved = [x0, qkv0, mixed0, probs0, resid0, active0, slope0]
    (
        dhead, dtail, n1, field1, mixed1, low1, n2, hg1, active1, g1, sums1, gains1,
        *saved,
    ) = call(
        functools.partial(second_kernel, lat_total, len(saved)),
        [
            ((rows - cut, width), BF16),
            ((cut, width), BF16),
            (token, BF16),
            field_shape,
            (token, BF16),
            (token, BF16),
            (token, BF16),
            ((rows, hid), BF16),
            ((rows, hid), BF16),
            (token, BF16),
            sums_shape,
            ((2, width), F32),
            *[(value.shape, value.dtype) for value in saved],
        ],
        [
            (token, F32),
            (token, F32),
            field_shape,
            probs_shape,
            (token, BF16),
            stack_shape,
            stack_shape,
        ],
        (
            tail, lon_head, lat_tail, diag_head, bias1, qkv_weight, proj_weight, up_weight,
            down_turned, norm_gain,
            *[pltpu.with_memory_space_constraint(value, pltpu.VMEM) for value in saved],
        ),
        19,
        16,
        [pltpu.VMEM] * 10 + [pl.ANY] * len(saved),
        near=tuple(range(12, 12 + len(saved))),
        kept=len(saved),
    )
    x0, qkv0, mixed0, probs0, resid0, active0, slope0 = saved
    lon_tail = lon_send(dtail, 1)
    diag_tail = diag_send(dtail, 1)
    lat_dhead = lat_swap(dhead)

    keep_a, give_a, bias_a = call(
        outer_kernel,
        [units(lon_size, units_a), units(lon_size, units_a), units(lon_size, extra)],
        [m576, m192, m768, mdown, flat_scr(units_a)],
        (n1, field1, mixed1, low1, n2, hg1, active1, g1, sums1),
        3,
        14,
    )
    got_a = lat_swap(give_a)

    (part_a,) = call(
        lat_sums, [units(lon_size, units_a + extra)], [], (keep_a, got_a, bias_a), 1, 10
    )
    pieces_a = lax.all_to_all(part_a, "lon", 0, 0)

    keep_b, give_b, rg0, dmix0, gain_two = call(
        third_kernel,
        [
            units(lon_size, units_b),
            units(lon_size, units_b),
            (token, F32),
            (token, BF16),
            ((1, width), F32),
        ],
        [(token, F32), (token, F32), m192, m768, mdown, flat_scr(units_b)],
        (
            dhead, lon_tail, lat_dhead, diag_tail, resid0, slope0, active0, mixed0, proj_weight,
            up_weight, down_turned, norm_gain, part_a,
        ),
        3,
        14,
    )
    got_b = lat_swap(give_b)

    tokens_grad, keep_c, give_c, bias_c = call(
        fourth_kernel,
        [
            (tokens.shape, BF16),
            units(lon_size, units_c),
            units(lon_size, units_c),
            units(lon_size, extra),
        ],
        [
            field_shape,
            sums_shape,
            m576,
            flat_scr(units_c),
            token_scr,
            stack_shape,
            stack_shape,
        ],
        (x0, qkv0, probs0, dmix0, rg0, gain_two, gains1, qkv_weight, norm_gain),
        7,
        14,
    )
    got_c = lat_swap(give_c)
    units_bc = units_b + units_c + extra
    keep_x, give_x = call(
        lat_sums_split,
        [units(zs, units_bc)] * 2,
        [],
        (keep_b, got_b, keep_c, got_c, bias_c),
        1,
        10,
    )
    got_x = x_swap(give_x)
    (sum_a,) = call(sum_pieces, [units(units_a + extra)], [], (pieces_a, keep_x), 1, 10)
    moved_a = [lon_send(sum_a, 2 * k) for k in range(1, zs)]
    (part_z,) = call(add_pair, [units(zs, units_bc)], [], (keep_x, got_x, moved_a[0]), 1, 10)
    pieces_bc = lax.all_to_all(
        part_z,
        "lon",
        0,
        0,
        axis_index_groups=[[2 * z + x for z in range(zs)] for x in range(2)],
    )

    (same,) = call(join_z, [units(zs, units_a + extra)], [], [sum_a, *moved_a, part_z], 1, 10)
    same_x = x_swap(same)
    cross = lat_swap(same)
    cross_x = lat_swap(same_x)
    (sum_bc,) = call(
        sum_pieces,
        [units(lon_size, units_bc)],
        [],
        (pieces_bc, same_x),
        1,
        10,
    )
    whole_bc = lax.all_to_all(sum_bc, "lon", 0, 0)
    oth_bc = lat_swap(whole_bc)

    flat_rows = (2 * block_rows * 128 + norm_gain.size) // 128
    fold_scr = [((CHUNK * 8, PAIR), F32), wide_scr, tab_scr]
    flat_a, squares, bias_late = call(
        functools.partial(late_kernel, units_a),
        [((block_rows, 128), F32), ((UNIT, 128), F32), (table.shape[1:], F32)],
        [*fold_scr, units(2, lon_size, units_a + extra)],
        (spread, same, same_x, cross, cross_x),
        2,
        14,
    )
    update, bias_grad = call(
        functools.partial(last_kernel, units_b, units_c),
        [((flat_rows, 128), BF16), (table.shape, F32)],
        [
            ((block_rows + 8, 128), F32),
            *fold_scr,
            units(2, lon_size, units_b + units_c + extra),
        ],
        (spread, flat_a, squares, bias_late, whole_bc, oth_bc),
        2,
        14,
    )
    bias_grad = jnp.swapaxes(bias_grad, 1, 2)
    return (tokens_grad, update.reshape(-1), bias_grad)


def solution(mesh):
    return jax.shard_map(
        shards,
        mesh=mesh,
        in_specs=(
            P("grp", "lat", "lon", None),
            P("grp", "lat", "lon", None),
            P(),
            P(),
            P(),
            P(),
            P(),
            P(None, "lat", None, None),
        ),
        out_specs=(P("grp", "lat", "lon", None), P("grp"), P("grp", "lat", None, None)),
        check_vma=False,
    )
```

```python
import functools

import jax
import jax.numpy as jnp
import numpy as np
from jax import lax
from jax.experimental import pallas as pl
from jax.experimental.pallas import tpu as pltpu
from jax.sharding import PartitionSpec as P

WLAT = 12
WLON = 6
PAD = 5
LEVELS = 2
HEADS = 6
CHUNK = LEVELS * WLAT
WIN = CHUNK * WLON
SHIFTS = 2 * WLON - 1
PAIR = WLAT * SHIFTS
WIDE = 384

EPS = 1e-05
NEGATIVE = -1000000000.0
ROOT_HALF = 0.7071067811865476
INV_ROOT_TAU = 0.3989422804014327

F32 = jnp.float32
BF16 = jnp.bfloat16
UNIT = 8
BIAS_UNITS = (2 * HEADS + 1) * CHUNK // UNIT
MIB = 1024 * 1024


def dot(a, b):
    return lax.dot_general(a, b, (((1,), (0,)), ((), ())), preferred_element_type=F32)


def dot_nt(a, b):
    return lax.dot_general(a, b, (((1,), (1,)), ((), ())), preferred_element_type=F32)


def dot_tn(a, b):
    return lax.dot_general(a, b, (((0,), (0,)), ((), ())), preferred_element_type=F32)


def row_mean(v):
    return jnp.sum(v, axis=-1, keepdims=True) * (1.0 / v.shape[-1])


def standardize(x):
    centred = x - row_mean(x)
    inv = lax.rsqrt(row_mean(centred * centred) + EPS)
    return centred * inv, inv


def norm_back(d, gain, stand, inv):
    scaled = d * gain
    first = row_mean(scaled)
    second = row_mean(scaled * stand)
    gain_grad = jnp.sum(d * stand, axis=0, keepdims=True)
    return inv * (scaled - first - stand * second), gain_grad


def gelu_value(hidden):
    return 0.5 * hidden * (1.0 + lax.erf(hidden * ROOT_HALF))


def gelu_parts(hidden):
    half = 0.5 * (1.0 + lax.erf(hidden * ROOT_HALF))
    slope = half + hidden * jnp.exp(-0.5 * hidden * hidden) * INV_ROOT_TAU
    return hidden * half, slope


def split3(v):
    hi = v.astype(BF16)
    rest = v - hi.astype(F32)
    mid = rest.astype(BF16)
    low = (rest - mid.astype(F32)).astype(BF16)
    return hi, mid, low


def spread_matrices():
    out = np.zeros((LEVELS, PAIR, WIDE), np.float32)
    for zj in range(LEVELS):
        for aj in range(WLAT):
            for d in range(SHIFTS):
                out[zj, aj * SHIFTS + d, (SHIFTS - 1 - d) * CHUNK + zj * WLAT + aj] = 1.0
    return out


def put(scr, rows, value):
    width = value.shape[1]
    for tile in range(-(-width // 128)):
        lanes = min(128, width - tile * 128)
        scr[tile, rows, 0:lanes] = value[:, tile * 128 : tile * 128 + lanes]


def get(scr, rows, width):
    parts = [scr[tile, rows, :] for tile in range(-(-width // 128))]
    return jnp.concatenate(parts, axis=1)[:, 0:width]


def head_masks(width, dtype):
    lane = lax.broadcasted_iota(jnp.int32, (1, width), 1)
    size = width // HEADS
    return [((lane >= h * size) & (lane < (h + 1) * size)).astype(dtype) for h in range(HEADS)]


def lat_inside(n):
    return lax.rem(n, WLAT)


def lat_row(row_iota, lat, shifted, lat_total):
    row = lat * WLAT + lat_inside(row_iota)
    if shifted:
        row = row + WLAT // 2
        row = jnp.where(row >= lat_total, row - lat_total, row)
    return row


def expand_bias(table, spread, tab_scr, rows_scr, wide_scr, bias_scr, lat, shifted, lat_total):
    for h in range(HEADS):
        tab_scr[h : h + 1, :] = table[h]
    for zi in range(LEVELS):
        for zj in range(LEVELS):
            for ai in range(WLAT):
                at = ((zi * LEVELS + zj) * WLAT + ai) * PAIR
                row = zj * CHUNK * 8 + (zi * WLAT + ai) * 8
                rows_scr[row : row + HEADS, 0:PAIR] = tab_scr[0:HEADS, at : at + PAIR]
    count = CHUNK * 8
    total = jnp.zeros((count, WIDE), F32)
    for zj in range(LEVELS):
        parts = split3(rows_scr[zj * count : (zj + 1) * count, 0:PAIR])
        for part in parts:
            total = total + dot(part, spread[zj])
    put(wide_scr, slice(None), total)
    i = lax.broadcasted_iota(jnp.int32, (CHUNK, WIN), 0)
    j = lax.broadcasted_iota(jnp.int32, (CHUNK, WIN), 1)
    allowed = lat_row(j, lat, shifted, lat_total) < lat_total - PAD
    if shifted:
        last = lat_total - WLAT // 2
        region_i = (lat * WLAT + lat_inside(i)) >= last
        region_j = (lat * WLAT + lat_inside(j)) >= last
        allowed = allowed & (region_i == region_j)
    for h in range(HEADS):
        wide = get(wide_scr, pl.ds(h, CHUNK, stride=8), WIDE)
        for oi in range(WLON):
            back = (WLON - 1 - oi) * CHUNK
            moved = wide if back == 0 else pltpu.roll(wide, WIDE - back, axis=1)
            at = h * WIN + oi * CHUNK
            bias_scr[at : at + CHUNK, :] = jnp.where(allowed, moved[:, 0:WIN], NEGATIVE)


def fold_bias(sums, put_unit):
    rest = jnp.zeros((CHUNK, 128), F32)

    def emit(at, value):
        for r in range(CHUNK // UNIT):
            put_unit(at * (CHUNK // UNIT) + r, value[r * UNIT : (r + 1) * UNIT, :].astype(BF16))

    for h in range(HEADS):
        total = jnp.zeros((CHUNK, WIDE), F32)
        for oi in range(WLON):
            back = (WLON - 1 - oi) * CHUNK
            at = h * WIN + oi * CHUNK
            part = sums[at : at + CHUNK, :]
            total = total + (part if back == 0 else pltpu.roll(part, back, axis=1))
        emit(h, total[:, 0:128])
        emit(HEADS + h, total[:, 128:256])
        last = total[:, 256:384]
        rest = rest + (last if h == 0 else pltpu.roll(last, 8 * h, axis=1))
    emit(2 * HEADS, rest)

def stack_heads(v, masks):
    return jnp.concatenate([v * mask for mask in masks], axis=0)


def pick_heads(v, masks):
    total = v[0:WIN] * masks[0]
    for h in range(1, HEADS):
        total = total + v[h * WIN : (h + 1) * WIN] * masks[h]
    return total


def attend(qkv, bias, mixed, probs, stack_scr, width):
    masks = head_masks(width, BF16)
    masks32 = head_masks(width, F32)
    scale = (width // HEADS) ** -0.5

    def window(w, carry):
        rows = pl.ds(pl.multiple_of(w * WIN, 16), WIN)
        q = qkv[rows, 0:width]
        k = qkv[rows, width : 2 * width]
        v = qkv[rows, 2 * width : 3 * width]
        scores = dot_nt(stack_heads(q, masks), k)
        for h in range(HEADS):
            part = slice(h * WIN, (h + 1) * WIN)
            logits = scores[part] * scale + bias[part, :]
            weights = jnp.exp(logits - jnp.max(logits, axis=-1, keepdims=True))
            p = weights * (1.0 / jnp.sum(weights, axis=-1, keepdims=True))
            probs[w, h] = p
            stack_scr[part, :] = p.astype(BF16)
        mixed[rows, :] = pick_heads(dot(stack_scr[...], v), masks32).astype(BF16)
        return carry

    lax.fori_loop(0, probs.shape[0], window, 0, unroll=True)


def attend_back(qkv, probs, dmix, field, sums, low_scr, prob_scr, width):
    masks = head_masks(width, BF16)
    masks32 = head_masks(width, F32)
    scale = (width // HEADS) ** -0.5

    def window(w, carry):
        rows = pl.ds(pl.multiple_of(w * WIN, 16), WIN)
        q = qkv[rows, 0:width]
        k = qkv[rows, width : 2 * width]
        v = qkv[rows, 2 * width : 3 * width]
        up = stack_heads(dmix[rows, :], masks)
        prob_grad = dot_nt(up, v)
        for h in range(HEADS):
            part = slice(h * WIN, (h + 1) * WIN)
            p = probs[w, h]
            weighted = p * prob_grad[part]
            ds = weighted - p * jnp.sum(weighted, axis=-1, keepdims=True)
            sums[part, 0:WIN] += ds
            low_scr[part, :] = ds.astype(BF16)
            prob_scr[part, :] = p.astype(BF16)
        low = low_scr[...]
        dq = pick_heads(dot(low, k), masks32)
        dk = dot_tn(low, stack_heads(q, masks))
        dv = dot_tn(prob_scr[...], up)
        field[rows, 0:width] = (dq * scale).astype(BF16)
        field[rows, width : 2 * width] = (dk * scale).astype(BF16)
        field[rows, 2 * width : 3 * width] = dv.astype(BF16)
        return carry

    lax.fori_loop(0, probs.shape[0], window, 0, unroll=True)


def lon_major(src, scr):
    levels, lats, lons, width = src.shape
    for z in range(levels):
        for a in range(lats):
            at = (z * lats + a) * lons
            put(scr, slice(at, at + lons), src[z, a].astype(F32))


def lon_column(scr, lon, lons, width):
    return get(scr, pl.ds(lon, CHUNK, stride=lons), width)


def flat_store(dst, at, mat, cols):
    rows = mat.shape[1]
    if cols % 128 == 0:
        per = cols // 128
        for c in range(per):
            dst[pl.ds(at + c, rows, stride=per), :] = mat[c]
        return rows * per
    per = 2 * cols // 128
    half = cols // 128
    even = get(mat, pl.ds(0, rows // 2, stride=2), cols)
    odd = get(mat, pl.ds(1, rows // 2, stride=2), cols)
    for c in range(half):
        dst[pl.ds(at + c, rows // 2, stride=per), :] = even[:, c * 128 : (c + 1) * 128]
    dst[pl.ds(at + half, rows // 2, stride=per), :] = jnp.concatenate(
        [even[:, half * 128 : half * 128 + 64], odd[:, 0:64]], axis=1
    )
    for c in range(half):
        dst[pl.ds(at + half + 1 + c, rows // 2, stride=per), :] = odd[
            :, 64 + c * 128 : 64 + (c + 1) * 128
        ]
    return rows * cols // 128


def send_units(scr, base, out):
    lons, units = out.shape[:2]
    for j in range(lons):
        for u in range(units):
            at = base + (j * units + u) * UNIT
            if not isinstance(at, int):
                at = pl.multiple_of(at, UNIT)
            out[j, u] = scr[pl.ds(at, UNIT), :].astype(BF16)


def halves(scr, lat, keep, give):
    half = keep.shape[0] * keep.shape[1] * UNIT
    send_units(scr, lat * half, keep)
    send_units(scr, (1 - lat) * half, give)


def bias_units(sums, out):
    lons, per = out.shape[:2]

    def put_unit(k, value):
        out[k // per, k % per] = value

    fold_bias(sums, put_unit)
    for k in range(BIAS_UNITS, lons * per):
        put_unit(k, jnp.zeros((UNIT, 128), BF16))

def forward_core(x, b, refs, qkv_scr, bias_scr, mixed, probs, stack_scr):
    qkv_w, proj_w, gains = refs
    width = x.shape[-1]
    stand, inv = standardize(x)
    normed = (stand * gains[b, 0:1, :]).astype(BF16)
    qkv_scr[...] = dot(normed, qkv_w[b]).astype(BF16)
    attend(qkv_scr, bias_scr, mixed, probs, stack_scr, width)
    att = dot(mixed[...], proj_w[b]).astype(BF16)
    resid = (x + att.astype(F32)).astype(BF16).astype(F32)
    return resid, normed


def first_kernel(
    lat_total, tokens_in, cot_in, table_in, spread_in, qkv_in, proj_in, up_in, down_in, gains_in,
    x_out, tail_out, head_out, qkv_out, mixed_out, probs_out, resid_out, hidden_out, active_out,
    scr, cot_scr, tab_scr, rows_scr, wide_scr, bias_scr,
    cot, table, spread, tokens, qkv_w, gains, proj_w, up_w, down_w, stack_scr, sems,
):
    copies = []
    for source, target in (
        (cot_in, cot),
        (table_in.at[0:1], table),
        (spread_in, spread),
        (tokens_in, tokens),
        (qkv_in.at[0:1], qkv_w),
        (gains_in, gains),
        (proj_in.at[0:1], proj_w),
        (up_in.at[0:1], up_w),
        (down_in.at[0:1], down_w),
    ):
        copies.append(pltpu.make_async_copy(source, target, sems.at[len(copies)]))
    for copy in copies:
        copy.start()
    lat = lax.axis_index("lat")
    width = tokens.shape[-1]
    lons = tokens.shape[2]
    cut = CHUNK * (WLON // 2)
    copies[0].wait()
    lon_major(cot, cot_scr)
    g = jnp.concatenate([lon_column(cot_scr, lon, lons, width) for lon in range(lons)], axis=0)
    head_out[1] = g[0:cut, :].astype(BF16)
    tail_out[1] = g[cut:, :].astype(BF16)
    copies[1].wait()
    copies[2].wait()
    expand_bias(
        table.at[0], spread, tab_scr, rows_scr, wide_scr, bias_scr, lat, False, lat_total
    )
    copies[3].wait()
    lon_major(tokens, scr)
    x = jnp.concatenate([lon_column(scr, lon, lons, width) for lon in range(lons)], axis=0)
    x_out[...] = x.astype(BF16)
    for copy in copies[4:]:
        copy.wait()

    resid, _ = forward_core(
        x, 0, (qkv_w, proj_w, gains), qkv_out, bias_scr, mixed_out, probs_out, stack_scr
    )
    resid_out[...] = resid.astype(BF16)
    stand, _ = standardize(resid)
    normed = (stand * gains[0, 1:2, :]).astype(BF16)
    hidden = dot(normed, up_w[0])
    hidden_out[...] = hidden
    active = gelu_value(hidden).astype(BF16)
    active_out[...] = active
    result = resid + dot_nt(active, down_w[0])
    head_out[0] = result[0:cut, :].astype(BF16)
    tail_out[0] = result[cut:, :].astype(BF16)


def bias_kernel(
    lat_total, table, spread, hidden, bias_out, slope_out, tab_scr, rows_scr, wide_scr
):
    lat = lax.axis_index("lat")
    slope_out[...] = gelu_parts(hidden[...])[1].astype(BF16)
    expand_bias(
        table.at[1], spread, tab_scr, rows_scr, wide_scr, bias_out, lat, True, lat_total
    )


def merge_ahead(scr_own, scr_oth, rows):
    half = WLAT // 2
    n = lax.broadcasted_iota(jnp.int32, (rows, 1), 0)
    return jnp.where(
        lat_inside(n) < half,
        pltpu.roll(scr_own[...], rows - half, axis=0),
        pltpu.roll(scr_oth[...], half, axis=0),
    )


def merge_behind(scr_own, scr_oth, rows):
    half = WLAT // 2
    n = lax.broadcasted_iota(jnp.int32, (rows, 1), 0)
    return jnp.where(
        lat_inside(n) >= half,
        pltpu.roll(scr_own[...], half, axis=0),
        pltpu.roll(scr_oth[...], rows - half, axis=0),
    )


def second_kernel(
    lat_total,
    kept, tail, lon_head, lat_tail, diag_head, bias, qkv_w, proj_w, up_w, down_w, gains, *rest
):
    run_second(
        lat_total, tail, lon_head, lat_tail, diag_head, bias, qkv_w, proj_w, up_w, down_w, gains,
        *rest[kept:kept + 12], *rest[2 * kept + 12 :]
    )


def run_second(
    lat_total,
    tail, lon_head, lat_tail, diag_head, bias, qkv_w, proj_w, up_w, down_w, gains,
    head_out, tail_out, n1_out, field_out, mixed_out, low_out, n2_out, hg_out, active_out, g_out,
    sums_out, gain_out,
    scr_own, scr_oth, qkv_scr, probs_scr, dmix_scr, low_scr, prob_scr,
):
    lat = lax.axis_index("lat")
    rows, width = scr_own.shape
    cut = CHUNK * (WLON // 2)

    def rolled(which):
        scr_own[0 : rows - cut, :] = tail[which].astype(F32)
        scr_own[rows - cut :, :] = lon_head[which].astype(F32)
        scr_oth[0 : rows - cut, :] = lat_tail[which].astype(F32)
        scr_oth[rows - cut :, :] = diag_head[which].astype(F32)
        return merge_ahead(scr_own, scr_oth, rows)

    g = rolled(1)
    n = lax.broadcasted_iota(jnp.int32, (rows, 1), 0)
    keep = lat_row(n, lat, True, lat_total) < lat_total - PAD
    g = jnp.where(keep, g, 0.0)
    g_out[...] = g.astype(BF16)

    x = rolled(0)

    resid, normed = forward_core(
        x, 1, (qkv_w, proj_w, gains), qkv_scr, bias, mixed_out, probs_scr, low_scr
    )
    n1_out[...] = normed
    stand2, inv2 = standardize(resid)
    normed2 = (stand2 * gains[1, 1:2, :]).astype(BF16)
    n2_out[...] = normed2
    active, slope = gelu_parts(dot(normed2, up_w[1]))
    active_out[...] = active.astype(BF16)

    hg = (dot(g_out[...], down_w[1]) * slope).astype(BF16)
    hg_out[...] = hg
    part, gain_two = norm_back(dot_nt(hg, up_w[1]), gains[1, 1:2, :], stand2, inv2)
    rg = g + part
    low = rg.astype(BF16)
    low_out[...] = low
    dmix_scr[...] = dot_nt(low, proj_w[1]).astype(BF16)
    sums_out[...] = jnp.zeros(sums_out.shape, F32)
    attend_back(
        qkv_scr, probs_scr, dmix_scr, field_out, sums_out, low_scr, prob_scr, width
    )
    ng = dot_nt(field_out[...], qkv_w[1]).astype(BF16).astype(F32)
    stand1, inv1 = standardize(x)
    part, gain_one = norm_back(ng, gains[1, 0:1, :], stand1, inv1)
    dx = rg + part
    head_out[...] = dx[0 : rows - cut, :].astype(BF16)
    tail_out[...] = dx[rows - cut :, :].astype(BF16)
    gain_out[0:1, :] = gain_one
    gain_out[1:2, :] = gain_two


def outer_kernel(
    n1, field, mixed, low, n2, hg, active, g, sums,
    keep, give, bias_out,
    m576, m192, m768, mdown, flat_scr,
):
    put(m576, slice(None), dot_tn(n1[...], field[...]))
    at = flat_store(flat_scr, 0, m576, field.shape[1])
    put(m192, slice(None), dot_tn(mixed[...], low[...]))
    at += flat_store(flat_scr, at, m192, mixed.shape[1])
    put(m768, slice(None), dot_tn(n2[...], hg[...]))
    at += flat_store(flat_scr, at, m768, active.shape[1])
    put(mdown, slice(None), dot_tn(active[...], g[...]))
    at += flat_store(flat_scr, at, mdown, mixed.shape[1])
    halves(flat_scr, lax.axis_index("lat"), keep, give)
    bias_units(sums, bias_out)


def lat_sums_split(*refs):
    keep_out, give_out = refs[-2:]
    x = lax.rem(lax.axis_index("lon"), 2)
    for out, side in ((keep_out, x), (give_out, 1 - x)):
        for z in range(out.shape[0]):
            j = 2 * z + side
            at = 0
            for k in range(0, len(refs) - 3, 2):
                keep, got = refs[k], refs[k + 1]
                count = keep.shape[1]
                total = keep[j].astype(F32) + got[j].astype(F32)
                out[z, at : at + count] = total.astype(BF16)
                at += count
            out[z, at:] = refs[-3][j]


def split_z(keep, got, order, own_out, *give_outs):
    count = keep.shape[0]
    z = lax.div(lax.axis_index("lon"), 2)
    for k, out in enumerate((own_out,) + give_outs):
        at = lax.rem(z + k, count)
        out[...] = (keep[at].astype(F32) + got[at].astype(F32)).astype(BF16)


def sum_refs(*refs):
    total = refs[0][...].astype(F32)
    for ref in refs[1:-2]:
        total = total + ref[...].astype(F32)
    refs[-1][...] = total.astype(BF16)


def add_pair(keep, got, order, out):
    out[...] = (keep[...].astype(F32) + got[...].astype(F32)).astype(BF16)


def sum_pieces(pieces, order, out):
    total = pieces[0].astype(F32)
    for k in range(1, pieces.shape[0]):
        total = total + pieces[k].astype(F32)
    total = total.astype(BF16)
    if len(out.shape) == len(pieces.shape):
        for k in range(out.shape[0]):
            out[k] = total
    else:
        out[...] = total


def join_z(*refs):
    out = refs[-1]
    count = out.shape[0]
    z = lax.div(lax.axis_index("lon"), 2)
    for k in range(count):
        out[lax.rem(z + count - k, count)] = refs[k][...]


def third_kernel(
    head, lon_tail, lat_head, diag_tail, resid, slope, active, mixed,
    proj_w, up_w, down_w, gains, order,
    keep_out, give_out, rg_out, dmix_out, gain_out,
    scr_own, scr_oth, m192, m768, mdown, flat_scr,
):
    rows, width = scr_own.shape
    cut = CHUNK * (WLON // 2)
    scr_own[0:cut, :] = lon_tail[...].astype(F32)
    scr_own[cut:, :] = head[...].astype(F32)
    scr_oth[0:cut, :] = diag_tail[...].astype(F32)
    scr_oth[cut:, :] = lat_head[...].astype(F32)
    g = merge_behind(scr_own, scr_oth, rows)
    g_low = g.astype(BF16)
    hg = dot(g_low, down_w[0])
    stand2, inv2 = standardize(resid[...].astype(F32))
    normed2 = (stand2 * gains[0, 1:2, :]).astype(BF16)
    hg = (hg * slope[...].astype(F32)).astype(BF16)
    part, gain_two = norm_back(dot_nt(hg, up_w[0]), gains[0, 1:2, :], stand2, inv2)
    rg = g + part
    rg_out[...] = rg
    low = rg.astype(BF16)
    dmix_out[...] = dot_nt(low, proj_w[0]).astype(BF16)
    gain_out[...] = gain_two
    put(m192, slice(None), dot_tn(mixed[...], low))
    at = flat_store(flat_scr, 0, m192, mixed.shape[1])
    put(m768, slice(None), dot_tn(normed2, hg))
    at += flat_store(flat_scr, at, m768, active.shape[1])
    put(mdown, slice(None), dot_tn(active[...], g_low))
    at += flat_store(flat_scr, at, mdown, mixed.shape[1])
    flat_scr[at:, :] = jnp.zeros((flat_scr.shape[0] - at, 128), F32)
    halves(flat_scr, lax.axis_index("lat"), keep_out, give_out)


def gain_rows(one, two):
    return jnp.concatenate(
        [
            one[:, 0:128],
            jnp.concatenate([one[:, 128:192], two[:, 0:64]], axis=1),
            two[:, 64:192],
        ],
        axis=0,
    )


def fourth_kernel(
    x_in, qkv, probs, dmix, rg, gain_two, gains_late, qkv_w, gains,
    tokens_out, keep, give, bias_out,
    field, sums, m576, flat_scr, dx_scr, low_scr, prob_scr,
):
    width = x_in.shape[-1]
    levels, lats, lons = tokens_out.shape[:3]
    sums[...] = jnp.zeros(sums.shape, F32)
    attend_back(qkv, probs, dmix, field, sums, low_scr, prob_scr, width)
    stand1, inv1 = standardize(x_in[...].astype(F32))
    normed = (stand1 * gains[0, 0:1, :]).astype(BF16)
    ng = dot_nt(field[...], qkv_w[0]).astype(BF16).astype(F32)
    part, gain_one = norm_back(ng, gains[0, 0:1, :], stand1, inv1)
    put(m576, slice(None), dot_tn(normed, field[...]))
    at = flat_store(flat_scr, 0, m576, field.shape[1])
    flat_scr[at:, :] = jnp.zeros((flat_scr.shape[0] - at, 128), F32)
    flat_scr[at : at + 3, :] = gain_rows(gain_one, gain_two[...])
    flat_scr[at + 3 : at + 6, :] = gain_rows(gains_late[0:1, :], gains_late[1:2, :])
    bias_units(sums, bias_out)
    halves(flat_scr, lax.axis_index("lat"), keep, give)
    put(dx_scr, slice(None), rg[...] + part)
    for z in range(levels):
        for a in range(lats):
            tokens_out[z, a] = get(
                dx_scr, pl.ds(z * lats + a, lons, stride=CHUNK), width
            ).astype(BF16)


def place(pieces, first, last, dests, scr):
    total = jnp.zeros((UNIT, 128), F32)
    lons = pieces.shape[1]
    per = last - first
    k = 0
    for where, room in dests:
        for at in range(where, where + room, UNIT):
            half, j, u = k // (per * lons), k // per % lons, k % per
            value = pieces[half, j, first + u].astype(F32)
            scr[at : at + UNIT, :] = value
            total = total + value * value
            k += 1
    return total


def bias_rows(piece, base, spread, out, rows_scr, wide_scr, tab_scr):
    lat = lax.axis_index("lat")
    extra = -(-BIAS_UNITS // piece.shape[1])

    def read(at):
        parts = []
        for r in range(CHUNK // UNIT):
            k = at * (CHUNK // UNIT) + r
            parts.append(piece[lat, k // extra, base + k % extra].astype(F32))
        return jnp.concatenate(parts, axis=0)

    rest = read(2 * HEADS)
    for h in range(HEADS):
        rows = pl.ds(h, CHUNK, stride=8)
        wide_scr[0, rows, :] = read(h)
        wide_scr[1, rows, :] = read(HEADS + h)
        wide_scr[2, rows, :] = rest if h == 0 else pltpu.roll(rest, 128 - 8 * h, axis=1)
    low = get(wide_scr, slice(None), WIDE).astype(BF16)
    for zj in range(LEVELS):
        rows_scr[...] = dot_nt(low, spread[zj])
        for zi in range(LEVELS):
            for ai in range(WLAT):
                at = ((zi * LEVELS + zj) * WLAT + ai) * PAIR
                row = (zi * WLAT + ai) * 8
                tab_scr[0:HEADS, at : at + PAIR] = rows_scr[row : row + HEADS, 0:PAIR]
    for h in range(HEADS):
        out[h] = tab_scr[h : h + 1, :]


def late_kernel(
    units_a, spread, same, same_x, cross, cross_x, flat_out, squares_out, bias_out,
    rows_scr, wide_scr, tab_scr, a,
):
    lat = lax.axis_index("lat")
    x = lax.rem(lax.axis_index("lon"), 2)
    for z in range(same.shape[0]):
        a[lat, 2 * z + x] = same[z]
        a[lat, 2 * z + 1 - x] = same_x[z]
        a[1 - lat, 2 * z + x] = cross[z]
        a[1 - lat, 2 * z + 1 - x] = cross_x[z]
    squares_out[...] = place(a, 0, units_a, [(0, flat_out.shape[0])], flat_out)
    bias_rows(a, units_a, spread, bias_out, rows_scr, wide_scr, tab_scr)


def last_kernel(
    units_b, units_c, spread, flat_a, squares, bias_late, own_bc, oth_bc, update_out, bias_out,
    scr, rows_scr, wide_scr, tab_scr, bc,
):
    lat = lax.axis_index("lat")
    for j in range(own_bc.shape[0]):
        bc[lat, j] = own_bc[j]
        bc[1 - lat, j] = oth_bc[j]
    total = squares[...]
    total = total + place(bc, 0, units_b, [(864, 288), (1152, 1152), (2304, 1152)], scr)
    total = total + place(bc, units_b, units_b + units_c, [(0, 864), (3456, 8)], scr)
    count = update_out.shape[0]
    mean = jnp.sum(total) * (1.0 / (count * 128))
    scale = lax.rsqrt(mean + 1e-06)
    early, late = (0, 1728, 2304, 4608), (864, 2016, 3456, 5760)
    at = 0
    for first, second, rows in zip(early, late, (864, 288, 1152, 1152)):
        update_out[first : first + rows, :] = (scr[at : at + rows, :] * scale).astype(BF16)
        update_out[second : second + rows, :] = (flat_a[at : at + rows, :] * scale).astype(BF16)
        at += rows
    update_out[6912:count, :] = (scr[at : at + count - 6912, :] * scale).astype(BF16)
    bias_rows(bc, units_b + units_c, spread, bias_out.at[0], rows_scr, wide_scr, tab_scr)
    bias_out[1] = bias_late[...]


def call(kernel, outs, scratch, args, micros, mib, spaces=None, near=(), kept=0):
    spaces = spaces or [pltpu.VMEM] * len(args)
    return pl.pallas_call(
        kernel,
        out_shape=[
            (pltpu.VMEM if at in near else jax.ShapeDtypeStruct)(*entry)
            for at, entry in enumerate(outs)
        ],
        in_specs=[pl.BlockSpec(memory_space=space) for space in spaces],
        out_specs=[
            pl.BlockSpec(memory_space=pltpu.VMEM if at < len(outs) - kept else pl.ANY)
            for at in range(len(outs))
        ],
        input_output_aliases={
            len(args) - kept + k: len(outs) - kept + k for k in range(kept)
        },
        scratch_shapes=[
            pltpu.VMEM(*entry) if isinstance(entry, tuple) else entry for entry in scratch
        ],
        compiler_params=pltpu.CompilerParams(vmem_limit_bytes=mib * MIB),
        cost_estimate=pl.CostEstimate(
            flops=int(micros * 1.1e9), bytes_accessed=10**5, transcendentals=0
        ),
    )(*args)


def lat_swap(value):
    return lax.ppermute(value, "lat", [(0, 1), (1, 0)])


def lon_send(value, step):
    count = lax.axis_size("lon")
    return lax.ppermute(value, "lon", [(s, (s + step) % count) for s in range(count)])


def x_swap(value):
    count = lax.axis_size("lon")
    return lax.ppermute(value, "lon", [(s, s ^ 1) for s in range(count)])


def diag_send(value, step):
    count = lax.axis_size("lon")
    pairs = []
    for s in range(count):
        for t in range(2):
            pairs.append((2 * s + t, 2 * ((s + step) % count) + 1 - t))
    return lax.ppermute(value, ("lon", "lat"), pairs)


def shards(
    tokens, cotangent, qkv_weight, proj_weight, up_weight, down_weight, norm_gain, bias_table
):
    levels, lats, lons, width = tokens.shape
    rows = levels * lats * lons
    wins = rows // WIN
    hid = up_weight.shape[-1]
    heads = bias_table.shape[2]
    lon_size = lax.axis_size("lon")
    zs = lon_size // 2
    lat_total = lats * lax.axis_size("lat")
    cut = CHUNK * (WLON // 2)
    spread = jnp.asarray(spread_matrices(), BF16)
    down_turned = jnp.swapaxes(down_weight, 1, 2)
    table = jnp.swapaxes(bias_table, 1, 2)
    token = (rows, width)
    field_shape = ((rows, 3 * width), BF16)
    probs_shape = ((wins, heads, WIN, WIN), F32)
    stack_shape = ((heads * WIN, WIN), BF16)
    bias_shape = ((heads * WIN, WIN), F32)
    sums_shape = ((heads * WIN, WIDE), F32)
    tab_scr = ((8, table.shape[-1]), F32)
    rows_scr = ((LEVELS * CHUNK * 8, PAIR), F32)
    wide_scr = ((WIDE // 128, CHUNK * 8, 128), F32)
    tiles = -(-width // 128)
    token_scr = ((tiles, rows, 128), F32)
    m576 = ((-(-3 * width // 128), width, 128), F32)
    m192 = ((tiles, width, 128), F32)
    m768 = ((hid // 128, width, 128), F32)
    mdown = ((tiles, hid, 128), F32)

    block_rows = (qkv_weight[0].size + proj_weight[0].size + 2 * up_weight[0].size) // 128
    qkv_rows = qkv_weight[0].size // 128
    counts = (block_rows, block_rows - qkv_rows, qkv_rows + 8)
    units_a, units_b, units_c = [-(-count // (2 * lon_size * UNIT)) for count in counts]
    extra = -(-BIAS_UNITS // lon_size)

    def units(*lead):
        return (lead + (UNIT, 128), BF16)

    def flat_scr(per):
        return ((2 * lon_size * per * UNIT, 128), F32)

    x0, tail, head, qkv0, mixed0, probs0, resid0, hidden0, active0 = call(
        functools.partial(first_kernel, lat_total),
        [
            (token, BF16),
            ((2, rows - cut, width), BF16),
            ((2, cut, width), BF16),
            field_shape,
            (token, BF16),
            probs_shape,
            (token, BF16),
            ((rows, hid), F32),
            ((rows, hid), BF16),
        ],
        [
            token_scr,
            token_scr,
            tab_scr,
            rows_scr,
            wide_scr,
            bias_shape,
            (cotangent.shape, BF16),
            ((1,) + table.shape[1:], F32),
            (spread.shape, BF16),
            (tokens.shape, BF16),
            ((1,) + qkv_weight.shape[1:], BF16),
            (norm_gain.shape, F32),
            ((1,) + proj_weight.shape[1:], BF16),
            ((1,) + up_weight.shape[1:], BF16),
            ((1,) + down_turned.shape[1:], BF16),
            stack_shape,
            pltpu.SemaphoreType.DMA((9,)),
        ],
        [
            pltpu.with_memory_space_constraint(arg, pltpu.HBM)
            for arg in (
                tokens, cotangent, table, spread, qkv_weight, proj_weight, up_weight, down_turned,
                norm_gain,
            )
        ],
        8,
        16,
        [pltpu.HBM] * 9,
        near=(0, 3, 4, 5, 6, 8),
    )
    lon_head = lon_send(head, -1)
    diag_head = diag_send(head, -1)
    lat_tail = lat_swap(tail)
    bias1, slope0 = call(
        functools.partial(bias_kernel, lat_total),
        [bias_shape, ((rows, hid), BF16)],
        [tab_scr, rows_scr, wide_scr],
        (table, spread, hidden0),
        3,
        12,
        near=(1,),
    )

    saved = [x0, qkv0, mixed0, probs0, resid0, active0, slope0]
    (
        dhead, dtail, n1, field1, mixed1, low1, n2, hg1, active1, g1, sums1, gains1,
        *saved,
    ) = call(
        functools.partial(second_kernel, lat_total, len(saved)),
        [
            ((rows - cut, width), BF16),
            ((cut, width), BF16),
            (token, BF16),
            field_shape,
            (token, BF16),
            (token, BF16),
            (token, BF16),
            ((rows, hid), BF16),
            ((rows, hid), BF16),
            (token, BF16),
            sums_shape,
            ((2, width), F32),
            *[(value.shape, value.dtype) for value in saved],
        ],
        [
            (token, F32),
            (token, F32),
            field_shape,
            probs_shape,
            (token, BF16),
            stack_shape,
            stack_shape,
        ],
        (
            tail, lon_head, lat_tail, diag_head, bias1, qkv_weight, proj_weight, up_weight,
            down_turned, norm_gain,
            *[pltpu.with_memory_space_constraint(value, pltpu.VMEM) for value in saved],
        ),
        19,
        16,
        [pltpu.VMEM] * 10 + [pl.ANY] * len(saved),
        near=tuple(range(12, 12 + len(saved))),
        kept=len(saved),
    )
    x0, qkv0, mixed0, probs0, resid0, active0, slope0 = saved
    lon_tail = lon_send(dtail, 1)
    diag_tail = diag_send(dtail, 1)
    lat_dhead = lat_swap(dhead)

    keep_a, give_a, bias_a = call(
        outer_kernel,
        [units(lon_size, units_a), units(lon_size, units_a), units(lon_size, extra)],
        [m576, m192, m768, mdown, flat_scr(units_a)],
        (n1, field1, mixed1, low1, n2, hg1, active1, g1, sums1),
        3,
        14,
    )
    got_a = lat_swap(give_a)

    units_xa = units_a + extra
    keep_xa, give_xa = call(
        lat_sums_split, [units(zs, units_xa)] * 2, [], (keep_a, got_a, bias_a), 1, 10
    )
    got_xa = x_swap(give_xa)

    keep_b, give_b, rg0, dmix0, gain_two = call(
        third_kernel,
        [
            units(lon_size, units_b),
            units(lon_size, units_b),
            (token, F32),
            (token, BF16),
            ((1, width), F32),
        ],
        [(token, F32), (token, F32), m192, m768, mdown, flat_scr(units_b)],
        (
            dhead, lon_tail, lat_dhead, diag_tail, resid0, slope0, active0, mixed0, proj_weight,
            up_weight, down_turned, norm_gain, keep_xa,
        ),
        3,
        14,
    )
    got_b = lat_swap(give_b)

    tokens_grad, keep_c, give_c, bias_c = call(
        fourth_kernel,
        [
            (tokens.shape, BF16),
            units(lon_size, units_c),
            units(lon_size, units_c),
            units(lon_size, extra),
        ],
        [
            field_shape,
            sums_shape,
            m576,
            flat_scr(units_c),
            token_scr,
            stack_shape,
            stack_shape,
        ],
        (x0, qkv0, probs0, dmix0, rg0, gain_two, gains1, qkv_weight, norm_gain),
        7,
        14,
    )
    got_c = lat_swap(give_c)
    units_bc = units_b + units_c + extra
    keep_x, give_x = call(
        lat_sums_split,
        [units(zs, units_bc)] * 2,
        [],
        (keep_b, got_b, keep_c, got_c, bias_c),
        1,
        10,
    )
    got_x = x_swap(give_x)
    own_a, *gives_a = call(
        split_z, [units(units_xa)] * zs, [], (keep_xa, got_xa, keep_x), 1, 10
    )
    gots_a = [lon_send(give, 2 * (k + 1)) for k, give in enumerate(gives_a)]
    (part_z,) = call(add_pair, [units(zs, units_bc)], [], (keep_x, got_x, gots_a[0]), 1, 10)
    pieces_bc = lax.all_to_all(
        part_z,
        "lon",
        0,
        0,
        axis_index_groups=[[2 * z + x for z in range(zs)] for x in range(2)],
    )
    (sum_a,) = call(sum_refs, [units(units_xa)], [], (own_a, *gots_a, part_z), 1, 10)
    moved_a = [lon_send(sum_a, 2 * k) for k in range(1, zs)]
    (same,) = call(join_z, [units(zs, units_xa)], [], [sum_a, *moved_a, part_z], 1, 10)
    same_x = x_swap(same)
    cross = lat_swap(same)
    cross_x = lat_swap(same_x)
    (sum_bc,) = call(
        sum_pieces, [units(lon_size, units_bc)], [], (pieces_bc, same), 1, 10
    )
    whole_bc = lax.all_to_all(sum_bc, "lon", 0, 0)
    oth_bc = lat_swap(whole_bc)

    flat_rows = (2 * block_rows * 128 + norm_gain.size) // 128
    fold_scr = [((CHUNK * 8, PAIR), F32), wide_scr, tab_scr]
    flat_a, squares, bias_late = call(
        functools.partial(late_kernel, units_a),
        [((block_rows, 128), F32), ((UNIT, 128), F32), (table.shape[1:], F32)],
        [*fold_scr, units(2, lon_size, units_a + extra)],
        (spread, same, same_x, cross, cross_x),
        2,
        14,
    )
    update, bias_grad = call(
        functools.partial(last_kernel, units_b, units_c),
        [((flat_rows, 128), BF16), (table.shape, F32)],
        [
            ((block_rows + 8, 128), F32),
            *fold_scr,
            units(2, lon_size, units_b + units_c + extra),
        ],
        (spread, flat_a, squares, bias_late, whole_bc, oth_bc),
        2,
        14,
    )
    bias_grad = jnp.swapaxes(bias_grad, 1, 2)
    return (tokens_grad, update.reshape(-1), bias_grad)


def solution(mesh):
    return jax.shard_map(
        shards,
        mesh=mesh,
        in_specs=(
            P("grp", "lat", "lon", None),
            P("grp", "lat", "lon", None),
            P(),
            P(),
            P(),
            P(),
            P(),
            P(None, "lat", None, None),
        ),
        out_specs=(P("grp", "lat", "lon", None), P("grp"), P("grp", "lat", None, None)),
        check_vma=False,
    )
```

```python
import functools

import jax
import jax.numpy as jnp
import numpy as np
from jax import lax
from jax.experimental import pallas as pl
from jax.experimental.pallas import tpu as pltpu
from jax.sharding import PartitionSpec as P

WLAT = 12
WLON = 6
PAD = 5
LEVELS = 2
HEADS = 6
CHUNK = LEVELS * WLAT
WIN = CHUNK * WLON
SHIFTS = 2 * WLON - 1
PAIR = WLAT * SHIFTS
WIDE = 384

EPS = 1e-05
NEGATIVE = -1000000000.0
ROOT_HALF = 0.7071067811865476
INV_ROOT_TAU = 0.3989422804014327

F32 = jnp.float32
BF16 = jnp.bfloat16
UNIT = 8
BIAS_UNITS = (2 * HEADS + 1) * CHUNK // UNIT
MIB = 1024 * 1024


def dot(a, b):
    return lax.dot_general(a, b, (((1,), (0,)), ((), ())), preferred_element_type=F32)


def dot_nt(a, b):
    return lax.dot_general(a, b, (((1,), (1,)), ((), ())), preferred_element_type=F32)


def dot_tn(a, b):
    return lax.dot_general(a, b, (((0,), (0,)), ((), ())), preferred_element_type=F32)


def row_mean(v):
    return jnp.sum(v, axis=-1, keepdims=True) * (1.0 / v.shape[-1])


def standardize(x):
    centred = x - row_mean(x)
    inv = lax.rsqrt(row_mean(centred * centred) + EPS)
    return centred * inv, inv


def norm_back(d, gain, stand, inv):
    scaled = d * gain
    first = row_mean(scaled)
    second = row_mean(scaled * stand)
    gain_grad = jnp.sum(d * stand, axis=0, keepdims=True)
    return inv * (scaled - first - stand * second), gain_grad


def gelu_value(hidden):
    return 0.5 * hidden * (1.0 + lax.erf(hidden * ROOT_HALF))


def gelu_parts(hidden):
    half = 0.5 * (1.0 + lax.erf(hidden * ROOT_HALF))
    slope = half + hidden * jnp.exp(-0.5 * hidden * hidden) * INV_ROOT_TAU
    return hidden * half, slope


def split3(v):
    hi = v.astype(BF16)
    rest = v - hi.astype(F32)
    mid = rest.astype(BF16)
    low = (rest - mid.astype(F32)).astype(BF16)
    return hi, mid, low


def spread_matrices():
    out = np.zeros((LEVELS, PAIR, WIDE), np.float32)
    for zj in range(LEVELS):
        for aj in range(WLAT):
            for d in range(SHIFTS):
                out[zj, aj * SHIFTS + d, (SHIFTS - 1 - d) * CHUNK + zj * WLAT + aj] = 1.0
    return out


def put(scr, rows, value):
    width = value.shape[1]
    for tile in range(-(-width // 128)):
        lanes = min(128, width - tile * 128)
        scr[tile, rows, 0:lanes] = value[:, tile * 128 : tile * 128 + lanes]


def get(scr, rows, width):
    parts = [scr[tile, rows, :] for tile in range(-(-width // 128))]
    return jnp.concatenate(parts, axis=1)[:, 0:width]


def head_masks(width, dtype):
    lane = lax.broadcasted_iota(jnp.int32, (1, width), 1)
    size = width // HEADS
    return [((lane >= h * size) & (lane < (h + 1) * size)).astype(dtype) for h in range(HEADS)]


def lat_inside(n):
    return lax.rem(n, WLAT)


def lat_row(row_iota, lat, shifted, lat_total):
    row = lat * WLAT + lat_inside(row_iota)
    if shifted:
        row = row + WLAT // 2
        row = jnp.where(row >= lat_total, row - lat_total, row)
    return row


def expand_bias(table, spread, tab_scr, rows_scr, wide_scr, bias_scr, lat, shifted, lat_total):
    for h in range(HEADS):
        tab_scr[h : h + 1, :] = table[h]
    for zi in range(LEVELS):
        for zj in range(LEVELS):
            for ai in range(WLAT):
                at = ((zi * LEVELS + zj) * WLAT + ai) * PAIR
                row = zj * CHUNK * 8 + (zi * WLAT + ai) * 8
                rows_scr[row : row + HEADS, 0:PAIR] = tab_scr[0:HEADS, at : at + PAIR]
    count = CHUNK * 8
    total = jnp.zeros((count, WIDE), F32)
    for zj in range(LEVELS):
        parts = split3(rows_scr[zj * count : (zj + 1) * count, 0:PAIR])
        for part in parts:
            total = total + dot(part, spread[zj])
    put(wide_scr, slice(None), total)
    i = lax.broadcasted_iota(jnp.int32, (CHUNK, WIN), 0)
    j = lax.broadcasted_iota(jnp.int32, (CHUNK, WIN), 1)
    allowed = lat_row(j, lat, shifted, lat_total) < lat_total - PAD
    if shifted:
        last = lat_total - WLAT // 2
        region_i = (lat * WLAT + lat_inside(i)) >= last
        region_j = (lat * WLAT + lat_inside(j)) >= last
        allowed = allowed & (region_i == region_j)
    for h in range(HEADS):
        wide = get(wide_scr, pl.ds(h, CHUNK, stride=8), WIDE)
        for oi in range(WLON):
            back = (WLON - 1 - oi) * CHUNK
            moved = wide if back == 0 else pltpu.roll(wide, WIDE - back, axis=1)
            at = h * WIN + oi * CHUNK
            bias_scr[at : at + CHUNK, :] = jnp.where(allowed, moved[:, 0:WIN], NEGATIVE)


def fold_bias(sums, put_unit):
    rest = jnp.zeros((CHUNK, 128), F32)

    def emit(at, value):
        for r in range(CHUNK // UNIT):
            put_unit(at * (CHUNK // UNIT) + r, value[r * UNIT : (r + 1) * UNIT, :].astype(BF16))

    for h in range(HEADS):
        total = jnp.zeros((CHUNK, WIDE), F32)
        for oi in range(WLON):
            back = (WLON - 1 - oi) * CHUNK
            at = h * WIN + oi * CHUNK
            part = sums[at : at + CHUNK, :]
            total = total + (part if back == 0 else pltpu.roll(part, back, axis=1))
        emit(h, total[:, 0:128])
        emit(HEADS + h, total[:, 128:256])
        last = total[:, 256:384]
        rest = rest + (last if h == 0 else pltpu.roll(last, 8 * h, axis=1))
    emit(2 * HEADS, rest)

def stack_heads(v, masks):
    return jnp.concatenate([v * mask for mask in masks], axis=0)


def pick_heads(v, masks):
    total = v[0:WIN] * masks[0]
    for h in range(1, HEADS):
        total = total + v[h * WIN : (h + 1) * WIN] * masks[h]
    return total


def attend(qkv, bias, mixed, probs, stack_scr, width):
    masks = head_masks(width, BF16)
    masks32 = head_masks(width, F32)
    scale = (width // HEADS) ** -0.5

    def window(w, carry):
        rows = pl.ds(pl.multiple_of(w * WIN, 16), WIN)
        q = qkv[rows, 0:width]
        k = qkv[rows, width : 2 * width]
        v = qkv[rows, 2 * width : 3 * width]
        scores = dot_nt(stack_heads(q, masks), k)
        for h in range(HEADS):
            part = slice(h * WIN, (h + 1) * WIN)
            logits = scores[part] * scale + bias[part, :]
            weights = jnp.exp(logits - jnp.max(logits, axis=-1, keepdims=True))
            p = weights * (1.0 / jnp.sum(weights, axis=-1, keepdims=True))
            probs[w, h] = p
            stack_scr[part, :] = p.astype(BF16)
        mixed[rows, :] = pick_heads(dot(stack_scr[...], v), masks32).astype(BF16)
        return carry

    lax.fori_loop(0, probs.shape[0], window, 0, unroll=True)


def attend_back(qkv, probs, dmix, field, sums, low_scr, prob_scr, width):
    masks = head_masks(width, BF16)
    masks32 = head_masks(width, F32)
    scale = (width // HEADS) ** -0.5

    def window(w, carry):
        rows = pl.ds(pl.multiple_of(w * WIN, 16), WIN)
        q = qkv[rows, 0:width]
        k = qkv[rows, width : 2 * width]
        v = qkv[rows, 2 * width : 3 * width]
        up = stack_heads(dmix[rows, :], masks)
        prob_grad = dot_nt(up, v)
        for h in range(HEADS):
            part = slice(h * WIN, (h + 1) * WIN)
            p = probs[w, h]
            weighted = p * prob_grad[part]
            ds = weighted - p * jnp.sum(weighted, axis=-1, keepdims=True)
            sums[part, 0:WIN] += ds
            low_scr[part, :] = ds.astype(BF16)
            prob_scr[part, :] = p.astype(BF16)
        low = low_scr[...]
        dq = pick_heads(dot(low, k), masks32)
        dk = dot_tn(low, stack_heads(q, masks))
        dv = dot_tn(prob_scr[...], up)
        field[rows, 0:width] = (dq * scale).astype(BF16)
        field[rows, width : 2 * width] = (dk * scale).astype(BF16)
        field[rows, 2 * width : 3 * width] = dv.astype(BF16)
        return carry

    lax.fori_loop(0, probs.shape[0], window, 0, unroll=True)


def lon_major(src, scr):
    levels, lats, lons, width = src.shape
    for z in range(levels):
        for a in range(lats):
            at = (z * lats + a) * lons
            put(scr, slice(at, at + lons), src[z, a].astype(F32))


def lon_column(scr, lon, lons, width):
    return get(scr, pl.ds(lon, CHUNK, stride=lons), width)


def flat_store(dst, at, mat, cols):
    rows = mat.shape[1]
    if cols % 128 == 0:
        per = cols // 128
        for c in range(per):
            dst[pl.ds(at + c, rows, stride=per), :] = mat[c]
        return rows * per
    per = 2 * cols // 128
    half = cols // 128
    even = get(mat, pl.ds(0, rows // 2, stride=2), cols)
    odd = get(mat, pl.ds(1, rows // 2, stride=2), cols)
    for c in range(half):
        dst[pl.ds(at + c, rows // 2, stride=per), :] = even[:, c * 128 : (c + 1) * 128]
    dst[pl.ds(at + half, rows // 2, stride=per), :] = jnp.concatenate(
        [even[:, half * 128 : half * 128 + 64], odd[:, 0:64]], axis=1
    )
    for c in range(half):
        dst[pl.ds(at + half + 1 + c, rows // 2, stride=per), :] = odd[
            :, 64 + c * 128 : 64 + (c + 1) * 128
        ]
    return rows * cols // 128


def send_units(scr, base, out):
    lons, units = out.shape[:2]
    for j in range(lons):
        for u in range(units):
            at = base + (j * units + u) * UNIT
            if not isinstance(at, int):
                at = pl.multiple_of(at, UNIT)
            out[j, u] = scr[pl.ds(at, UNIT), :].astype(BF16)


def halves(scr, lat, keep, give):
    half = keep.shape[0] * keep.shape[1] * UNIT
    send_units(scr, lat * half, keep)
    send_units(scr, (1 - lat) * half, give)


def bias_units(sums, out):
    lons, per = out.shape[:2]

    def put_unit(k, value):
        out[k // per, k % per] = value

    fold_bias(sums, put_unit)
    for k in range(BIAS_UNITS, lons * per):
        put_unit(k, jnp.zeros((UNIT, 128), BF16))

def forward_core(x, b, refs, qkv_scr, bias_scr, mixed, probs, stack_scr):
    qkv_w, proj_w, gains = refs
    width = x.shape[-1]
    stand, inv = standardize(x)
    normed = (stand * gains[b, 0:1, :]).astype(BF16)
    qkv_scr[...] = dot(normed, qkv_w[b]).astype(BF16)
    attend(qkv_scr, bias_scr, mixed, probs, stack_scr, width)
    att = dot(mixed[...], proj_w[b]).astype(BF16)
    resid = (x + att.astype(F32)).astype(BF16).astype(F32)
    return resid, normed


def first_kernel(
    lat_total, tokens_in, cot_in, table_in, spread_in, qkv_in, proj_in, up_in, down_in, gains_in,
    x_out, tail_out, head_out, qkv_out, mixed_out, probs_out, resid_out, hidden_out, active_out,
    scr, cot_scr, tab_scr, rows_scr, wide_scr, bias_scr,
    cot, table, spread, tokens, qkv_w, gains, proj_w, up_w, down_w, stack_scr, sems,
):
    copies = []
    for source, target in (
        (cot_in, cot),
        (table_in.at[0:1], table),
        (spread_in, spread),
        (tokens_in, tokens),
        (qkv_in.at[0:1], qkv_w),
        (gains_in, gains),
        (proj_in.at[0:1], proj_w),
        (up_in.at[0:1], up_w),
        (down_in.at[0:1], down_w),
    ):
        copies.append(pltpu.make_async_copy(source, target, sems.at[len(copies)]))
    for copy in copies:
        copy.start()
    lat = lax.axis_index("lat")
    width = tokens.shape[-1]
    lons = tokens.shape[2]
    cut = CHUNK * (WLON // 2)
    copies[0].wait()
    lon_major(cot, cot_scr)
    g = jnp.concatenate([lon_column(cot_scr, lon, lons, width) for lon in range(lons)], axis=0)
    head_out[1] = g[0:cut, :].astype(BF16)
    tail_out[1] = g[cut:, :].astype(BF16)
    copies[1].wait()
    copies[2].wait()
    expand_bias(
        table.at[0], spread, tab_scr, rows_scr, wide_scr, bias_scr, lat, False, lat_total
    )
    copies[3].wait()
    lon_major(tokens, scr)
    x = jnp.concatenate([lon_column(scr, lon, lons, width) for lon in range(lons)], axis=0)
    x_out[...] = x.astype(BF16)
    for copy in copies[4:]:
        copy.wait()

    resid, _ = forward_core(
        x, 0, (qkv_w, proj_w, gains), qkv_out, bias_scr, mixed_out, probs_out, stack_scr
    )
    resid_out[...] = resid.astype(BF16)
    stand, _ = standardize(resid)
    normed = (stand * gains[0, 1:2, :]).astype(BF16)
    hidden = dot(normed, up_w[0])
    hidden_out[...] = hidden
    active = gelu_value(hidden).astype(BF16)
    active_out[...] = active
    result = resid + dot_nt(active, down_w[0])
    head_out[0] = result[0:cut, :].astype(BF16)
    tail_out[0] = result[cut:, :].astype(BF16)


def bias_kernel(
    lat_total, table, spread, hidden, bias_out, slope_out, tab_scr, rows_scr, wide_scr
):
    lat = lax.axis_index("lat")
    slope_out[...] = gelu_parts(hidden[...])[1].astype(BF16)
    expand_bias(
        table.at[1], spread, tab_scr, rows_scr, wide_scr, bias_out, lat, True, lat_total
    )


def merge_ahead(scr_own, scr_oth, rows):
    half = WLAT // 2
    n = lax.broadcasted_iota(jnp.int32, (rows, 1), 0)
    return jnp.where(
        lat_inside(n) < half,
        pltpu.roll(scr_own[...], rows - half, axis=0),
        pltpu.roll(scr_oth[...], half, axis=0),
    )


def merge_behind(scr_own, scr_oth, rows):
    half = WLAT // 2
    n = lax.broadcasted_iota(jnp.int32, (rows, 1), 0)
    return jnp.where(
        lat_inside(n) >= half,
        pltpu.roll(scr_own[...], half, axis=0),
        pltpu.roll(scr_oth[...], rows - half, axis=0),
    )


def second_kernel(
    lat_total,
    kept, tail, lon_head, lat_tail, diag_head, bias, qkv_w, proj_w, up_w, down_w, gains, *rest
):
    run_second(
        lat_total, tail, lon_head, lat_tail, diag_head, bias, qkv_w, proj_w, up_w, down_w, gains,
        *rest[kept:kept + 12], *rest[2 * kept + 12 :]
    )


def run_second(
    lat_total,
    tail, lon_head, lat_tail, diag_head, bias, qkv_w, proj_w, up_w, down_w, gains,
    head_out, tail_out, n1_out, field_out, mixed_out, low_out, n2_out, hg_out, active_out, g_out,
    sums_out, gain_out,
    scr_own, scr_oth, qkv_scr, probs_scr, dmix_scr, low_scr, prob_scr,
):
    lat = lax.axis_index("lat")
    rows, width = scr_own.shape
    cut = CHUNK * (WLON // 2)

    def rolled(which):
        scr_own[0 : rows - cut, :] = tail[which].astype(F32)
        scr_own[rows - cut :, :] = lon_head[which].astype(F32)
        scr_oth[0 : rows - cut, :] = lat_tail[which].astype(F32)
        scr_oth[rows - cut :, :] = diag_head[which].astype(F32)
        return merge_ahead(scr_own, scr_oth, rows)

    g = rolled(1)
    n = lax.broadcasted_iota(jnp.int32, (rows, 1), 0)
    keep = lat_row(n, lat, True, lat_total) < lat_total - PAD
    g = jnp.where(keep, g, 0.0)
    g_out[...] = g.astype(BF16)

    x = rolled(0)

    resid, normed = forward_core(
        x, 1, (qkv_w, proj_w, gains), qkv_scr, bias, mixed_out, probs_scr, low_scr
    )
    n1_out[...] = normed
    stand2, inv2 = standardize(resid)
    normed2 = (stand2 * gains[1, 1:2, :]).astype(BF16)
    n2_out[...] = normed2
    active, slope = gelu_parts(dot(normed2, up_w[1]))
    active_out[...] = active.astype(BF16)

    hg = (dot(g_out[...], down_w[1]) * slope).astype(BF16)
    hg_out[...] = hg
    part, gain_two = norm_back(dot_nt(hg, up_w[1]), gains[1, 1:2, :], stand2, inv2)
    rg = g + part
    low = rg.astype(BF16)
    low_out[...] = low
    dmix_scr[...] = dot_nt(low, proj_w[1]).astype(BF16)
    sums_out[...] = jnp.zeros(sums_out.shape, F32)
    attend_back(
        qkv_scr, probs_scr, dmix_scr, field_out, sums_out, low_scr, prob_scr, width
    )
    ng = dot_nt(field_out[...], qkv_w[1]).astype(BF16).astype(F32)
    stand1, inv1 = standardize(x)
    part, gain_one = norm_back(ng, gains[1, 0:1, :], stand1, inv1)
    dx = rg + part
    head_out[...] = dx[0 : rows - cut, :].astype(BF16)
    tail_out[...] = dx[rows - cut :, :].astype(BF16)
    gain_out[0:1, :] = gain_one
    gain_out[1:2, :] = gain_two


def outer_kernel(
    n1, field, mixed, low, n2, hg, active, g, sums,
    keep, give, bias_out,
    m576, m192, m768, mdown, flat_scr,
):
    put(m576, slice(None), dot_tn(n1[...], field[...]))
    at = flat_store(flat_scr, 0, m576, field.shape[1])
    put(m192, slice(None), dot_tn(mixed[...], low[...]))
    at += flat_store(flat_scr, at, m192, mixed.shape[1])
    put(m768, slice(None), dot_tn(n2[...], hg[...]))
    at += flat_store(flat_scr, at, m768, active.shape[1])
    put(mdown, slice(None), dot_tn(active[...], g[...]))
    at += flat_store(flat_scr, at, mdown, mixed.shape[1])
    halves(flat_scr, lax.axis_index("lat"), keep, give)
    bias_units(sums, bias_out)


def lat_sums_split(*refs):
    keep_out, give_out = refs[-2:]
    x = lax.rem(lax.axis_index("lon"), 2)
    for out, side in ((keep_out, x), (give_out, 1 - x)):
        for z in range(out.shape[0]):
            j = 2 * z + side
            at = 0
            for k in range(0, len(refs) - 4, 2):
                keep, got = refs[k], refs[k + 1]
                count = keep.shape[1]
                total = keep[j].astype(F32) + got[j].astype(F32)
                out[z, at : at + count] = total.astype(BF16)
                at += count
            out[z, at:] = refs[-4][j]


def split_z(keep, got, own_out, *give_outs):
    count = keep.shape[0]
    z = lax.div(lax.axis_index("lon"), 2)
    for k, out in enumerate((own_out,) + give_outs):
        at = lax.rem(z + k, count)
        out[...] = (keep[at].astype(F32) + got[at].astype(F32)).astype(BF16)


def sum_refs(*refs):
    total = refs[0][...].astype(F32)
    for ref in refs[1:-2]:
        total = total + ref[...].astype(F32)
    refs[-1][...] = total.astype(BF16)


def add_pair(keep, got, order, out):
    out[...] = (keep[...].astype(F32) + got[...].astype(F32)).astype(BF16)


def sum_pieces(pieces, order, out):
    total = pieces[0].astype(F32)
    for k in range(1, pieces.shape[0]):
        total = total + pieces[k].astype(F32)
    total = total.astype(BF16)
    if len(out.shape) == len(pieces.shape):
        for k in range(out.shape[0]):
            out[k] = total
    else:
        out[...] = total


def join_z(*refs):
    out = refs[-1]
    count = out.shape[0]
    z = lax.div(lax.axis_index("lon"), 2)
    for k in range(count):
        out[lax.rem(z + count - k, count)] = refs[k][...]


def third_kernel(
    head, lon_tail, lat_head, diag_tail, resid, slope, active, mixed,
    proj_w, up_w, down_w, gains, order,
    keep_out, give_out, rg_out, dmix_out, gain_out,
    scr_own, scr_oth, m192, m768, mdown, flat_scr,
):
    rows, width = scr_own.shape
    cut = CHUNK * (WLON // 2)
    scr_own[0:cut, :] = lon_tail[...].astype(F32)
    scr_own[cut:, :] = head[...].astype(F32)
    scr_oth[0:cut, :] = diag_tail[...].astype(F32)
    scr_oth[cut:, :] = lat_head[...].astype(F32)
    g = merge_behind(scr_own, scr_oth, rows)
    g_low = g.astype(BF16)
    hg = dot(g_low, down_w[0])
    stand2, inv2 = standardize(resid[...].astype(F32))
    normed2 = (stand2 * gains[0, 1:2, :]).astype(BF16)
    hg = (hg * slope[...].astype(F32)).astype(BF16)
    part, gain_two = norm_back(dot_nt(hg, up_w[0]), gains[0, 1:2, :], stand2, inv2)
    rg = g + part
    rg_out[...] = rg
    low = rg.astype(BF16)
    dmix_out[...] = dot_nt(low, proj_w[0]).astype(BF16)
    gain_out[...] = gain_two
    put(m192, slice(None), dot_tn(mixed[...], low))
    at = flat_store(flat_scr, 0, m192, mixed.shape[1])
    put(m768, slice(None), dot_tn(normed2, hg))
    at += flat_store(flat_scr, at, m768, active.shape[1])
    put(mdown, slice(None), dot_tn(active[...], g_low))
    at += flat_store(flat_scr, at, mdown, mixed.shape[1])
    flat_scr[at:, :] = jnp.zeros((flat_scr.shape[0] - at, 128), F32)
    halves(flat_scr, lax.axis_index("lat"), keep_out, give_out)


def gain_rows(one, two):
    return jnp.concatenate(
        [
            one[:, 0:128],
            jnp.concatenate([one[:, 128:192], two[:, 0:64]], axis=1),
            two[:, 64:192],
        ],
        axis=0,
    )


def fourth_kernel(
    x_in, qkv, probs, dmix, rg, gain_two, gains_late, qkv_w, gains,
    tokens_out, keep, give, bias_out,
    field, sums, m576, flat_scr, dx_scr, low_scr, prob_scr,
):
    width = x_in.shape[-1]
    levels, lats, lons = tokens_out.shape[:3]
    sums[...] = jnp.zeros(sums.shape, F32)
    attend_back(qkv, probs, dmix, field, sums, low_scr, prob_scr, width)
    stand1, inv1 = standardize(x_in[...].astype(F32))
    normed = (stand1 * gains[0, 0:1, :]).astype(BF16)
    ng = dot_nt(field[...], qkv_w[0]).astype(BF16).astype(F32)
    part, gain_one = norm_back(ng, gains[0, 0:1, :], stand1, inv1)
    put(m576, slice(None), dot_tn(normed, field[...]))
    at = flat_store(flat_scr, 0, m576, field.shape[1])
    flat_scr[at:, :] = jnp.zeros((flat_scr.shape[0] - at, 128), F32)
    flat_scr[at : at + 3, :] = gain_rows(gain_one, gain_two[...])
    flat_scr[at + 3 : at + 6, :] = gain_rows(gains_late[0:1, :], gains_late[1:2, :])
    bias_units(sums, bias_out)
    halves(flat_scr, lax.axis_index("lat"), keep, give)
    put(dx_scr, slice(None), rg[...] + part)
    for z in range(levels):
        for a in range(lats):
            tokens_out[z, a] = get(
                dx_scr, pl.ds(z * lats + a, lons, stride=CHUNK), width
            ).astype(BF16)


def place(pieces, first, last, dests, scr):
    total = jnp.zeros((UNIT, 128), F32)
    lons = pieces.shape[1]
    per = last - first
    k = 0
    for where, room in dests:
        for at in range(where, where + room, UNIT):
            half, j, u = k // (per * lons), k // per % lons, k % per
            value = pieces[half, j, first + u].astype(F32)
            scr[at : at + UNIT, :] = value
            total = total + value * value
            k += 1
    return total


def bias_rows(piece, base, spread, out, rows_scr, wide_scr, tab_scr):
    lat = lax.axis_index("lat")
    extra = -(-BIAS_UNITS // piece.shape[1])

    def read(at):
        parts = []
        for r in range(CHUNK // UNIT):
            k = at * (CHUNK // UNIT) + r
            parts.append(piece[lat, k // extra, base + k % extra].astype(F32))
        return jnp.concatenate(parts, axis=0)

    rest = read(2 * HEADS)
    for h in range(HEADS):
        rows = pl.ds(h, CHUNK, stride=8)
        wide_scr[0, rows, :] = read(h)
        wide_scr[1, rows, :] = read(HEADS + h)
        wide_scr[2, rows, :] = rest if h == 0 else pltpu.roll(rest, 128 - 8 * h, axis=1)
    low = get(wide_scr, slice(None), WIDE).astype(BF16)
    for zj in range(LEVELS):
        rows_scr[...] = dot_nt(low, spread[zj])
        for zi in range(LEVELS):
            for ai in range(WLAT):
                at = ((zi * LEVELS + zj) * WLAT + ai) * PAIR
                row = (zi * WLAT + ai) * 8
                tab_scr[0:HEADS, at : at + PAIR] = rows_scr[row : row + HEADS, 0:PAIR]
    for h in range(HEADS):
        out[h] = tab_scr[h : h + 1, :]


def late_kernel(
    units_a, spread, same, same_x, cross, cross_x, flat_out, squares_out, bias_out,
    rows_scr, wide_scr, tab_scr, a,
):
    lat = lax.axis_index("lat")
    x = lax.rem(lax.axis_index("lon"), 2)
    for z in range(same.shape[0]):
        a[lat, 2 * z + x] = same[z]
        a[lat, 2 * z + 1 - x] = same_x[z]
        a[1 - lat, 2 * z + x] = cross[z]
        a[1 - lat, 2 * z + 1 - x] = cross_x[z]
    squares_out[...] = place(a, 0, units_a, [(0, flat_out.shape[0])], flat_out)
    bias_rows(a, units_a, spread, bias_out, rows_scr, wide_scr, tab_scr)


def last_kernel(
    units_b, units_c, spread, flat_a, squares, bias_late, own_bc, oth_bc, update_out, bias_out,
    scr, rows_scr, wide_scr, tab_scr, bc,
):
    lat = lax.axis_index("lat")
    for j in range(own_bc.shape[0]):
        bc[lat, j] = own_bc[j]
        bc[1 - lat, j] = oth_bc[j]
    total = squares[...]
    total = total + place(bc, 0, units_b, [(864, 288), (1152, 1152), (2304, 1152)], scr)
    total = total + place(bc, units_b, units_b + units_c, [(0, 864), (3456, 8)], scr)
    count = update_out.shape[0]
    mean = jnp.sum(total) * (1.0 / (count * 128))
    scale = lax.rsqrt(mean + 1e-06)
    early, late = (0, 1728, 2304, 4608), (864, 2016, 3456, 5760)
    at = 0
    for first, second, rows in zip(early, late, (864, 288, 1152, 1152)):
        update_out[first : first + rows, :] = (scr[at : at + rows, :] * scale).astype(BF16)
        update_out[second : second + rows, :] = (flat_a[at : at + rows, :] * scale).astype(BF16)
        at += rows
    update_out[6912:count, :] = (scr[at : at + count - 6912, :] * scale).astype(BF16)
    bias_rows(bc, units_b + units_c, spread, bias_out.at[0], rows_scr, wide_scr, tab_scr)
    bias_out[1] = bias_late[...]


def call(kernel, outs, scratch, args, micros, mib, spaces=None, near=(), kept=0):
    spaces = spaces or [pltpu.VMEM] * len(args)
    return pl.pallas_call(
        kernel,
        out_shape=[
            (pltpu.VMEM if at in near else jax.ShapeDtypeStruct)(*entry)
            for at, entry in enumerate(outs)
        ],
        in_specs=[pl.BlockSpec(memory_space=space) for space in spaces],
        out_specs=[
            pl.BlockSpec(memory_space=pltpu.VMEM if at < len(outs) - kept else pl.ANY)
            for at in range(len(outs))
        ],
        input_output_aliases={
            len(args) - kept + k: len(outs) - kept + k for k in range(kept)
        },
        scratch_shapes=[
            pltpu.VMEM(*entry) if isinstance(entry, tuple) else entry for entry in scratch
        ],
        compiler_params=pltpu.CompilerParams(vmem_limit_bytes=mib * MIB),
        cost_estimate=pl.CostEstimate(
            flops=int(micros * 1.1e9), bytes_accessed=10**5, transcendentals=0
        ),
    )(*args)


def lat_swap(value):
    return lax.ppermute(value, "lat", [(0, 1), (1, 0)])


def lon_send(value, step):
    count = lax.axis_size("lon")
    return lax.ppermute(value, "lon", [(s, (s + step) % count) for s in range(count)])


def x_swap(value):
    count = lax.axis_size("lon")
    return lax.ppermute(value, "lon", [(s, s ^ 1) for s in range(count)])


def diag_send(value, step):
    count = lax.axis_size("lon")
    pairs = []
    for s in range(count):
        for t in range(2):
            pairs.append((2 * s + t, 2 * ((s + step) % count) + 1 - t))
    return lax.ppermute(value, ("lon", "lat"), pairs)


def shards(
    tokens, cotangent, qkv_weight, proj_weight, up_weight, down_weight, norm_gain, bias_table
):
    levels, lats, lons, width = tokens.shape
    rows = levels * lats * lons
    wins = rows // WIN
    hid = up_weight.shape[-1]
    heads = bias_table.shape[2]
    lon_size = lax.axis_size("lon")
    zs = lon_size // 2
    lat_total = lats * lax.axis_size("lat")
    cut = CHUNK * (WLON // 2)
    spread = jnp.asarray(spread_matrices(), BF16)
    down_turned = jnp.swapaxes(down_weight, 1, 2)
    table = jnp.swapaxes(bias_table, 1, 2)
    token = (rows, width)
    field_shape = ((rows, 3 * width), BF16)
    probs_shape = ((wins, heads, WIN, WIN), F32)
    stack_shape = ((heads * WIN, WIN), BF16)
    bias_shape = ((heads * WIN, WIN), F32)
    sums_shape = ((heads * WIN, WIDE), F32)
    tab_scr = ((8, table.shape[-1]), F32)
    rows_scr = ((LEVELS * CHUNK * 8, PAIR), F32)
    wide_scr = ((WIDE // 128, CHUNK * 8, 128), F32)
    tiles = -(-width // 128)
    token_scr = ((tiles, rows, 128), F32)
    m576 = ((-(-3 * width // 128), width, 128), F32)
    m192 = ((tiles, width, 128), F32)
    m768 = ((hid // 128, width, 128), F32)
    mdown = ((tiles, hid, 128), F32)

    block_rows = (qkv_weight[0].size + proj_weight[0].size + 2 * up_weight[0].size) // 128
    qkv_rows = qkv_weight[0].size // 128
    counts = (block_rows, block_rows - qkv_rows, qkv_rows + 8)
    units_a, units_b, units_c = [-(-count // (2 * lon_size * UNIT)) for count in counts]
    extra = -(-BIAS_UNITS // lon_size)

    def units(*lead):
        return (lead + (UNIT, 128), BF16)

    def flat_scr(per):
        return ((2 * lon_size * per * UNIT, 128), F32)

    x0, tail, head, qkv0, mixed0, probs0, resid0, hidden0, active0 = call(
        functools.partial(first_kernel, lat_total),
        [
            (token, BF16),
            ((2, rows - cut, width), BF16),
            ((2, cut, width), BF16),
            field_shape,
            (token, BF16),
            probs_shape,
            (token, BF16),
            ((rows, hid), F32),
            ((rows, hid), BF16),
        ],
        [
            token_scr,
            token_scr,
            tab_scr,
            rows_scr,
            wide_scr,
            bias_shape,
            (cotangent.shape, BF16),
            ((1,) + table.shape[1:], F32),
            (spread.shape, BF16),
            (tokens.shape, BF16),
            ((1,) + qkv_weight.shape[1:], BF16),
            (norm_gain.shape, F32),
            ((1,) + proj_weight.shape[1:], BF16),
            ((1,) + up_weight.shape[1:], BF16),
            ((1,) + down_turned.shape[1:], BF16),
            stack_shape,
            pltpu.SemaphoreType.DMA((9,)),
        ],
        [
            pltpu.with_memory_space_constraint(arg, pltpu.HBM)
            for arg in (
                tokens, cotangent, table, spread, qkv_weight, proj_weight, up_weight, down_turned,
                norm_gain,
            )
        ],
        8,
        16,
        [pltpu.HBM] * 9,
        near=(0, 3, 4, 5, 6, 8),
    )
    lon_head = lon_send(head, -1)
    diag_head = diag_send(head, -1)
    lat_tail = lat_swap(tail)
    bias1, slope0 = call(
        functools.partial(bias_kernel, lat_total),
        [bias_shape, ((rows, hid), BF16)],
        [tab_scr, rows_scr, wide_scr],
        (table, spread, hidden0),
        3,
        12,
        near=(1,),
    )

    saved = [x0, qkv0, mixed0, probs0, resid0, active0, slope0]
    (
        dhead, dtail, n1, field1, mixed1, low1, n2, hg1, active1, g1, sums1, gains1,
        *saved,
    ) = call(
        functools.partial(second_kernel, lat_total, len(saved)),
        [
            ((rows - cut, width), BF16),
            ((cut, width), BF16),
            (token, BF16),
            field_shape,
            (token, BF16),
            (token, BF16),
            (token, BF16),
            ((rows, hid), BF16),
            ((rows, hid), BF16),
            (token, BF16),
            sums_shape,
            ((2, width), F32),
            *[(value.shape, value.dtype) for value in saved],
        ],
        [
            (token, F32),
            (token, F32),
            field_shape,
            probs_shape,
            (token, BF16),
            stack_shape,
            stack_shape,
        ],
        (
            tail, lon_head, lat_tail, diag_head, bias1, qkv_weight, proj_weight, up_weight,
            down_turned, norm_gain,
            *[pltpu.with_memory_space_constraint(value, pltpu.VMEM) for value in saved],
        ),
        19,
        16,
        [pltpu.VMEM] * 10 + [pl.ANY] * len(saved),
        near=tuple(range(12, 12 + len(saved))),
        kept=len(saved),
    )
    x0, qkv0, mixed0, probs0, resid0, active0, slope0 = saved
    lon_tail = lon_send(dtail, 1)
    diag_tail = diag_send(dtail, 1)
    lat_dhead = lat_swap(dhead)

    keep_a, give_a, bias_a = call(
        outer_kernel,
        [units(lon_size, units_a), units(lon_size, units_a), units(lon_size, extra)],
        [m576, m192, m768, mdown, flat_scr(units_a)],
        (n1, field1, mixed1, low1, n2, hg1, active1, g1, sums1),
        3,
        14,
    )
    got_a = lat_swap(give_a)

    units_xa = units_a + extra
    keep_xa, give_xa = call(
        lat_sums_split, [units(zs, units_xa)] * 2, [], (keep_a, got_a, bias_a, keep_a), 1, 10
    )
    got_xa = x_swap(give_xa)

    keep_b, give_b, rg0, dmix0, gain_two = call(
        third_kernel,
        [
            units(lon_size, units_b),
            units(lon_size, units_b),
            (token, F32),
            (token, BF16),
            ((1, width), F32),
        ],
        [(token, F32), (token, F32), m192, m768, mdown, flat_scr(units_b)],
        (
            dhead, lon_tail, lat_dhead, diag_tail, resid0, slope0, active0, mixed0, proj_weight,
            up_weight, down_turned, norm_gain, keep_xa,
        ),
        3,
        14,
    )
    got_b = lat_swap(give_b)

    tokens_grad, keep_c, give_c, bias_c = call(
        fourth_kernel,
        [
            (tokens.shape, BF16),
            units(lon_size, units_c),
            units(lon_size, units_c),
            units(lon_size, extra),
        ],
        [
            field_shape,
            sums_shape,
            m576,
            flat_scr(units_c),
            token_scr,
            stack_shape,
            stack_shape,
        ],
        (x0, qkv0, probs0, dmix0, rg0, gain_two, gains1, qkv_weight, norm_gain),
        7,
        14,
    )
    got_c = lat_swap(give_c)
    own_a, *gives_a = call(
        split_z, [units(units_xa)] * zs, [], (keep_xa, got_xa), 1, 10
    )
    gots_a = [lon_send(give, 2 * (k + 1)) for k, give in enumerate(gives_a)]
    units_bc = units_b + units_c + extra
    keep_x, give_x = call(
        lat_sums_split,
        [units(zs, units_bc)] * 2,
        [],
        (keep_b, got_b, keep_c, got_c, bias_c, own_a),
        1,
        10,
    )
    got_x = x_swap(give_x)
    (sum_a,) = call(sum_refs, [units(units_xa)], [], (own_a, *gots_a, keep_x), 1, 10)
    (part_z,) = call(add_pair, [units(zs, units_bc)], [], (keep_x, got_x, sum_a), 1, 10)
    pieces_bc = lax.all_to_all(
        part_z,
        "lon",
        0,
        0,
        axis_index_groups=[[2 * z + x for z in range(zs)] for x in range(2)],
    )
    moved_a = [lon_send(sum_a, 2 * k) for k in range(1, zs)]
    (same,) = call(join_z, [units(zs, units_xa)], [], [sum_a, *moved_a, part_z], 1, 10)
    same_x = x_swap(same)
    cross = lat_swap(same)
    cross_x = lat_swap(same_x)
    (sum_bc,) = call(
        sum_pieces, [units(lon_size, units_bc)], [], (pieces_bc, same), 1, 10
    )
    whole_bc = lax.all_to_all(sum_bc, "lon", 0, 0)
    oth_bc = lat_swap(whole_bc)

    flat_rows = (2 * block_rows * 128 + norm_gain.size) // 128
    fold_scr = [((CHUNK * 8, PAIR), F32), wide_scr, tab_scr]
    flat_a, squares, bias_late = call(
        functools.partial(late_kernel, units_a),
        [((block_rows, 128), F32), ((UNIT, 128), F32), (table.shape[1:], F32)],
        [*fold_scr, units(2, lon_size, units_a + extra)],
        (spread, same, same_x, cross, cross_x),
        2,
        14,
    )
    update, bias_grad = call(
        functools.partial(last_kernel, units_b, units_c),
        [((flat_rows, 128), BF16), (table.shape, F32)],
        [
            ((block_rows + 8, 128), F32),
            *fold_scr,
            units(2, lon_size, units_b + units_c + extra),
        ],
        (spread, flat_a, squares, bias_late, whole_bc, oth_bc),
        2,
        14,
    )
    bias_grad = jnp.swapaxes(bias_grad, 1, 2)
    return (tokens_grad, update.reshape(-1), bias_grad)


def solution(mesh):
    return jax.shard_map(
        shards,
        mesh=mesh,
        in_specs=(
            P("grp", "lat", "lon", None),
            P("grp", "lat", "lon", None),
            P(),
            P(),
            P(),
            P(),
            P(),
            P(None, "lat", None, None),
        ),
        out_specs=(P("grp", "lat", "lon", None), P("grp"), P("grp", "lat", None, None)),
        check_vma=False,
    )
```

```python
import functools

import jax
import jax.numpy as jnp
import numpy as np
from jax import lax
from jax.experimental import pallas as pl
from jax.experimental.pallas import tpu as pltpu
from jax.sharding import PartitionSpec as P

WLAT = 12
WLON = 6
PAD = 5
LEVELS = 2
HEADS = 6
CHUNK = LEVELS * WLAT
WIN = CHUNK * WLON
SHIFTS = 2 * WLON - 1
PAIR = WLAT * SHIFTS
WIDE = 384

EPS = 1e-05
NEGATIVE = -1000000000.0
ROOT_HALF = 0.7071067811865476
INV_ROOT_TAU = 0.3989422804014327

F32 = jnp.float32
BF16 = jnp.bfloat16
UNIT = 8
BIAS_UNITS = (2 * HEADS + 1) * CHUNK // UNIT
MIB = 1024 * 1024


def dot(a, b):
    return lax.dot_general(a, b, (((1,), (0,)), ((), ())), preferred_element_type=F32)


def dot_nt(a, b):
    return lax.dot_general(a, b, (((1,), (1,)), ((), ())), preferred_element_type=F32)


def dot_tn(a, b):
    return lax.dot_general(a, b, (((0,), (0,)), ((), ())), preferred_element_type=F32)


def row_mean(v):
    return jnp.sum(v, axis=-1, keepdims=True) * (1.0 / v.shape[-1])


def standardize(x):
    centred = x - row_mean(x)
    inv = lax.rsqrt(row_mean(centred * centred) + EPS)
    return centred * inv, inv


def norm_back(d, gain, stand, inv):
    scaled = d * gain
    first = row_mean(scaled)
    second = row_mean(scaled * stand)
    gain_grad = jnp.sum(d * stand, axis=0, keepdims=True)
    return inv * (scaled - first - stand * second), gain_grad


def gelu_value(hidden):
    return 0.5 * hidden * (1.0 + lax.erf(hidden * ROOT_HALF))


def gelu_parts(hidden):
    half = 0.5 * (1.0 + lax.erf(hidden * ROOT_HALF))
    slope = half + hidden * jnp.exp(-0.5 * hidden * hidden) * INV_ROOT_TAU
    return hidden * half, slope


def split3(v):
    hi = v.astype(BF16)
    rest = v - hi.astype(F32)
    mid = rest.astype(BF16)
    low = (rest - mid.astype(F32)).astype(BF16)
    return hi, mid, low


def spread_matrices():
    out = np.zeros((LEVELS, PAIR, WIDE), np.float32)
    for zj in range(LEVELS):
        for aj in range(WLAT):
            for d in range(SHIFTS):
                out[zj, aj * SHIFTS + d, (SHIFTS - 1 - d) * CHUNK + zj * WLAT + aj] = 1.0
    return out


def put(scr, rows, value):
    width = value.shape[1]
    for tile in range(-(-width // 128)):
        lanes = min(128, width - tile * 128)
        scr[tile, rows, 0:lanes] = value[:, tile * 128 : tile * 128 + lanes]


def get(scr, rows, width):
    parts = [scr[tile, rows, :] for tile in range(-(-width // 128))]
    return jnp.concatenate(parts, axis=1)[:, 0:width]


def head_masks(width, dtype):
    lane = lax.broadcasted_iota(jnp.int32, (1, width), 1)
    size = width // HEADS
    return [((lane >= h * size) & (lane < (h + 1) * size)).astype(dtype) for h in range(HEADS)]


def lat_inside(n):
    return lax.rem(n, WLAT)


def lat_row(row_iota, lat, shifted, lat_total):
    row = lat * WLAT + lat_inside(row_iota)
    if shifted:
        row = row + WLAT // 2
        row = jnp.where(row >= lat_total, row - lat_total, row)
    return row


def expand_bias(table, spread, tab_scr, rows_scr, wide_scr, bias_scr, lat, shifted, lat_total):
    for h in range(HEADS):
        tab_scr[h : h + 1, :] = table[h]
    for zi in range(LEVELS):
        for zj in range(LEVELS):
            for ai in range(WLAT):
                at = ((zi * LEVELS + zj) * WLAT + ai) * PAIR
                row = zj * CHUNK * 8 + (zi * WLAT + ai) * 8
                rows_scr[row : row + HEADS, 0:PAIR] = tab_scr[0:HEADS, at : at + PAIR]
    count = CHUNK * 8
    total = jnp.zeros((count, WIDE), F32)
    for zj in range(LEVELS):
        parts = split3(rows_scr[zj * count : (zj + 1) * count, 0:PAIR])
        for part in parts:
            total = total + dot(part, spread[zj])
    put(wide_scr, slice(None), total)
    i = lax.broadcasted_iota(jnp.int32, (CHUNK, WIN), 0)
    j = lax.broadcasted_iota(jnp.int32, (CHUNK, WIN), 1)
    allowed = lat_row(j, lat, shifted, lat_total) < lat_total - PAD
    if shifted:
        last = lat_total - WLAT // 2
        region_i = (lat * WLAT + lat_inside(i)) >= last
        region_j = (lat * WLAT + lat_inside(j)) >= last
        allowed = allowed & (region_i == region_j)
    for h in range(HEADS):
        wide = get(wide_scr, pl.ds(h, CHUNK, stride=8), WIDE)
        for oi in range(WLON):
            back = (WLON - 1 - oi) * CHUNK
            moved = wide if back == 0 else pltpu.roll(wide, WIDE - back, axis=1)
            at = h * WIN + oi * CHUNK
            bias_scr[at : at + CHUNK, :] = jnp.where(allowed, moved[:, 0:WIN], NEGATIVE)


def fold_bias(sums, put_unit):
    rest = jnp.zeros((CHUNK, 128), F32)

    def emit(at, value):
        for r in range(CHUNK // UNIT):
            put_unit(at * (CHUNK // UNIT) + r, value[r * UNIT : (r + 1) * UNIT, :].astype(BF16))

    for h in range(HEADS):
        total = jnp.zeros((CHUNK, WIDE), F32)
        for oi in range(WLON):
            back = (WLON - 1 - oi) * CHUNK
            at = h * WIN + oi * CHUNK
            part = sums[at : at + CHUNK, :]
            total = total + (part if back == 0 else pltpu.roll(part, back, axis=1))
        emit(h, total[:, 0:128])
        emit(HEADS + h, total[:, 128:256])
        last = total[:, 256:384]
        rest = rest + (last if h == 0 else pltpu.roll(last, 8 * h, axis=1))
    emit(2 * HEADS, rest)

def stack_heads(v, masks):
    return jnp.concatenate([v * mask for mask in masks], axis=0)


def pick_heads(v, masks):
    total = v[0:WIN] * masks[0]
    for h in range(1, HEADS):
        total = total + v[h * WIN : (h + 1) * WIN] * masks[h]
    return total


def attend(qkv, bias, mixed, probs, stack_scr, width):
    masks = head_masks(width, BF16)
    masks32 = head_masks(width, F32)
    scale = (width // HEADS) ** -0.5

    def window(w, carry):
        rows = pl.ds(pl.multiple_of(w * WIN, 16), WIN)
        q = qkv[rows, 0:width]
        k = qkv[rows, width : 2 * width]
        v = qkv[rows, 2 * width : 3 * width]
        scores = dot_nt(stack_heads(q, masks), k)
        for h in range(HEADS):
            part = slice(h * WIN, (h + 1) * WIN)
            logits = scores[part] * scale + bias[part, :]
            weights = jnp.exp(logits - jnp.max(logits, axis=-1, keepdims=True))
            p = weights * (1.0 / jnp.sum(weights, axis=-1, keepdims=True))
            probs[w, h] = p
            stack_scr[part, :] = p.astype(BF16)
        mixed[rows, :] = pick_heads(dot(stack_scr[...], v), masks32).astype(BF16)
        return carry

    lax.fori_loop(0, probs.shape[0], window, 0, unroll=True)


def attend_back(qkv, probs, dmix, field, sums, low_scr, prob_scr, width):
    masks = head_masks(width, BF16)
    masks32 = head_masks(width, F32)
    scale = (width // HEADS) ** -0.5

    def window(w, carry):
        rows = pl.ds(pl.multiple_of(w * WIN, 16), WIN)
        q = qkv[rows, 0:width]
        k = qkv[rows, width : 2 * width]
        v = qkv[rows, 2 * width : 3 * width]
        up = stack_heads(dmix[rows, :], masks)
        prob_grad = dot_nt(up, v)
        for h in range(HEADS):
            part = slice(h * WIN, (h + 1) * WIN)
            p = probs[w, h]
            weighted = p * prob_grad[part]
            ds = weighted - p * jnp.sum(weighted, axis=-1, keepdims=True)
            sums[part, 0:WIN] += ds
            low_scr[part, :] = ds.astype(BF16)
            prob_scr[part, :] = p.astype(BF16)
        low = low_scr[...]
        dq = pick_heads(dot(low, k), masks32)
        dk = dot_tn(low, stack_heads(q, masks))
        dv = dot_tn(prob_scr[...], up)
        field[rows, 0:width] = (dq * scale).astype(BF16)
        field[rows, width : 2 * width] = (dk * scale).astype(BF16)
        field[rows, 2 * width : 3 * width] = dv.astype(BF16)
        return carry

    lax.fori_loop(0, probs.shape[0], window, 0, unroll=True)


def lon_major(src, scr):
    levels, lats, lons, width = src.shape
    for z in range(levels):
        for a in range(lats):
            at = (z * lats + a) * lons
            put(scr, slice(at, at + lons), src[z, a].astype(F32))


def lon_column(scr, lon, lons, width):
    return get(scr, pl.ds(lon, CHUNK, stride=lons), width)


def flat_store(dst, at, mat, cols):
    rows = mat.shape[1]
    if cols % 128 == 0:
        per = cols // 128
        for c in range(per):
            dst[pl.ds(at + c, rows, stride=per), :] = mat[c]
        return rows * per
    per = 2 * cols // 128
    half = cols // 128
    even = get(mat, pl.ds(0, rows // 2, stride=2), cols)
    odd = get(mat, pl.ds(1, rows // 2, stride=2), cols)
    for c in range(half):
        dst[pl.ds(at + c, rows // 2, stride=per), :] = even[:, c * 128 : (c + 1) * 128]
    dst[pl.ds(at + half, rows // 2, stride=per), :] = jnp.concatenate(
        [even[:, half * 128 : half * 128 + 64], odd[:, 0:64]], axis=1
    )
    for c in range(half):
        dst[pl.ds(at + half + 1 + c, rows // 2, stride=per), :] = odd[
            :, 64 + c * 128 : 64 + (c + 1) * 128
        ]
    return rows * cols // 128


def send_units(scr, base, out):
    lons, units = out.shape[:2]
    for j in range(lons):
        for u in range(units):
            at = base + (j * units + u) * UNIT
            if not isinstance(at, int):
                at = pl.multiple_of(at, UNIT)
            out[j, u] = scr[pl.ds(at, UNIT), :].astype(BF16)


def halves(scr, lat, keep, give):
    half = keep.shape[0] * keep.shape[1] * UNIT
    send_units(scr, lat * half, keep)
    send_units(scr, (1 - lat) * half, give)


def bias_units(sums, out):
    lons, per = out.shape[:2]

    def put_unit(k, value):
        out[k // per, k % per] = value

    fold_bias(sums, put_unit)
    for k in range(BIAS_UNITS, lons * per):
        put_unit(k, jnp.zeros((UNIT, 128), BF16))

def forward_core(x, b, refs, qkv_scr, bias_scr, mixed, probs, stack_scr):
    qkv_w, proj_w, gains = refs
    width = x.shape[-1]
    stand, inv = standardize(x)
    normed = (stand * gains[b, 0:1, :]).astype(BF16)
    qkv_scr[...] = dot(normed, qkv_w[b]).astype(BF16)
    attend(qkv_scr, bias_scr, mixed, probs, stack_scr, width)
    att = dot(mixed[...], proj_w[b]).astype(BF16)
    resid = (x + att.astype(F32)).astype(BF16).astype(F32)
    return resid, normed


def first_kernel(
    lat_total, tokens_in, cot_in, table_in, spread_in, qkv_in, proj_in, up_in, down_in, gains_in,
    x_out, tail_out, head_out, qkv_out, mixed_out, probs_out, resid_out, hidden_out, active_out,
    scr, cot_scr, tab_scr, rows_scr, wide_scr, bias_scr,
    cot, table, spread, tokens, qkv_w, gains, proj_w, up_w, down_w, stack_scr, sems,
):
    copies = []
    for source, target in (
        (cot_in, cot),
        (table_in.at[0:1], table),
        (spread_in, spread),
        (tokens_in, tokens),
        (qkv_in.at[0:1], qkv_w),
        (gains_in, gains),
        (proj_in.at[0:1], proj_w),
        (up_in.at[0:1], up_w),
        (down_in.at[0:1], down_w),
    ):
        copies.append(pltpu.make_async_copy(source, target, sems.at[len(copies)]))
    for copy in copies:
        copy.start()
    lat = lax.axis_index("lat")
    width = tokens.shape[-1]
    lons = tokens.shape[2]
    cut = CHUNK * (WLON // 2)
    copies[0].wait()
    lon_major(cot, cot_scr)
    g = jnp.concatenate([lon_column(cot_scr, lon, lons, width) for lon in range(lons)], axis=0)
    head_out[1] = g[0:cut, :].astype(BF16)
    tail_out[1] = g[cut:, :].astype(BF16)
    copies[1].wait()
    copies[2].wait()
    expand_bias(
        table.at[0], spread, tab_scr, rows_scr, wide_scr, bias_scr, lat, False, lat_total
    )
    copies[3].wait()
    lon_major(tokens, scr)
    x = jnp.concatenate([lon_column(scr, lon, lons, width) for lon in range(lons)], axis=0)
    x_out[...] = x.astype(BF16)
    for copy in copies[4:]:
        copy.wait()

    resid, _ = forward_core(
        x, 0, (qkv_w, proj_w, gains), qkv_out, bias_scr, mixed_out, probs_out, stack_scr
    )
    resid_out[...] = resid.astype(BF16)
    stand, _ = standardize(resid)
    normed = (stand * gains[0, 1:2, :]).astype(BF16)
    hidden = dot(normed, up_w[0])
    hidden_out[...] = hidden
    active = gelu_value(hidden).astype(BF16)
    active_out[...] = active
    result = resid + dot_nt(active, down_w[0])
    head_out[0] = result[0:cut, :].astype(BF16)
    tail_out[0] = result[cut:, :].astype(BF16)


def bias_kernel(
    lat_total, table, spread, hidden, bias_out, slope_out, tab_scr, rows_scr, wide_scr
):
    lat = lax.axis_index("lat")
    slope_out[...] = gelu_parts(hidden[...])[1].astype(BF16)
    expand_bias(
        table.at[1], spread, tab_scr, rows_scr, wide_scr, bias_out, lat, True, lat_total
    )


def merge_ahead(scr_own, scr_oth, rows):
    half = WLAT // 2
    n = lax.broadcasted_iota(jnp.int32, (rows, 1), 0)
    return jnp.where(
        lat_inside(n) < half,
        pltpu.roll(scr_own[...], rows - half, axis=0),
        pltpu.roll(scr_oth[...], half, axis=0),
    )


def merge_behind(scr_own, scr_oth, rows):
    half = WLAT // 2
    n = lax.broadcasted_iota(jnp.int32, (rows, 1), 0)
    return jnp.where(
        lat_inside(n) >= half,
        pltpu.roll(scr_own[...], half, axis=0),
        pltpu.roll(scr_oth[...], rows - half, axis=0),
    )


def second_kernel(
    lat_total,
    kept, tail, lon_head, lat_tail, diag_head, bias, qkv_w, proj_w, up_w, down_w, gains, *rest
):
    run_second(
        lat_total, tail, lon_head, lat_tail, diag_head, bias, qkv_w, proj_w, up_w, down_w, gains,
        *rest[kept:kept + 12], *rest[2 * kept + 12 :]
    )


def run_second(
    lat_total,
    tail, lon_head, lat_tail, diag_head, bias, qkv_w, proj_w, up_w, down_w, gains,
    head_out, tail_out, n1_out, field_out, mixed_out, low_out, n2_out, hg_out, active_out, g_out,
    sums_out, gain_out,
    scr_own, scr_oth, qkv_scr, probs_scr, dmix_scr, low_scr, prob_scr,
):
    lat = lax.axis_index("lat")
    rows, width = scr_own.shape
    cut = CHUNK * (WLON // 2)

    def rolled(which):
        scr_own[0 : rows - cut, :] = tail[which].astype(F32)
        scr_own[rows - cut :, :] = lon_head[which].astype(F32)
        scr_oth[0 : rows - cut, :] = lat_tail[which].astype(F32)
        scr_oth[rows - cut :, :] = diag_head[which].astype(F32)
        return merge_ahead(scr_own, scr_oth, rows)

    g = rolled(1)
    n = lax.broadcasted_iota(jnp.int32, (rows, 1), 0)
    keep = lat_row(n, lat, True, lat_total) < lat_total - PAD
    g = jnp.where(keep, g, 0.0)
    g_out[...] = g.astype(BF16)

    x = rolled(0)

    resid, normed = forward_core(
        x, 1, (qkv_w, proj_w, gains), qkv_scr, bias, mixed_out, probs_scr, low_scr
    )
    n1_out[...] = normed
    stand2, inv2 = standardize(resid)
    normed2 = (stand2 * gains[1, 1:2, :]).astype(BF16)
    n2_out[...] = normed2
    active, slope = gelu_parts(dot(normed2, up_w[1]))
    active_out[...] = active.astype(BF16)

    hg = (dot(g_out[...], down_w[1]) * slope).astype(BF16)
    hg_out[...] = hg
    part, gain_two = norm_back(dot_nt(hg, up_w[1]), gains[1, 1:2, :], stand2, inv2)
    rg = g + part
    low = rg.astype(BF16)
    low_out[...] = low
    dmix_scr[...] = dot_nt(low, proj_w[1]).astype(BF16)
    sums_out[...] = jnp.zeros(sums_out.shape, F32)
    attend_back(
        qkv_scr, probs_scr, dmix_scr, field_out, sums_out, low_scr, prob_scr, width
    )
    ng = dot_nt(field_out[...], qkv_w[1]).astype(BF16).astype(F32)
    stand1, inv1 = standardize(x)
    part, gain_one = norm_back(ng, gains[1, 0:1, :], stand1, inv1)
    dx = rg + part
    head_out[...] = dx[0 : rows - cut, :].astype(BF16)
    tail_out[...] = dx[rows - cut :, :].astype(BF16)
    gain_out[0:1, :] = gain_one
    gain_out[1:2, :] = gain_two


def outer_kernel(
    n1, field, mixed, low, n2, hg, active, g, sums,
    keep, give, bias_out,
    m576, m192, m768, mdown, flat_scr,
):
    put(m576, slice(None), dot_tn(n1[...], field[...]))
    at = flat_store(flat_scr, 0, m576, field.shape[1])
    put(m192, slice(None), dot_tn(mixed[...], low[...]))
    at += flat_store(flat_scr, at, m192, mixed.shape[1])
    put(m768, slice(None), dot_tn(n2[...], hg[...]))
    at += flat_store(flat_scr, at, m768, active.shape[1])
    put(mdown, slice(None), dot_tn(active[...], g[...]))
    at += flat_store(flat_scr, at, mdown, mixed.shape[1])
    halves(flat_scr, lax.axis_index("lat"), keep, give)
    bias_units(sums, bias_out)


def lat_split(keep, got, *refs):
    keep_out, give_out = refs[-2:]
    units = keep.shape[1]
    x = lax.rem(lax.axis_index("lon"), 2)
    for out, side in ((keep_out, x), (give_out, 1 - x)):
        for z in range(out.shape[0]):
            j = 2 * z + side
            out[z, 0:units] = (keep[j].astype(F32) + got[j].astype(F32)).astype(BF16)
            if out.shape[1] > units:
                out[z, units:] = refs[0][j]


def split_z(first, second, got_first, got_second, *outs):
    count, cut = first.shape[:2]
    z = lax.div(lax.axis_index("lon"), 2)
    for k, out in enumerate(outs):
        at = lax.rem(z + k, count)
        out[0:cut] = (first[at].astype(F32) + got_first[at].astype(F32)).astype(BF16)
        out[cut:] = (second[at].astype(F32) + got_second[at].astype(F32)).astype(BF16)


def sum_refs(*refs):
    total = refs[0][...].astype(F32)
    for ref in refs[1:-2]:
        total = total + ref[...].astype(F32)
    refs[-1][...] = total.astype(BF16)


def add_pair(keep, got, order, out):
    out[...] = (keep[...].astype(F32) + got[...].astype(F32)).astype(BF16)


def sum_pieces(pieces, order, out):
    total = pieces[0].astype(F32)
    for k in range(1, pieces.shape[0]):
        total = total + pieces[k].astype(F32)
    total = total.astype(BF16)
    if len(out.shape) == len(pieces.shape):
        for k in range(out.shape[0]):
            out[k] = total
    else:
        out[...] = total


def join_z(*refs):
    out = refs[-1]
    count = out.shape[0]
    z = lax.div(lax.axis_index("lon"), 2)
    for k in range(count):
        out[lax.rem(z + count - k, count)] = refs[k][...]


def third_kernel(
    head, lon_tail, lat_head, diag_tail, resid, slope, active, mixed,
    proj_w, up_w, down_w, gains, order,
    keep_out, give_out, rg_out, dmix_out, gain_out,
    scr_own, scr_oth, m192, m768, mdown, flat_scr,
):
    rows, width = scr_own.shape
    cut = CHUNK * (WLON // 2)
    scr_own[0:cut, :] = lon_tail[...].astype(F32)
    scr_own[cut:, :] = head[...].astype(F32)
    scr_oth[0:cut, :] = diag_tail[...].astype(F32)
    scr_oth[cut:, :] = lat_head[...].astype(F32)
    g = merge_behind(scr_own, scr_oth, rows)
    g_low = g.astype(BF16)
    hg = dot(g_low, down_w[0])
    stand2, inv2 = standardize(resid[...].astype(F32))
    normed2 = (stand2 * gains[0, 1:2, :]).astype(BF16)
    hg = (hg * slope[...].astype(F32)).astype(BF16)
    part, gain_two = norm_back(dot_nt(hg, up_w[0]), gains[0, 1:2, :], stand2, inv2)
    rg = g + part
    rg_out[...] = rg
    low = rg.astype(BF16)
    dmix_out[...] = dot_nt(low, proj_w[0]).astype(BF16)
    gain_out[...] = gain_two
    put(m192, slice(None), dot_tn(mixed[...], low))
    at = flat_store(flat_scr, 0, m192, mixed.shape[1])
    put(m768, slice(None), dot_tn(normed2, hg))
    at += flat_store(flat_scr, at, m768, active.shape[1])
    put(mdown, slice(None), dot_tn(active[...], g_low))
    at += flat_store(flat_scr, at, mdown, mixed.shape[1])
    flat_scr[at:, :] = jnp.zeros((flat_scr.shape[0] - at, 128), F32)
    halves(flat_scr, lax.axis_index("lat"), keep_out, give_out)


def gain_rows(one, two):
    return jnp.concatenate(
        [
            one[:, 0:128],
            jnp.concatenate([one[:, 128:192], two[:, 0:64]], axis=1),
            two[:, 64:192],
        ],
        axis=0,
    )


def fourth_kernel(
    x_in, qkv, probs, dmix, rg, gain_two, gains_late, order, qkv_w, gains,
    tokens_out, keep, give, bias_out,
    field, sums, m576, flat_scr, dx_scr, low_scr, prob_scr,
):
    width = x_in.shape[-1]
    levels, lats, lons = tokens_out.shape[:3]
    sums[...] = jnp.zeros(sums.shape, F32)
    attend_back(qkv, probs, dmix, field, sums, low_scr, prob_scr, width)
    stand1, inv1 = standardize(x_in[...].astype(F32))
    normed = (stand1 * gains[0, 0:1, :]).astype(BF16)
    ng = dot_nt(field[...], qkv_w[0]).astype(BF16).astype(F32)
    part, gain_one = norm_back(ng, gains[0, 0:1, :], stand1, inv1)
    put(m576, slice(None), dot_tn(normed, field[...]))
    at = flat_store(flat_scr, 0, m576, field.shape[1])
    flat_scr[at:, :] = jnp.zeros((flat_scr.shape[0] - at, 128), F32)
    flat_scr[at : at + 3, :] = gain_rows(gain_one, gain_two[...])
    flat_scr[at + 3 : at + 6, :] = gain_rows(gains_late[0:1, :], gains_late[1:2, :])
    bias_units(sums, bias_out)
    halves(flat_scr, lax.axis_index("lat"), keep, give)
    put(dx_scr, slice(None), rg[...] + part)
    for z in range(levels):
        for a in range(lats):
            tokens_out[z, a] = get(
                dx_scr, pl.ds(z * lats + a, lons, stride=CHUNK), width
            ).astype(BF16)


def place(pieces, first, last, dests, scr):
    total = jnp.zeros((UNIT, 128), F32)
    lons = pieces.shape[1]
    per = last - first
    k = 0
    for where, room in dests:
        for at in range(where, where + room, UNIT):
            half, j, u = k // (per * lons), k // per % lons, k % per
            value = pieces[half, j, first + u].astype(F32)
            scr[at : at + UNIT, :] = value
            total = total + value * value
            k += 1
    return total


def bias_rows(piece, base, spread, out, rows_scr, wide_scr, tab_scr):
    lat = lax.axis_index("lat")
    extra = -(-BIAS_UNITS // piece.shape[1])

    def read(at):
        parts = []
        for r in range(CHUNK // UNIT):
            k = at * (CHUNK // UNIT) + r
            parts.append(piece[lat, k // extra, base + k % extra].astype(F32))
        return jnp.concatenate(parts, axis=0)

    rest = read(2 * HEADS)
    for h in range(HEADS):
        rows = pl.ds(h, CHUNK, stride=8)
        wide_scr[0, rows, :] = read(h)
        wide_scr[1, rows, :] = read(HEADS + h)
        wide_scr[2, rows, :] = rest if h == 0 else pltpu.roll(rest, 128 - 8 * h, axis=1)
    low = get(wide_scr, slice(None), WIDE).astype(BF16)
    for zj in range(LEVELS):
        rows_scr[...] = dot_nt(low, spread[zj])
        for zi in range(LEVELS):
            for ai in range(WLAT):
                at = ((zi * LEVELS + zj) * WLAT + ai) * PAIR
                row = (zi * WLAT + ai) * 8
                tab_scr[0:HEADS, at : at + PAIR] = rows_scr[row : row + HEADS, 0:PAIR]
    for h in range(HEADS):
        out[h] = tab_scr[h : h + 1, :]


def late_kernel(
    units_a, extra, spread, same, same_x, cross, cross_x, flat_out, squares_out, bias_out,
    rows_scr, wide_scr, tab_scr, a,
):
    lat = lax.axis_index("lat")
    x = lax.rem(lax.axis_index("lon"), 2)
    for z in range(same.shape[0]):
        a[lat, 2 * z + x] = same[z]
        a[lat, 2 * z + 1 - x] = same_x[z]
        a[1 - lat, 2 * z + x] = cross[z]
        a[1 - lat, 2 * z + 1 - x] = cross_x[z]
    total = place(a, 0, units_a, [(0, 3456)], flat_out)
    squares_out[...] = total + place(
        a, units_a + extra, a.shape[2], [(3456, flat_out.shape[0] - 3456)], flat_out
    )
    bias_rows(a, units_a, spread, bias_out, rows_scr, wide_scr, tab_scr)


def last_kernel(
    units_c, spread, flat_ab, squares, bias_late, own_c, oth_c, update_out, bias_out,
    scr, rows_scr, wide_scr, tab_scr, c,
):
    lat = lax.axis_index("lat")
    for j in range(own_c.shape[0]):
        c[lat, j] = own_c[j]
        c[1 - lat, j] = oth_c[j]
    total = squares[...] + place(c, 0, units_c, [(0, 872)], scr)
    count = update_out.shape[0]
    mean = jnp.sum(total) * (1.0 / (count * 128))
    scale = lax.rsqrt(mean + 1e-06)
    update_out[0:864, :] = (scr[0:864, :] * scale).astype(BF16)
    at = 0
    for where, rows in (
        (864, 864), (2016, 288), (3456, 1152), (5760, 1152), (1728, 288), (2304, 1152), (4608, 1152)
    ):
        update_out[where : where + rows, :] = (flat_ab[at : at + rows, :] * scale).astype(BF16)
        at += rows
    update_out[6912:count, :] = (scr[864 : 864 + count - 6912, :] * scale).astype(BF16)
    bias_rows(c, units_c, spread, bias_out.at[0], rows_scr, wide_scr, tab_scr)
    bias_out[1] = bias_late[...]


def call(kernel, outs, scratch, args, micros, mib, spaces=None, near=(), kept=0):
    spaces = spaces or [pltpu.VMEM] * len(args)
    return pl.pallas_call(
        kernel,
        out_shape=[
            (pltpu.VMEM if at in near else jax.ShapeDtypeStruct)(*entry)
            for at, entry in enumerate(outs)
        ],
        in_specs=[pl.BlockSpec(memory_space=space) for space in spaces],
        out_specs=[
            pl.BlockSpec(memory_space=pltpu.VMEM if at < len(outs) - kept else pl.ANY)
            for at in range(len(outs))
        ],
        input_output_aliases={
            len(args) - kept + k: len(outs) - kept + k for k in range(kept)
        },
        scratch_shapes=[
            pltpu.VMEM(*entry) if isinstance(entry, tuple) else entry for entry in scratch
        ],
        compiler_params=pltpu.CompilerParams(vmem_limit_bytes=mib * MIB),
        cost_estimate=pl.CostEstimate(
            flops=int(micros * 1.1e9), bytes_accessed=10**5, transcendentals=0
        ),
    )(*args)


def lat_swap(value):
    return lax.ppermute(value, "lat", [(0, 1), (1, 0)])


def lon_send(value, step):
    count = lax.axis_size("lon")
    return lax.ppermute(value, "lon", [(s, (s + step) % count) for s in range(count)])


def x_swap(value):
    count = lax.axis_size("lon")
    return lax.ppermute(value, "lon", [(s, s ^ 1) for s in range(count)])


def diag_send(value, step):
    count = lax.axis_size("lon")
    pairs = []
    for s in range(count):
        for t in range(2):
            pairs.append((2 * s + t, 2 * ((s + step) % count) + 1 - t))
    return lax.ppermute(value, ("lon", "lat"), pairs)


def shards(
    tokens, cotangent, qkv_weight, proj_weight, up_weight, down_weight, norm_gain, bias_table
):
    levels, lats, lons, width = tokens.shape
    rows = levels * lats * lons
    wins = rows // WIN
    hid = up_weight.shape[-1]
    heads = bias_table.shape[2]
    lon_size = lax.axis_size("lon")
    zs = lon_size // 2
    lat_total = lats * lax.axis_size("lat")
    cut = CHUNK * (WLON // 2)
    spread = jnp.asarray(spread_matrices(), BF16)
    down_turned = jnp.swapaxes(down_weight, 1, 2)
    table = jnp.swapaxes(bias_table, 1, 2)
    token = (rows, width)
    field_shape = ((rows, 3 * width), BF16)
    probs_shape = ((wins, heads, WIN, WIN), F32)
    stack_shape = ((heads * WIN, WIN), BF16)
    bias_shape = ((heads * WIN, WIN), F32)
    sums_shape = ((heads * WIN, WIDE), F32)
    tab_scr = ((8, table.shape[-1]), F32)
    rows_scr = ((LEVELS * CHUNK * 8, PAIR), F32)
    wide_scr = ((WIDE // 128, CHUNK * 8, 128), F32)
    tiles = -(-width // 128)
    token_scr = ((tiles, rows, 128), F32)
    m576 = ((-(-3 * width // 128), width, 128), F32)
    m192 = ((tiles, width, 128), F32)
    m768 = ((hid // 128, width, 128), F32)
    mdown = ((tiles, hid, 128), F32)

    block_rows = (qkv_weight[0].size + proj_weight[0].size + 2 * up_weight[0].size) // 128
    qkv_rows = qkv_weight[0].size // 128
    counts = (block_rows, block_rows - qkv_rows, qkv_rows + 8)
    units_a, units_b, units_c = [-(-count // (2 * lon_size * UNIT)) for count in counts]
    extra = -(-BIAS_UNITS // lon_size)

    def units(*lead):
        return (lead + (UNIT, 128), BF16)

    def flat_scr(per):
        return ((2 * lon_size * per * UNIT, 128), F32)

    x0, tail, head, qkv0, mixed0, probs0, resid0, hidden0, active0 = call(
        functools.partial(first_kernel, lat_total),
        [
            (token, BF16),
            ((2, rows - cut, width), BF16),
            ((2, cut, width), BF16),
            field_shape,
            (token, BF16),
            probs_shape,
            (token, BF16),
            ((rows, hid), F32),
            ((rows, hid), BF16),
        ],
        [
            token_scr,
            token_scr,
            tab_scr,
            rows_scr,
            wide_scr,
            bias_shape,
            (cotangent.shape, BF16),
            ((1,) + table.shape[1:], F32),
            (spread.shape, BF16),
            (tokens.shape, BF16),
            ((1,) + qkv_weight.shape[1:], BF16),
            (norm_gain.shape, F32),
            ((1,) + proj_weight.shape[1:], BF16),
            ((1,) + up_weight.shape[1:], BF16),
            ((1,) + down_turned.shape[1:], BF16),
            stack_shape,
            pltpu.SemaphoreType.DMA((9,)),
        ],
        [
            pltpu.with_memory_space_constraint(arg, pltpu.HBM)
            for arg in (
                tokens, cotangent, table, spread, qkv_weight, proj_weight, up_weight, down_turned,
                norm_gain,
            )
        ],
        8,
        16,
        [pltpu.HBM] * 9,
        near=(0, 3, 4, 5, 6, 8),
    )
    lon_head = lon_send(head, -1)
    diag_head = diag_send(head, -1)
    lat_tail = lat_swap(tail)
    bias1, slope0 = call(
        functools.partial(bias_kernel, lat_total),
        [bias_shape, ((rows, hid), BF16)],
        [tab_scr, rows_scr, wide_scr],
        (table, spread, hidden0),
        3,
        12,
        near=(1,),
    )

    saved = [x0, qkv0, mixed0, probs0, resid0, active0, slope0]
    (
        dhead, dtail, n1, field1, mixed1, low1, n2, hg1, active1, g1, sums1, gains1,
        *saved,
    ) = call(
        functools.partial(second_kernel, lat_total, len(saved)),
        [
            ((rows - cut, width), BF16),
            ((cut, width), BF16),
            (token, BF16),
            field_shape,
            (token, BF16),
            (token, BF16),
            (token, BF16),
            ((rows, hid), BF16),
            ((rows, hid), BF16),
            (token, BF16),
            sums_shape,
            ((2, width), F32),
            *[(value.shape, value.dtype) for value in saved],
        ],
        [
            (token, F32),
            (token, F32),
            field_shape,
            probs_shape,
            (token, BF16),
            stack_shape,
            stack_shape,
        ],
        (
            tail, lon_head, lat_tail, diag_head, bias1, qkv_weight, proj_weight, up_weight,
            down_turned, norm_gain,
            *[pltpu.with_memory_space_constraint(value, pltpu.VMEM) for value in saved],
        ),
        19,
        16,
        [pltpu.VMEM] * 10 + [pl.ANY] * len(saved),
        near=tuple(range(12, 12 + len(saved))),
        kept=len(saved),
    )
    x0, qkv0, mixed0, probs0, resid0, active0, slope0 = saved
    lon_tail = lon_send(dtail, 1)
    diag_tail = diag_send(dtail, 1)
    lat_dhead = lat_swap(dhead)

    keep_a, give_a, bias_a = call(
        outer_kernel,
        [units(lon_size, units_a), units(lon_size, units_a), units(lon_size, extra)],
        [m576, m192, m768, mdown, flat_scr(units_a)],
        (n1, field1, mixed1, low1, n2, hg1, active1, g1, sums1),
        3,
        14,
    )
    got_a = lat_swap(give_a)

    units_xa = units_a + extra
    keep_xa, give_xa = call(
        lat_split, [units(zs, units_xa)] * 2, [], (keep_a, got_a, bias_a), 1, 10
    )
    got_xa = x_swap(give_xa)

    keep_b, give_b, rg0, dmix0, gain_two = call(
        third_kernel,
        [
            units(lon_size, units_b),
            units(lon_size, units_b),
            (token, F32),
            (token, BF16),
            ((1, width), F32),
        ],
        [(token, F32), (token, F32), m192, m768, mdown, flat_scr(units_b)],
        (
            dhead, lon_tail, lat_dhead, diag_tail, resid0, slope0, active0, mixed0, proj_weight,
            up_weight, down_turned, norm_gain, keep_xa,
        ),
        3,
        14,
    )
    got_b = lat_swap(give_b)
    keep_xb, give_xb = call(
        lat_split, [units(zs, units_b)] * 2, [], (keep_b, got_b), 1, 10
    )
    got_xb = x_swap(give_xb)

    tokens_grad, keep_c, give_c, bias_c = call(
        fourth_kernel,
        [
            (tokens.shape, BF16),
            units(lon_size, units_c),
            units(lon_size, units_c),
            units(lon_size, extra),
        ],
        [
            field_shape,
            sums_shape,
            m576,
            flat_scr(units_c),
            token_scr,
            stack_shape,
            stack_shape,
        ],
        (x0, qkv0, probs0, dmix0, rg0, gain_two, gains1, keep_xb, qkv_weight, norm_gain),
        7,
        14,
    )
    got_c = lat_swap(give_c)
    units_ab = units_xa + units_b
    own_ab, *gives_ab = call(
        split_z, [units(units_ab)] * zs, [], (keep_xa, keep_xb, got_xa, got_xb), 1, 10
    )
    gots_ab = [lon_send(give, 2 * (k + 1)) for k, give in enumerate(gives_ab)]
    units_xc = units_c + extra
    keep_x, give_x = call(
        lat_split, [units(zs, units_xc)] * 2, [], (keep_c, got_c, bias_c, own_ab), 1, 10
    )
    got_x = x_swap(give_x)
    (sum_ab,) = call(sum_refs, [units(units_ab)], [], (own_ab, *gots_ab, keep_x), 1, 10)
    (part_z,) = call(add_pair, [units(zs, units_xc)], [], (keep_x, got_x, sum_ab), 1, 10)
    pieces_c = lax.all_to_all(
        part_z,
        "lon",
        0,
        0,
        axis_index_groups=[[2 * z + x for z in range(zs)] for x in range(2)],
    )
    moved_ab = [lon_send(sum_ab, 2 * k) for k in range(1, zs)]
    (sum_c,) = call(
        sum_pieces, [units(lon_size, units_xc)], [], (pieces_c, moved_ab[0]), 1, 10
    )
    whole_c = lax.all_to_all(sum_c, "lon", 0, 0)
    (same,) = call(join_z, [units(zs, units_ab)], [], [sum_ab, *moved_ab, sum_c], 1, 10)
    same_x = x_swap(same)
    cross = lat_swap(same)
    cross_x = lat_swap(same_x)
    oth_c = lat_swap(whole_c)

    flat_rows = (2 * block_rows * 128 + norm_gain.size) // 128
    fold_scr = [((CHUNK * 8, PAIR), F32), wide_scr, tab_scr]
    ab_rows = 2 * block_rows - qkv_rows
    flat_ab, squares, bias_late = call(
        functools.partial(late_kernel, units_a, extra),
        [((ab_rows, 128), F32), ((UNIT, 128), F32), (table.shape[1:], F32)],
        [*fold_scr, units(2, lon_size, units_ab)],
        (spread, same, same_x, cross, cross_x),
        2,
        14,
    )
    update, bias_grad = call(
        functools.partial(last_kernel, units_c),
        [((flat_rows, 128), BF16), (table.shape, F32)],
        [((872, 128), F32), *fold_scr, units(2, lon_size, units_xc)],
        (spread, flat_ab, squares, bias_late, whole_c, oth_c),
        2,
        14,
    )
    bias_grad = jnp.swapaxes(bias_grad, 1, 2)
    return (tokens_grad, update.reshape(-1), bias_grad)


def solution(mesh):
    return jax.shard_map(
        shards,
        mesh=mesh,
        in_specs=(
            P("grp", "lat", "lon", None),
            P("grp", "lat", "lon", None),
            P(),
            P(),
            P(),
            P(),
            P(),
            P(None, "lat", None, None),
        ),
        out_specs=(P("grp", "lat", "lon", None), P("grp"), P("grp", "lat", None, None)),
        check_vma=False,
    )
```

```python
import functools

import jax
import jax.numpy as jnp
import numpy as np
from jax import lax
from jax.experimental import pallas as pl
from jax.experimental.pallas import tpu as pltpu
from jax.sharding import PartitionSpec as P

WLAT = 12
WLON = 6
PAD = 5
LEVELS = 2
HEADS = 6
CHUNK = LEVELS * WLAT
WIN = CHUNK * WLON
SHIFTS = 2 * WLON - 1
PAIR = WLAT * SHIFTS
WIDE = 384

EPS = 1e-05
NEGATIVE = -1000000000.0
ROOT_HALF = 0.7071067811865476
INV_ROOT_TAU = 0.3989422804014327

F32 = jnp.float32
BF16 = jnp.bfloat16
UNIT = 8
BIAS_UNITS = (2 * HEADS + 1) * CHUNK // UNIT
MIB = 1024 * 1024


def dot(a, b):
    return lax.dot_general(a, b, (((1,), (0,)), ((), ())), preferred_element_type=F32)


def dot_nt(a, b):
    return lax.dot_general(a, b, (((1,), (1,)), ((), ())), preferred_element_type=F32)


def dot_tn(a, b):
    return lax.dot_general(a, b, (((0,), (0,)), ((), ())), preferred_element_type=F32)


def row_mean(v):
    return jnp.sum(v, axis=-1, keepdims=True) * (1.0 / v.shape[-1])


def standardize(x):
    centred = x - row_mean(x)
    inv = lax.rsqrt(row_mean(centred * centred) + EPS)
    return centred * inv, inv


def norm_back(d, gain, stand, inv):
    scaled = d * gain
    first = row_mean(scaled)
    second = row_mean(scaled * stand)
    gain_grad = jnp.sum(d * stand, axis=0, keepdims=True)
    return inv * (scaled - first - stand * second), gain_grad


def gelu_value(hidden):
    return 0.5 * hidden * (1.0 + lax.erf(hidden * ROOT_HALF))


def gelu_parts(hidden):
    half = 0.5 * (1.0 + lax.erf(hidden * ROOT_HALF))
    slope = half + hidden * jnp.exp(-0.5 * hidden * hidden) * INV_ROOT_TAU
    return hidden * half, slope


def split3(v):
    hi = v.astype(BF16)
    rest = v - hi.astype(F32)
    mid = rest.astype(BF16)
    low = (rest - mid.astype(F32)).astype(BF16)
    return hi, mid, low


def spread_matrices():
    out = np.zeros((LEVELS, PAIR, WIDE), np.float32)
    for zj in range(LEVELS):
        for aj in range(WLAT):
            for d in range(SHIFTS):
                out[zj, aj * SHIFTS + d, (SHIFTS - 1 - d) * CHUNK + zj * WLAT + aj] = 1.0
    return out


def put(scr, rows, value):
    width = value.shape[1]
    for tile in range(-(-width // 128)):
        lanes = min(128, width - tile * 128)
        scr[tile, rows, 0:lanes] = value[:, tile * 128 : tile * 128 + lanes]


def get(scr, rows, width):
    parts = [scr[tile, rows, :] for tile in range(-(-width // 128))]
    return jnp.concatenate(parts, axis=1)[:, 0:width]


def head_masks(width, dtype):
    lane = lax.broadcasted_iota(jnp.int32, (1, width), 1)
    size = width // HEADS
    return [((lane >= h * size) & (lane < (h + 1) * size)).astype(dtype) for h in range(HEADS)]


def lat_inside(n):
    return lax.rem(n, WLAT)


def lat_row(row_iota, lat, shifted, lat_total):
    row = lat * WLAT + lat_inside(row_iota)
    if shifted:
        row = row + WLAT // 2
        row = jnp.where(row >= lat_total, row - lat_total, row)
    return row


def expand_bias(table, spread, tab_scr, rows_scr, wide_scr, bias_scr, lat, shifted, lat_total):
    for h in range(HEADS):
        tab_scr[h : h + 1, :] = table[h]
    for zi in range(LEVELS):
        for zj in range(LEVELS):
            for ai in range(WLAT):
                at = ((zi * LEVELS + zj) * WLAT + ai) * PAIR
                row = zj * CHUNK * 8 + (zi * WLAT + ai) * 8
                rows_scr[row : row + HEADS, 0:PAIR] = tab_scr[0:HEADS, at : at + PAIR]
    count = CHUNK * 8
    total = jnp.zeros((count, WIDE), F32)
    for zj in range(LEVELS):
        parts = split3(rows_scr[zj * count : (zj + 1) * count, 0:PAIR])
        for part in parts:
            total = total + dot(part, spread[zj])
    put(wide_scr, slice(None), total)
    i = lax.broadcasted_iota(jnp.int32, (CHUNK, WIN), 0)
    j = lax.broadcasted_iota(jnp.int32, (CHUNK, WIN), 1)
    allowed = lat_row(j, lat, shifted, lat_total) < lat_total - PAD
    if shifted:
        last = lat_total - WLAT // 2
        region_i = (lat * WLAT + lat_inside(i)) >= last
        region_j = (lat * WLAT + lat_inside(j)) >= last
        allowed = allowed & (region_i == region_j)
    for h in range(HEADS):
        wide = get(wide_scr, pl.ds(h, CHUNK, stride=8), WIDE)
        for oi in range(WLON):
            back = (WLON - 1 - oi) * CHUNK
            moved = wide if back == 0 else pltpu.roll(wide, WIDE - back, axis=1)
            at = h * WIN + oi * CHUNK
            bias_scr[at : at + CHUNK, :] = jnp.where(allowed, moved[:, 0:WIN], NEGATIVE)


def fold_bias(sums, put_unit):
    rest = jnp.zeros((CHUNK, 128), F32)

    def emit(at, value):
        for r in range(CHUNK // UNIT):
            put_unit(at * (CHUNK // UNIT) + r, value[r * UNIT : (r + 1) * UNIT, :].astype(BF16))

    for h in range(HEADS):
        total = jnp.zeros((CHUNK, WIDE), F32)
        for oi in range(WLON):
            back = (WLON - 1 - oi) * CHUNK
            at = h * WIN + oi * CHUNK
            part = sums[at : at + CHUNK, :]
            total = total + (part if back == 0 else pltpu.roll(part, back, axis=1))
        emit(h, total[:, 0:128])
        emit(HEADS + h, total[:, 128:256])
        last = total[:, 256:384]
        rest = rest + (last if h == 0 else pltpu.roll(last, 8 * h, axis=1))
    emit(2 * HEADS, rest)

def stack_heads(v, masks):
    return jnp.concatenate([v * mask for mask in masks], axis=0)


def pick_heads(v, masks):
    total = v[0:WIN] * masks[0]
    for h in range(1, HEADS):
        total = total + v[h * WIN : (h + 1) * WIN] * masks[h]
    return total


def attend(qkv, bias, mixed, probs, stack_scr, width):
    masks = head_masks(width, BF16)
    masks32 = head_masks(width, F32)
    scale = (width // HEADS) ** -0.5

    def window(w, carry):
        rows = pl.ds(pl.multiple_of(w * WIN, 16), WIN)
        q = qkv[rows, 0:width]
        k = qkv[rows, width : 2 * width]
        v = qkv[rows, 2 * width : 3 * width]
        scores = dot_nt(stack_heads(q, masks), k)
        for h in range(HEADS):
            part = slice(h * WIN, (h + 1) * WIN)
            logits = scores[part] * scale + bias[part, :]
            weights = jnp.exp(logits - jnp.max(logits, axis=-1, keepdims=True))
            p = weights * (1.0 / jnp.sum(weights, axis=-1, keepdims=True))
            probs[w, h] = p
            stack_scr[part, :] = p.astype(BF16)
        mixed[rows, :] = pick_heads(dot(stack_scr[...], v), masks32).astype(BF16)
        return carry

    lax.fori_loop(0, probs.shape[0], window, 0, unroll=True)


def attend_back(qkv, probs, dmix, field, sums, low_scr, prob_scr, width):
    masks = head_masks(width, BF16)
    masks32 = head_masks(width, F32)
    scale = (width // HEADS) ** -0.5

    def window(w, carry):
        rows = pl.ds(pl.multiple_of(w * WIN, 16), WIN)
        q = qkv[rows, 0:width]
        k = qkv[rows, width : 2 * width]
        v = qkv[rows, 2 * width : 3 * width]
        up = stack_heads(dmix[rows, :], masks)
        prob_grad = dot_nt(up, v)
        for h in range(HEADS):
            part = slice(h * WIN, (h + 1) * WIN)
            p = probs[w, h]
            weighted = p * prob_grad[part]
            ds = weighted - p * jnp.sum(weighted, axis=-1, keepdims=True)
            sums[part, 0:WIN] += ds
            low_scr[part, :] = ds.astype(BF16)
            prob_scr[part, :] = p.astype(BF16)
        low = low_scr[...]
        dq = pick_heads(dot(low, k), masks32)
        dk = dot_tn(low, stack_heads(q, masks))
        dv = dot_tn(prob_scr[...], up)
        field[rows, 0:width] = (dq * scale).astype(BF16)
        field[rows, width : 2 * width] = (dk * scale).astype(BF16)
        field[rows, 2 * width : 3 * width] = dv.astype(BF16)
        return carry

    lax.fori_loop(0, probs.shape[0], window, 0, unroll=True)


def lon_major(src, scr):
    levels, lats, lons, width = src.shape
    for z in range(levels):
        for a in range(lats):
            at = (z * lats + a) * lons
            put(scr, slice(at, at + lons), src[z, a].astype(F32))


def lon_column(scr, lon, lons, width):
    return get(scr, pl.ds(lon, CHUNK, stride=lons), width)


def flat_store(dst, at, mat, cols):
    rows = mat.shape[1]
    if cols % 128 == 0:
        per = cols // 128
        for c in range(per):
            dst[pl.ds(at + c, rows, stride=per), :] = mat[c]
        return rows * per
    per = 2 * cols // 128
    half = cols // 128
    even = get(mat, pl.ds(0, rows // 2, stride=2), cols)
    odd = get(mat, pl.ds(1, rows // 2, stride=2), cols)
    for c in range(half):
        dst[pl.ds(at + c, rows // 2, stride=per), :] = even[:, c * 128 : (c + 1) * 128]
    dst[pl.ds(at + half, rows // 2, stride=per), :] = jnp.concatenate(
        [even[:, half * 128 : half * 128 + 64], odd[:, 0:64]], axis=1
    )
    for c in range(half):
        dst[pl.ds(at + half + 1 + c, rows // 2, stride=per), :] = odd[
            :, 64 + c * 128 : 64 + (c + 1) * 128
        ]
    return rows * cols // 128


def send_units(scr, base, out):
    lons, units = out.shape[:2]
    for j in range(lons):
        for u in range(units):
            at = base + (j * units + u) * UNIT
            if not isinstance(at, int):
                at = pl.multiple_of(at, UNIT)
            out[j, u] = scr[pl.ds(at, UNIT), :].astype(BF16)


def halves(scr, lat, keep, give):
    half = keep.shape[0] * keep.shape[1] * UNIT
    send_units(scr, lat * half, keep)
    send_units(scr, (1 - lat) * half, give)


def bias_units(sums, out):
    lons, per = out.shape[:2]

    def put_unit(k, value):
        out[k // per, k % per] = value

    fold_bias(sums, put_unit)
    for k in range(BIAS_UNITS, lons * per):
        put_unit(k, jnp.zeros((UNIT, 128), BF16))

def forward_core(x, b, refs, qkv_scr, bias_scr, mixed, probs, stack_scr):
    qkv_w, proj_w, gains = refs
    width = x.shape[-1]
    stand, inv = standardize(x)
    normed = (stand * gains[b, 0:1, :]).astype(BF16)
    qkv_scr[...] = dot(normed, qkv_w[b]).astype(BF16)
    attend(qkv_scr, bias_scr, mixed, probs, stack_scr, width)
    att = dot(mixed[...], proj_w[b]).astype(BF16)
    resid = (x + att.astype(F32)).astype(BF16).astype(F32)
    return resid, normed


def first_kernel(
    lat_total, tokens_in, cot_in, table_in, spread_in, qkv_in, proj_in, up_in, down_in, gains_in,
    x_out, tail_out, head_out, qkv_out, mixed_out, probs_out, resid_out, hidden_out, active_out,
    scr, cot_scr, tab_scr, rows_scr, wide_scr, bias_scr,
    cot, table, spread, tokens, qkv_w, gains, proj_w, up_w, down_w, stack_scr, sems,
):
    copies = []
    for source, target in (
        (cot_in, cot),
        (table_in.at[0:1], table),
        (spread_in, spread),
        (tokens_in, tokens),
        (qkv_in.at[0:1], qkv_w),
        (gains_in, gains),
        (proj_in.at[0:1], proj_w),
        (up_in.at[0:1], up_w),
        (down_in.at[0:1], down_w),
    ):
        copies.append(pltpu.make_async_copy(source, target, sems.at[len(copies)]))
    for copy in copies:
        copy.start()
    lat = lax.axis_index("lat")
    width = tokens.shape[-1]
    lons = tokens.shape[2]
    cut = CHUNK * (WLON // 2)
    copies[0].wait()
    lon_major(cot, cot_scr)
    g = jnp.concatenate([lon_column(cot_scr, lon, lons, width) for lon in range(lons)], axis=0)
    head_out[1] = g[0:cut, :].astype(BF16)
    tail_out[1] = g[cut:, :].astype(BF16)
    copies[1].wait()
    copies[2].wait()
    expand_bias(
        table.at[0], spread, tab_scr, rows_scr, wide_scr, bias_scr, lat, False, lat_total
    )
    copies[3].wait()
    lon_major(tokens, scr)
    x = jnp.concatenate([lon_column(scr, lon, lons, width) for lon in range(lons)], axis=0)
    x_out[...] = x.astype(BF16)
    for copy in copies[4:]:
        copy.wait()

    resid, _ = forward_core(
        x, 0, (qkv_w, proj_w, gains), qkv_out, bias_scr, mixed_out, probs_out, stack_scr
    )
    resid_out[...] = resid.astype(BF16)
    stand, _ = standardize(resid)
    normed = (stand * gains[0, 1:2, :]).astype(BF16)
    hidden = dot(normed, up_w[0])
    hidden_out[...] = hidden
    active = gelu_value(hidden).astype(BF16)
    active_out[...] = active
    result = resid + dot_nt(active, down_w[0])
    head_out[0] = result[0:cut, :].astype(BF16)
    tail_out[0] = result[cut:, :].astype(BF16)


def bias_kernel(
    lat_total, table, spread, hidden, bias_out, slope_out, tab_scr, rows_scr, wide_scr
):
    lat = lax.axis_index("lat")
    slope_out[...] = gelu_parts(hidden[...])[1].astype(BF16)
    expand_bias(
        table.at[1], spread, tab_scr, rows_scr, wide_scr, bias_out, lat, True, lat_total
    )


def merge_ahead(scr_own, scr_oth, rows):
    half = WLAT // 2
    n = lax.broadcasted_iota(jnp.int32, (rows, 1), 0)
    return jnp.where(
        lat_inside(n) < half,
        pltpu.roll(scr_own[...], rows - half, axis=0),
        pltpu.roll(scr_oth[...], half, axis=0),
    )


def merge_behind(scr_own, scr_oth, rows):
    half = WLAT // 2
    n = lax.broadcasted_iota(jnp.int32, (rows, 1), 0)
    return jnp.where(
        lat_inside(n) >= half,
        pltpu.roll(scr_own[...], half, axis=0),
        pltpu.roll(scr_oth[...], rows - half, axis=0),
    )


def second_kernel(
    lat_total,
    kept, tail, lon_head, lat_tail, diag_head, bias, qkv_w, proj_w, up_w, down_w, gains, *rest
):
    run_second(
        lat_total, tail, lon_head, lat_tail, diag_head, bias, qkv_w, proj_w, up_w, down_w, gains,
        *rest[kept:kept + 12], *rest[2 * kept + 12 :]
    )


def run_second(
    lat_total,
    tail, lon_head, lat_tail, diag_head, bias, qkv_w, proj_w, up_w, down_w, gains,
    head_out, tail_out, n1_out, field_out, mixed_out, low_out, n2_out, hg_out, active_out, g_out,
    sums_out, gain_out,
    scr_own, scr_oth, qkv_scr, probs_scr, dmix_scr, low_scr, prob_scr,
):
    lat = lax.axis_index("lat")
    rows, width = scr_own.shape
    cut = CHUNK * (WLON // 2)

    def rolled(which):
        scr_own[0 : rows - cut, :] = tail[which].astype(F32)
        scr_own[rows - cut :, :] = lon_head[which].astype(F32)
        scr_oth[0 : rows - cut, :] = lat_tail[which].astype(F32)
        scr_oth[rows - cut :, :] = diag_head[which].astype(F32)
        return merge_ahead(scr_own, scr_oth, rows)

    g = rolled(1)
    n = lax.broadcasted_iota(jnp.int32, (rows, 1), 0)
    keep = lat_row(n, lat, True, lat_total) < lat_total - PAD
    g = jnp.where(keep, g, 0.0)
    g_out[...] = g.astype(BF16)

    x = rolled(0)

    resid, normed = forward_core(
        x, 1, (qkv_w, proj_w, gains), qkv_scr, bias, mixed_out, probs_scr, low_scr
    )
    n1_out[...] = normed
    stand2, inv2 = standardize(resid)
    normed2 = (stand2 * gains[1, 1:2, :]).astype(BF16)
    n2_out[...] = normed2
    active, slope = gelu_parts(dot(normed2, up_w[1]))
    active_out[...] = active.astype(BF16)

    hg = (dot(g_out[...], down_w[1]) * slope).astype(BF16)
    hg_out[...] = hg
    part, gain_two = norm_back(dot_nt(hg, up_w[1]), gains[1, 1:2, :], stand2, inv2)
    rg = g + part
    low = rg.astype(BF16)
    low_out[...] = low
    dmix_scr[...] = dot_nt(low, proj_w[1]).astype(BF16)
    sums_out[...] = jnp.zeros(sums_out.shape, F32)
    attend_back(
        qkv_scr, probs_scr, dmix_scr, field_out, sums_out, low_scr, prob_scr, width
    )
    ng = dot_nt(field_out[...], qkv_w[1]).astype(BF16).astype(F32)
    stand1, inv1 = standardize(x)
    part, gain_one = norm_back(ng, gains[1, 0:1, :], stand1, inv1)
    dx = rg + part
    head_out[...] = dx[0 : rows - cut, :].astype(BF16)
    tail_out[...] = dx[rows - cut :, :].astype(BF16)
    gain_out[0:1, :] = gain_one
    gain_out[1:2, :] = gain_two


def outer_kernel(
    n1, field, mixed, low, n2, hg, active, g, sums,
    keep, give, bias_out,
    m576, m192, m768, mdown, flat_scr,
):
    put(m576, slice(None), dot_tn(n1[...], field[...]))
    at = flat_store(flat_scr, 0, m576, field.shape[1])
    put(m192, slice(None), dot_tn(mixed[...], low[...]))
    at += flat_store(flat_scr, at, m192, mixed.shape[1])
    put(m768, slice(None), dot_tn(n2[...], hg[...]))
    at += flat_store(flat_scr, at, m768, active.shape[1])
    put(mdown, slice(None), dot_tn(active[...], g[...]))
    at += flat_store(flat_scr, at, mdown, mixed.shape[1])
    halves(flat_scr, lax.axis_index("lat"), keep, give)
    bias_units(sums, bias_out)


def lat_split(keep, got, *refs):
    keep_out, give_out = refs[-2:]
    units = keep.shape[1]
    x = lax.rem(lax.axis_index("lon"), 2)
    for out, side in ((keep_out, x), (give_out, 1 - x)):
        for z in range(out.shape[0]):
            j = 2 * z + side
            out[z, 0:units] = (keep[j].astype(F32) + got[j].astype(F32)).astype(BF16)
            if out.shape[1] > units:
                out[z, units:] = refs[0][j]


def split_z(first, second, got_first, got_second, *outs):
    count, cut = first.shape[:2]
    z = lax.div(lax.axis_index("lon"), 2)
    for k, out in enumerate(outs):
        at = lax.rem(z + k, count)
        out[0:cut] = (first[at].astype(F32) + got_first[at].astype(F32)).astype(BF16)
        out[cut:] = (second[at].astype(F32) + got_second[at].astype(F32)).astype(BF16)


def sum_refs(*refs):
    total = refs[0][...].astype(F32)
    for ref in refs[1:-2]:
        total = total + ref[...].astype(F32)
    refs[-1][...] = total.astype(BF16)


def add_pair(keep, got, order, out):
    out[...] = (keep[...].astype(F32) + got[...].astype(F32)).astype(BF16)


def sum_pieces(pieces, order, out):
    total = pieces[0].astype(F32)
    for k in range(1, pieces.shape[0]):
        total = total + pieces[k].astype(F32)
    for k in range(out.shape[0]):
        out[k] = total.astype(BF16)


def join_z(*refs):
    out = refs[-1]
    count = out.shape[0]
    z = lax.div(lax.axis_index("lon"), 2)
    for k in range(count):
        out[lax.rem(z + count - k, count)] = refs[k][...]


def third_kernel(
    head, lon_tail, lat_head, diag_tail, resid, slope, active, mixed,
    proj_w, up_w, down_w, gains, order,
    keep_out, give_out, rg_out, dmix_out, gain_out,
    scr_own, scr_oth, m192, m768, mdown, flat_scr,
):
    rows, width = scr_own.shape
    cut = CHUNK * (WLON // 2)
    scr_own[0:cut, :] = lon_tail[...].astype(F32)
    scr_own[cut:, :] = head[...].astype(F32)
    scr_oth[0:cut, :] = diag_tail[...].astype(F32)
    scr_oth[cut:, :] = lat_head[...].astype(F32)
    g = merge_behind(scr_own, scr_oth, rows)
    g_low = g.astype(BF16)
    hg = dot(g_low, down_w[0])
    stand2, inv2 = standardize(resid[...].astype(F32))
    normed2 = (stand2 * gains[0, 1:2, :]).astype(BF16)
    hg = (hg * slope[...].astype(F32)).astype(BF16)
    part, gain_two = norm_back(dot_nt(hg, up_w[0]), gains[0, 1:2, :], stand2, inv2)
    rg = g + part
    rg_out[...] = rg
    low = rg.astype(BF16)
    dmix_out[...] = dot_nt(low, proj_w[0]).astype(BF16)
    gain_out[...] = gain_two
    put(m192, slice(None), dot_tn(mixed[...], low))
    at = flat_store(flat_scr, 0, m192, mixed.shape[1])
    put(m768, slice(None), dot_tn(normed2, hg))
    at += flat_store(flat_scr, at, m768, active.shape[1])
    put(mdown, slice(None), dot_tn(active[...], g_low))
    at += flat_store(flat_scr, at, mdown, mixed.shape[1])
    flat_scr[at:, :] = jnp.zeros((flat_scr.shape[0] - at, 128), F32)
    halves(flat_scr, lax.axis_index("lat"), keep_out, give_out)


def gain_rows(one, two):
    return jnp.concatenate(
        [
            one[:, 0:128],
            jnp.concatenate([one[:, 128:192], two[:, 0:64]], axis=1),
            two[:, 64:192],
        ],
        axis=0,
    )


def fourth_kernel(
    x_in, qkv, probs, dmix, rg, gain_two, gains_late, order, qkv_w, gains,
    tokens_out, keep, give, bias_out,
    field, sums, m576, flat_scr, dx_scr, low_scr, prob_scr,
):
    width = x_in.shape[-1]
    levels, lats, lons = tokens_out.shape[:3]
    sums[...] = jnp.zeros(sums.shape, F32)
    attend_back(qkv, probs, dmix, field, sums, low_scr, prob_scr, width)
    stand1, inv1 = standardize(x_in[...].astype(F32))
    normed = (stand1 * gains[0, 0:1, :]).astype(BF16)
    ng = dot_nt(field[...], qkv_w[0]).astype(BF16).astype(F32)
    part, gain_one = norm_back(ng, gains[0, 0:1, :], stand1, inv1)
    put(m576, slice(None), dot_tn(normed, field[...]))
    at = flat_store(flat_scr, 0, m576, field.shape[1])
    flat_scr[at:, :] = jnp.zeros((flat_scr.shape[0] - at, 128), F32)
    flat_scr[at : at + 3, :] = gain_rows(gain_one, gain_two[...])
    flat_scr[at + 3 : at + 6, :] = gain_rows(gains_late[0:1, :], gains_late[1:2, :])
    bias_units(sums, bias_out)
    halves(flat_scr, lax.axis_index("lat"), keep, give)
    put(dx_scr, slice(None), rg[...] + part)
    for z in range(levels):
        for a in range(lats):
            tokens_out[z, a] = get(
                dx_scr, pl.ds(z * lats + a, lons, stride=CHUNK), width
            ).astype(BF16)


def place(pieces, first, last, dests, scr):
    total = jnp.zeros((UNIT, 128), F32)
    lons = pieces.shape[1]
    per = last - first
    k = 0
    for where, room in dests:
        for at in range(where, where + room, UNIT):
            half, j, u = k // (per * lons), k // per % lons, k % per
            value = pieces[half, j, first + u].astype(F32)
            scr[at : at + UNIT, :] = value
            total = total + value * value
            k += 1
    return total


def bias_rows(piece, base, spread, out, rows_scr, wide_scr, tab_scr):
    lat = lax.axis_index("lat")
    extra = -(-BIAS_UNITS // piece.shape[1])

    def read(at):
        parts = []
        for r in range(CHUNK // UNIT):
            k = at * (CHUNK // UNIT) + r
            parts.append(piece[lat, k // extra, base + k % extra].astype(F32))
        return jnp.concatenate(parts, axis=0)

    rest = read(2 * HEADS)
    for h in range(HEADS):
        rows = pl.ds(h, CHUNK, stride=8)
        wide_scr[0, rows, :] = read(h)
        wide_scr[1, rows, :] = read(HEADS + h)
        wide_scr[2, rows, :] = rest if h == 0 else pltpu.roll(rest, 128 - 8 * h, axis=1)
    low = get(wide_scr, slice(None), WIDE).astype(BF16)
    for zj in range(LEVELS):
        rows_scr[...] = dot_nt(low, spread[zj])
        for zi in range(LEVELS):
            for ai in range(WLAT):
                at = ((zi * LEVELS + zj) * WLAT + ai) * PAIR
                row = (zi * WLAT + ai) * 8
                tab_scr[0:HEADS, at : at + PAIR] = rows_scr[row : row + HEADS, 0:PAIR]
    for h in range(HEADS):
        out[h] = tab_scr[h : h + 1, :]


def late_kernel(
    units_a, extra, spread, same, same_x, cross, cross_x, flat_out, squares_out, bias_out,
    rows_scr, wide_scr, tab_scr, a,
):
    lat = lax.axis_index("lat")
    x = lax.rem(lax.axis_index("lon"), 2)
    for z in range(same.shape[0]):
        a[lat, 2 * z + x] = same[z]
        a[lat, 2 * z + 1 - x] = same_x[z]
        a[1 - lat, 2 * z + x] = cross[z]
        a[1 - lat, 2 * z + 1 - x] = cross_x[z]
    total = place(a, 0, units_a, [(0, 3456)], flat_out)
    squares_out[...] = total + place(
        a, units_a + extra, a.shape[2], [(3456, flat_out.shape[0] - 3456)], flat_out
    )
    bias_rows(a, units_a, spread, bias_out, rows_scr, wide_scr, tab_scr)


def near_kernel(
    units_c, spread, own_c, oth_c, flat_out, squares_out, bias_out,
    rows_scr, wide_scr, tab_scr, c,
):
    lat = lax.axis_index("lat")
    for j in range(own_c.shape[0]):
        c[lat, j] = own_c[j]
        c[1 - lat, j] = oth_c[j]
    squares_out[...] = place(c, 0, units_c, [(0, flat_out.shape[0])], flat_out)
    bias_rows(c, units_c, spread, bias_out, rows_scr, wide_scr, tab_scr)


def last_kernel(
    flat_ab, squares_ab, bias_late, flat_c, squares_c, bias_near, update_out, bias_out
):
    count = update_out.shape[0]
    mean = jnp.sum(squares_ab[...] + squares_c[...]) * (1.0 / (count * 128))
    scale = lax.rsqrt(mean + 1e-06)
    update_out[0:864, :] = (flat_c[0:864, :] * scale).astype(BF16)
    at = 0
    for where, rows in (
        (864, 864), (2016, 288), (3456, 1152), (5760, 1152), (1728, 288), (2304, 1152), (4608, 1152)
    ):
        update_out[where : where + rows, :] = (flat_ab[at : at + rows, :] * scale).astype(BF16)
        at += rows
    update_out[6912:count, :] = (flat_c[864 : 864 + count - 6912, :] * scale).astype(BF16)
    bias_out[0] = bias_near[...]
    bias_out[1] = bias_late[...]


def call(kernel, outs, scratch, args, micros, mib, spaces=None, near=(), kept=0):
    spaces = spaces or [pltpu.VMEM] * len(args)
    return pl.pallas_call(
        kernel,
        out_shape=[
            (pltpu.VMEM if at in near else jax.ShapeDtypeStruct)(*entry)
            for at, entry in enumerate(outs)
        ],
        in_specs=[pl.BlockSpec(memory_space=space) for space in spaces],
        out_specs=[
            pl.BlockSpec(memory_space=pltpu.VMEM if at < len(outs) - kept else pl.ANY)
            for at in range(len(outs))
        ],
        input_output_aliases={
            len(args) - kept + k: len(outs) - kept + k for k in range(kept)
        },
        scratch_shapes=[
            pltpu.VMEM(*entry) if isinstance(entry, tuple) else entry for entry in scratch
        ],
        compiler_params=pltpu.CompilerParams(vmem_limit_bytes=mib * MIB),
        cost_estimate=pl.CostEstimate(
            flops=int(micros * 1.1e9), bytes_accessed=10**5, transcendentals=0
        ),
    )(*args)


def lat_swap(value):
    return lax.ppermute(value, "lat", [(0, 1), (1, 0)])


def lon_send(value, step):
    count = lax.axis_size("lon")
    return lax.ppermute(value, "lon", [(s, (s + step) % count) for s in range(count)])


def x_swap(value):
    count = lax.axis_size("lon")
    return lax.ppermute(value, "lon", [(s, s ^ 1) for s in range(count)])


def diag_send(value, step):
    count = lax.axis_size("lon")
    pairs = []
    for s in range(count):
        for t in range(2):
            pairs.append((2 * s + t, 2 * ((s + step) % count) + 1 - t))
    return lax.ppermute(value, ("lon", "lat"), pairs)


def shards(
    tokens, cotangent, qkv_weight, proj_weight, up_weight, down_weight, norm_gain, bias_table
):
    levels, lats, lons, width = tokens.shape
    rows = levels * lats * lons
    wins = rows // WIN
    hid = up_weight.shape[-1]
    heads = bias_table.shape[2]
    lon_size = lax.axis_size("lon")
    zs = lon_size // 2
    lat_total = lats * lax.axis_size("lat")
    cut = CHUNK * (WLON // 2)
    spread = jnp.asarray(spread_matrices(), BF16)
    down_turned = jnp.swapaxes(down_weight, 1, 2)
    table = jnp.swapaxes(bias_table, 1, 2)
    token = (rows, width)
    field_shape = ((rows, 3 * width), BF16)
    probs_shape = ((wins, heads, WIN, WIN), F32)
    stack_shape = ((heads * WIN, WIN), BF16)
    bias_shape = ((heads * WIN, WIN), F32)
    sums_shape = ((heads * WIN, WIDE), F32)
    tab_scr = ((8, table.shape[-1]), F32)
    rows_scr = ((LEVELS * CHUNK * 8, PAIR), F32)
    wide_scr = ((WIDE // 128, CHUNK * 8, 128), F32)
    tiles = -(-width // 128)
    token_scr = ((tiles, rows, 128), F32)
    m576 = ((-(-3 * width // 128), width, 128), F32)
    m192 = ((tiles, width, 128), F32)
    m768 = ((hid // 128, width, 128), F32)
    mdown = ((tiles, hid, 128), F32)

    block_rows = (qkv_weight[0].size + proj_weight[0].size + 2 * up_weight[0].size) // 128
    qkv_rows = qkv_weight[0].size // 128
    counts = (block_rows, block_rows - qkv_rows, qkv_rows + 8)
    units_a, units_b, units_c = [-(-count // (2 * lon_size * UNIT)) for count in counts]
    extra = -(-BIAS_UNITS // lon_size)

    def units(*lead):
        return (lead + (UNIT, 128), BF16)

    def flat_scr(per):
        return ((2 * lon_size * per * UNIT, 128), F32)

    x0, tail, head, qkv0, mixed0, probs0, resid0, hidden0, active0 = call(
        functools.partial(first_kernel, lat_total),
        [
            (token, BF16),
            ((2, rows - cut, width), BF16),
            ((2, cut, width), BF16),
            field_shape,
            (token, BF16),
            probs_shape,
            (token, BF16),
            ((rows, hid), F32),
            ((rows, hid), BF16),
        ],
        [
            token_scr,
            token_scr,
            tab_scr,
            rows_scr,
            wide_scr,
            bias_shape,
            (cotangent.shape, BF16),
            ((1,) + table.shape[1:], F32),
            (spread.shape, BF16),
            (tokens.shape, BF16),
            ((1,) + qkv_weight.shape[1:], BF16),
            (norm_gain.shape, F32),
            ((1,) + proj_weight.shape[1:], BF16),
            ((1,) + up_weight.shape[1:], BF16),
            ((1,) + down_turned.shape[1:], BF16),
            stack_shape,
            pltpu.SemaphoreType.DMA((9,)),
        ],
        [
            pltpu.with_memory_space_constraint(arg, pltpu.HBM)
            for arg in (
                tokens, cotangent, table, spread, qkv_weight, proj_weight, up_weight, down_turned,
                norm_gain,
            )
        ],
        8,
        16,
        [pltpu.HBM] * 9,
        near=(0, 3, 4, 5, 6, 8),
    )
    lon_head = lon_send(head, -1)
    diag_head = diag_send(head, -1)
    lat_tail = lat_swap(tail)
    bias1, slope0 = call(
        functools.partial(bias_kernel, lat_total),
        [bias_shape, ((rows, hid), BF16)],
        [tab_scr, rows_scr, wide_scr],
        (table, spread, hidden0),
        3,
        12,
        near=(1,),
    )

    saved = [x0, qkv0, mixed0, probs0, resid0, active0, slope0]
    (
        dhead, dtail, n1, field1, mixed1, low1, n2, hg1, active1, g1, sums1, gains1,
        *saved,
    ) = call(
        functools.partial(second_kernel, lat_total, len(saved)),
        [
            ((rows - cut, width), BF16),
            ((cut, width), BF16),
            (token, BF16),
            field_shape,
            (token, BF16),
            (token, BF16),
            (token, BF16),
            ((rows, hid), BF16),
            ((rows, hid), BF16),
            (token, BF16),
            sums_shape,
            ((2, width), F32),
            *[(value.shape, value.dtype) for value in saved],
        ],
        [
            (token, F32),
            (token, F32),
            field_shape,
            probs_shape,
            (token, BF16),
            stack_shape,
            stack_shape,
        ],
        (
            tail, lon_head, lat_tail, diag_head, bias1, qkv_weight, proj_weight, up_weight,
            down_turned, norm_gain,
            *[pltpu.with_memory_space_constraint(value, pltpu.VMEM) for value in saved],
        ),
        19,
        16,
        [pltpu.VMEM] * 10 + [pl.ANY] * len(saved),
        near=tuple(range(12, 12 + len(saved))),
        kept=len(saved),
    )
    x0, qkv0, mixed0, probs0, resid0, active0, slope0 = saved
    lon_tail = lon_send(dtail, 1)
    diag_tail = diag_send(dtail, 1)
    lat_dhead = lat_swap(dhead)

    keep_a, give_a, bias_a = call(
        outer_kernel,
        [units(lon_size, units_a), units(lon_size, units_a), units(lon_size, extra)],
        [m576, m192, m768, mdown, flat_scr(units_a)],
        (n1, field1, mixed1, low1, n2, hg1, active1, g1, sums1),
        3,
        14,
    )
    got_a = lat_swap(give_a)

    units_xa = units_a + extra
    keep_xa, give_xa = call(
        lat_split, [units(zs, units_xa)] * 2, [], (keep_a, got_a, bias_a), 1, 10
    )
    got_xa = x_swap(give_xa)

    keep_b, give_b, rg0, dmix0, gain_two = call(
        third_kernel,
        [
            units(lon_size, units_b),
            units(lon_size, units_b),
            (token, F32),
            (token, BF16),
            ((1, width), F32),
        ],
        [(token, F32), (token, F32), m192, m768, mdown, flat_scr(units_b)],
        (
            dhead, lon_tail, lat_dhead, diag_tail, resid0, slope0, active0, mixed0, proj_weight,
            up_weight, down_turned, norm_gain, got_xa,
        ),
        0.1,
        14,
    )
    got_b = lat_swap(give_b)
    keep_xb, give_xb = call(
        lat_split, [units(zs, units_b)] * 2, [], (keep_b, got_b), 1, 10
    )
    got_xb = x_swap(give_xb)

    tokens_grad, keep_c, give_c, bias_c = call(
        fourth_kernel,
        [
            (tokens.shape, BF16),
            units(lon_size, units_c),
            units(lon_size, units_c),
            units(lon_size, extra),
        ],
        [
            field_shape,
            sums_shape,
            m576,
            flat_scr(units_c),
            token_scr,
            stack_shape,
            stack_shape,
        ],
        (x0, qkv0, probs0, dmix0, rg0, gain_two, gains1, keep_xb, qkv_weight, norm_gain),
        2,
        14,
    )
    got_c = lat_swap(give_c)
    units_ab = units_xa + units_b
    own_ab, *gives_ab = call(
        split_z, [units(units_ab)] * zs, [], (keep_xa, keep_xb, got_xa, got_xb), 1, 10
    )
    gots_ab = [lon_send(give, 2 * (k + 1)) for k, give in enumerate(gives_ab)]
    units_xc = units_c + extra
    keep_x, give_x = call(
        lat_split, [units(zs, units_xc)] * 2, [], (keep_c, got_c, bias_c, own_ab), 1, 10
    )
    got_x = x_swap(give_x)
    (sum_ab,) = call(sum_refs, [units(units_ab)], [], (own_ab, *gots_ab, keep_x), 1, 10)
    (part_z,) = call(add_pair, [units(zs, units_xc)], [], (keep_x, got_x, sum_ab), 1, 10)
    pieces_c = lax.all_to_all(
        part_z,
        "lon",
        0,
        0,
        axis_index_groups=[[2 * z + x for z in range(zs)] for x in range(2)],
    )
    moved_ab = [lon_send(sum_ab, 2 * k) for k in range(1, zs)]
    (sum_c,) = call(
        sum_pieces, [units(lon_size, units_xc)], [], (pieces_c, sum_ab), 1, 10
    )
    (same,) = call(join_z, [units(zs, units_ab)], [], [sum_ab, *moved_ab, sum_c], 1, 10)
    same_x = x_swap(same)
    cross = lat_swap(same)
    cross_x = lat_swap(same_x)
    whole_c = lax.all_to_all(sum_c, "lon", 0, 0)
    oth_c = lat_swap(whole_c)

    flat_rows = (2 * block_rows * 128 + norm_gain.size) // 128
    fold_scr = [((CHUNK * 8, PAIR), F32), wide_scr, tab_scr]
    ab_rows = 2 * block_rows - qkv_rows
    flat_ab, squares_ab, bias_late = call(
        functools.partial(late_kernel, units_a, extra),
        [((ab_rows, 128), F32), ((UNIT, 128), F32), (table.shape[1:], F32)],
        [*fold_scr, units(2, lon_size, units_ab)],
        (spread, same, same_x, cross, cross_x),
        2,
        14,
    )
    flat_c, squares_c, bias_near = call(
        functools.partial(near_kernel, units_c),
        [((872, 128), F32), ((UNIT, 128), F32), (table.shape[1:], F32)],
        [*fold_scr, units(2, lon_size, units_xc)],
        (spread, whole_c, oth_c),
        20,
        14,
    )
    update, bias_grad = call(
        last_kernel,
        [((flat_rows, 128), BF16), (table.shape, F32)],
        [],
        (flat_ab, squares_ab, bias_late, flat_c, squares_c, bias_near),
        2,
        14,
    )
    bias_grad = jnp.swapaxes(bias_grad, 1, 2)
    return (tokens_grad, update.reshape(-1), bias_grad)


def solution(mesh):
    return jax.shard_map(
        shards,
        mesh=mesh,
        in_specs=(
            P("grp", "lat", "lon", None),
            P("grp", "lat", "lon", None),
            P(),
            P(),
            P(),
            P(),
            P(),
            P(None, "lat", None, None),
        ),
        out_specs=(P("grp", "lat", "lon", None), P("grp"), P("grp", "lat", None, None)),
        check_vma=False,
    )
```

```python
import functools

import jax
import jax.numpy as jnp
import numpy as np
from jax import lax
from jax.experimental import pallas as pl
from jax.experimental.pallas import tpu as pltpu
from jax.sharding import PartitionSpec as P

WLAT = 12
WLON = 6
PAD = 5
LEVELS = 2
HEADS = 6
CHUNK = LEVELS * WLAT
WIN = CHUNK * WLON
SHIFTS = 2 * WLON - 1
PAIR = WLAT * SHIFTS
WIDE = 384

EPS = 1e-05
NEGATIVE = -1000000000.0
ROOT_HALF = 0.7071067811865476
INV_ROOT_TAU = 0.3989422804014327

F32 = jnp.float32
BF16 = jnp.bfloat16
UNIT = 8
BIAS_UNITS = (2 * HEADS + 1) * CHUNK // UNIT
MIB = 1024 * 1024


def dot(a, b):
    return lax.dot_general(a, b, (((1,), (0,)), ((), ())), preferred_element_type=F32)


def dot_nt(a, b):
    return lax.dot_general(a, b, (((1,), (1,)), ((), ())), preferred_element_type=F32)


def dot_tn(a, b):
    return lax.dot_general(a, b, (((0,), (0,)), ((), ())), preferred_element_type=F32)


def row_mean(v):
    return jnp.sum(v, axis=-1, keepdims=True) * (1.0 / v.shape[-1])


def standardize(x):
    centred = x - row_mean(x)
    inv = lax.rsqrt(row_mean(centred * centred) + EPS)
    return centred * inv, inv


def norm_back(d, gain, stand, inv):
    scaled = d * gain
    first = row_mean(scaled)
    second = row_mean(scaled * stand)
    gain_grad = jnp.sum(d * stand, axis=0, keepdims=True)
    return inv * (scaled - first - stand * second), gain_grad


def gelu_value(hidden):
    return 0.5 * hidden * (1.0 + lax.erf(hidden * ROOT_HALF))


def gelu_parts(hidden):
    half = 0.5 * (1.0 + lax.erf(hidden * ROOT_HALF))
    slope = half + hidden * jnp.exp(-0.5 * hidden * hidden) * INV_ROOT_TAU
    return hidden * half, slope


def split3(v):
    hi = v.astype(BF16)
    rest = v - hi.astype(F32)
    mid = rest.astype(BF16)
    low = (rest - mid.astype(F32)).astype(BF16)
    return hi, mid, low


def spread_matrices():
    out = np.zeros((LEVELS, PAIR, WIDE), np.float32)
    for zj in range(LEVELS):
        for aj in range(WLAT):
            for d in range(SHIFTS):
                out[zj, aj * SHIFTS + d, (SHIFTS - 1 - d) * CHUNK + zj * WLAT + aj] = 1.0
    return out


def put(scr, rows, value):
    width = value.shape[1]
    for tile in range(-(-width // 128)):
        lanes = min(128, width - tile * 128)
        scr[tile, rows, 0:lanes] = value[:, tile * 128 : tile * 128 + lanes]


def get(scr, rows, width):
    parts = [scr[tile, rows, :] for tile in range(-(-width // 128))]
    return jnp.concatenate(parts, axis=1)[:, 0:width]


def head_masks(width, dtype):
    lane = lax.broadcasted_iota(jnp.int32, (1, width), 1)
    size = width // HEADS
    return [((lane >= h * size) & (lane < (h + 1) * size)).astype(dtype) for h in range(HEADS)]


def lat_inside(n):
    return lax.rem(n, WLAT)


def lat_row(row_iota, lat, shifted, lat_total):
    row = lat * WLAT + lat_inside(row_iota)
    if shifted:
        row = row + WLAT // 2
        row = jnp.where(row >= lat_total, row - lat_total, row)
    return row


def expand_bias(table, spread, tab_scr, rows_scr, wide_scr, bias_scr, lat, shifted, lat_total):
    for h in range(HEADS):
        tab_scr[h : h + 1, :] = table[h]
    for zi in range(LEVELS):
        for zj in range(LEVELS):
            for ai in range(WLAT):
                at = ((zi * LEVELS + zj) * WLAT + ai) * PAIR
                row = zj * CHUNK * 8 + (zi * WLAT + ai) * 8
                rows_scr[row : row + HEADS, 0:PAIR] = tab_scr[0:HEADS, at : at + PAIR]
    count = CHUNK * 8
    total = jnp.zeros((count, WIDE), F32)
    for zj in range(LEVELS):
        parts = split3(rows_scr[zj * count : (zj + 1) * count, 0:PAIR])
        for part in parts:
            total = total + dot(part, spread[zj])
    put(wide_scr, slice(None), total)
    i = lax.broadcasted_iota(jnp.int32, (CHUNK, WIN), 0)
    j = lax.broadcasted_iota(jnp.int32, (CHUNK, WIN), 1)
    allowed = lat_row(j, lat, shifted, lat_total) < lat_total - PAD
    if shifted:
        last = lat_total - WLAT // 2
        region_i = (lat * WLAT + lat_inside(i)) >= last
        region_j = (lat * WLAT + lat_inside(j)) >= last
        allowed = allowed & (region_i == region_j)
    for h in range(HEADS):
        wide = get(wide_scr, pl.ds(h, CHUNK, stride=8), WIDE)
        for oi in range(WLON):
            back = (WLON - 1 - oi) * CHUNK
            moved = wide if back == 0 else pltpu.roll(wide, WIDE - back, axis=1)
            at = h * WIN + oi * CHUNK
            bias_scr[at : at + CHUNK, :] = jnp.where(allowed, moved[:, 0:WIN], NEGATIVE)


def fold_bias(sums, put_unit):
    rest = jnp.zeros((CHUNK, 128), F32)

    def emit(at, value):
        for r in range(CHUNK // UNIT):
            put_unit(at * (CHUNK // UNIT) + r, value[r * UNIT : (r + 1) * UNIT, :].astype(BF16))

    for h in range(HEADS):
        total = jnp.zeros((CHUNK, WIDE), F32)
        for oi in range(WLON):
            back = (WLON - 1 - oi) * CHUNK
            at = h * WIN + oi * CHUNK
            part = sums[at : at + CHUNK, :]
            total = total + (part if back == 0 else pltpu.roll(part, back, axis=1))
        emit(h, total[:, 0:128])
        emit(HEADS + h, total[:, 128:256])
        last = total[:, 256:384]
        rest = rest + (last if h == 0 else pltpu.roll(last, 8 * h, axis=1))
    emit(2 * HEADS, rest)

def stack_heads(v, masks):
    return jnp.concatenate([v * mask for mask in masks], axis=0)


def pick_heads(v, width):
    lane = lax.broadcasted_iota(jnp.int32, (1, width), 1)
    size = width // HEADS
    total = v[(HEADS - 1) * WIN :]
    for h in range(HEADS - 1, 0, -1):
        total = jnp.where(lane < h * size, v[(h - 1) * WIN : h * WIN], total)
    return total


def attend(qkv, bias, mixed, probs, stack_scr, width):
    masks = head_masks(width, BF16)
    scale = (width // HEADS) ** -0.5

    def window(w, carry):
        rows = pl.ds(pl.multiple_of(w * WIN, 16), WIN)
        q = qkv[rows, 0:width]
        k = qkv[rows, width : 2 * width]
        v = qkv[rows, 2 * width : 3 * width]
        scores = dot_nt(stack_heads(q, masks), k)
        for h in range(HEADS):
            part = slice(h * WIN, (h + 1) * WIN)
            logits = scores[part] * scale + bias[part, :]
            weights = jnp.exp(logits - jnp.max(logits, axis=-1, keepdims=True))
            p = weights * (1.0 / jnp.sum(weights, axis=-1, keepdims=True))
            probs[w, h] = p
            stack_scr[part, :] = p.astype(BF16)
        mixed[rows, :] = pick_heads(dot(stack_scr[...], v), width).astype(BF16)
        return carry

    lax.fori_loop(0, probs.shape[0], window, 0, unroll=True)


def attend_back(qkv, probs, dmix, field, sums, low_scr, prob_scr, width):
    masks = head_masks(width, BF16)
    scale = (width // HEADS) ** -0.5

    def window(w, carry):
        rows = pl.ds(pl.multiple_of(w * WIN, 16), WIN)
        q = qkv[rows, 0:width]
        k = qkv[rows, width : 2 * width]
        v = qkv[rows, 2 * width : 3 * width]
        up = stack_heads(dmix[rows, :], masks)
        prob_grad = dot_nt(up, v)
        for h in range(HEADS):
            part = slice(h * WIN, (h + 1) * WIN)
            p = probs[w, h]
            weighted = p * prob_grad[part]
            ds = weighted - p * jnp.sum(weighted, axis=-1, keepdims=True)
            sums[part, 0:WIN] += ds
            low_scr[part, :] = ds.astype(BF16)
            prob_scr[part, :] = p.astype(BF16)
        low = low_scr[...]
        dq = pick_heads(dot(low, k), width)
        dk = dot_tn(low, stack_heads(q, masks))
        dv = dot_tn(prob_scr[...], up)
        field[rows, 0:width] = (dq * scale).astype(BF16)
        field[rows, width : 2 * width] = (dk * scale).astype(BF16)
        field[rows, 2 * width : 3 * width] = dv.astype(BF16)
        return carry

    lax.fori_loop(0, probs.shape[0], window, 0, unroll=True)


def lon_major(src, scr):
    levels, lats, lons, width = src.shape
    for z in range(levels):
        for a in range(lats):
            at = (z * lats + a) * lons
            put(scr, slice(at, at + lons), src[z, a].astype(F32))


def lon_column(scr, lon, lons, width):
    return get(scr, pl.ds(lon, CHUNK, stride=lons), width)


def flat_store(dst, at, mat, cols):
    rows = mat.shape[1]
    if cols % 128 == 0:
        per = cols // 128
        for c in range(per):
            dst[pl.ds(at + c, rows, stride=per), :] = mat[c]
        return rows * per
    per = 2 * cols // 128
    half = cols // 128
    even = get(mat, pl.ds(0, rows // 2, stride=2), cols)
    odd = get(mat, pl.ds(1, rows // 2, stride=2), cols)
    for c in range(half):
        dst[pl.ds(at + c, rows // 2, stride=per), :] = even[:, c * 128 : (c + 1) * 128]
    dst[pl.ds(at + half, rows // 2, stride=per), :] = jnp.concatenate(
        [even[:, half * 128 : half * 128 + 64], odd[:, 0:64]], axis=1
    )
    for c in range(half):
        dst[pl.ds(at + half + 1 + c, rows // 2, stride=per), :] = odd[
            :, 64 + c * 128 : 64 + (c + 1) * 128
        ]
    return rows * cols // 128


def send_units(scr, base, out):
    lons, units = out.shape[:2]
    for j in range(lons):
        for u in range(units):
            at = base + (j * units + u) * UNIT
            if not isinstance(at, int):
                at = pl.multiple_of(at, UNIT)
            out[j, u] = scr[pl.ds(at, UNIT), :].astype(BF16)


def halves(scr, lat, keep, give):
    half = keep.shape[0] * keep.shape[1] * UNIT
    send_units(scr, lat * half, keep)
    send_units(scr, (1 - lat) * half, give)


def bias_units(sums, out):
    lons, per = out.shape[:2]

    def put_unit(k, value):
        out[k // per, k % per] = value

    fold_bias(sums, put_unit)
    for k in range(BIAS_UNITS, lons * per):
        put_unit(k, jnp.zeros((UNIT, 128), BF16))

def forward_core(x, b, refs, qkv_scr, bias_scr, mixed, probs, stack_scr):
    qkv_w, proj_w, gains = refs
    width = x.shape[-1]
    stand, inv = standardize(x)
    normed = (stand * gains[b, 0:1, :]).astype(BF16)
    qkv_scr[...] = dot(normed, qkv_w[b]).astype(BF16)
    attend(qkv_scr, bias_scr, mixed, probs, stack_scr, width)
    att = dot(mixed[...], proj_w[b]).astype(BF16)
    resid = (x + att.astype(F32)).astype(BF16).astype(F32)
    return resid, normed


def first_kernel(
    lat_total, tokens_in, cot_in, table_in, spread_in, qkv_in, proj_in, up_in, down_in, gains_in,
    x_out, tail_out, head_out, qkv_out, mixed_out, probs_out, resid_out, hidden_out, active_out,
    scr, cot_scr, tab_scr, rows_scr, wide_scr, bias_scr,
    cot, table, spread, tokens, qkv_w, gains, proj_w, up_w, down_w, stack_scr, sems,
):
    copies = []
    for source, target in (
        (cot_in, cot),
        (table_in.at[0:1], table),
        (spread_in, spread),
        (tokens_in, tokens),
        (qkv_in.at[0:1], qkv_w),
        (gains_in, gains),
        (proj_in.at[0:1], proj_w),
        (up_in.at[0:1], up_w),
        (down_in.at[0:1], down_w),
    ):
        copies.append(pltpu.make_async_copy(source, target, sems.at[len(copies)]))
    for copy in copies:
        copy.start()
    lat = lax.axis_index("lat")
    width = tokens.shape[-1]
    lons = tokens.shape[2]
    cut = CHUNK * (WLON // 2)
    copies[0].wait()
    lon_major(cot, cot_scr)
    g = jnp.concatenate([lon_column(cot_scr, lon, lons, width) for lon in range(lons)], axis=0)
    head_out[1] = g[0:cut, :].astype(BF16)
    tail_out[1] = g[cut:, :].astype(BF16)
    copies[1].wait()
    copies[2].wait()
    expand_bias(
        table.at[0], spread, tab_scr, rows_scr, wide_scr, bias_scr, lat, False, lat_total
    )
    copies[3].wait()
    lon_major(tokens, scr)
    x = jnp.concatenate([lon_column(scr, lon, lons, width) for lon in range(lons)], axis=0)
    x_out[...] = x.astype(BF16)
    for copy in copies[4:]:
        copy.wait()

    resid, _ = forward_core(
        x, 0, (qkv_w, proj_w, gains), qkv_out, bias_scr, mixed_out, probs_out, stack_scr
    )
    resid_out[...] = resid.astype(BF16)
    stand, _ = standardize(resid)
    normed = (stand * gains[0, 1:2, :]).astype(BF16)
    hidden = dot(normed, up_w[0])
    hidden_out[...] = hidden
    active = gelu_value(hidden).astype(BF16)
    active_out[...] = active
    result = resid + dot_nt(active, down_w[0])
    head_out[0] = result[0:cut, :].astype(BF16)
    tail_out[0] = result[cut:, :].astype(BF16)


def bias_kernel(
    lat_total, table, spread, hidden, bias_out, slope_out, tab_scr, rows_scr, wide_scr
):
    lat = lax.axis_index("lat")
    slope_out[...] = gelu_parts(hidden[...])[1].astype(BF16)
    expand_bias(
        table.at[1], spread, tab_scr, rows_scr, wide_scr, bias_out, lat, True, lat_total
    )


def merge_ahead(scr_own, scr_oth, rows):
    half = WLAT // 2
    n = lax.broadcasted_iota(jnp.int32, (rows, 1), 0)
    return jnp.where(
        lat_inside(n) < half,
        pltpu.roll(scr_own[...], rows - half, axis=0),
        pltpu.roll(scr_oth[...], half, axis=0),
    )


def merge_behind(scr_own, scr_oth, rows):
    half = WLAT // 2
    n = lax.broadcasted_iota(jnp.int32, (rows, 1), 0)
    return jnp.where(
        lat_inside(n) >= half,
        pltpu.roll(scr_own[...], half, axis=0),
        pltpu.roll(scr_oth[...], rows - half, axis=0),
    )


def second_kernel(
    lat_total,
    kept, tail, lon_head, lat_tail, diag_head, bias, qkv_w, proj_w, up_w, down_w, gains, *rest
):
    run_second(
        lat_total, tail, lon_head, lat_tail, diag_head, bias, qkv_w, proj_w, up_w, down_w, gains,
        *rest[kept:kept + 12], *rest[2 * kept + 12 :]
    )


def run_second(
    lat_total,
    tail, lon_head, lat_tail, diag_head, bias, qkv_w, proj_w, up_w, down_w, gains,
    head_out, tail_out, n1_out, field_out, mixed_out, low_out, n2_out, hg_out, active_out, g_out,
    sums_out, gain_out,
    scr_own, scr_oth, qkv_scr, probs_scr, dmix_scr, low_scr, prob_scr,
):
    lat = lax.axis_index("lat")
    rows, width = scr_own.shape
    cut = CHUNK * (WLON // 2)

    def rolled(which):
        scr_own[0 : rows - cut, :] = tail[which].astype(F32)
        scr_own[rows - cut :, :] = lon_head[which].astype(F32)
        scr_oth[0 : rows - cut, :] = lat_tail[which].astype(F32)
        scr_oth[rows - cut :, :] = diag_head[which].astype(F32)
        return merge_ahead(scr_own, scr_oth, rows)

    g = rolled(1)
    n = lax.broadcasted_iota(jnp.int32, (rows, 1), 0)
    keep = lat_row(n, lat, True, lat_total) < lat_total - PAD
    g = jnp.where(keep, g, 0.0)
    g_out[...] = g.astype(BF16)

    x = rolled(0)

    resid, normed = forward_core(
        x, 1, (qkv_w, proj_w, gains), qkv_scr, bias, mixed_out, probs_scr, low_scr
    )
    n1_out[...] = normed
    stand2, inv2 = standardize(resid)
    normed2 = (stand2 * gains[1, 1:2, :]).astype(BF16)
    n2_out[...] = normed2
    active, slope = gelu_parts(dot(normed2, up_w[1]))
    active_out[...] = active.astype(BF16)

    hg = (dot(g_out[...], down_w[1]) * slope).astype(BF16)
    hg_out[...] = hg
    part, gain_two = norm_back(dot_nt(hg, up_w[1]), gains[1, 1:2, :], stand2, inv2)
    rg = g + part
    low = rg.astype(BF16)
    low_out[...] = low
    dmix_scr[...] = dot_nt(low, proj_w[1]).astype(BF16)
    sums_out[...] = jnp.zeros(sums_out.shape, F32)
    attend_back(
        qkv_scr, probs_scr, dmix_scr, field_out, sums_out, low_scr, prob_scr, width
    )
    ng = dot_nt(field_out[...], qkv_w[1]).astype(BF16).astype(F32)
    stand1, inv1 = standardize(x)
    part, gain_one = norm_back(ng, gains[1, 0:1, :], stand1, inv1)
    dx = rg + part
    head_out[...] = dx[0 : rows - cut, :].astype(BF16)
    tail_out[...] = dx[rows - cut :, :].astype(BF16)
    gain_out[0:1, :] = gain_one
    gain_out[1:2, :] = gain_two


def outer_kernel(
    n1, field, mixed, low, n2, hg, active, g, sums,
    keep, give, bias_out,
    m576, m192, m768, mdown, flat_scr,
):
    put(m576, slice(None), dot_tn(n1[...], field[...]))
    at = flat_store(flat_scr, 0, m576, field.shape[1])
    put(m192, slice(None), dot_tn(mixed[...], low[...]))
    at += flat_store(flat_scr, at, m192, mixed.shape[1])
    put(m768, slice(None), dot_tn(n2[...], hg[...]))
    at += flat_store(flat_scr, at, m768, active.shape[1])
    put(mdown, slice(None), dot_tn(active[...], g[...]))
    at += flat_store(flat_scr, at, mdown, mixed.shape[1])
    halves(flat_scr, lax.axis_index("lat"), keep, give)
    bias_units(sums, bias_out)


def lat_sums_split(*refs):
    keep_out, give_out = refs[-2:]
    x = lax.rem(lax.axis_index("lon"), 2)
    for out, side in ((keep_out, x), (give_out, 1 - x)):
        for z in range(out.shape[0]):
            j = 2 * z + side
            at = 0
            for k in range(0, len(refs) - 4, 2):
                keep, got = refs[k], refs[k + 1]
                count = keep.shape[1]
                total = keep[j].astype(F32) + got[j].astype(F32)
                out[z, at : at + count] = total.astype(BF16)
                at += count
            out[z, at:] = refs[-4][j]


def split_z(keep, got, own_out, *give_outs):
    count = keep.shape[0]
    z = lax.div(lax.axis_index("lon"), 2)
    for k, out in enumerate((own_out,) + give_outs):
        at = lax.rem(z + k, count)
        out[...] = (keep[at].astype(F32) + got[at].astype(F32)).astype(BF16)


def sum_refs(*refs):
    total = refs[0][...].astype(F32)
    for ref in refs[1:-2]:
        total = total + ref[...].astype(F32)
    refs[-1][...] = total.astype(BF16)


def add_pair(keep, got, order, out):
    out[...] = (keep[...].astype(F32) + got[...].astype(F32)).astype(BF16)


def sum_pieces(pieces, order, out):
    total = pieces[0].astype(F32)
    for k in range(1, pieces.shape[0]):
        total = total + pieces[k].astype(F32)
    total = total.astype(BF16)
    if len(out.shape) == len(pieces.shape):
        for k in range(out.shape[0]):
            out[k] = total
    else:
        out[...] = total


def join_z(*refs):
    out = refs[-1]
    count = out.shape[0]
    z = lax.div(lax.axis_index("lon"), 2)
    for k in range(count):
        out[lax.rem(z + count - k, count)] = refs[k][...]


def third_kernel(
    head, lon_tail, lat_head, diag_tail, resid, slope, active, mixed,
    proj_w, up_w, down_w, gains, order,
    keep_out, give_out, rg_out, dmix_out, gain_out,
    scr_own, scr_oth, m192, m768, mdown, flat_scr,
):
    rows, width = scr_own.shape
    cut = CHUNK * (WLON // 2)
    scr_own[0:cut, :] = lon_tail[...].astype(F32)
    scr_own[cut:, :] = head[...].astype(F32)
    scr_oth[0:cut, :] = diag_tail[...].astype(F32)
    scr_oth[cut:, :] = lat_head[...].astype(F32)
    g = merge_behind(scr_own, scr_oth, rows)
    g_low = g.astype(BF16)
    hg = dot(g_low, down_w[0])
    stand2, inv2 = standardize(resid[...].astype(F32))
    normed2 = (stand2 * gains[0, 1:2, :]).astype(BF16)
    hg = (hg * slope[...].astype(F32)).astype(BF16)
    part, gain_two = norm_back(dot_nt(hg, up_w[0]), gains[0, 1:2, :], stand2, inv2)
    rg = g + part
    rg_out[...] = rg
    low = rg.astype(BF16)
    dmix_out[...] = dot_nt(low, proj_w[0]).astype(BF16)
    gain_out[...] = gain_two
    put(m192, slice(None), dot_tn(mixed[...], low))
    at = flat_store(flat_scr, 0, m192, mixed.shape[1])
    put(m768, slice(None), dot_tn(normed2, hg))
    at += flat_store(flat_scr, at, m768, active.shape[1])
    put(mdown, slice(None), dot_tn(active[...], g_low))
    at += flat_store(flat_scr, at, mdown, mixed.shape[1])
    flat_scr[at:, :] = jnp.zeros((flat_scr.shape[0] - at, 128), F32)
    halves(flat_scr, lax.axis_index("lat"), keep_out, give_out)


def gain_rows(one, two):
    return jnp.concatenate(
        [
            one[:, 0:128],
            jnp.concatenate([one[:, 128:192], two[:, 0:64]], axis=1),
            two[:, 64:192],
        ],
        axis=0,
    )


def fourth_kernel(
    x_in, qkv, probs, dmix, rg, gain_two, gains_late, qkv_w, gains,
    tokens_out, keep, give, bias_out,
    field, sums, m576, flat_scr, dx_scr, low_scr, prob_scr,
):
    width = x_in.shape[-1]
    levels, lats, lons = tokens_out.shape[:3]
    sums[...] = jnp.zeros(sums.shape, F32)
    attend_back(qkv, probs, dmix, field, sums, low_scr, prob_scr, width)
    stand1, inv1 = standardize(x_in[...].astype(F32))
    normed = (stand1 * gains[0, 0:1, :]).astype(BF16)
    ng = dot_nt(field[...], qkv_w[0]).astype(BF16).astype(F32)
    part, gain_one = norm_back(ng, gains[0, 0:1, :], stand1, inv1)
    put(m576, slice(None), dot_tn(normed, field[...]))
    at = flat_store(flat_scr, 0, m576, field.shape[1])
    flat_scr[at:, :] = jnp.zeros((flat_scr.shape[0] - at, 128), F32)
    flat_scr[at : at + 3, :] = gain_rows(gain_one, gain_two[...])
    flat_scr[at + 3 : at + 6, :] = gain_rows(gains_late[0:1, :], gains_late[1:2, :])
    bias_units(sums, bias_out)
    halves(flat_scr, lax.axis_index("lat"), keep, give)
    put(dx_scr, slice(None), rg[...] + part)
    for z in range(levels):
        for a in range(lats):
            tokens_out[z, a] = get(
                dx_scr, pl.ds(z * lats + a, lons, stride=CHUNK), width
            ).astype(BF16)


def place(pieces, first, last, dests, scr):
    total = jnp.zeros((UNIT, 128), F32)
    lons = pieces.shape[1]
    per = last - first
    k = 0
    for where, room in dests:
        for at in range(where, where + room, UNIT):
            half, j, u = k // (per * lons), k // per % lons, k % per
            value = pieces[half, j, first + u].astype(F32)
            scr[at : at + UNIT, :] = value
            total = total + value * value
            k += 1
    return total


def bias_rows(piece, base, spread, out, rows_scr, wide_scr, tab_scr):
    lat = lax.axis_index("lat")
    extra = -(-BIAS_UNITS // piece.shape[1])

    def read(at):
        parts = []
        for r in range(CHUNK // UNIT):
            k = at * (CHUNK // UNIT) + r
            parts.append(piece[lat, k // extra, base + k % extra].astype(F32))
        return jnp.concatenate(parts, axis=0)

    rest = read(2 * HEADS)
    for h in range(HEADS):
        rows = pl.ds(h, CHUNK, stride=8)
        wide_scr[0, rows, :] = read(h)
        wide_scr[1, rows, :] = read(HEADS + h)
        wide_scr[2, rows, :] = rest if h == 0 else pltpu.roll(rest, 128 - 8 * h, axis=1)
    low = get(wide_scr, slice(None), WIDE).astype(BF16)
    for zj in range(LEVELS):
        rows_scr[...] = dot_nt(low, spread[zj])
        for zi in range(LEVELS):
            for ai in range(WLAT):
                at = ((zi * LEVELS + zj) * WLAT + ai) * PAIR
                row = (zi * WLAT + ai) * 8
                tab_scr[0:HEADS, at : at + PAIR] = rows_scr[row : row + HEADS, 0:PAIR]
    for h in range(HEADS):
        out[h] = tab_scr[h : h + 1, :]


def late_kernel(
    units_a, spread, same, same_x, cross, cross_x, flat_out, squares_out, bias_out,
    rows_scr, wide_scr, tab_scr, a,
):
    lat = lax.axis_index("lat")
    x = lax.rem(lax.axis_index("lon"), 2)
    for z in range(same.shape[0]):
        a[lat, 2 * z + x] = same[z]
        a[lat, 2 * z + 1 - x] = same_x[z]
        a[1 - lat, 2 * z + x] = cross[z]
        a[1 - lat, 2 * z + 1 - x] = cross_x[z]
    squares_out[...] = place(a, 0, units_a, [(0, flat_out.shape[0])], flat_out)
    bias_rows(a, units_a, spread, bias_out, rows_scr, wide_scr, tab_scr)


def last_kernel(
    units_b, units_c, spread, flat_a, squares, bias_late, own_bc, oth_bc, update_out, bias_out,
    scr, rows_scr, wide_scr, tab_scr, bc,
):
    lat = lax.axis_index("lat")
    for j in range(own_bc.shape[0]):
        bc[lat, j] = own_bc[j]
        bc[1 - lat, j] = oth_bc[j]
    total = squares[...]
    total = total + place(bc, 0, units_b, [(864, 288), (1152, 1152), (2304, 1152)], scr)
    total = total + place(bc, units_b, units_b + units_c, [(0, 864), (3456, 8)], scr)
    count = update_out.shape[0]
    mean = jnp.sum(total) * (1.0 / (count * 128))
    scale = lax.rsqrt(mean + 1e-06)
    early, late = (0, 1728, 2304, 4608), (864, 2016, 3456, 5760)
    at = 0
    for first, second, rows in zip(early, late, (864, 288, 1152, 1152)):
        update_out[first : first + rows, :] = (scr[at : at + rows, :] * scale).astype(BF16)
        update_out[second : second + rows, :] = (flat_a[at : at + rows, :] * scale).astype(BF16)
        at += rows
    update_out[6912:count, :] = (scr[at : at + count - 6912, :] * scale).astype(BF16)
    bias_rows(bc, units_b + units_c, spread, bias_out.at[0], rows_scr, wide_scr, tab_scr)
    bias_out[1] = bias_late[...]


def call(kernel, outs, scratch, args, micros, mib, spaces=None, near=(), kept=0):
    spaces = spaces or [pltpu.VMEM] * len(args)
    return pl.pallas_call(
        kernel,
        out_shape=[
            (pltpu.VMEM if at in near else jax.ShapeDtypeStruct)(*entry)
            for at, entry in enumerate(outs)
        ],
        in_specs=[pl.BlockSpec(memory_space=space) for space in spaces],
        out_specs=[
            pl.BlockSpec(memory_space=pltpu.VMEM if at < len(outs) - kept else pl.ANY)
            for at in range(len(outs))
        ],
        input_output_aliases={
            len(args) - kept + k: len(outs) - kept + k for k in range(kept)
        },
        scratch_shapes=[
            pltpu.VMEM(*entry) if isinstance(entry, tuple) else entry for entry in scratch
        ],
        compiler_params=pltpu.CompilerParams(vmem_limit_bytes=mib * MIB),
        cost_estimate=pl.CostEstimate(
            flops=int(micros * 1.1e9), bytes_accessed=10**5, transcendentals=0
        ),
    )(*args)


def lat_swap(value):
    return lax.ppermute(value, "lat", [(0, 1), (1, 0)])


def lon_send(value, step):
    count = lax.axis_size("lon")
    return lax.ppermute(value, "lon", [(s, (s + step) % count) for s in range(count)])


def x_swap(value):
    count = lax.axis_size("lon")
    return lax.ppermute(value, "lon", [(s, s ^ 1) for s in range(count)])


def diag_send(value, step):
    count = lax.axis_size("lon")
    pairs = []
    for s in range(count):
        for t in range(2):
            pairs.append((2 * s + t, 2 * ((s + step) % count) + 1 - t))
    return lax.ppermute(value, ("lon", "lat"), pairs)


def shards(
    tokens, cotangent, qkv_weight, proj_weight, up_weight, down_weight, norm_gain, bias_table
):
    levels, lats, lons, width = tokens.shape
    rows = levels * lats * lons
    wins = rows // WIN
    hid = up_weight.shape[-1]
    heads = bias_table.shape[2]
    lon_size = lax.axis_size("lon")
    zs = lon_size // 2
    lat_total = lats * lax.axis_size("lat")
    cut = CHUNK * (WLON // 2)
    spread = jnp.asarray(spread_matrices(), BF16)
    down_turned = jnp.swapaxes(down_weight, 1, 2)
    table = jnp.swapaxes(bias_table, 1, 2)
    token = (rows, width)
    field_shape = ((rows, 3 * width), BF16)
    probs_shape = ((wins, heads, WIN, WIN), F32)
    stack_shape = ((heads * WIN, WIN), BF16)
    bias_shape = ((heads * WIN, WIN), F32)
    sums_shape = ((heads * WIN, WIDE), F32)
    tab_scr = ((8, table.shape[-1]), F32)
    rows_scr = ((LEVELS * CHUNK * 8, PAIR), F32)
    wide_scr = ((WIDE // 128, CHUNK * 8, 128), F32)
    tiles = -(-width // 128)
    token_scr = ((tiles, rows, 128), F32)
    m576 = ((-(-3 * width // 128), width, 128), F32)
    m192 = ((tiles, width, 128), F32)
    m768 = ((hid // 128, width, 128), F32)
    mdown = ((tiles, hid, 128), F32)

    block_rows = (qkv_weight[0].size + proj_weight[0].size + 2 * up_weight[0].size) // 128
    qkv_rows = qkv_weight[0].size // 128
    counts = (block_rows, block_rows - qkv_rows, qkv_rows + 8)
    units_a, units_b, units_c = [-(-count // (2 * lon_size * UNIT)) for count in counts]
    extra = -(-BIAS_UNITS // lon_size)

    def units(*lead):
        return (lead + (UNIT, 128), BF16)

    def flat_scr(per):
        return ((2 * lon_size * per * UNIT, 128), F32)

    x0, tail, head, qkv0, mixed0, probs0, resid0, hidden0, active0 = call(
        functools.partial(first_kernel, lat_total),
        [
            (token, BF16),
            ((2, rows - cut, width), BF16),
            ((2, cut, width), BF16),
            field_shape,
            (token, BF16),
            probs_shape,
            (token, BF16),
            ((rows, hid), F32),
            ((rows, hid), BF16),
        ],
        [
            token_scr,
            token_scr,
            tab_scr,
            rows_scr,
            wide_scr,
            bias_shape,
            (cotangent.shape, BF16),
            ((1,) + table.shape[1:], F32),
            (spread.shape, BF16),
            (tokens.shape, BF16),
            ((1,) + qkv_weight.shape[1:], BF16),
            (norm_gain.shape, F32),
            ((1,) + proj_weight.shape[1:], BF16),
            ((1,) + up_weight.shape[1:], BF16),
            ((1,) + down_turned.shape[1:], BF16),
            stack_shape,
            pltpu.SemaphoreType.DMA((9,)),
        ],
        [
            pltpu.with_memory_space_constraint(arg, pltpu.HBM)
            for arg in (
                tokens, cotangent, table, spread, qkv_weight, proj_weight, up_weight, down_turned,
                norm_gain,
            )
        ],
        8,
        16,
        [pltpu.HBM] * 9,
        near=(0, 3, 4, 5, 6, 8),
    )
    lon_head = lon_send(head, -1)
    diag_head = diag_send(head, -1)
    lat_tail = lat_swap(tail)
    bias1, slope0 = call(
        functools.partial(bias_kernel, lat_total),
        [bias_shape, ((rows, hid), BF16)],
        [tab_scr, rows_scr, wide_scr],
        (table, spread, hidden0),
        3,
        12,
        near=(1,),
    )

    saved = [x0, qkv0, mixed0, probs0, resid0, active0, slope0]
    (
        dhead, dtail, n1, field1, mixed1, low1, n2, hg1, active1, g1, sums1, gains1,
        *saved,
    ) = call(
        functools.partial(second_kernel, lat_total, len(saved)),
        [
            ((rows - cut, width), BF16),
            ((cut, width), BF16),
            (token, BF16),
            field_shape,
            (token, BF16),
            (token, BF16),
            (token, BF16),
            ((rows, hid), BF16),
            ((rows, hid), BF16),
            (token, BF16),
            sums_shape,
            ((2, width), F32),
            *[(value.shape, value.dtype) for value in saved],
        ],
        [
            (token, F32),
            (token, F32),
            field_shape,
            probs_shape,
            (token, BF16),
            stack_shape,
            stack_shape,
        ],
        (
            tail, lon_head, lat_tail, diag_head, bias1, qkv_weight, proj_weight, up_weight,
            down_turned, norm_gain,
            *[pltpu.with_memory_space_constraint(value, pltpu.VMEM) for value in saved],
        ),
        19,
        16,
        [pltpu.VMEM] * 10 + [pl.ANY] * len(saved),
        near=tuple(range(12, 12 + len(saved))),
        kept=len(saved),
    )
    x0, qkv0, mixed0, probs0, resid0, active0, slope0 = saved
    lon_tail = lon_send(dtail, 1)
    diag_tail = diag_send(dtail, 1)
    lat_dhead = lat_swap(dhead)

    keep_a, give_a, bias_a = call(
        outer_kernel,
        [units(lon_size, units_a), units(lon_size, units_a), units(lon_size, extra)],
        [m576, m192, m768, mdown, flat_scr(units_a)],
        (n1, field1, mixed1, low1, n2, hg1, active1, g1, sums1),
        0.01,
        14,
    )
    got_a = lat_swap(give_a)

    units_xa = units_a + extra
    keep_xa, give_xa = call(
        lat_sums_split, [units(zs, units_xa)] * 2, [], (keep_a, got_a, bias_a, keep_a), 0.01, 10
    )
    got_xa = x_swap(give_xa)

    keep_b, give_b, rg0, dmix0, gain_two = call(
        third_kernel,
        [
            units(lon_size, units_b),
            units(lon_size, units_b),
            (token, F32),
            (token, BF16),
            ((1, width), F32),
        ],
        [(token, F32), (token, F32), m192, m768, mdown, flat_scr(units_b)],
        (
            dhead, lon_tail, lat_dhead, diag_tail, resid0, slope0, active0, mixed0, proj_weight,
            up_weight, down_turned, norm_gain, keep_xa,
        ),
        3,
        14,
    )
    got_b = lat_swap(give_b)

    tokens_grad, keep_c, give_c, bias_c = call(
        fourth_kernel,
        [
            (tokens.shape, BF16),
            units(lon_size, units_c),
            units(lon_size, units_c),
            units(lon_size, extra),
        ],
        [
            field_shape,
            sums_shape,
            m576,
            flat_scr(units_c),
            token_scr,
            stack_shape,
            stack_shape,
        ],
        (x0, qkv0, probs0, dmix0, rg0, gain_two, gains1, qkv_weight, norm_gain),
        7,
        14,
    )
    got_c = lat_swap(give_c)
    own_a, *gives_a = call(
        split_z, [units(units_xa)] * zs, [], (keep_xa, got_xa), 1, 10
    )
    gots_a = [lon_send(give, 2 * (k + 1)) for k, give in enumerate(gives_a)]
    units_bc = units_b + units_c + extra
    keep_x, give_x = call(
        lat_sums_split,
        [units(zs, units_bc)] * 2,
        [],
        (keep_b, got_b, keep_c, got_c, bias_c, own_a),
        1,
        10,
    )
    got_x = x_swap(give_x)
    (sum_a,) = call(sum_refs, [units(units_xa)], [], (own_a, *gots_a, keep_x), 1, 10)
    (part_z,) = call(add_pair, [units(zs, units_bc)], [], (keep_x, got_x, sum_a), 1, 10)
    pieces_bc = lax.all_to_all(
        part_z,
        "lon",
        0,
        0,
        axis_index_groups=[[2 * z + x for z in range(zs)] for x in range(2)],
    )
    moved_a = [lon_send(sum_a, 2 * k) for k in range(1, zs)]
    (same,) = call(join_z, [units(zs, units_xa)], [], [sum_a, *moved_a, part_z], 1, 10)
    same_x = x_swap(same)
    cross = lat_swap(same)
    cross_x = lat_swap(same_x)
    (sum_bc,) = call(
        sum_pieces, [units(lon_size, units_bc)], [], (pieces_bc, same), 1, 10
    )
    whole_bc = lax.all_to_all(sum_bc, "lon", 0, 0)
    oth_bc = lat_swap(whole_bc)

    flat_rows = (2 * block_rows * 128 + norm_gain.size) // 128
    fold_scr = [((CHUNK * 8, PAIR), F32), wide_scr, tab_scr]
    flat_a, squares, bias_late = call(
        functools.partial(late_kernel, units_a),
        [((block_rows, 128), F32), ((UNIT, 128), F32), (table.shape[1:], F32)],
        [*fold_scr, units(2, lon_size, units_a + extra)],
        (spread, same, same_x, cross, cross_x),
        2,
        14,
    )
    update, bias_grad = call(
        functools.partial(last_kernel, units_b, units_c),
        [((flat_rows, 128), BF16), (table.shape, F32)],
        [
            ((block_rows + 8, 128), F32),
            *fold_scr,
            units(2, lon_size, units_b + units_c + extra),
        ],
        (spread, flat_a, squares, bias_late, whole_bc, oth_bc),
        2,
        14,
    )
    bias_grad = jnp.swapaxes(bias_grad, 1, 2)
    return (tokens_grad, update.reshape(-1), bias_grad)


def solution(mesh):
    return jax.shard_map(
        shards,
        mesh=mesh,
        in_specs=(
            P("grp", "lat", "lon", None),
            P("grp", "lat", "lon", None),
            P(),
            P(),
            P(),
            P(),
            P(),
            P(None, "lat", None, None),
        ),
        out_specs=(P("grp", "lat", "lon", None), P("grp"), P("grp", "lat", None, None)),
        check_vma=False,
    )
```

```python
import functools

import jax
import jax.numpy as jnp
import numpy as np
from jax import lax
from jax.experimental import pallas as pl
from jax.experimental.pallas import tpu as pltpu
from jax.sharding import PartitionSpec as P

WLAT = 12
WLON = 6
PAD = 5
LEVELS = 2
HEADS = 6
CHUNK = LEVELS * WLAT
WIN = CHUNK * WLON
SHIFTS = 2 * WLON - 1
PAIR = WLAT * SHIFTS
WIDE = 384

EPS = 1e-05
NEGATIVE = -1000000000.0
ROOT_HALF = 0.7071067811865476
INV_ROOT_TAU = 0.3989422804014327

F32 = jnp.float32
BF16 = jnp.bfloat16
UNIT = 8
BIAS_UNITS = (2 * HEADS + 1) * CHUNK // UNIT
MIB = 1024 * 1024


def dot(a, b):
    return lax.dot_general(a, b, (((1,), (0,)), ((), ())), preferred_element_type=F32)


def dot_nt(a, b):
    return lax.dot_general(a, b, (((1,), (1,)), ((), ())), preferred_element_type=F32)


def dot_tn(a, b):
    return lax.dot_general(a, b, (((0,), (0,)), ((), ())), preferred_element_type=F32)


def row_mean(v):
    return jnp.sum(v, axis=-1, keepdims=True) * (1.0 / v.shape[-1])


def standardize(x):
    centred = x - row_mean(x)
    inv = lax.rsqrt(row_mean(centred * centred) + EPS)
    return centred * inv, inv


def norm_back(d, gain, stand, inv):
    scaled = d * gain
    first = row_mean(scaled)
    second = row_mean(scaled * stand)
    gain_grad = jnp.sum(d * stand, axis=0, keepdims=True)
    return inv * (scaled - first - stand * second), gain_grad


def gelu_value(hidden):
    return 0.5 * hidden * (1.0 + lax.erf(hidden * ROOT_HALF))


def gelu_parts(hidden):
    half = 0.5 * (1.0 + lax.erf(hidden * ROOT_HALF))
    slope = half + hidden * jnp.exp(-0.5 * hidden * hidden) * INV_ROOT_TAU
    return hidden * half, slope


def split3(v):
    hi = v.astype(BF16)
    rest = v - hi.astype(F32)
    mid = rest.astype(BF16)
    low = (rest - mid.astype(F32)).astype(BF16)
    return hi, mid, low


def spread_matrices():
    out = np.zeros((LEVELS, PAIR, WIDE), np.float32)
    for zj in range(LEVELS):
        for aj in range(WLAT):
            for d in range(SHIFTS):
                out[zj, aj * SHIFTS + d, (SHIFTS - 1 - d) * CHUNK + zj * WLAT + aj] = 1.0
    return out


def put(scr, rows, value):
    width = value.shape[1]
    for tile in range(-(-width // 128)):
        lanes = min(128, width - tile * 128)
        scr[tile, rows, 0:lanes] = value[:, tile * 128 : tile * 128 + lanes]


def get(scr, rows, width):
    parts = [scr[tile, rows, :] for tile in range(-(-width // 128))]
    return jnp.concatenate(parts, axis=1)[:, 0:width]


def head_masks(width, dtype):
    lane = lax.broadcasted_iota(jnp.int32, (1, width), 1)
    size = width // HEADS
    return [((lane >= h * size) & (lane < (h + 1) * size)).astype(dtype) for h in range(HEADS)]


def lat_inside(n):
    return lax.rem(n, WLAT)


def lat_row(row_iota, lat, shifted, lat_total):
    row = lat * WLAT + lat_inside(row_iota)
    if shifted:
        row = row + WLAT // 2
        row = jnp.where(row >= lat_total, row - lat_total, row)
    return row


def expand_bias(table, spread, tab_scr, rows_scr, wide_scr, bias_scr, lat, shifted, lat_total):
    for h in range(HEADS):
        tab_scr[h : h + 1, :] = table[h]
    for zi in range(LEVELS):
        for zj in range(LEVELS):
            for ai in range(WLAT):
                at = ((zi * LEVELS + zj) * WLAT + ai) * PAIR
                row = zj * CHUNK * 8 + (zi * WLAT + ai) * 8
                rows_scr[row : row + HEADS, 0:PAIR] = tab_scr[0:HEADS, at : at + PAIR]
    count = CHUNK * 8
    total = jnp.zeros((count, WIDE), F32)
    for zj in range(LEVELS):
        parts = split3(rows_scr[zj * count : (zj + 1) * count, 0:PAIR])
        for part in parts:
            total = total + dot(part, spread[zj])
    put(wide_scr, slice(None), total)
    i = lax.broadcasted_iota(jnp.int32, (CHUNK, WIN), 0)
    j = lax.broadcasted_iota(jnp.int32, (CHUNK, WIN), 1)
    allowed = lat_row(j, lat, shifted, lat_total) < lat_total - PAD
    if shifted:
        last = lat_total - WLAT // 2
        region_i = (lat * WLAT + lat_inside(i)) >= last
        region_j = (lat * WLAT + lat_inside(j)) >= last
        allowed = allowed & (region_i == region_j)
    for h in range(HEADS):
        wide = get(wide_scr, pl.ds(h, CHUNK, stride=8), WIDE)
        for oi in range(WLON):
            back = (WLON - 1 - oi) * CHUNK
            moved = wide if back == 0 else pltpu.roll(wide, WIDE - back, axis=1)
            at = h * WIN + oi * CHUNK
            bias_scr[at : at + CHUNK, :] = jnp.where(allowed, moved[:, 0:WIN], NEGATIVE)


def fold_bias(sums, put_unit):
    rest = jnp.zeros((CHUNK, 128), F32)

    def emit(at, value):
        for r in range(CHUNK // UNIT):
            put_unit(at * (CHUNK // UNIT) + r, value[r * UNIT : (r + 1) * UNIT, :].astype(BF16))

    for h in range(HEADS):
        total = jnp.zeros((CHUNK, WIDE), F32)
        for oi in range(WLON):
            back = (WLON - 1 - oi) * CHUNK
            at = h * WIN + oi * CHUNK
            part = sums[at : at + CHUNK, :]
            total = total + (part if back == 0 else pltpu.roll(part, back, axis=1))
        emit(h, total[:, 0:128])
        emit(HEADS + h, total[:, 128:256])
        last = total[:, 256:384]
        rest = rest + (last if h == 0 else pltpu.roll(last, 8 * h, axis=1))
    emit(2 * HEADS, rest)

def stack_heads(v, masks):
    return jnp.concatenate([v * mask for mask in masks], axis=0)


def pick_heads(v, width):
    lane = lax.broadcasted_iota(jnp.int32, (1, width), 1)
    size = width // HEADS
    total = v[(HEADS - 1) * WIN :]
    for h in range(HEADS - 1, 0, -1):
        total = jnp.where(lane < h * size, v[(h - 1) * WIN : h * WIN], total)
    return total


def attend(qkv, bias, mixed, probs, stack_scr, width):
    masks = head_masks(width, BF16)
    scale = (width // HEADS) ** -0.5

    def window(w, carry):
        rows = pl.ds(pl.multiple_of(w * WIN, 16), WIN)
        q = qkv[rows, 0:width]
        k = qkv[rows, width : 2 * width]
        v = qkv[rows, 2 * width : 3 * width]
        scores = dot_nt(stack_heads(q, masks), k)
        for h in range(HEADS):
            part = slice(h * WIN, (h + 1) * WIN)
            logits = scores[part] * scale + bias[part, :]
            weights = jnp.exp(logits - jnp.max(logits, axis=-1, keepdims=True))
            p = weights * (1.0 / jnp.sum(weights, axis=-1, keepdims=True))
            probs[w, h] = p
            stack_scr[part, :] = p.astype(BF16)
        mixed[rows, :] = pick_heads(dot(stack_scr[...], v), width).astype(BF16)
        return carry

    lax.fori_loop(0, probs.shape[0], window, 0, unroll=True)


def attend_back(qkv, probs, dmix, field, sums, low_scr, prob_scr, width):
    masks = head_masks(width, BF16)
    scale = (width // HEADS) ** -0.5

    def window(w, carry):
        rows = pl.ds(pl.multiple_of(w * WIN, 16), WIN)
        q = qkv[rows, 0:width]
        k = qkv[rows, width : 2 * width]
        v = qkv[rows, 2 * width : 3 * width]
        up = stack_heads(dmix[rows, :], masks)
        prob_grad = dot_nt(up, v)
        for h in range(HEADS):
            part = slice(h * WIN, (h + 1) * WIN)
            p = probs[w, h]
            weighted = p * prob_grad[part]
            ds = weighted - p * jnp.sum(weighted, axis=-1, keepdims=True)
            sums[part, 0:WIN] += ds
            low_scr[part, :] = ds.astype(BF16)
            prob_scr[part, :] = p.astype(BF16)
        low = low_scr[...]
        dq = pick_heads(dot(low, k), width)
        dk = dot_tn(low, stack_heads(q, masks))
        dv = dot_tn(prob_scr[...], up)
        field[rows, 0:width] = (dq * scale).astype(BF16)
        field[rows, width : 2 * width] = (dk * scale).astype(BF16)
        field[rows, 2 * width : 3 * width] = dv.astype(BF16)
        return carry

    lax.fori_loop(0, probs.shape[0], window, 0, unroll=True)


def lon_major(src, scr):
    levels, lats, lons, width = src.shape
    for z in range(levels):
        for a in range(lats):
            at = (z * lats + a) * lons
            put(scr, slice(at, at + lons), src[z, a].astype(F32))


def lon_column(scr, lon, lons, width):
    return get(scr, pl.ds(lon, CHUNK, stride=lons), width)


def flat_store(dst, at, mat, cols):
    rows = mat.shape[1]
    if cols % 128 == 0:
        per = cols // 128
        for c in range(per):
            dst[pl.ds(at + c, rows, stride=per), :] = mat[c]
        return rows * per
    per = 2 * cols // 128
    half = cols // 128
    even = get(mat, pl.ds(0, rows // 2, stride=2), cols)
    odd = get(mat, pl.ds(1, rows // 2, stride=2), cols)
    for c in range(half):
        dst[pl.ds(at + c, rows // 2, stride=per), :] = even[:, c * 128 : (c + 1) * 128]
    dst[pl.ds(at + half, rows // 2, stride=per), :] = jnp.concatenate(
        [even[:, half * 128 : half * 128 + 64], odd[:, 0:64]], axis=1
    )
    for c in range(half):
        dst[pl.ds(at + half + 1 + c, rows // 2, stride=per), :] = odd[
            :, 64 + c * 128 : 64 + (c + 1) * 128
        ]
    return rows * cols // 128


def send_units(scr, base, out):
    lons, units = out.shape[:2]
    for j in range(lons):
        for u in range(units):
            at = base + (j * units + u) * UNIT
            if not isinstance(at, int):
                at = pl.multiple_of(at, UNIT)
            out[j, u] = scr[pl.ds(at, UNIT), :].astype(BF16)


def halves(scr, lat, keep, give):
    half = keep.shape[0] * keep.shape[1] * UNIT
    send_units(scr, lat * half, keep)
    send_units(scr, (1 - lat) * half, give)


def bias_units(sums, out):
    lons, per = out.shape[:2]

    def put_unit(k, value):
        out[k // per, k % per] = value

    fold_bias(sums, put_unit)
    for k in range(BIAS_UNITS, lons * per):
        put_unit(k, jnp.zeros((UNIT, 128), BF16))

def forward_core(x, b, refs, qkv_scr, bias_scr, mixed, probs, stack_scr):
    qkv_w, proj_w, gains = refs
    width = x.shape[-1]
    stand, inv = standardize(x)
    normed = (stand * gains[b, 0:1, :]).astype(BF16)
    qkv_scr[...] = dot(normed, qkv_w[b]).astype(BF16)
    attend(qkv_scr, bias_scr, mixed, probs, stack_scr, width)
    att = dot(mixed[...], proj_w[b]).astype(BF16)
    resid = (x + att.astype(F32)).astype(BF16).astype(F32)
    return resid, normed


def first_kernel(
    lat_total, tokens_in, cot_in, table_in, spread_in, qkv_in, proj_in, up_in, down_in, gains_in,
    x_out, tail_out, head_out, qkv_out, mixed_out, probs_out, resid_out, hidden_out, active_out,
    scr, cot_scr, tab_scr, rows_scr, wide_scr, bias_scr,
    cot, table, spread, tokens, qkv_w, gains, proj_w, up_w, down_w, stack_scr, sems,
):
    copies = []
    for source, target in (
        (cot_in, cot),
        (table_in.at[0:1], table),
        (spread_in, spread),
        (tokens_in, tokens),
        (qkv_in.at[0:1], qkv_w),
        (gains_in, gains),
        (proj_in.at[0:1], proj_w),
        (up_in.at[0:1], up_w),
        (down_in.at[0:1], down_w),
    ):
        copies.append(pltpu.make_async_copy(source, target, sems.at[len(copies)]))
    for copy in copies:
        copy.start()
    lat = lax.axis_index("lat")
    width = tokens.shape[-1]
    lons = tokens.shape[2]
    cut = CHUNK * (WLON // 2)
    copies[0].wait()
    lon_major(cot, cot_scr)
    g = jnp.concatenate([lon_column(cot_scr, lon, lons, width) for lon in range(lons)], axis=0)
    head_out[1] = g[0:cut, :].astype(BF16)
    tail_out[1] = g[cut:, :].astype(BF16)
    copies[1].wait()
    copies[2].wait()
    expand_bias(
        table.at[0], spread, tab_scr, rows_scr, wide_scr, bias_scr, lat, False, lat_total
    )
    copies[3].wait()
    lon_major(tokens, scr)
    x = jnp.concatenate([lon_column(scr, lon, lons, width) for lon in range(lons)], axis=0)
    x_out[...] = x.astype(BF16)
    for copy in copies[4:]:
        copy.wait()

    resid, _ = forward_core(
        x, 0, (qkv_w, proj_w, gains), qkv_out, bias_scr, mixed_out, probs_out, stack_scr
    )
    resid_out[...] = resid.astype(BF16)
    stand, _ = standardize(resid)
    normed = (stand * gains[0, 1:2, :]).astype(BF16)
    hidden = dot(normed, up_w[0])
    hidden_out[...] = hidden
    active = gelu_value(hidden).astype(BF16)
    active_out[...] = active
    result = resid + dot_nt(active, down_w[0])
    head_out[0] = result[0:cut, :].astype(BF16)
    tail_out[0] = result[cut:, :].astype(BF16)


def bias_kernel(
    lat_total, table, spread, hidden, bias_out, slope_out, tab_scr, rows_scr, wide_scr
):
    lat = lax.axis_index("lat")
    slope_out[...] = gelu_parts(hidden[...])[1].astype(BF16)
    expand_bias(
        table.at[1], spread, tab_scr, rows_scr, wide_scr, bias_out, lat, True, lat_total
    )


def merge_ahead(scr_own, scr_oth, rows):
    half = WLAT // 2
    n = lax.broadcasted_iota(jnp.int32, (rows, 1), 0)
    return jnp.where(
        lat_inside(n) < half,
        pltpu.roll(scr_own[...], rows - half, axis=0),
        pltpu.roll(scr_oth[...], half, axis=0),
    )


def merge_behind(scr_own, scr_oth, rows):
    half = WLAT // 2
    n = lax.broadcasted_iota(jnp.int32, (rows, 1), 0)
    return jnp.where(
        lat_inside(n) >= half,
        pltpu.roll(scr_own[...], half, axis=0),
        pltpu.roll(scr_oth[...], rows - half, axis=0),
    )


def second_kernel(
    lat_total,
    kept, tail, lon_head, lat_tail, diag_head, bias, qkv_w, proj_w, up_w, down_w, gains, *rest
):
    run_second(
        lat_total, tail, lon_head, lat_tail, diag_head, bias, qkv_w, proj_w, up_w, down_w, gains,
        *rest[kept:kept + 12], *rest[2 * kept + 12 :]
    )


def run_second(
    lat_total,
    tail, lon_head, lat_tail, diag_head, bias, qkv_w, proj_w, up_w, down_w, gains,
    head_out, tail_out, n1_out, field_out, mixed_out, low_out, n2_out, hg_out, active_out, g_out,
    sums_out, gain_out,
    scr_own, scr_oth, qkv_scr, probs_scr, dmix_scr, low_scr, prob_scr,
):
    lat = lax.axis_index("lat")
    rows, width = scr_own.shape
    cut = CHUNK * (WLON // 2)

    def rolled(which):
        scr_own[0 : rows - cut, :] = tail[which].astype(F32)
        scr_own[rows - cut :, :] = lon_head[which].astype(F32)
        scr_oth[0 : rows - cut, :] = lat_tail[which].astype(F32)
        scr_oth[rows - cut :, :] = diag_head[which].astype(F32)
        return merge_ahead(scr_own, scr_oth, rows)

    g = rolled(1)
    n = lax.broadcasted_iota(jnp.int32, (rows, 1), 0)
    keep = lat_row(n, lat, True, lat_total) < lat_total - PAD
    g = jnp.where(keep, g, 0.0)
    g_out[...] = g.astype(BF16)

    x = rolled(0)

    resid, normed = forward_core(
        x, 1, (qkv_w, proj_w, gains), qkv_scr, bias, mixed_out, probs_scr, low_scr
    )
    n1_out[...] = normed
    stand2, inv2 = standardize(resid)
    normed2 = (stand2 * gains[1, 1:2, :]).astype(BF16)
    n2_out[...] = normed2
    active, slope = gelu_parts(dot(normed2, up_w[1]))
    active_out[...] = active.astype(BF16)

    hg = (dot(g_out[...], down_w[1]) * slope).astype(BF16)
    hg_out[...] = hg
    part, gain_two = norm_back(dot_nt(hg, up_w[1]), gains[1, 1:2, :], stand2, inv2)
    rg = g + part
    low = rg.astype(BF16)
    low_out[...] = low
    dmix_scr[...] = dot_nt(low, proj_w[1]).astype(BF16)
    sums_out[...] = jnp.zeros(sums_out.shape, F32)
    attend_back(
        qkv_scr, probs_scr, dmix_scr, field_out, sums_out, low_scr, prob_scr, width
    )
    ng = dot_nt(field_out[...], qkv_w[1]).astype(BF16).astype(F32)
    stand1, inv1 = standardize(x)
    part, gain_one = norm_back(ng, gains[1, 0:1, :], stand1, inv1)
    dx = rg + part
    head_out[...] = dx[0 : rows - cut, :].astype(BF16)
    tail_out[...] = dx[rows - cut :, :].astype(BF16)
    gain_out[0:1, :] = gain_one
    gain_out[1:2, :] = gain_two


def outer_kernel(
    n1, field, mixed, low, n2, hg, active, g, sums,
    keep, give, bias_out,
    m576, m192, m768, mdown, flat_scr,
):
    put(m576, slice(None), dot_tn(n1[...], field[...]))
    at = flat_store(flat_scr, 0, m576, field.shape[1])
    put(m192, slice(None), dot_tn(mixed[...], low[...]))
    at += flat_store(flat_scr, at, m192, mixed.shape[1])
    put(m768, slice(None), dot_tn(n2[...], hg[...]))
    at += flat_store(flat_scr, at, m768, active.shape[1])
    put(mdown, slice(None), dot_tn(active[...], g[...]))
    at += flat_store(flat_scr, at, mdown, mixed.shape[1])
    halves(flat_scr, lax.axis_index("lat"), keep, give)
    bias_units(sums, bias_out)


def lat_sums_split(*refs):
    keep_out, give_out = refs[-2:]
    x = lax.rem(lax.axis_index("lon"), 2)
    for out, side in ((keep_out, x), (give_out, 1 - x)):
        for z in range(out.shape[0]):
            j = 2 * z + side
            at = 0
            for k in range(0, len(refs) - 4, 2):
                keep, got = refs[k], refs[k + 1]
                count = keep.shape[1]
                total = keep[j].astype(F32) + got[j].astype(F32)
                out[z, at : at + count] = total.astype(BF16)
                at += count
            out[z, at:] = refs[-4][j]


def split_z(keep, got, own_out, *give_outs):
    count = keep.shape[0]
    z = lax.div(lax.axis_index("lon"), 2)
    for k, out in enumerate((own_out,) + give_outs):
        at = lax.rem(z + k, count)
        out[...] = (keep[at].astype(F32) + got[at].astype(F32)).astype(BF16)


def sum_refs(*refs):
    total = refs[0][...].astype(F32)
    for ref in refs[1:-2]:
        total = total + ref[...].astype(F32)
    refs[-1][...] = total.astype(BF16)


def add_pair(keep, got, order, out):
    out[...] = (keep[...].astype(F32) + got[...].astype(F32)).astype(BF16)


def sum_pieces(pieces, order, out):
    total = pieces[0].astype(F32)
    for k in range(1, pieces.shape[0]):
        total = total + pieces[k].astype(F32)
    total = total.astype(BF16)
    if len(out.shape) == len(pieces.shape):
        for k in range(out.shape[0]):
            out[k] = total
    else:
        out[...] = total


def join_z(*refs):
    out = refs[-1]
    count = out.shape[0]
    z = lax.div(lax.axis_index("lon"), 2)
    for k in range(count):
        out[lax.rem(z + count - k, count)] = refs[k][...]


def third_kernel(
    head, lon_tail, lat_head, diag_tail, resid, slope, active, mixed,
    proj_w, up_w, down_w, gains, order,
    keep_out, give_out, rg_out, dmix_out, gain_out,
    scr_own, scr_oth, m192, m768, mdown, flat_scr,
):
    rows, width = scr_own.shape
    cut = CHUNK * (WLON // 2)
    scr_own[0:cut, :] = lon_tail[...].astype(F32)
    scr_own[cut:, :] = head[...].astype(F32)
    scr_oth[0:cut, :] = diag_tail[...].astype(F32)
    scr_oth[cut:, :] = lat_head[...].astype(F32)
    g = merge_behind(scr_own, scr_oth, rows)
    g_low = g.astype(BF16)
    hg = dot(g_low, down_w[0])
    stand2, inv2 = standardize(resid[...].astype(F32))
    normed2 = (stand2 * gains[0, 1:2, :]).astype(BF16)
    hg = (hg * slope[...].astype(F32)).astype(BF16)
    part, gain_two = norm_back(dot_nt(hg, up_w[0]), gains[0, 1:2, :], stand2, inv2)
    rg = g + part
    rg_out[...] = rg
    low = rg.astype(BF16)
    dmix_out[...] = dot_nt(low, proj_w[0]).astype(BF16)
    gain_out[...] = gain_two
    put(m192, slice(None), dot_tn(mixed[...], low))
    at = flat_store(flat_scr, 0, m192, mixed.shape[1])
    put(m768, slice(None), dot_tn(normed2, hg))
    at += flat_store(flat_scr, at, m768, active.shape[1])
    put(mdown, slice(None), dot_tn(active[...], g_low))
    at += flat_store(flat_scr, at, mdown, mixed.shape[1])
    flat_scr[at:, :] = jnp.zeros((flat_scr.shape[0] - at, 128), F32)
    halves(flat_scr, lax.axis_index("lat"), keep_out, give_out)


def gain_rows(one, two):
    return jnp.concatenate(
        [
            one[:, 0:128],
            jnp.concatenate([one[:, 128:192], two[:, 0:64]], axis=1),
            two[:, 64:192],
        ],
        axis=0,
    )


def fourth_kernel(
    x_in, qkv, probs, dmix, rg, gain_two, gains_late, qkv_w, gains,
    tokens_out, keep, give, bias_out,
    field, sums, m576, flat_scr, dx_scr, low_scr, prob_scr,
):
    width = x_in.shape[-1]
    levels, lats, lons = tokens_out.shape[:3]
    sums[...] = jnp.zeros(sums.shape, F32)
    attend_back(qkv, probs, dmix, field, sums, low_scr, prob_scr, width)
    stand1, inv1 = standardize(x_in[...].astype(F32))
    normed = (stand1 * gains[0, 0:1, :]).astype(BF16)
    ng = dot_nt(field[...], qkv_w[0]).astype(BF16).astype(F32)
    part, gain_one = norm_back(ng, gains[0, 0:1, :], stand1, inv1)
    put(m576, slice(None), dot_tn(normed, field[...]))
    at = flat_store(flat_scr, 0, m576, field.shape[1])
    flat_scr[at:, :] = jnp.zeros((flat_scr.shape[0] - at, 128), F32)
    flat_scr[at : at + 3, :] = gain_rows(gain_one, gain_two[...])
    flat_scr[at + 3 : at + 6, :] = gain_rows(gains_late[0:1, :], gains_late[1:2, :])
    bias_units(sums, bias_out)
    halves(flat_scr, lax.axis_index("lat"), keep, give)
    put(dx_scr, slice(None), rg[...] + part)
    for z in range(levels):
        for a in range(lats):
            tokens_out[z, a] = get(
                dx_scr, pl.ds(z * lats + a, lons, stride=CHUNK), width
            ).astype(BF16)


def place(pieces, first, last, dests, scr):
    total = jnp.zeros((UNIT, 128), F32)
    lons = pieces.shape[1]
    per = last - first
    k = 0
    for where, room in dests:
        for at in range(where, where + room, UNIT):
            half, j, u = k // (per * lons), k // per % lons, k % per
            value = pieces[half, j, first + u].astype(F32)
            scr[at : at + UNIT, :] = value
            total = total + value * value
            k += 1
    return total


def bias_rows(piece, base, spread, out, rows_scr, wide_scr, tab_scr):
    lat = lax.axis_index("lat")
    extra = -(-BIAS_UNITS // piece.shape[1])

    def read(at):
        parts = []
        for r in range(CHUNK // UNIT):
            k = at * (CHUNK // UNIT) + r
            parts.append(piece[lat, k // extra, base + k % extra].astype(F32))
        return jnp.concatenate(parts, axis=0)

    rest = read(2 * HEADS)
    for h in range(HEADS):
        rows = pl.ds(h, CHUNK, stride=8)
        wide_scr[0, rows, :] = read(h)
        wide_scr[1, rows, :] = read(HEADS + h)
        wide_scr[2, rows, :] = rest if h == 0 else pltpu.roll(rest, 128 - 8 * h, axis=1)
    low = get(wide_scr, slice(None), WIDE).astype(BF16)
    for zj in range(LEVELS):
        rows_scr[...] = dot_nt(low, spread[zj])
        for zi in range(LEVELS):
            for ai in range(WLAT):
                at = ((zi * LEVELS + zj) * WLAT + ai) * PAIR
                row = (zi * WLAT + ai) * 8
                tab_scr[0:HEADS, at : at + PAIR] = rows_scr[row : row + HEADS, 0:PAIR]
    for h in range(HEADS):
        out[h] = tab_scr[h : h + 1, :]


def late_kernel(
    units_a, spread, same, same_x, cross, cross_x, flat_out, squares_out, bias_out,
    rows_scr, wide_scr, tab_scr, a,
):
    lat = lax.axis_index("lat")
    x = lax.rem(lax.axis_index("lon"), 2)
    for z in range(same.shape[0]):
        a[lat, 2 * z + x] = same[z]
        a[lat, 2 * z + 1 - x] = same_x[z]
        a[1 - lat, 2 * z + x] = cross[z]
        a[1 - lat, 2 * z + 1 - x] = cross_x[z]
    squares_out[...] = place(a, 0, units_a, [(0, flat_out.shape[0])], flat_out)
    bias_rows(a, units_a, spread, bias_out, rows_scr, wide_scr, tab_scr)


def near_kernel(
    units_b, units_c, spread, own_bc, oth_bc, flat_out, squares_out, bias_out,
    rows_scr, wide_scr, tab_scr, bc,
):
    lat = lax.axis_index("lat")
    for j in range(own_bc.shape[0]):
        bc[lat, j] = own_bc[j]
        bc[1 - lat, j] = oth_bc[j]
    total = place(bc, 0, units_b, [(864, 288), (1152, 1152), (2304, 1152)], flat_out)
    squares_out[...] = total + place(
        bc, units_b, units_b + units_c, [(0, 864), (3456, 8)], flat_out
    )
    bias_rows(bc, units_b + units_c, spread, bias_out, rows_scr, wide_scr, tab_scr)


def last_kernel(
    flat_a, squares_a, bias_late, flat_bc, squares_bc, bias_near, update_out, bias_out
):
    count = update_out.shape[0]
    mean = jnp.sum(squares_a[...] + squares_bc[...]) * (1.0 / (count * 128))
    scale = lax.rsqrt(mean + 1e-06)
    early, late = (0, 1728, 2304, 4608), (864, 2016, 3456, 5760)
    at = 0
    for first, second, rows in zip(early, late, (864, 288, 1152, 1152)):
        update_out[first : first + rows, :] = (flat_bc[at : at + rows, :] * scale).astype(BF16)
        update_out[second : second + rows, :] = (flat_a[at : at + rows, :] * scale).astype(BF16)
        at += rows
    update_out[6912:count, :] = (flat_bc[at : at + count - 6912, :] * scale).astype(BF16)
    bias_out[0] = bias_near[...]
    bias_out[1] = bias_late[...]


def call(kernel, outs, scratch, args, micros, mib, spaces=None, near=(), kept=0):
    spaces = spaces or [pltpu.VMEM] * len(args)
    return pl.pallas_call(
        kernel,
        out_shape=[
            (pltpu.VMEM if at in near else jax.ShapeDtypeStruct)(*entry)
            for at, entry in enumerate(outs)
        ],
        in_specs=[pl.BlockSpec(memory_space=space) for space in spaces],
        out_specs=[
            pl.BlockSpec(memory_space=pltpu.VMEM if at < len(outs) - kept else pl.ANY)
            for at in range(len(outs))
        ],
        input_output_aliases={
            len(args) - kept + k: len(outs) - kept + k for k in range(kept)
        },
        scratch_shapes=[
            pltpu.VMEM(*entry) if isinstance(entry, tuple) else entry for entry in scratch
        ],
        compiler_params=pltpu.CompilerParams(vmem_limit_bytes=mib * MIB),
        cost_estimate=pl.CostEstimate(
            flops=int(micros * 1.1e9), bytes_accessed=10**5, transcendentals=0
        ),
    )(*args)


def lat_swap(value):
    return lax.ppermute(value, "lat", [(0, 1), (1, 0)])


def lon_send(value, step):
    count = lax.axis_size("lon")
    return lax.ppermute(value, "lon", [(s, (s + step) % count) for s in range(count)])


def x_swap(value):
    count = lax.axis_size("lon")
    return lax.ppermute(value, "lon", [(s, s ^ 1) for s in range(count)])


def diag_send(value, step):
    count = lax.axis_size("lon")
    pairs = []
    for s in range(count):
        for t in range(2):
            pairs.append((2 * s + t, 2 * ((s + step) % count) + 1 - t))
    return lax.ppermute(value, ("lon", "lat"), pairs)


def shards(
    tokens, cotangent, qkv_weight, proj_weight, up_weight, down_weight, norm_gain, bias_table
):
    levels, lats, lons, width = tokens.shape
    rows = levels * lats * lons
    wins = rows // WIN
    hid = up_weight.shape[-1]
    heads = bias_table.shape[2]
    lon_size = lax.axis_size("lon")
    zs = lon_size // 2
    lat_total = lats * lax.axis_size("lat")
    cut = CHUNK * (WLON // 2)
    spread = jnp.asarray(spread_matrices(), BF16)
    down_turned = jnp.swapaxes(down_weight, 1, 2)
    table = jnp.swapaxes(bias_table, 1, 2)
    token = (rows, width)
    field_shape = ((rows, 3 * width), BF16)
    probs_shape = ((wins, heads, WIN, WIN), F32)
    stack_shape = ((heads * WIN, WIN), BF16)
    bias_shape = ((heads * WIN, WIN), F32)
    sums_shape = ((heads * WIN, WIDE), F32)
    tab_scr = ((8, table.shape[-1]), F32)
    rows_scr = ((LEVELS * CHUNK * 8, PAIR), F32)
    wide_scr = ((WIDE // 128, CHUNK * 8, 128), F32)
    tiles = -(-width // 128)
    token_scr = ((tiles, rows, 128), F32)
    m576 = ((-(-3 * width // 128), width, 128), F32)
    m192 = ((tiles, width, 128), F32)
    m768 = ((hid // 128, width, 128), F32)
    mdown = ((tiles, hid, 128), F32)

    block_rows = (qkv_weight[0].size + proj_weight[0].size + 2 * up_weight[0].size) // 128
    qkv_rows = qkv_weight[0].size // 128
    counts = (block_rows, block_rows - qkv_rows, qkv_rows + 8)
    units_a, units_b, units_c = [-(-count // (2 * lon_size * UNIT)) for count in counts]
    extra = -(-BIAS_UNITS // lon_size)

    def units(*lead):
        return (lead + (UNIT, 128), BF16)

    def flat_scr(per):
        return ((2 * lon_size * per * UNIT, 128), F32)

    x0, tail, head, qkv0, mixed0, probs0, resid0, hidden0, active0 = call(
        functools.partial(first_kernel, lat_total),
        [
            (token, BF16),
            ((2, rows - cut, width), BF16),
            ((2, cut, width), BF16),
            field_shape,
            (token, BF16),
            probs_shape,
            (token, BF16),
            ((rows, hid), F32),
            ((rows, hid), BF16),
        ],
        [
            token_scr,
            token_scr,
            tab_scr,
            rows_scr,
            wide_scr,
            bias_shape,
            (cotangent.shape, BF16),
            ((1,) + table.shape[1:], F32),
            (spread.shape, BF16),
            (tokens.shape, BF16),
            ((1,) + qkv_weight.shape[1:], BF16),
            (norm_gain.shape, F32),
            ((1,) + proj_weight.shape[1:], BF16),
            ((1,) + up_weight.shape[1:], BF16),
            ((1,) + down_turned.shape[1:], BF16),
            stack_shape,
            pltpu.SemaphoreType.DMA((9,)),
        ],
        [
            pltpu.with_memory_space_constraint(arg, pltpu.HBM)
            for arg in (
                tokens, cotangent, table, spread, qkv_weight, proj_weight, up_weight, down_turned,
                norm_gain,
            )
        ],
        8,
        16,
        [pltpu.HBM] * 9,
        near=(0, 3, 4, 5, 6, 8),
    )
    lon_head = lon_send(head, -1)
    diag_head = diag_send(head, -1)
    lat_tail = lat_swap(tail)
    bias1, slope0 = call(
        functools.partial(bias_kernel, lat_total),
        [bias_shape, ((rows, hid), BF16)],
        [tab_scr, rows_scr, wide_scr],
        (table, spread, hidden0),
        3,
        12,
        near=(1,),
    )

    saved = [x0, qkv0, mixed0, probs0, resid0, active0, slope0]
    (
        dhead, dtail, n1, field1, mixed1, low1, n2, hg1, active1, g1, sums1, gains1,
        *saved,
    ) = call(
        functools.partial(second_kernel, lat_total, len(saved)),
        [
            ((rows - cut, width), BF16),
            ((cut, width), BF16),
            (token, BF16),
            field_shape,
            (token, BF16),
            (token, BF16),
            (token, BF16),
            ((rows, hid), BF16),
            ((rows, hid), BF16),
            (token, BF16),
            sums_shape,
            ((2, width), F32),
            *[(value.shape, value.dtype) for value in saved],
        ],
        [
            (token, F32),
            (token, F32),
            field_shape,
            probs_shape,
            (token, BF16),
            stack_shape,
            stack_shape,
        ],
        (
            tail, lon_head, lat_tail, diag_head, bias1, qkv_weight, proj_weight, up_weight,
            down_turned, norm_gain,
            *[pltpu.with_memory_space_constraint(value, pltpu.VMEM) for value in saved],
        ),
        19,
        16,
        [pltpu.VMEM] * 10 + [pl.ANY] * len(saved),
        near=tuple(range(12, 12 + len(saved))),
        kept=len(saved),
    )
    x0, qkv0, mixed0, probs0, resid0, active0, slope0 = saved
    lon_tail = lon_send(dtail, 1)
    diag_tail = diag_send(dtail, 1)
    lat_dhead = lat_swap(dhead)

    keep_a, give_a, bias_a = call(
        outer_kernel,
        [units(lon_size, units_a), units(lon_size, units_a), units(lon_size, extra)],
        [m576, m192, m768, mdown, flat_scr(units_a)],
        (n1, field1, mixed1, low1, n2, hg1, active1, g1, sums1),
        0.01,
        14,
    )
    got_a = lat_swap(give_a)

    units_xa = units_a + extra
    keep_xa, give_xa = call(
        lat_sums_split, [units(zs, units_xa)] * 2, [], (keep_a, got_a, bias_a, keep_a), 0.01, 10
    )
    got_xa = x_swap(give_xa)

    keep_b, give_b, rg0, dmix0, gain_two = call(
        third_kernel,
        [
            units(lon_size, units_b),
            units(lon_size, units_b),
            (token, F32),
            (token, BF16),
            ((1, width), F32),
        ],
        [(token, F32), (token, F32), m192, m768, mdown, flat_scr(units_b)],
        (
            dhead, lon_tail, lat_dhead, diag_tail, resid0, slope0, active0, mixed0, proj_weight,
            up_weight, down_turned, norm_gain, keep_xa,
        ),
        3,
        14,
    )
    got_b = lat_swap(give_b)

    tokens_grad, keep_c, give_c, bias_c = call(
        fourth_kernel,
        [
            (tokens.shape, BF16),
            units(lon_size, units_c),
            units(lon_size, units_c),
            units(lon_size, extra),
        ],
        [
            field_shape,
            sums_shape,
            m576,
            flat_scr(units_c),
            token_scr,
            stack_shape,
            stack_shape,
        ],
        (x0, qkv0, probs0, dmix0, rg0, gain_two, gains1, qkv_weight, norm_gain),
        7,
        14,
    )
    got_c = lat_swap(give_c)
    own_a, *gives_a = call(
        split_z, [units(units_xa)] * zs, [], (keep_xa, got_xa), 1, 10
    )
    gots_a = [lon_send(give, 2 * (k + 1)) for k, give in enumerate(gives_a)]
    units_bc = units_b + units_c + extra
    keep_x, give_x = call(
        lat_sums_split,
        [units(zs, units_bc)] * 2,
        [],
        (keep_b, got_b, keep_c, got_c, bias_c, own_a),
        1,
        10,
    )
    got_x = x_swap(give_x)
    (sum_a,) = call(sum_refs, [units(units_xa)], [], (own_a, *gots_a, keep_x), 1, 10)
    (part_z,) = call(add_pair, [units(zs, units_bc)], [], (keep_x, got_x, sum_a), 1, 10)
    pieces_bc = lax.all_to_all(
        part_z,
        "lon",
        0,
        0,
        axis_index_groups=[[2 * z + x for z in range(zs)] for x in range(2)],
    )
    moved_a = [lon_send(sum_a, 2 * k) for k in range(1, zs)]
    (same,) = call(join_z, [units(zs, units_xa)], [], [sum_a, *moved_a, part_z], 1, 10)
    same_x = x_swap(same)
    cross = lat_swap(same)
    cross_x = lat_swap(same_x)
    (sum_bc,) = call(
        sum_pieces, [units(lon_size, units_bc)], [], (pieces_bc, moved_a[0]), 1, 10
    )
    whole_bc = lax.all_to_all(sum_bc, "lon", 0, 0)
    oth_bc = lat_swap(whole_bc)

    flat_rows = (2 * block_rows * 128 + norm_gain.size) // 128
    fold_scr = [((CHUNK * 8, PAIR), F32), wide_scr, tab_scr]
    flat_a, squares, bias_late = call(
        functools.partial(late_kernel, units_a),
        [((block_rows, 128), F32), ((UNIT, 128), F32), (table.shape[1:], F32)],
        [*fold_scr, units(2, lon_size, units_a + extra)],
        (spread, same, same_x, cross, cross_x),
        2,
        14,
    )
    flat_bc, squares_bc, bias_near = call(
        functools.partial(near_kernel, units_b, units_c),
        [((block_rows + 8, 128), F32), ((UNIT, 128), F32), (table.shape[1:], F32)],
        [*fold_scr, units(2, lon_size, units_bc)],
        (spread, whole_bc, oth_bc),
        20,
        14,
    )
    update, bias_grad = call(
        last_kernel,
        [((flat_rows, 128), BF16), (table.shape, F32)],
        [],
        (flat_a, squares, bias_late, flat_bc, squares_bc, bias_near),
        2,
        14,
    )
    bias_grad = jnp.swapaxes(bias_grad, 1, 2)
    return (tokens_grad, update.reshape(-1), bias_grad)


def solution(mesh):
    return jax.shard_map(
        shards,
        mesh=mesh,
        in_specs=(
            P("grp", "lat", "lon", None),
            P("grp", "lat", "lon", None),
            P(),
            P(),
            P(),
            P(),
            P(),
            P(None, "lat", None, None),
        ),
        out_specs=(P("grp", "lat", "lon", None), P("grp"), P("grp", "lat", None, None)),
        check_vma=False,
    )
```
